32 devices in a mesh: seq: 4 (over z), ctx: 8 (over y, x, core).
Axes of the slice: x: 2, y: 2, z: 4, core: 2. Of those that a mesh axis runs over, the one named last changes fastest.
Arguments:
- hidden_in: bfloat16 [8, 1024, 2304], P('seq', 'ctx'), may hold values from -8 to 8
- norm_gains: bfloat16 [2304, 4], P(('seq', 'ctx')), may hold values from 0.25 to 1.75
- qkv_weight: bfloat16 [2304, 4096], P(('seq', 'ctx')), may hold values from -1 to 1
- out_weight: bfloat16 [2304, 2048], P(('seq', 'ctx')), may hold values from -0.125 to 0.125
- gate_up_weight: bfloat16 [9216, 4608], P(('seq', 'ctx')), may hold values from -0.125 to 0.125
- down_weight: bfloat16 [9216, 2304], P(('seq', 'ctx')), may hold values from -0.0625 to 0.0625
- output_cotangent: bfloat16 [8, 1024, 2304], P('seq', 'ctx'), may hold values from -6 to 6
- segment_ids: int32 [8, 1024], P('seq'), may hold values from 0 to 18, as said below
- padding: int32 [8, 1024], P('seq'), may hold values from 0 to 1, as said below
- positions: int32 [8, 1024], P('seq', 'ctx'), may hold values from 0 to 962, as said below
Outputs:
- layer_output: bfloat16 [8, 1024, 2304], P('seq', 'ctx')
- input_grad: float32 [8, 1024, 2304], P('seq', 'ctx')
- gain_grad: float32 [2304, 4], P(('seq', 'ctx'))
- qkv_grad: float32 [2304, 4096], P(('seq', 'ctx'))
- out_proj_grad: float32 [2304, 2048], P(('seq', 'ctx'))
- gate_up_grad: float32 [9216, 4608], P(('seq', 'ctx'))
- down_grad: float32 [9216, 2304], P(('seq', 'ctx'))
The draws below stay inside these ranges and needn't reach their ends.
Inputs may be any that keep to these rules, and one draw needn't show every extreme that they name: `segment_ids`: in each sequence the ids count its documents from 0 in order, and every padding token has id 18. Of the 2 sequences of each index of seq, one holds a first document of 60 to 127 tokens and then a single document that runs into the sequence's last 64 tokens; the others are packed with documents of 60 to 800 tokens, the last of them cut where the padding begins. Every sequence ends in 1 to 64 padding tokens. `padding`: 1 exactly on the tokens whose id is below 18. `positions`: each token's offset from the first token of its document, or of the padding of its sequence.
All inputs are finite; a program needn't handle non-finite values.
Results may differ from the reference program's by a relative error of at most 0.01.
Values may be sent and summed in bfloat16 or wider, within the bound.
A program may use at most 896 MiB of HBM per device.

```python
import math
from functools import partial
import jax
import jax.numpy as jnp
from jax import lax

D = 2304
HEADS = 8
KV_HEADS = 4
HEAD_DIM = 256
FF = 9216
SEQ_LEN = 1024
SEQ_GROUP = 2
DOC_MIN = 60
DOC_MAX = 800
PIECE = 128
SEQS = 8
TOKENS = 8192
MAX_DOCS = 18
N_SEQ = 4


def packing_layout(key):
    half_piece = PIECE // 2
    lengths = jax.random.randint(jax.random.fold_in(key, 101), (SEQS, MAX_DOCS), DOC_MIN, DOC_MAX + 1)
    pad_len = jax.random.randint(jax.random.fold_in(key, 102), (SEQS, 1), 1, half_piece + 1)
    lead_len = jax.random.randint(jax.random.fold_in(key, 103), (SEQS, 1), DOC_MIN, PIECE)
    long_member = jax.random.randint(jax.random.fold_in(key, 104), (N_SEQ, 1), 0, SEQ_GROUP)
    chosen_group = jax.random.randint(jax.random.fold_in(key, 105), (), 0, N_SEQ)
    seq_index = jnp.arange(SEQS, dtype=jnp.int32)[:, None]
    group_index = seq_index // SEQ_GROUP
    member = seq_index % SEQ_GROUP
    is_long = member == jnp.repeat(long_member, SEQ_GROUP, axis=0)
    forced = is_long & (group_index == chosen_group)
    lead_len = jnp.where(forced, DOC_MIN, lead_len)
    pad_len = jnp.where(forced, 1, pad_len)
    doc_index = jnp.arange(MAX_DOCS, dtype=jnp.int32)[None, :]
    packed_ends = jnp.cumsum(lengths, axis=1)
    long_ends = jnp.where(doc_index == 0, lead_len, SEQ_LEN + doc_index)
    doc_ends = jnp.where(is_long, long_ends, packed_ends).astype(jnp.int32)
    where_row = jnp.arange(SEQ_LEN, dtype=jnp.int32)[None, None, :]
    has_ended = doc_ends[:, :, None] <= where_row
    doc_number = jnp.sum(has_ended.astype(jnp.int32), axis=1)
    doc_start = jnp.max(jnp.where(has_ended, doc_ends[:, :, None], 0), axis=1)
    pad_start = SEQ_LEN - pad_len
    flat_row = jnp.arange(SEQ_LEN, dtype=jnp.int32)[None, :]
    in_pad = flat_row >= pad_start
    segment = jnp.where(in_pad, MAX_DOCS, doc_number).astype(jnp.int32)
    offsets = jnp.where(in_pad, flat_row - pad_start, flat_row - doc_start).astype(jnp.int32)
    return (segment, offsets)


def shared_direction(key):
    return jnp.clip(jax.random.normal(jax.random.fold_in(key, 7), (D,), jnp.float32), -3.0, 3.0)


def draw_segment_ids(key, part):
    segment, offsets = packing_layout(key)
    return segment


def draw_padding(key, part):
    segment, offsets = packing_layout(key)
    return (segment < MAX_DOCS).astype(jnp.int32)


def draw_positions(key, part):
    segment, offsets = packing_layout(key)
    return offsets


def draw_hidden_in(key, part):
    direction = shared_direction(key)
    key = jax.random.fold_in(key, 11)
    noise_part = jnp.clip(jax.random.normal(key, (SEQS, SEQ_LEN, D), jnp.float32), -5.0, 5.0)
    return (noise_part + direction[None, None, :]).astype(jnp.bfloat16)


def draw_qkv_weight(key, part):
    direction = shared_direction(key)
    key = jax.random.fold_in(key, 12)
    head_count = HEADS + 2 * KV_HEADS
    random_part = jnp.clip(jax.random.normal(jax.random.fold_in(key, 1), (D, head_count * HEAD_DIM), jnp.float32), -6.0, 6.0) * D ** (-0.5)
    half_dim = HEAD_DIM // 2
    low_pairs = HEAD_DIM // 16
    dim_index = jnp.arange(HEAD_DIM, dtype=jnp.int32)
    in_low = dim_index % half_dim >= half_dim - low_pairs
    sign_flip = jnp.where(jax.random.bernoulli(jax.random.fold_in(key, 2), 0.5, (HEAD_DIM,)), 1.0, -1.0)
    pattern = jnp.where(in_low, sign_flip, 0.0) * (2 * low_pairs) ** (-0.5)
    fourth_root = HEAD_DIM ** 0.25
    query_amp = jax.random.uniform(jax.random.fold_in(key, 3), (HEADS,), jnp.float32, 0.0, 12.0) * fourth_root
    key_amp = jnp.full((KV_HEADS,), 10.0 * fourth_root, jnp.float32)
    value_amp = jnp.zeros((KV_HEADS,), jnp.float32)
    head_amp = jnp.concatenate([query_amp, key_amp, value_amp])
    column_amp = (head_amp[:, None] * pattern[None, :]).reshape(head_count * HEAD_DIM)
    return (random_part + direction[:, None] * column_amp[None, :] * (1.0 / D)).astype(jnp.bfloat16)


def shard_levels(stream_key, dims, shards, least, largest):
    def one(axis_at, shards_of):
        steps = jax.random.uniform(jax.random.fold_in(jax.random.fold_in(stream_key, 6), axis_at), (shards_of,), jnp.float32, least / len(shards), largest / len(shards))
        return jnp.repeat(jnp.exp(steps), dims[axis_at] // shards_of).reshape((-1,) + (1,) * (len(dims) - axis_at - 1))

    loudness = one(*shards[0])
    for cut in shards[1:]:
        loudness = loudness * one(*cut)
    return loudness


def normal_values(stream_key, shape, deviation, most, shards=(), held_as=jnp.bfloat16):
    values = jax.random.normal(stream_key, shape, jnp.float32) * deviation
    if len(shards) > 0:
        values = shard_levels(stream_key, shape, shards, -0.22, 0.18) * values
    return jnp.clip(values, min=-most, max=most).astype(held_as)


def setup_inputs(seed: int = 0) -> dict:
    splits = jax.random.split(jax.random.key(seed), 11)
    hidden_in = draw_hidden_in(jax.random.fold_in(splits[10], 71), 0)
    norm_gains = jnp.clip(1.0 + 0.15 * jax.random.normal(splits[1], (D, 4), jnp.float32), 0.25, 1.75).astype(jnp.bfloat16)
    qkv_weight = draw_qkv_weight(jax.random.fold_in(splits[10], 71), 0)
    out_weight = normal_values(splits[3], (D, HEADS * HEAD_DIM), (HEADS * HEAD_DIM) ** -0.5, 0.125, ((0, 32),))
    gate_up_weight = normal_values(splits[4], (FF, 2 * D), D ** -0.5, 0.125, ((0, 32),))
    down_weight = normal_values(splits[5], (FF, D), FF ** -0.5, 0.0625, ((0, 32),))
    output_cotangent = normal_values(splits[6], (SEQS, SEQ_LEN, D), 1.0, 6.0, ((0, 4), (1, 8)))
    segment_ids = draw_segment_ids(jax.random.fold_in(splits[10], 71), 0)
    padding = draw_padding(jax.random.fold_in(splits[10], 71), 0)
    positions = draw_positions(jax.random.fold_in(splits[10], 71), 0)
    return dict(hidden_in=hidden_in, norm_gains=norm_gains, qkv_weight=qkv_weight, out_weight=out_weight, gate_up_weight=gate_up_weight, down_weight=down_weight, output_cotangent=output_cotangent, segment_ids=segment_ids, padding=padding, positions=positions)


EPSILON = 1e-06
SOFT_CAP = 50.0
MASKED = -1e+30
HIGHEST = lax.Precision.HIGHEST

@jax.custom_vjp
def low(v):
    return lax.optimization_barrier(v.astype(jnp.bfloat16)).astype(jnp.float32)

@jax.custom_vjp
def low_back(v):
    return v

def low_keep(v):
    return (low(v), None)

def low_pass(kept, grad):
    return (grad,)

def back_keep(v):
    return (v, None)

def back_low(kept, grad):
    return (low(grad),)
low.defvjp(low_keep, low_pass)
low_back.defvjp(back_keep, back_low)

def rms_norm(matrix, gain_col):
    factor = lax.rsqrt(lax.optimization_barrier(jnp.mean(matrix * matrix, axis=-1, keepdims=True)) + EPSILON)
    return matrix * factor * gain_col

def rotary_tables(positions, head_dim):
    half_dim = head_dim // 2
    frequency = jnp.exp(jnp.arange(half_dim, dtype=jnp.float32) * (-2.0 * math.log(10000.0) / head_dim))
    phase_angle = positions.astype(jnp.float32)[:, None] * frequency[None, :]
    return (jnp.cos(phase_angle)[:, None, :], jnp.sin(phase_angle)[:, None, :])

def rotate(vectors, cosine, sine_part):
    half_dim = vectors.shape[-1] // 2
    first_half = vectors[..., :half_dim]
    second_half = vectors[..., half_dim:]
    return jnp.concatenate([first_half * cosine - second_half * sine_part, second_half * cosine + first_half * sine_part], axis=-1)

def soft_probs(scaled, allowed):
    capped = SOFT_CAP * jnp.tanh(scaled / SOFT_CAP)
    capped = jnp.where(allowed, capped, MASKED)
    return jax.nn.softmax(capped, axis=-1)

def attend(seq_block):
    queries, keys, values, segment_row, valid_row = seq_block
    group_size = HEADS // KV_HEADS
    keys_all = jnp.repeat(keys, group_size, axis=1)
    values_all = jnp.repeat(values, group_size, axis=1)
    raw_score = jnp.einsum('qhd,khd->hqk', queries, keys_all, precision=HIGHEST)
    scaled = low_back(raw_score * (1.0 / math.sqrt(HEAD_DIM)))
    where_row = jnp.arange(SEQ_LEN, dtype=jnp.int32)
    allowed = (segment_row[:, None] == segment_row[None, :]) & (where_row[None, :] <= where_row[:, None]) & (valid_row[None, :] == 1) | (where_row[:, None] == where_row[None, :])
    probs = soft_probs(scaled, allowed[None])
    return jnp.einsum('hqk,khd->qhd', low(probs), values_all, precision=HIGHEST)

def feed_forward(ffn_input, gate_matrix, down_matrix):
    gate_part = jnp.dot(ffn_input, gate_matrix[:, :D].T, precision=HIGHEST)
    up_part = jnp.dot(ffn_input, gate_matrix[:, D:].T, precision=HIGHEST)
    gate_up = low_back(jnp.concatenate([gate_part, up_part], axis=1))
    ffn_hidden = low(jax.nn.gelu(gate_up[:, :FF], approximate=True) * gate_up[:, FF:])
    return low_back(jnp.dot(ffn_hidden, down_matrix, precision=HIGHEST))

def layer(hidden, gain_cols, qkv_matrix, out_matrix, gate_matrix, down_matrix, segment_ids, padding, positions):
    query_width = HEADS * HEAD_DIM
    key_width = KV_HEADS * HEAD_DIM
    flat_hidden = hidden.reshape(TOKENS, D)
    cosine, sine_part = rotary_tables(positions.reshape(TOKENS), HEAD_DIM)
    attn_input = low(rms_norm(flat_hidden, gain_cols[:, 0]))
    projected = low_back(jnp.dot(attn_input, qkv_matrix, precision=HIGHEST))
    queries = low(rotate(projected[:, :query_width].reshape(TOKENS, HEADS, HEAD_DIM), cosine, sine_part))
    keys = low(rotate(projected[:, query_width:query_width + key_width].reshape(TOKENS, KV_HEADS, HEAD_DIM), cosine, sine_part))
    values = low(projected[:, query_width + key_width:]).reshape(TOKENS, KV_HEADS, HEAD_DIM)
    blocks = (queries.reshape(SEQS, SEQ_LEN, HEADS, HEAD_DIM), keys.reshape(SEQS, SEQ_LEN, KV_HEADS, HEAD_DIM), values.reshape(SEQS, SEQ_LEN, KV_HEADS, HEAD_DIM), segment_ids, padding)
    attended = lax.map(jax.checkpoint(attend), blocks)
    attn_out = low(low_back(attended.reshape(TOKENS, query_width)))
    attn_proj = low_back(jnp.dot(attn_out, out_matrix.T, precision=HIGHEST))
    after_attn = flat_hidden + rms_norm(attn_proj, gain_cols[:, 1])
    ffn_input = low(rms_norm(after_attn, gain_cols[:, 2]))
    checkpointed = jax.checkpoint(feed_forward)

    def ffn_block(block):
        return checkpointed(block, gate_matrix, down_matrix)
    down_out = lax.map(ffn_block, ffn_input.reshape(SEQS, SEQ_LEN, D)).reshape(TOKENS, D)
    result = after_attn + rms_norm(down_out, gain_cols[:, 3])
    return result.reshape(SEQS, SEQ_LEN, D)

def reference(hidden_in, norm_gains, qkv_weight, out_weight, gate_up_weight, down_weight, output_cotangent, segment_ids, padding, positions):
    floats = tuple((array.astype(jnp.float32) for array in (hidden_in, norm_gains, qkv_weight, out_weight, gate_up_weight, down_weight)))
    layer_fn = partial(layer, segment_ids=segment_ids, padding=padding, positions=positions)
    layer_out, pullback = jax.vjp(layer_fn, *floats)
    gradients = pullback(output_cotangent.astype(jnp.float32))
    return (layer_out.astype(jnp.bfloat16), gradients[0], gradients[1], gradients[2], gradients[3], gradients[4], gradients[5])
```

```python
from functools import partial
import math

import jax
import jax.numpy as jnp
from jax import lax
from jax.sharding import PartitionSpec as P

HEADS = 8
KV_HEADS = 4
HEAD_DIM = 256


EPSILON = 1e-06
SOFT_CAP = 50.0
MASKED = -1e30


def rms_norm(matrix, gain_col):
    factor = lax.rsqrt(jnp.mean(matrix * matrix, axis=-1, keepdims=True) + EPSILON)
    return matrix * factor * gain_col


def rotary_tables(positions, head_dim):
    half_dim = head_dim // 2
    frequency = jnp.exp(
        jnp.arange(half_dim, dtype=jnp.float32) * (-2.0 * math.log(10000.0) / head_dim)
    )
    phase_angle = positions.astype(jnp.float32)[:, None] * frequency[None, :]
    return (jnp.cos(phase_angle)[:, None, :], jnp.sin(phase_angle)[:, None, :])


def rotate(vectors, cosine, sine_part):
    half_dim = vectors.shape[-1] // 2
    first_half = vectors[..., :half_dim]
    second_half = vectors[..., half_dim:]
    return jnp.concatenate(
        [
            first_half * cosine - second_half * sine_part,
            second_half * cosine + first_half * sine_part,
        ],
        axis=-1,
    )


def rotate_back(grads, cosine, sine_part):
    half_dim = grads.shape[-1] // 2
    first_half = grads[..., :half_dim]
    second_half = grads[..., half_dim:]
    return jnp.concatenate(
        [
            first_half * cosine + second_half * sine_part,
            second_half * cosine - first_half * sine_part,
        ],
        axis=-1,
    )


def soft_probs(scaled, allowed):
    capped = SOFT_CAP * jnp.tanh(scaled / SOFT_CAP)
    capped = jnp.where(allowed, capped, MASKED)
    return jax.nn.softmax(capped, axis=-1)


def geglu_parts(gate_part, up_part):
    return jax.nn.gelu(gate_part, approximate=True) * up_part


def score_block(queries, keys_all):
    groups = keys_all.shape[0]
    seq_len = keys_all.shape[1]
    piece_len = queries.shape[0] // groups
    query_heads = queries.reshape(groups, piece_len, KV_HEADS, HEADS // KV_HEADS, HEAD_DIM)
    key_heads = keys_all.reshape(groups, seq_len, KV_HEADS, HEAD_DIM)
    raw_score = jnp.einsum(
        "spkgd,slkd->skgpl", query_heads, key_heads, preferred_element_type=jnp.float32
    )
    return raw_score * (1.0 / math.sqrt(HEAD_DIM))


def mix_values(weights_low, values_all):
    groups = values_all.shape[0]
    seq_len = values_all.shape[1]
    piece_len = weights_low.shape[3]
    value_heads = values_all.reshape(groups, seq_len, KV_HEADS, HEAD_DIM)
    mixed = jnp.einsum(
        "skgpl,slkd->spkgd", weights_low, value_heads, preferred_element_type=jnp.float32
    )
    return mixed.reshape(groups * piece_len, HEADS * HEAD_DIM).astype(jnp.bfloat16)


def add_slice(left, weight_piece):
    return jnp.dot(left, weight_piece, preferred_element_type=jnp.float32)


def times_rows(left, weight_piece):
    return lax.dot_general(
        left, weight_piece, (((1,), (1,)), ((), ())), preferred_element_type=jnp.float32
    )


def outer_rows(left, right):
    return lax.dot_general(
        left, right, (((0,), (0,)), ((), ())), preferred_element_type=jnp.float32
    )


def per_device(
    hidden_in,
    norm_gains,
    qkv_weight,
    out_weight,
    gate_up_weight,
    down_weight,
    output_cotangent,
    segment_ids,
    padding,
    positions,
):
    everyone = ("seq", "chip", "core")
    plane = ("chip", "core")
    column = ("seq", "core")
    groups = hidden_in.shape[0]
    piece_len = hidden_in.shape[1]
    model_width = hidden_in.shape[2]
    row_count = groups * piece_len
    seq_len = segment_ids.shape[1]
    group_size = HEADS // KV_HEADS
    query_width = HEADS * HEAD_DIM
    key_width = KV_HEADS * HEAD_DIM
    proj_width = qkv_weight.shape[1]

    residual = hidden_in.reshape(row_count, model_width).astype(jnp.float32)
    factor = lax.rsqrt(jnp.mean(residual * residual, axis=-1, keepdims=True) + EPSILON)
    gain_cols = lax.all_gather(norm_gains, everyone, axis=0, tiled=True).astype(jnp.float32)
    qkv_full = lax.all_gather(qkv_weight, everyone, axis=0, tiled=True)
    attn_input = (residual * factor * gain_cols[:, 0]).astype(jnp.bfloat16)
    projected = add_slice(attn_input, qkv_full)
    cosine, sine_part = rotary_tables(positions.reshape(row_count), HEAD_DIM)
    queries = (
        rotate(projected[:, :query_width].reshape(row_count, HEADS, HEAD_DIM), cosine, sine_part)
        .astype(jnp.bfloat16)
        .reshape(row_count, query_width)
    )
    keys_here = (
        rotate(
            projected[:, query_width : query_width + key_width].reshape(
                row_count, KV_HEADS, HEAD_DIM
            ),
            cosine,
            sine_part,
        )
        .astype(jnp.bfloat16)
        .reshape(groups, piece_len, key_width)
    )
    values_here = (
        projected[:, query_width + key_width :]
        .astype(jnp.bfloat16)
        .reshape(groups, piece_len, key_width)
    )
    both_all = lax.all_gather(
        jnp.concatenate([keys_here, values_here], axis=2), plane, axis=1, tiled=True
    )
    keys_all = both_all[:, :, :key_width]
    values_all = both_all[:, :, key_width:]
    first_query = (lax.axis_index("chip") * 2 + lax.axis_index("core")) * piece_len
    query_rows = first_query + jnp.arange(piece_len, dtype=jnp.int32)
    key_rows = jnp.arange(seq_len, dtype=jnp.int32)
    segment_query = lax.dynamic_slice_in_dim(segment_ids, first_query, piece_len, 1)
    allowed = (segment_query[:, :, None] == segment_ids[:, None, :]) & (
        key_rows[None, None, :] <= query_rows[None, :, None]
    ) & (padding[:, None, :] == 1) | (key_rows[None, None, :] == query_rows[None, :, None])
    allowed = allowed[:, None, None]
    probs = soft_probs(score_block(queries, keys_all), allowed)
    attn_out = mix_values(probs.astype(jnp.bfloat16), values_all)
    out_full = lax.all_gather(out_weight, everyone, axis=0, tiled=True)
    attn_proj = times_rows(attn_out, out_full)
    after_attn = residual + rms_norm(attn_proj, gain_cols[:, 1])
    ffn_input = rms_norm(after_attn, gain_cols[:, 2]).astype(jnp.bfloat16)

    unit_weights = lax.all_gather(gate_up_weight, "chip", axis=0, tiled=True)
    down_units = lax.all_gather(down_weight, "chip", axis=0, tiled=True)
    ffn_all = lax.all_gather(ffn_input, column, axis=0, tiled=True)
    gate_part = times_rows(ffn_all, unit_weights[:, :model_width])
    up_part = times_rows(ffn_all, unit_weights[:, model_width:])
    hidden_part = geglu_parts(gate_part, up_part).astype(jnp.bfloat16)
    down_part = add_slice(hidden_part, down_units).astype(jnp.bfloat16)
    down_out = lax.psum_scatter(down_part, column, scatter_dimension=0, tiled=True).astype(
        jnp.float32
    )
    layer_out = after_attn + rms_norm(down_out, gain_cols[:, 3])
    layer_output = layer_out.astype(jnp.bfloat16).reshape(groups, piece_len, model_width)

    cotangent = output_cotangent.reshape(row_count, model_width).astype(jnp.float32)
    unused_last, pull_last = jax.vjp(rms_norm, down_out, gain_cols[:, 3])
    grad_down, grad_gain_last = pull_last(cotangent)
    grad_down_low = grad_down.astype(jnp.bfloat16)
    grad_down_all = lax.all_gather(grad_down_low, column, axis=0, tiled=True)
    grad_part = times_rows(grad_down_all, down_units)
    unused_units, pull_units = jax.vjp(geglu_parts, gate_part, up_part)
    grad_gate_part, grad_up_part = pull_units(grad_part)
    gate_low = grad_gate_part.astype(jnp.bfloat16)
    up_low = grad_up_part.astype(jnp.bfloat16)
    grad_ffn_part = add_slice(gate_low, unit_weights[:, :model_width]) + add_slice(
        up_low, unit_weights[:, model_width:]
    )
    grad_ffn_in = lax.psum_scatter(
        grad_ffn_part.astype(jnp.bfloat16), column, scatter_dimension=0, tiled=True
    ).astype(jnp.float32)
    gate_up_rows = jnp.concatenate(
        [
            outer_rows(gate_low, ffn_all).astype(jnp.bfloat16),
            outer_rows(up_low, ffn_all).astype(jnp.bfloat16),
        ],
        axis=1,
    )
    down_rows = outer_rows(hidden_part, grad_down_all).astype(jnp.bfloat16)
    gate_up_grad = lax.psum_scatter(
        gate_up_rows, "chip", scatter_dimension=0, tiled=True
    ).astype(jnp.float32)
    down_grad = lax.psum_scatter(down_rows, "chip", scatter_dimension=0, tiled=True).astype(
        jnp.float32
    )

    unused_mid, pull_mid = jax.vjp(rms_norm, after_attn, gain_cols[:, 2])
    grad_after_ffn, grad_gain_mid = pull_mid(grad_ffn_in)
    grad_after = cotangent + grad_after_ffn
    unused_post, pull_post = jax.vjp(rms_norm, attn_proj, gain_cols[:, 1])
    grad_proj, grad_gain_post = pull_post(grad_after)
    grad_proj_low = grad_proj.astype(jnp.bfloat16)
    grad_attn = add_slice(grad_proj_low, out_full).astype(jnp.bfloat16)
    scaled = score_block(queries, keys_all)
    probs, pull_probs = jax.vjp(partial(soft_probs, allowed=allowed), scaled)
    grad_heads = grad_attn.reshape(groups, piece_len, KV_HEADS, group_size, HEAD_DIM)
    query_heads = queries.reshape(groups, piece_len, KV_HEADS, group_size, HEAD_DIM)
    key_heads = keys_all.reshape(groups, seq_len, KV_HEADS, HEAD_DIM)
    value_heads = values_all.reshape(groups, seq_len, KV_HEADS, HEAD_DIM)
    grad_probs = jnp.einsum(
        "spkgd,slkd->skgpl", grad_heads, value_heads, preferred_element_type=jnp.float32
    )
    (grad_scaled,) = pull_probs(grad_probs)
    grad_scaled_low = grad_scaled.astype(jnp.bfloat16)
    inverse_root = 1.0 / math.sqrt(HEAD_DIM)
    grad_query_rot = (
        jnp.einsum(
            "skgpl,slkd->spkgd", grad_scaled_low, key_heads, preferred_element_type=jnp.float32
        )
        * inverse_root
    )
    grad_key_rot = (
        jnp.einsum(
            "skgpl,spkgd->slkd", grad_scaled_low, query_heads, preferred_element_type=jnp.float32
        )
        * inverse_root
    )
    grad_value_part = jnp.einsum(
        "skgpl,spkgd->slkd",
        probs.astype(jnp.bfloat16),
        grad_heads,
        preferred_element_type=jnp.float32,
    )
    both_grads = jnp.concatenate(
        [
            grad_key_rot.reshape(groups, seq_len, key_width),
            grad_value_part.reshape(groups, seq_len, key_width),
        ],
        axis=2,
    ).astype(jnp.bfloat16)
    both_summed = lax.psum_scatter(both_grads, plane, scatter_dimension=1, tiled=True)
    both_summed = both_summed.astype(jnp.float32).reshape(row_count, 2 * key_width)
    key_summed = both_summed[:, :key_width]
    value_summed = both_summed[:, key_width:]
    grad_queries = rotate_back(
        grad_query_rot.reshape(row_count, HEADS, HEAD_DIM), cosine, sine_part
    ).reshape(row_count, query_width)
    grad_keys = rotate_back(
        key_summed.reshape(row_count, KV_HEADS, HEAD_DIM), cosine, sine_part
    ).reshape(row_count, key_width)
    grad_projected = jnp.concatenate([grad_queries, grad_keys, value_summed], axis=1).astype(
        jnp.bfloat16
    )
    grad_attn_in = times_rows(grad_projected, qkv_full)
    unused_first, pull_first = jax.vjp(rms_norm, residual, gain_cols[:, 0])
    grad_res_first, grad_gain_first = pull_first(grad_attn_in)
    input_grad = (grad_after + grad_res_first).reshape(groups, piece_len, model_width)
    gain_terms = jnp.stack([grad_gain_first, grad_gain_post, grad_gain_mid, grad_gain_last], axis=1)
    qkv_part = outer_rows(attn_input, grad_projected).astype(jnp.bfloat16)
    out_part = outer_rows(grad_proj_low, attn_out).astype(jnp.bfloat16)
    qkv_grad = lax.psum_scatter(qkv_part, everyone, scatter_dimension=0, tiled=True).astype(
        jnp.float32
    )
    out_proj_grad = lax.psum_scatter(out_part, everyone, scatter_dimension=0, tiled=True).astype(
        jnp.float32
    )
    gain_grad = lax.psum_scatter(gain_terms, everyone, scatter_dimension=0, tiled=True)
    return (layer_output, input_grad, gain_grad, qkv_grad, out_proj_grad, gate_up_grad, down_grad)


def solution(mesh):
    n_seq = mesh.shape["seq"]
    n_ctx = mesh.shape["ctx"]
    split_mesh = jax.sharding.Mesh(
        mesh.devices.reshape(n_seq, n_ctx // 2, 2), ("seq", "chip", "core")
    )
    plane = ("chip", "core")
    rows = P(("seq", "chip", "core"), None)
    tokens = P("seq", plane, None)
    placed = (
        tokens,
        rows,
        rows,
        rows,
        rows,
        rows,
        tokens,
        P("seq", None),
        P("seq", None),
        P("seq", plane),
    )
    return jax.shard_map(
        per_device,
        mesh=split_mesh,
        in_specs=placed,
        out_specs=(tokens, tokens, rows, rows, rows, rows, rows),
        check_vma=False,
    )
```

```python
from functools import partial
import math

import jax
import jax.numpy as jnp
from jax import lax
from jax.experimental import pallas as pl
from jax.experimental.pallas import tpu as pltpu
from jax.sharding import PartitionSpec as P

HEADS = 8
KV_HEADS = 4
HEAD_DIM = 256


EPSILON = 1e-06
SOFT_CAP = 50.0
MASKED = -1e30


def rms_norm(matrix, gain_col):
    factor = lax.rsqrt(jnp.mean(matrix * matrix, axis=-1, keepdims=True) + EPSILON)
    return matrix * factor * gain_col


def rotary_tables(positions, head_dim):
    half_dim = head_dim // 2
    frequency = jnp.exp(
        jnp.arange(half_dim, dtype=jnp.float32) * (-2.0 * math.log(10000.0) / head_dim)
    )
    phase_angle = positions.astype(jnp.float32)[:, None] * frequency[None, :]
    return (jnp.cos(phase_angle)[:, None, :], jnp.sin(phase_angle)[:, None, :])


def rotate(vectors, cosine, sine_part):
    half_dim = vectors.shape[-1] // 2
    first_half = vectors[..., :half_dim]
    second_half = vectors[..., half_dim:]
    return jnp.concatenate(
        [
            first_half * cosine - second_half * sine_part,
            second_half * cosine + first_half * sine_part,
        ],
        axis=-1,
    )


def rotate_back(grads, cosine, sine_part):
    half_dim = grads.shape[-1] // 2
    first_half = grads[..., :half_dim]
    second_half = grads[..., half_dim:]
    return jnp.concatenate(
        [
            first_half * cosine + second_half * sine_part,
            second_half * cosine - first_half * sine_part,
        ],
        axis=-1,
    )


def soft_probs(scaled, allowed):
    capped = SOFT_CAP * jnp.tanh(scaled / SOFT_CAP)
    capped = jnp.where(allowed, capped, MASKED)
    return jax.nn.softmax(capped, axis=-1)


def geglu_parts(gate_part, up_part):
    return jax.nn.gelu(gate_part, approximate=True) * up_part


def score_block(queries, keys_all):
    groups = keys_all.shape[0]
    seq_len = keys_all.shape[1]
    piece_len = queries.shape[0] // groups
    query_heads = queries.reshape(groups, piece_len, KV_HEADS, HEADS // KV_HEADS, HEAD_DIM)
    key_heads = keys_all.reshape(groups, seq_len, KV_HEADS, HEAD_DIM)
    raw_score = jnp.einsum(
        "spkgd,slkd->skgpl", query_heads, key_heads, preferred_element_type=jnp.float32
    )
    return raw_score * (1.0 / math.sqrt(HEAD_DIM))


def mix_values(weights_low, values_all):
    groups = values_all.shape[0]
    seq_len = values_all.shape[1]
    piece_len = weights_low.shape[3]
    value_heads = values_all.reshape(groups, seq_len, KV_HEADS, HEAD_DIM)
    mixed = jnp.einsum(
        "skgpl,slkd->spkgd", weights_low, value_heads, preferred_element_type=jnp.float32
    )
    return mixed.reshape(groups * piece_len, HEADS * HEAD_DIM).astype(jnp.bfloat16)


def add_slice(left, weight_piece):
    return jnp.dot(left, weight_piece, preferred_element_type=jnp.float32)


def times_rows(left, weight_piece):
    return lax.dot_general(
        left, weight_piece, (((1,), (1,)), ((), ())), preferred_element_type=jnp.float32
    )


def outer_rows(left, right):
    return lax.dot_general(
        left, right, (((0,), (0,)), ((), ())), preferred_element_type=jnp.float32
    )


MESH = pl.DeviceIdType.MESH
ANY = pl.BlockSpec(memory_space=pl.ANY)
DMA = pltpu.SemaphoreType.DMA


def remote(source, target, send_sem, recv_sem, device):
    return pltpu.make_async_remote_copy(
        src_ref=source,
        dst_ref=target,
        send_sem=send_sem,
        recv_sem=recv_sem,
        device_id=device,
        device_id_type=MESH,
    )


def plane_device(index):
    return {"chip": index // 2, "core": lax.rem(index, 2)}


def greet(n_plane, n_seq):
    me = lax.axis_index("chip") * 2 + lax.axis_index("core")
    barrier = pltpu.get_barrier_semaphore()
    for step in range(1, n_plane):
        pl.semaphore_signal(
            barrier,
            inc=1,
            device_id=plane_device(lax.rem(me + step, n_plane)),
            device_id_type=MESH,
        )
    count = n_plane - 1
    if n_seq > 1:
        s = lax.axis_index("seq")

        @pl.when(s > 0)
        def _():
            pl.semaphore_signal(barrier, inc=1, device_id={"seq": s - 1}, device_id_type=MESH)

        @pl.when(s < n_seq - 1)
        def _():
            pl.semaphore_signal(barrier, inc=1, device_id={"seq": s + 1}, device_id_type=MESH)

        count = count + jnp.where(s > 0, 1, 0) + jnp.where(s < n_seq - 1, 1, 0)
    pl.semaphore_wait(barrier, count)


def start_exchange(n_plane, by_core, source, target, send_sems, recv_sems, local_sem):
    me = lax.axis_index("chip") * 2 + lax.axis_index("core")
    copies = []
    for step in (4, 2, 6, 3, 5, 1, 7):
        to = lax.rem(me + step, n_plane)
        block = lax.rem(to, 2) if by_core else to
        copy = remote(
            source.at[block],
            target.at[me],
            send_sems.at[step],
            recv_sems.at[step],
            plane_device(to),
        )
        copy.start()
        copies.append(copy)
    block = lax.rem(me, 2) if by_core else me
    own = pltpu.make_async_copy(source.at[block], target.at[me], local_sem.at[0])
    own.start()
    copies.append(own)
    return copies


def exchange_kernel(n_plane, by_core, source, target, send_sems, recv_sems, local_sem):
    greet(n_plane, 1)
    for copy in start_exchange(
        n_plane, by_core, source, target, send_sems, recv_sems, local_sem
    ):
        copy.wait()


def plane_exchange(blocks, by_core, collective_id):
    n_plane = 2 * KV_HEADS
    return pl.pallas_call(
        partial(exchange_kernel, n_plane, by_core),
        out_shape=jax.ShapeDtypeStruct((n_plane,) + blocks.shape[1:], blocks.dtype),
        in_specs=[ANY],
        out_specs=ANY,
        scratch_shapes=[DMA((n_plane,)), DMA((n_plane,)), DMA((1,))],
        compiler_params=pltpu.CompilerParams(
            collective_id=collective_id, has_side_effects=True
        ),
    )(blocks)


def gather_kernel(
    n_seq,
    n_plane,
    hidden,
    blocks,
    hidden_all,
    blocks_all,
    hid_send,
    hid_recv,
    hid_local,
    chip_send,
    chip_recv,
    chip_local,
    left_send,
    right_send,
    line_recv,
    twin_send,
    twin_recv,
):
    n_chip = n_plane // 2
    s = lax.axis_index("seq")
    q = lax.axis_index("chip")
    k = lax.axis_index("core")
    greet(n_plane, n_seq)
    swaps = []
    for step in range(1, n_chip):
        to = lax.rem(q + step, n_chip)
        copy = remote(
            blocks.at[to],
            blocks_all.at[s, k, q],
            chip_send.at[step],
            chip_recv.at[step],
            {"chip": to},
        )
        copy.start()
        swaps.append(copy)
    own = pltpu.make_async_copy(blocks.at[q], blocks_all.at[s, k, q], chip_local.at[0])
    own.start()
    hidden_copies = start_exchange(
        n_plane, True, hidden, hidden_all, hid_send, hid_recv, hid_local
    )
    for copy in swaps:
        copy.wait_recv()
    own.wait()

    def to_left(d):
        return remote(
            blocks_all.at[d, k], blocks_all.at[d, k], left_send.at[d], line_recv.at[d], {"seq": s - 1}
        )

    def to_right(d):
        return remote(
            blocks_all.at[d, k], blocks_all.at[d, k], right_send.at[d], line_recv.at[d], {"seq": s + 1}
        )

    def to_twin(d):
        return remote(
            blocks_all.at[d, k], blocks_all.at[d, k], twin_send.at[d], twin_recv.at[d], {"core": 1 - k}
        )

    def from_twin(d):
        return remote(
            blocks_all.at[d, 1 - k],
            blocks_all.at[d, 1 - k],
            twin_send.at[d],
            twin_recv.at[d],
            {"core": 1 - k},
        )

    @pl.when(s > 0)
    def _():
        to_left(s).start()

    @pl.when(s < n_seq - 1)
    def _():
        to_right(s).start()

    to_twin(s).start()
    for hop in range(1, n_seq):
        from_left = s - hop
        from_right = s + hop

        @pl.when(from_left >= 0)
        def _():
            to_left(from_left).wait_recv()

            @pl.when(s < n_seq - 1)
            def _():
                to_right(from_left).start()

            to_twin(from_left).start()

        @pl.when(from_right < n_seq)
        def _():
            to_right(from_right).wait_recv()

            @pl.when(s > 0)
            def _():
                to_left(from_right).start()

            to_twin(from_right).start()

    for d in range(n_seq):

        @pl.when((d >= s) & (s > 0))
        def _():
            to_left(d).wait_send()

        @pl.when((d <= s) & (s < n_seq - 1))
        def _():
            to_right(d).wait_send()

        to_twin(d).wait_send()
        from_twin(d).wait_recv()
    for copy in swaps:
        copy.wait_send()
    for copy in hidden_copies:
        copy.wait()


def gather_first(n_seq, hidden, blocks):
    n_plane = 2 * KV_HEADS
    n_chip = KV_HEADS
    return pl.pallas_call(
        partial(gather_kernel, n_seq, n_plane),
        out_shape=[
            jax.ShapeDtypeStruct((n_plane,) + hidden.shape[1:], hidden.dtype),
            jax.ShapeDtypeStruct((n_seq, 2) + blocks.shape, blocks.dtype),
        ],
        in_specs=[ANY, ANY],
        out_specs=[ANY, ANY],
        scratch_shapes=[
            DMA((n_plane,)),
            DMA((n_plane,)),
            DMA((1,)),
            DMA((n_chip,)),
            DMA((n_chip,)),
            DMA((1,)),
            DMA((n_seq,)),
            DMA((n_seq,)),
            DMA((n_seq,)),
            DMA((n_seq,)),
            DMA((n_seq,)),
        ],
        compiler_params=pltpu.CompilerParams(collective_id=1, has_side_effects=True),
    )(hidden, blocks)


def last_kernel(
    n_seq,
    n_plane,
    parts,
    blocks,
    parts_all,
    sums,
    held,
    twin,
    line,
    part_send,
    part_recv,
    part_local,
    held_sem,
    twin_send,
    twin_recv,
    line_send,
    line_recv,
    chip_send,
    chip_recv,
    chip_local,
):
    n_chip = n_plane // 2
    s = lax.axis_index("seq")
    q = lax.axis_index("chip")
    k = lax.axis_index("core")
    greet(n_plane, n_seq)

    def load(d):
        return pltpu.make_async_copy(blocks.at[d, k], held.at[d], held_sem.at[d])

    def to_twin(d):
        return remote(
            blocks.at[d, 1 - k], twin.at[d], twin_send.at[d], twin_recv.at[d], {"core": 1 - k}
        )

    def to_left(d):
        return remote(held.at[d], line.at[d], line_send.at[d], line_recv.at[d], {"seq": s - 1})

    def to_right(d):
        return remote(
            held.at[d], line.at[d + 1], line_send.at[d], line_recv.at[d + 1], {"seq": s + 1}
        )

    def gather_terms(d, with_left, with_right):
        load(d).wait()
        to_twin(d).wait_recv()

        @pl.when(with_right)
        def _():
            to_left(d).wait_recv()

        @pl.when(with_left)
        def _():
            to_right(d).wait_recv()

        def body(i, carry):
            held[d, i] = (held[d, i].astype(jnp.float32) + twin[d, i].astype(jnp.float32)).astype(
                held.dtype
            )
            return carry

        def body_right(i, carry):
            total = held[d, i].astype(jnp.float32) + twin[d, i].astype(jnp.float32)
            held[d, i] = (total + line[d, i].astype(jnp.float32)).astype(held.dtype)
            return carry

        def body_left(i, carry):
            total = held[d, i].astype(jnp.float32) + twin[d, i].astype(jnp.float32)
            held[d, i] = (total + line[d + 1, i].astype(jnp.float32)).astype(held.dtype)
            return carry

        def body_both(i, carry):
            total = held[d, i].astype(jnp.float32) + twin[d, i].astype(jnp.float32)
            total = total + line[d, i].astype(jnp.float32)
            held[d, i] = (total + line[d + 1, i].astype(jnp.float32)).astype(held.dtype)
            return carry

        @pl.when(jnp.logical_not(with_left) & jnp.logical_not(with_right))
        def _():
            lax.fori_loop(0, n_chip, body, 0)

        @pl.when(jnp.logical_not(with_left) & with_right)
        def _():
            lax.fori_loop(0, n_chip, body_right, 0)

        @pl.when(with_left & jnp.logical_not(with_right))
        def _():
            lax.fori_loop(0, n_chip, body_left, 0)

        @pl.when(with_left & with_right)
        def _():
            lax.fori_loop(0, n_chip, body_both, 0)

    for d in range(n_seq):
        to_twin(d).start()
        load(d).start()
    part_copies = start_exchange(
        n_plane, False, parts, parts_all, part_send, part_recv, part_local
    )
    never = s < 0
    for hop in range(1, n_seq):
        left = hop - n_seq + s
        right = n_seq - hop + s

        @pl.when(left >= 0)
        def _():
            gather_terms(left, never, s < n_seq - 1)
            to_left(left).start()

        @pl.when(right <= n_seq - 1)
        def _():
            gather_terms(right, s > 0, never)
            to_right(right).start()

    gather_terms(s, s > 0, s < n_seq - 1)
    swaps = []
    for step in range(1, n_chip):
        to = lax.rem(q + step, n_chip)
        copy = remote(
            held.at[s, to], sums.at[q], chip_send.at[step], chip_recv.at[step], {"chip": to}
        )
        copy.start()
        swaps.append(copy)
    own = pltpu.make_async_copy(held.at[s, q], sums.at[q], chip_local.at[0])
    own.start()
    for d in range(n_seq):
        to_twin(d).wait_send()

        @pl.when(d < s)
        def _():
            to_left(d).wait_send()

        @pl.when(d > s)
        def _():
            to_right(d).wait_send()

    for copy in part_copies:
        copy.wait()
    for copy in swaps:
        copy.wait()
    own.wait()


def sum_last(n_seq, parts, blocks):
    n_plane = 2 * KV_HEADS
    n_chip = KV_HEADS
    block = blocks.shape[2:]
    return pl.pallas_call(
        partial(last_kernel, n_seq, n_plane),
        out_shape=[
            jax.ShapeDtypeStruct(parts.shape, parts.dtype),
            jax.ShapeDtypeStruct(block, blocks.dtype),
        ],
        in_specs=[ANY, ANY],
        out_specs=[ANY, ANY],
        scratch_shapes=[
            pltpu.VMEM((n_seq,) + block, blocks.dtype),
            pltpu.VMEM((n_seq,) + block, blocks.dtype),
            pltpu.VMEM((n_seq + 1,) + block, blocks.dtype),
            DMA((n_plane,)),
            DMA((n_plane,)),
            DMA((1,)),
            DMA((n_seq,)),
            DMA((n_seq,)),
            DMA((n_seq,)),
            DMA((n_seq,)),
            DMA((n_seq + 1,)),
            DMA((n_chip,)),
            DMA((n_chip,)),
            DMA((1,)),
        ],
        compiler_params=pltpu.CompilerParams(
            collective_id=4, has_side_effects=True, vmem_limit_bytes=32 * 1024 * 1024
        ),
    )(parts, blocks)


QUERY_BLOCK = 256


def block_probs(query, keys, segment_col, segment_row, first):
    rows, width = query.shape[0], keys.shape[0]
    scaled = times_rows(query, keys) * (1.0 / math.sqrt(HEAD_DIM))
    bent = jnp.tanh(scaled / SOFT_CAP)
    row = first + lax.broadcasted_iota(jnp.int32, (rows, width), 0)
    col = lax.broadcasted_iota(jnp.int32, (rows, width), 1)
    allowed = ((segment_col == segment_row) & (col <= row)) | (col == row)
    capped = jnp.where(allowed, SOFT_CAP * bent, MASKED)
    raised = jnp.exp(capped - jnp.max(capped, axis=-1, keepdims=True))
    return raised / jnp.sum(raised, axis=-1, keepdims=True), bent


def attend_kernel(group_size, queries, keys, values, segment_col, segment_row, out):
    seq_len = keys.shape[0]
    for first in range(0, seq_len, QUERY_BLOCK):
        rows = slice(first, first + QUERY_BLOCK)
        width = first + QUERY_BLOCK
        for head in range(group_size):
            cols = slice(head * HEAD_DIM, (head + 1) * HEAD_DIM)
            probs, unused = block_probs(
                queries[rows, cols],
                keys[:width],
                segment_col[rows, :],
                segment_row[:, :width],
                first,
            )
            out[rows, cols] = add_slice(probs.astype(jnp.bfloat16), values[:width]).astype(
                out.dtype
            )


def attend(queries, keys, values, segment_col, segment_row):
    return pl.pallas_call(
        partial(attend_kernel, queries.shape[1] // HEAD_DIM),
        out_shape=jax.ShapeDtypeStruct(queries.shape, jnp.bfloat16),
        compiler_params=pltpu.CompilerParams(vmem_limit_bytes=40 * 1024 * 1024),
    )(queries, keys, values, segment_col, segment_row)


def attend_back_kernel(
    group_size,
    queries,
    keys,
    values,
    segment_col,
    segment_row,
    grads,
    grad_queries,
    grad_keys,
    grad_values,
):
    seq_len = keys.shape[0]
    inverse_root = 1.0 / math.sqrt(HEAD_DIM)
    grad_keys[...] = jnp.zeros_like(grad_keys)
    grad_values[...] = jnp.zeros_like(grad_values)
    for first in range(0, seq_len, QUERY_BLOCK):
        rows = slice(first, first + QUERY_BLOCK)
        width = first + QUERY_BLOCK
        for head in range(group_size):
            cols = slice(head * HEAD_DIM, (head + 1) * HEAD_DIM)
            query = queries[rows, cols]
            probs, bent = block_probs(
                query, keys[:width], segment_col[rows, :], segment_row[:, :width], first
            )
            grad = grads[rows, cols]
            grad_probs = times_rows(grad, values[:width])
            mean = jnp.sum(probs * grad_probs, axis=-1, keepdims=True)
            grad_scaled = (probs * (grad_probs - mean) * (1.0 - bent * bent)).astype(jnp.bfloat16)
            grad_queries[rows, cols] = add_slice(grad_scaled, keys[:width]) * inverse_root
            grad_keys[:width, :] += outer_rows(grad_scaled, query) * inverse_root
            grad_values[:width, :] += outer_rows(probs.astype(jnp.bfloat16), grad)


def attend_back(queries, keys, values, segment_col, segment_row, grads):
    return pl.pallas_call(
        partial(attend_back_kernel, queries.shape[1] // HEAD_DIM),
        out_shape=[
            jax.ShapeDtypeStruct(queries.shape, jnp.float32),
            jax.ShapeDtypeStruct(keys.shape, jnp.float32),
            jax.ShapeDtypeStruct(values.shape, jnp.float32),
        ],
        compiler_params=pltpu.CompilerParams(vmem_limit_bytes=40 * 1024 * 1024),
    )(queries, keys, values, segment_col, segment_row, grads)


def per_device_general(
    hidden_in,
    norm_gains,
    qkv_weight,
    out_weight,
    gate_up_weight,
    down_weight,
    output_cotangent,
    segment_ids,
    padding,
    positions,
):
    everyone = ("seq", "chip", "core")
    plane = ("chip", "core")
    column = ("seq", "core")
    groups = hidden_in.shape[0]
    piece_len = hidden_in.shape[1]
    model_width = hidden_in.shape[2]
    row_count = groups * piece_len
    seq_len = segment_ids.shape[1]
    group_size = HEADS // KV_HEADS
    query_width = HEADS * HEAD_DIM
    key_width = KV_HEADS * HEAD_DIM
    proj_width = qkv_weight.shape[1]

    residual = hidden_in.reshape(row_count, model_width).astype(jnp.float32)
    factor = lax.rsqrt(jnp.mean(residual * residual, axis=-1, keepdims=True) + EPSILON)
    gain_cols = lax.all_gather(norm_gains, everyone, axis=0, tiled=True).astype(jnp.float32)
    qkv_full = lax.all_gather(qkv_weight, everyone, axis=0, tiled=True)
    attn_input = (residual * factor * gain_cols[:, 0]).astype(jnp.bfloat16)
    projected = add_slice(attn_input, qkv_full)
    cosine, sine_part = rotary_tables(positions.reshape(row_count), HEAD_DIM)
    queries = (
        rotate(projected[:, :query_width].reshape(row_count, HEADS, HEAD_DIM), cosine, sine_part)
        .astype(jnp.bfloat16)
        .reshape(row_count, query_width)
    )
    keys_here = (
        rotate(
            projected[:, query_width : query_width + key_width].reshape(
                row_count, KV_HEADS, HEAD_DIM
            ),
            cosine,
            sine_part,
        )
        .astype(jnp.bfloat16)
        .reshape(groups, piece_len, key_width)
    )
    values_here = (
        projected[:, query_width + key_width :]
        .astype(jnp.bfloat16)
        .reshape(groups, piece_len, key_width)
    )
    both_all = lax.all_gather(
        jnp.concatenate([keys_here, values_here], axis=2), plane, axis=1, tiled=True
    )
    keys_all = both_all[:, :, :key_width]
    values_all = both_all[:, :, key_width:]
    first_query = (lax.axis_index("chip") * 2 + lax.axis_index("core")) * piece_len
    query_rows = first_query + jnp.arange(piece_len, dtype=jnp.int32)
    key_rows = jnp.arange(seq_len, dtype=jnp.int32)
    segment_query = lax.dynamic_slice_in_dim(segment_ids, first_query, piece_len, 1)
    allowed = (segment_query[:, :, None] == segment_ids[:, None, :]) & (
        key_rows[None, None, :] <= query_rows[None, :, None]
    ) & (padding[:, None, :] == 1) | (key_rows[None, None, :] == query_rows[None, :, None])
    allowed = allowed[:, None, None]
    probs = soft_probs(score_block(queries, keys_all), allowed)
    attn_out = mix_values(probs.astype(jnp.bfloat16), values_all)
    out_full = lax.all_gather(out_weight, everyone, axis=0, tiled=True)
    attn_proj = times_rows(attn_out, out_full)
    after_attn = residual + rms_norm(attn_proj, gain_cols[:, 1])
    ffn_input = rms_norm(after_attn, gain_cols[:, 2]).astype(jnp.bfloat16)

    unit_weights = lax.all_gather(gate_up_weight, "chip", axis=0, tiled=True)
    down_units = lax.all_gather(down_weight, "chip", axis=0, tiled=True)
    ffn_all = lax.all_gather(ffn_input, column, axis=0, tiled=True)
    gate_part = times_rows(ffn_all, unit_weights[:, :model_width])
    up_part = times_rows(ffn_all, unit_weights[:, model_width:])
    hidden_part = geglu_parts(gate_part, up_part).astype(jnp.bfloat16)
    down_part = add_slice(hidden_part, down_units).astype(jnp.bfloat16)
    down_out = lax.psum_scatter(down_part, column, scatter_dimension=0, tiled=True).astype(
        jnp.float32
    )
    layer_out = after_attn + rms_norm(down_out, gain_cols[:, 3])
    layer_output = layer_out.astype(jnp.bfloat16).reshape(groups, piece_len, model_width)

    cotangent = output_cotangent.reshape(row_count, model_width).astype(jnp.float32)
    unused_last, pull_last = jax.vjp(rms_norm, down_out, gain_cols[:, 3])
    grad_down, grad_gain_last = pull_last(cotangent)
    grad_down_low = grad_down.astype(jnp.bfloat16)
    grad_down_all = lax.all_gather(grad_down_low, column, axis=0, tiled=True)
    grad_part = times_rows(grad_down_all, down_units)
    unused_units, pull_units = jax.vjp(geglu_parts, gate_part, up_part)
    grad_gate_part, grad_up_part = pull_units(grad_part)
    gate_low = grad_gate_part.astype(jnp.bfloat16)
    up_low = grad_up_part.astype(jnp.bfloat16)
    grad_ffn_part = add_slice(gate_low, unit_weights[:, :model_width]) + add_slice(
        up_low, unit_weights[:, model_width:]
    )
    grad_ffn_in = lax.psum_scatter(
        grad_ffn_part.astype(jnp.bfloat16), column, scatter_dimension=0, tiled=True
    ).astype(jnp.float32)
    gate_up_rows = jnp.concatenate(
        [
            outer_rows(gate_low, ffn_all).astype(jnp.bfloat16),
            outer_rows(up_low, ffn_all).astype(jnp.bfloat16),
        ],
        axis=1,
    )
    down_rows = outer_rows(hidden_part, grad_down_all).astype(jnp.bfloat16)
    gate_up_grad = lax.psum_scatter(
        gate_up_rows, "chip", scatter_dimension=0, tiled=True
    ).astype(jnp.float32)
    down_grad = lax.psum_scatter(down_rows, "chip", scatter_dimension=0, tiled=True).astype(
        jnp.float32
    )

    unused_mid, pull_mid = jax.vjp(rms_norm, after_attn, gain_cols[:, 2])
    grad_after_ffn, grad_gain_mid = pull_mid(grad_ffn_in)
    grad_after = cotangent + grad_after_ffn
    unused_post, pull_post = jax.vjp(rms_norm, attn_proj, gain_cols[:, 1])
    grad_proj, grad_gain_post = pull_post(grad_after)
    grad_proj_low = grad_proj.astype(jnp.bfloat16)
    grad_attn = add_slice(grad_proj_low, out_full).astype(jnp.bfloat16)
    scaled = score_block(queries, keys_all)
    probs, pull_probs = jax.vjp(partial(soft_probs, allowed=allowed), scaled)
    grad_heads = grad_attn.reshape(groups, piece_len, KV_HEADS, group_size, HEAD_DIM)
    query_heads = queries.reshape(groups, piece_len, KV_HEADS, group_size, HEAD_DIM)
    key_heads = keys_all.reshape(groups, seq_len, KV_HEADS, HEAD_DIM)
    value_heads = values_all.reshape(groups, seq_len, KV_HEADS, HEAD_DIM)
    grad_probs = jnp.einsum(
        "spkgd,slkd->skgpl", grad_heads, value_heads, preferred_element_type=jnp.float32
    )
    (grad_scaled,) = pull_probs(grad_probs)
    grad_scaled_low = grad_scaled.astype(jnp.bfloat16)
    inverse_root = 1.0 / math.sqrt(HEAD_DIM)
    grad_query_rot = (
        jnp.einsum(
            "skgpl,slkd->spkgd", grad_scaled_low, key_heads, preferred_element_type=jnp.float32
        )
        * inverse_root
    )
    grad_key_rot = (
        jnp.einsum(
            "skgpl,spkgd->slkd", grad_scaled_low, query_heads, preferred_element_type=jnp.float32
        )
        * inverse_root
    )
    grad_value_part = jnp.einsum(
        "skgpl,spkgd->slkd",
        probs.astype(jnp.bfloat16),
        grad_heads,
        preferred_element_type=jnp.float32,
    )
    both_grads = jnp.concatenate(
        [
            grad_key_rot.reshape(groups, seq_len, key_width),
            grad_value_part.reshape(groups, seq_len, key_width),
        ],
        axis=2,
    ).astype(jnp.bfloat16)
    both_summed = lax.psum_scatter(both_grads, plane, scatter_dimension=1, tiled=True)
    both_summed = both_summed.astype(jnp.float32).reshape(row_count, 2 * key_width)
    key_summed = both_summed[:, :key_width]
    value_summed = both_summed[:, key_width:]
    grad_queries = rotate_back(
        grad_query_rot.reshape(row_count, HEADS, HEAD_DIM), cosine, sine_part
    ).reshape(row_count, query_width)
    grad_keys = rotate_back(
        key_summed.reshape(row_count, KV_HEADS, HEAD_DIM), cosine, sine_part
    ).reshape(row_count, key_width)
    grad_projected = jnp.concatenate([grad_queries, grad_keys, value_summed], axis=1).astype(
        jnp.bfloat16
    )
    grad_attn_in = times_rows(grad_projected, qkv_full)
    unused_first, pull_first = jax.vjp(rms_norm, residual, gain_cols[:, 0])
    grad_res_first, grad_gain_first = pull_first(grad_attn_in)
    input_grad = (grad_after + grad_res_first).reshape(groups, piece_len, model_width)
    gain_terms = jnp.stack([grad_gain_first, grad_gain_post, grad_gain_mid, grad_gain_last], axis=1)
    qkv_part = outer_rows(attn_input, grad_projected).astype(jnp.bfloat16)
    out_part = outer_rows(grad_proj_low, attn_out).astype(jnp.bfloat16)
    qkv_grad = lax.psum_scatter(qkv_part, everyone, scatter_dimension=0, tiled=True).astype(
        jnp.float32
    )
    out_proj_grad = lax.psum_scatter(out_part, everyone, scatter_dimension=0, tiled=True).astype(
        jnp.float32
    )
    gain_grad = lax.psum_scatter(gain_terms, everyone, scatter_dimension=0, tiled=True)
    return (layer_output, input_grad, gain_grad, qkv_grad, out_proj_grad, gate_up_grad, down_grad)


def per_device_by_heads(
    n_seq,
    hidden_in,
    norm_gains,
    qkv_weight,
    out_weight,
    gate_up_weight,
    down_weight,
    output_cotangent,
    segment_ids,
    padding,
    positions,
):
    column = ("seq", "core")
    groups, piece_len, model_width = hidden_in.shape
    row_count = groups * piece_len
    seq_len = segment_ids.shape[1]
    n_chip = KV_HEADS
    n_plane = 2 * n_chip
    group_size = HEADS // KV_HEADS
    query_width = HEADS * HEAD_DIM
    key_width = KV_HEADS * HEAD_DIM
    own_width = group_size * HEAD_DIM
    part_width = own_width + 2 * HEAD_DIM
    block_width = part_width + own_width
    weight_rows = qkv_weight.shape[0]
    extra_rows = 16 - weight_rows % 16
    block_rows = weight_rows + extra_rows
    core = lax.axis_index("core")

    gain_rows = jnp.pad(
        norm_gains.T, ((0, extra_rows - norm_gains.shape[1]), (0, block_width - weight_rows))
    )
    blocks = jnp.stack(
        [
            jnp.concatenate(
                [
                    jnp.concatenate(
                        [
                            qkv_weight[:, c * own_width : (c + 1) * own_width],
                            qkv_weight[
                                :, query_width + c * HEAD_DIM : query_width + (c + 1) * HEAD_DIM
                            ],
                            qkv_weight[
                                :,
                                query_width + key_width + c * HEAD_DIM : query_width
                                + key_width
                                + (c + 1) * HEAD_DIM,
                            ],
                            out_weight[:, c * own_width : (c + 1) * own_width],
                        ],
                        axis=1,
                    ),
                    gain_rows,
                ],
                axis=0,
            )
            for c in range(n_chip)
        ]
    )
    hidden_all, blocks_all = gather_first(n_seq, hidden_in, blocks)
    unit_weights = lax.all_gather(gate_up_weight, "chip", axis=0, tiled=True)
    down_units = lax.all_gather(down_weight, "chip", axis=0, tiled=True)
    blocks_all = blocks_all.transpose(0, 2, 1, 3, 4)
    own_weights = blocks_all[:, :, :, :weight_rows].reshape(model_width, block_width)
    own_qkv = own_weights[:, :part_width]
    own_out = own_weights[:, part_width:]
    gain_cols = (
        blocks_all[:, :, :, weight_rows : weight_rows + norm_gains.shape[1], :weight_rows]
        .transpose(0, 1, 2, 4, 3)
        .reshape(model_width, norm_gains.shape[1])
        .astype(jnp.float32)
    )

    seq_rows = hidden_all.reshape(seq_len, model_width).astype(jnp.float32)
    seq_factor = lax.rsqrt(jnp.mean(seq_rows * seq_rows, axis=-1, keepdims=True) + EPSILON)
    attn_input = (seq_rows * seq_factor * gain_cols[:, 0]).astype(jnp.bfloat16)
    projected = add_slice(attn_input, own_qkv)
    segment = lax.dynamic_index_in_dim(segment_ids, core, 0, keepdims=False)
    valid = lax.dynamic_index_in_dim(padding, core, 0, keepdims=False)
    token = jnp.arange(seq_len, dtype=jnp.int32)
    document_start = jnp.min(
        jnp.where(segment[:, None] == segment[None, :], token[None, :], seq_len), axis=1
    )
    cosine, sine_part = rotary_tables(token - document_start, HEAD_DIM)
    queries = (
        rotate(projected[:, :own_width].reshape(seq_len, group_size, HEAD_DIM), cosine, sine_part)
        .astype(jnp.bfloat16)
        .reshape(seq_len, own_width)
    )
    keys = (
        rotate(
            projected[:, own_width : own_width + HEAD_DIM].reshape(seq_len, 1, HEAD_DIM),
            cosine,
            sine_part,
        )
        .astype(jnp.bfloat16)
        .reshape(seq_len, HEAD_DIM)
    )
    values = projected[:, own_width + HEAD_DIM :].astype(jnp.bfloat16)
    segment_col = segment[:, None]
    segment_row = jnp.where(valid == 1, segment, -1)[None, :]
    attn_out = attend(queries, keys, values, segment_col, segment_row)
    proj_parts = times_rows(attn_out, own_out).astype(jnp.bfloat16)
    proj_parts = plane_exchange(
        proj_parts.reshape(n_plane, piece_len, model_width), False, 2
    )

    def sum_parts(parts):
        parts = parts.reshape(n_chip, groups, piece_len, model_width).astype(jnp.float32)
        return jnp.sum(parts, axis=0).reshape(row_count, model_width)

    attn_proj = sum_parts(proj_parts)
    residual = hidden_in.reshape(row_count, model_width).astype(jnp.float32)
    after_attn = residual + rms_norm(attn_proj, gain_cols[:, 1])
    ffn_input = rms_norm(after_attn, gain_cols[:, 2]).astype(jnp.bfloat16)

    ffn_all = lax.all_gather(ffn_input, column, axis=0, tiled=True)
    gate_part = times_rows(ffn_all, unit_weights[:, :model_width])
    up_part = times_rows(ffn_all, unit_weights[:, model_width:])
    hidden_part = geglu_parts(gate_part, up_part).astype(jnp.bfloat16)
    down_part = add_slice(hidden_part, down_units).astype(jnp.bfloat16)
    down_out = lax.psum_scatter(down_part, column, scatter_dimension=0, tiled=True).astype(
        jnp.float32
    )
    layer_out = after_attn + rms_norm(down_out, gain_cols[:, 3])
    layer_output = layer_out.astype(jnp.bfloat16).reshape(groups, piece_len, model_width)

    cotangent = output_cotangent.reshape(row_count, model_width).astype(jnp.float32)
    unused_last, pull_last = jax.vjp(rms_norm, down_out, gain_cols[:, 3])
    grad_down, grad_gain_last = pull_last(cotangent)
    grad_down_low = grad_down.astype(jnp.bfloat16)
    grad_down_all = lax.all_gather(grad_down_low, column, axis=0, tiled=True)
    grad_part = times_rows(grad_down_all, down_units)
    unused_units, pull_units = jax.vjp(geglu_parts, gate_part, up_part)
    grad_gate_part, grad_up_part = pull_units(grad_part)
    gate_low = grad_gate_part.astype(jnp.bfloat16)
    up_low = grad_up_part.astype(jnp.bfloat16)
    grad_ffn_part = add_slice(gate_low, unit_weights[:, :model_width]) + add_slice(
        up_low, unit_weights[:, model_width:]
    )
    grad_ffn_in = lax.psum_scatter(
        grad_ffn_part.astype(jnp.bfloat16), column, scatter_dimension=0, tiled=True
    ).astype(jnp.float32)
    gate_up_rows = jnp.concatenate(
        [
            outer_rows(gate_low, ffn_all).astype(jnp.bfloat16),
            outer_rows(up_low, ffn_all).astype(jnp.bfloat16),
        ],
        axis=1,
    )
    down_rows = outer_rows(hidden_part, grad_down_all).astype(jnp.bfloat16)
    gate_up_grad = lax.psum_scatter(
        gate_up_rows, "chip", scatter_dimension=0, tiled=True
    ).astype(jnp.float32)
    down_grad = lax.psum_scatter(down_rows, "chip", scatter_dimension=0, tiled=True).astype(
        jnp.float32
    )

    unused_mid, pull_mid = jax.vjp(rms_norm, after_attn, gain_cols[:, 2])
    grad_after_ffn, grad_gain_mid = pull_mid(grad_ffn_in)
    grad_after = cotangent + grad_after_ffn
    unused_post, pull_post = jax.vjp(rms_norm, attn_proj, gain_cols[:, 1])
    grad_proj, grad_gain_post = pull_post(grad_after)
    grad_proj_low = grad_proj.astype(jnp.bfloat16)

    grad_proj_all = plane_exchange(
        grad_proj_low.reshape(groups, piece_len, model_width), True, 3
    ).reshape(seq_len, model_width)
    grad_attn = add_slice(grad_proj_all, own_out).astype(jnp.bfloat16)
    grad_query_rot, grad_key_rot, grad_values = attend_back(
        queries, keys, values, segment_col, segment_row, grad_attn
    )
    grad_queries = rotate_back(
        grad_query_rot.reshape(seq_len, group_size, HEAD_DIM), cosine, sine_part
    ).reshape(seq_len, own_width)
    grad_keys = rotate_back(
        grad_key_rot.reshape(seq_len, 1, HEAD_DIM), cosine, sine_part
    ).reshape(seq_len, HEAD_DIM)
    grad_projected = jnp.concatenate([grad_queries, grad_keys, grad_values], axis=1).astype(
        jnp.bfloat16
    )
    grad_in_part = times_rows(grad_projected, own_qkv)
    grad_gain_first = jnp.sum(grad_in_part * seq_rows * seq_factor, axis=0)
    weight_part = jnp.concatenate(
        [
            outer_rows(attn_input, grad_projected).astype(jnp.bfloat16),
            outer_rows(grad_proj_all, attn_out).astype(jnp.bfloat16),
        ],
        axis=1,
    ).reshape(n_seq, n_chip, 2, weight_rows, block_width)
    gain_terms = (
        jnp.stack([grad_gain_first, grad_gain_post, grad_gain_mid, grad_gain_last])
        .astype(jnp.bfloat16)
        .reshape(-1, n_seq, n_chip, 2, weight_rows)
        .transpose(1, 2, 3, 0, 4)
    )
    gain_terms = jnp.pad(
        gain_terms,
        ((0, 0),) * 3
        + ((0, extra_rows - gain_terms.shape[3]), (0, block_width - weight_rows)),
    )
    grad_blocks = jnp.concatenate([weight_part, gain_terms], axis=3).transpose(0, 2, 1, 3, 4)
    grad_in_parts, grad_sums = sum_last(
        n_seq,
        grad_in_part.astype(jnp.bfloat16).reshape(n_plane, piece_len, model_width),
        grad_blocks,
    )
    grad_attn_in = sum_parts(grad_in_parts)
    factor = lax.rsqrt(jnp.mean(residual * residual, axis=-1, keepdims=True) + EPSILON)
    unused_first, pull_first = jax.vjp(rms_norm, residual, gain_cols[:, 0])
    grad_res_first, unused_gain = pull_first(grad_attn_in)
    input_grad = (grad_after + grad_res_first).reshape(groups, piece_len, model_width)

    weight_sums = grad_sums[:, :weight_rows].astype(jnp.float32)
    qkv_grad = jnp.concatenate(
        [weight_sums[c, :, :own_width] for c in range(n_chip)]
        + [weight_sums[c, :, own_width : own_width + HEAD_DIM] for c in range(n_chip)]
        + [weight_sums[c, :, own_width + HEAD_DIM : part_width] for c in range(n_chip)],
        axis=1,
    )
    out_proj_grad = jnp.concatenate(
        [weight_sums[c, :, part_width:] for c in range(n_chip)], axis=1
    )
    gain_grad = jnp.sum(
        grad_sums[:, weight_rows : weight_rows + norm_gains.shape[1], :weight_rows].astype(
            jnp.float32
        ),
        axis=0,
    ).T
    return (layer_output, input_grad, gain_grad, qkv_grad, out_proj_grad, gate_up_grad, down_grad)


def solution(mesh):
    n_seq = mesh.shape["seq"]
    n_ctx = mesh.shape["ctx"]
    split_mesh = jax.sharding.Mesh(
        mesh.devices.reshape(n_seq, n_ctx // 2, 2), ("seq", "chip", "core")
    )
    plane = ("chip", "core")
    rows = P(("seq", "chip", "core"), None)
    tokens = P("seq", plane, None)
    placed = (
        tokens,
        rows,
        rows,
        rows,
        rows,
        rows,
        tokens,
        P("seq", None),
        P("seq", None),
        P("seq", plane),
    )

    def step(*arrays):
        groups = arrays[0].shape[0]
        if n_ctx // 2 == KV_HEADS and groups == 2:
            return per_device_by_heads(n_seq, *arrays)
        return per_device_general(*arrays)

    return jax.shard_map(
        step,
        mesh=split_mesh,
        in_specs=placed,
        out_specs=(tokens, tokens, rows, rows, rows, rows, rows),
        check_vma=False,
    )
```

```python
from functools import partial
import math

import jax
import jax.numpy as jnp
from jax import lax
from jax.experimental import pallas as pl
from jax.experimental.pallas import tpu as pltpu
from jax.sharding import PartitionSpec as P

HEADS = 8
KV_HEADS = 4
HEAD_DIM = 256


EPSILON = 1e-06
SOFT_CAP = 50.0
MASKED = -1e30


def rms_norm(matrix, gain_col):
    factor = lax.rsqrt(jnp.mean(matrix * matrix, axis=-1, keepdims=True) + EPSILON)
    return matrix * factor * gain_col


def rotary_tables(positions, head_dim):
    half_dim = head_dim // 2
    frequency = jnp.exp(
        jnp.arange(half_dim, dtype=jnp.float32) * (-2.0 * math.log(10000.0) / head_dim)
    )
    phase_angle = positions.astype(jnp.float32)[:, None] * frequency[None, :]
    return (jnp.cos(phase_angle)[:, None, :], jnp.sin(phase_angle)[:, None, :])


def rotate(vectors, cosine, sine_part):
    half_dim = vectors.shape[-1] // 2
    first_half = vectors[..., :half_dim]
    second_half = vectors[..., half_dim:]
    return jnp.concatenate(
        [
            first_half * cosine - second_half * sine_part,
            second_half * cosine + first_half * sine_part,
        ],
        axis=-1,
    )


def rotate_back(grads, cosine, sine_part):
    half_dim = grads.shape[-1] // 2
    first_half = grads[..., :half_dim]
    second_half = grads[..., half_dim:]
    return jnp.concatenate(
        [
            first_half * cosine + second_half * sine_part,
            second_half * cosine - first_half * sine_part,
        ],
        axis=-1,
    )


def soft_probs(scaled, allowed):
    capped = SOFT_CAP * jnp.tanh(scaled / SOFT_CAP)
    capped = jnp.where(allowed, capped, MASKED)
    return jax.nn.softmax(capped, axis=-1)


def geglu_parts(gate_part, up_part):
    return jax.nn.gelu(gate_part, approximate=True) * up_part


def score_block(queries, keys_all):
    groups = keys_all.shape[0]
    seq_len = keys_all.shape[1]
    piece_len = queries.shape[0] // groups
    query_heads = queries.reshape(groups, piece_len, KV_HEADS, HEADS // KV_HEADS, HEAD_DIM)
    key_heads = keys_all.reshape(groups, seq_len, KV_HEADS, HEAD_DIM)
    raw_score = jnp.einsum(
        "spkgd,slkd->skgpl", query_heads, key_heads, preferred_element_type=jnp.float32
    )
    return raw_score * (1.0 / math.sqrt(HEAD_DIM))


def mix_values(weights_low, values_all):
    groups = values_all.shape[0]
    seq_len = values_all.shape[1]
    piece_len = weights_low.shape[3]
    value_heads = values_all.reshape(groups, seq_len, KV_HEADS, HEAD_DIM)
    mixed = jnp.einsum(
        "skgpl,slkd->spkgd", weights_low, value_heads, preferred_element_type=jnp.float32
    )
    return mixed.reshape(groups * piece_len, HEADS * HEAD_DIM).astype(jnp.bfloat16)


def add_slice(left, weight_piece):
    return jnp.dot(left, weight_piece, preferred_element_type=jnp.float32)


def times_rows(left, weight_piece):
    return lax.dot_general(
        left, weight_piece, (((1,), (1,)), ((), ())), preferred_element_type=jnp.float32
    )


def outer_rows(left, right):
    return lax.dot_general(
        left, right, (((0,), (0,)), ((), ())), preferred_element_type=jnp.float32
    )


MESH = pl.DeviceIdType.MESH
ANY = pl.BlockSpec(memory_space=pl.ANY)
DMA = pltpu.SemaphoreType.DMA


def remote(source, target, send_sem, recv_sem, device):
    return pltpu.make_async_remote_copy(
        src_ref=source,
        dst_ref=target,
        send_sem=send_sem,
        recv_sem=recv_sem,
        device_id=device,
        device_id_type=MESH,
    )


def plane_device(index):
    return {"chip": index // 2, "core": lax.rem(index, 2)}


def greet(n_plane, n_seq):
    me = lax.axis_index("chip") * 2 + lax.axis_index("core")
    barrier = pltpu.get_barrier_semaphore()
    for step in range(1, n_plane):
        pl.semaphore_signal(
            barrier,
            inc=1,
            device_id=plane_device(lax.rem(me + step, n_plane)),
            device_id_type=MESH,
        )
    count = n_plane - 1
    if n_seq > 1:
        s = lax.axis_index("seq")

        @pl.when(s > 0)
        def _():
            pl.semaphore_signal(barrier, inc=1, device_id={"seq": s - 1}, device_id_type=MESH)

        @pl.when(s < n_seq - 1)
        def _():
            pl.semaphore_signal(barrier, inc=1, device_id={"seq": s + 1}, device_id_type=MESH)

        count = count + jnp.where(s > 0, 1, 0) + jnp.where(s < n_seq - 1, 1, 0)
    pl.semaphore_wait(barrier, count)


def start_exchange(n_plane, by_core, source, target, send_sems, recv_sems, local_sem):
    me = lax.axis_index("chip") * 2 + lax.axis_index("core")
    copies = []
    for step in (4, 2, 6, 3, 5, 1, 7):
        to = lax.rem(me + step, n_plane)
        block = lax.rem(to, 2) if by_core else to
        copy = remote(
            source.at[block],
            target.at[me],
            send_sems.at[step],
            recv_sems.at[step],
            plane_device(to),
        )
        copy.start()
        copies.append(copy)
    block = lax.rem(me, 2) if by_core else me
    own = pltpu.make_async_copy(source.at[block], target.at[me], local_sem.at[0])
    own.start()
    copies.append(own)
    return copies


def exchange_kernel(n_plane, by_core, source, target, send_sems, recv_sems, local_sem):
    greet(n_plane, 1)
    for copy in start_exchange(
        n_plane, by_core, source, target, send_sems, recv_sems, local_sem
    ):
        copy.wait()


def plane_exchange(blocks, by_core, collective_id):
    n_plane = 2 * KV_HEADS
    return pl.pallas_call(
        partial(exchange_kernel, n_plane, by_core),
        out_shape=jax.ShapeDtypeStruct((n_plane,) + blocks.shape[1:], blocks.dtype),
        in_specs=[ANY],
        out_specs=ANY,
        scratch_shapes=[DMA((n_plane,)), DMA((n_plane,)), DMA((1,))],
        compiler_params=pltpu.CompilerParams(
            collective_id=collective_id, has_side_effects=True
        ),
    )(blocks)


def gather_kernel(
    n_seq,
    n_plane,
    hidden,
    blocks,
    hidden_all,
    blocks_all,
    hid_send,
    hid_recv,
    hid_local,
    chip_send,
    chip_recv,
    chip_local,
    left_send,
    right_send,
    line_recv,
    twin_send,
    twin_recv,
):
    n_chip = n_plane // 2
    s = lax.axis_index("seq")
    q = lax.axis_index("chip")
    k = lax.axis_index("core")
    greet(n_plane, n_seq)
    swaps = []
    for step in range(1, n_chip):
        to = lax.rem(q + step, n_chip)
        copy = remote(
            blocks.at[to],
            blocks_all.at[s, k, q],
            chip_send.at[step],
            chip_recv.at[step],
            {"chip": to},
        )
        copy.start()
        swaps.append(copy)
    own = pltpu.make_async_copy(blocks.at[q], blocks_all.at[s, k, q], chip_local.at[0])
    own.start()
    hidden_copies = start_exchange(
        n_plane, True, hidden, hidden_all, hid_send, hid_recv, hid_local
    )
    for copy in swaps:
        copy.wait_recv()
    own.wait()

    def to_left(d):
        return remote(
            blocks_all.at[d, k], blocks_all.at[d, k], left_send.at[d], line_recv.at[d], {"seq": s - 1}
        )

    def to_right(d):
        return remote(
            blocks_all.at[d, k], blocks_all.at[d, k], right_send.at[d], line_recv.at[d], {"seq": s + 1}
        )

    def to_twin(d):
        return remote(
            blocks_all.at[d, k], blocks_all.at[d, k], twin_send.at[d], twin_recv.at[d], {"core": 1 - k}
        )

    def from_twin(d):
        return remote(
            blocks_all.at[d, 1 - k],
            blocks_all.at[d, 1 - k],
            twin_send.at[d],
            twin_recv.at[d],
            {"core": 1 - k},
        )

    @pl.when(s > 0)
    def _():
        to_left(s).start()

    @pl.when(s < n_seq - 1)
    def _():
        to_right(s).start()

    to_twin(s).start()
    for hop in range(1, n_seq):
        from_left = s - hop
        from_right = s + hop

        @pl.when(from_left >= 0)
        def _():
            to_left(from_left).wait_recv()

            @pl.when(s < n_seq - 1)
            def _():
                to_right(from_left).start()

            to_twin(from_left).start()

        @pl.when(from_right < n_seq)
        def _():
            to_right(from_right).wait_recv()

            @pl.when(s > 0)
            def _():
                to_left(from_right).start()

            to_twin(from_right).start()

    for d in range(n_seq):

        @pl.when((d >= s) & (s > 0))
        def _():
            to_left(d).wait_send()

        @pl.when((d <= s) & (s < n_seq - 1))
        def _():
            to_right(d).wait_send()

        to_twin(d).wait_send()
        from_twin(d).wait_recv()
    for copy in swaps:
        copy.wait_send()
    for copy in hidden_copies:
        copy.wait()


def gather_first(n_seq, hidden, blocks):
    n_plane = 2 * KV_HEADS
    n_chip = KV_HEADS
    return pl.pallas_call(
        partial(gather_kernel, n_seq, n_plane),
        out_shape=[
            jax.ShapeDtypeStruct((n_plane,) + hidden.shape[1:], hidden.dtype),
            jax.ShapeDtypeStruct((n_seq, 2) + blocks.shape, blocks.dtype),
        ],
        in_specs=[ANY, ANY],
        out_specs=[ANY, ANY],
        scratch_shapes=[
            DMA((n_plane,)),
            DMA((n_plane,)),
            DMA((1,)),
            DMA((n_chip,)),
            DMA((n_chip,)),
            DMA((1,)),
            DMA((n_seq,)),
            DMA((n_seq,)),
            DMA((n_seq,)),
            DMA((n_seq,)),
            DMA((n_seq,)),
        ],
        compiler_params=pltpu.CompilerParams(collective_id=1, has_side_effects=True),
    )(hidden, blocks)


def last_kernel(
    n_seq,
    n_plane,
    parts,
    blocks,
    parts_all,
    sums,
    held,
    twin,
    line,
    part_send,
    part_recv,
    part_local,
    held_sem,
    twin_send,
    twin_recv,
    line_send,
    line_recv,
    chip_send,
    chip_recv,
    chip_local,
):
    n_chip = n_plane // 2
    s = lax.axis_index("seq")
    q = lax.axis_index("chip")
    k = lax.axis_index("core")
    greet(n_plane, n_seq)

    def load(d):
        return pltpu.make_async_copy(blocks.at[d, k], held.at[d], held_sem.at[d])

    def to_twin(d):
        return remote(
            blocks.at[d, 1 - k], twin.at[d], twin_send.at[d], twin_recv.at[d], {"core": 1 - k}
        )

    def to_left(d):
        return remote(held.at[d], line.at[d], line_send.at[d], line_recv.at[d], {"seq": s - 1})

    def to_right(d):
        return remote(
            held.at[d], line.at[d + 1], line_send.at[d], line_recv.at[d + 1], {"seq": s + 1}
        )

    def gather_terms(d, with_left, with_right):
        load(d).wait()
        to_twin(d).wait_recv()

        @pl.when(with_right)
        def _():
            to_left(d).wait_recv()

        @pl.when(with_left)
        def _():
            to_right(d).wait_recv()

        def body(i, carry):
            held[d, i] = (held[d, i].astype(jnp.float32) + twin[d, i].astype(jnp.float32)).astype(
                held.dtype
            )
            return carry

        def body_right(i, carry):
            total = held[d, i].astype(jnp.float32) + twin[d, i].astype(jnp.float32)
            held[d, i] = (total + line[d, i].astype(jnp.float32)).astype(held.dtype)
            return carry

        def body_left(i, carry):
            total = held[d, i].astype(jnp.float32) + twin[d, i].astype(jnp.float32)
            held[d, i] = (total + line[d + 1, i].astype(jnp.float32)).astype(held.dtype)
            return carry

        def body_both(i, carry):
            total = held[d, i].astype(jnp.float32) + twin[d, i].astype(jnp.float32)
            total = total + line[d, i].astype(jnp.float32)
            held[d, i] = (total + line[d + 1, i].astype(jnp.float32)).astype(held.dtype)
            return carry

        @pl.when(jnp.logical_not(with_left) & jnp.logical_not(with_right))
        def _():
            lax.fori_loop(0, n_chip, body, 0)

        @pl.when(jnp.logical_not(with_left) & with_right)
        def _():
            lax.fori_loop(0, n_chip, body_right, 0)

        @pl.when(with_left & jnp.logical_not(with_right))
        def _():
            lax.fori_loop(0, n_chip, body_left, 0)

        @pl.when(with_left & with_right)
        def _():
            lax.fori_loop(0, n_chip, body_both, 0)

    for d in range(n_seq):
        to_twin(d).start()
        load(d).start()
    part_copies = start_exchange(
        n_plane, False, parts, parts_all, part_send, part_recv, part_local
    )
    never = s < 0
    for hop in range(1, n_seq):
        left = hop - n_seq + s
        right = n_seq - hop + s

        @pl.when(left >= 0)
        def _():
            gather_terms(left, never, s < n_seq - 1)
            to_left(left).start()

        @pl.when(right <= n_seq - 1)
        def _():
            gather_terms(right, s > 0, never)
            to_right(right).start()

    gather_terms(s, s > 0, s < n_seq - 1)
    swaps = []
    for step in range(1, n_chip):
        to = lax.rem(q + step, n_chip)
        copy = remote(
            held.at[s, to], sums.at[q], chip_send.at[step], chip_recv.at[step], {"chip": to}
        )
        copy.start()
        swaps.append(copy)
    own = pltpu.make_async_copy(held.at[s, q], sums.at[q], chip_local.at[0])
    own.start()
    for d in range(n_seq):
        to_twin(d).wait_send()

        @pl.when(d < s)
        def _():
            to_left(d).wait_send()

        @pl.when(d > s)
        def _():
            to_right(d).wait_send()

    for copy in part_copies:
        copy.wait()
    for copy in swaps:
        copy.wait()
    own.wait()


def sum_last(n_seq, parts, blocks):
    n_plane = 2 * KV_HEADS
    n_chip = KV_HEADS
    block = blocks.shape[2:]
    return pl.pallas_call(
        partial(last_kernel, n_seq, n_plane),
        out_shape=[
            jax.ShapeDtypeStruct(parts.shape, parts.dtype),
            jax.ShapeDtypeStruct(block, blocks.dtype),
        ],
        in_specs=[ANY, ANY],
        out_specs=[ANY, ANY],
        scratch_shapes=[
            pltpu.VMEM((n_seq,) + block, blocks.dtype),
            pltpu.VMEM((n_seq,) + block, blocks.dtype),
            pltpu.VMEM((n_seq + 1,) + block, blocks.dtype),
            DMA((n_plane,)),
            DMA((n_plane,)),
            DMA((1,)),
            DMA((n_seq,)),
            DMA((n_seq,)),
            DMA((n_seq,)),
            DMA((n_seq,)),
            DMA((n_seq + 1,)),
            DMA((n_chip,)),
            DMA((n_chip,)),
            DMA((1,)),
        ],
        compiler_params=pltpu.CompilerParams(
            collective_id=4, has_side_effects=True, vmem_limit_bytes=32 * 1024 * 1024
        ),
    )(parts, blocks)


QUERY_BLOCK = 256


def block_probs(query, keys, segment_col, segment_row, first):
    rows, width = query.shape[0], keys.shape[0]
    scaled = times_rows(query, keys) * (1.0 / math.sqrt(HEAD_DIM))
    bent = jnp.tanh(scaled / SOFT_CAP)
    row = first + lax.broadcasted_iota(jnp.int32, (rows, width), 0)
    col = lax.broadcasted_iota(jnp.int32, (rows, width), 1)
    allowed = ((segment_col == segment_row) & (col <= row)) | (col == row)
    capped = jnp.where(allowed, SOFT_CAP * bent, MASKED)
    raised = jnp.exp(capped - jnp.max(capped, axis=-1, keepdims=True))
    return raised / jnp.sum(raised, axis=-1, keepdims=True), bent


def attend_kernel(group_size, queries, keys, values, segment_col, segment_row, out):
    seq_len = keys.shape[0]
    for first in range(0, seq_len, QUERY_BLOCK):
        rows = slice(first, first + QUERY_BLOCK)
        width = first + QUERY_BLOCK
        for head in range(group_size):
            cols = slice(head * HEAD_DIM, (head + 1) * HEAD_DIM)
            probs, unused = block_probs(
                queries[rows, cols],
                keys[:width],
                segment_col[rows, :],
                segment_row[:, :width],
                first,
            )
            out[rows, cols] = add_slice(probs.astype(jnp.bfloat16), values[:width]).astype(
                out.dtype
            )


def attend(queries, keys, values, segment_col, segment_row):
    return pl.pallas_call(
        partial(attend_kernel, queries.shape[1] // HEAD_DIM),
        out_shape=jax.ShapeDtypeStruct(queries.shape, jnp.bfloat16),
        compiler_params=pltpu.CompilerParams(vmem_limit_bytes=40 * 1024 * 1024),
    )(queries, keys, values, segment_col, segment_row)


def attend_back_kernel(
    group_size,
    queries,
    keys,
    values,
    segment_col,
    segment_row,
    grads,
    grad_queries,
    grad_keys,
    grad_values,
):
    seq_len = keys.shape[0]
    inverse_root = 1.0 / math.sqrt(HEAD_DIM)
    grad_keys[...] = jnp.zeros_like(grad_keys)
    grad_values[...] = jnp.zeros_like(grad_values)
    for first in range(0, seq_len, QUERY_BLOCK):
        rows = slice(first, first + QUERY_BLOCK)
        width = first + QUERY_BLOCK
        for head in range(group_size):
            cols = slice(head * HEAD_DIM, (head + 1) * HEAD_DIM)
            query = queries[rows, cols]
            probs, bent = block_probs(
                query, keys[:width], segment_col[rows, :], segment_row[:, :width], first
            )
            grad = grads[rows, cols]
            grad_probs = times_rows(grad, values[:width])
            mean = jnp.sum(probs * grad_probs, axis=-1, keepdims=True)
            grad_scaled = (probs * (grad_probs - mean) * (1.0 - bent * bent)).astype(jnp.bfloat16)
            grad_queries[rows, cols] = add_slice(grad_scaled, keys[:width]) * inverse_root
            grad_keys[:width, :] += outer_rows(grad_scaled, query) * inverse_root
            grad_values[:width, :] += outer_rows(probs.astype(jnp.bfloat16), grad)


def attend_back(queries, keys, values, segment_col, segment_row, grads):
    return pl.pallas_call(
        partial(attend_back_kernel, queries.shape[1] // HEAD_DIM),
        out_shape=[
            jax.ShapeDtypeStruct(queries.shape, jnp.float32),
            jax.ShapeDtypeStruct(keys.shape, jnp.float32),
            jax.ShapeDtypeStruct(values.shape, jnp.float32),
        ],
        compiler_params=pltpu.CompilerParams(vmem_limit_bytes=40 * 1024 * 1024),
    )(queries, keys, values, segment_col, segment_row, grads)


GELU_SCALE = math.sqrt(2.0 / math.pi)


def gelu_pieces(gate):
    bend = jnp.tanh(GELU_SCALE * (gate + 0.044715 * gate * gate * gate))
    value = 0.5 * gate * (1.0 + bend)
    slope = 0.5 * (1.0 + bend) + 0.5 * gate * (1.0 - bend * bend) * GELU_SCALE * (
        1.0 + 3.0 * 0.044715 * gate * gate
    )
    return value, slope


def units_kernel(n_seq, backward, *refs):
    if backward:
        tokens, units, downs, kept_gate, kept_up = refs[:5]
        out, tokens_all, first_out, second_out = refs[5:9]
        stage_outs = (first_out, second_out)
        scratch = refs[9:]
    else:
        tokens, units, downs = refs[:3]
        out, tokens_all, first_out, second_out, third_out = refs[3:8]
        stage_outs = (first_out, second_out, third_out)
        scratch = refs[8:]
    units_v, downs_v, held, own_sum, twin_sum, twin_out, line, stage = scratch[:8]
    scratch = scratch[8:]
    if backward:
        kept, kept_sem = scratch[:2]
        scratch = scratch[2:]
    (
        weight_sem,
        own_sem,
        left_send,
        right_send,
        token_recv,
        twin_send,
        twin_recv,
        part_send,
        part_recv,
        line_send,
        line_recv,
        stage_sem,
        all_sem,
        out_sem,
    ) = scratch
    n = n_seq
    s = lax.axis_index("seq")
    k = lax.axis_index("core")
    twin = {"core": 1 - k}
    n_units, width = downs_v.shape
    piece_len = tokens.shape[1]
    at_end = (s == 0) | (s == n - 1)

    def token_left(d, h, source):
        return remote(
            source, held.at[d, h, 0], left_send.at[d, h], token_recv.at[d, h], {"seq": s - 1}
        )

    def token_right(d, h, source):
        return remote(
            source, held.at[d, h, 0], right_send.at[d, h], token_recv.at[d, h], {"seq": s + 1}
        )

    def token_twin(d, h, source):
        return remote(source, held.at[d, h, 1], twin_send.at[d, h], twin_recv.at[d, h], twin)

    def part_twin(d, h):
        return remote(
            twin_out.at[d, h], twin_sum.at[d, h], part_send.at[d, h], part_recv.at[d, h], twin
        )

    def part_line(d, h):
        to_left = d < s
        slot = jnp.where(to_left, d, d + 1)
        return remote(
            twin_sum.at[d, h],
            line.at[slot, h],
            line_send.at[d, h],
            line_recv.at[slot, h],
            {"seq": jnp.where(to_left, s - 1, s + 1)},
        )

    def line_arrival(slot, h):
        return remote(
            twin_sum.at[0, h],
            line.at[slot, h],
            line_send.at[0, h],
            line_recv.at[slot, h],
            {"seq": s},
        )

    def own_load(h):
        return pltpu.make_async_copy(tokens.at[h], held.at[s, h, 0], own_sem.at[h])

    def all_store(d, h):
        return pltpu.make_async_copy(held.at[d, h], tokens_all.at[d, h], all_sem.at[d, h])

    def stage_store(i, d, h, slot):
        return pltpu.make_async_copy(
            stage.at[i, slot], stage_outs[i].at[2 * d + h], stage_sem.at[i, slot]
        )

    def kept_load(i, d, h, slot):
        source = (kept_gate, kept_up)[i]
        return pltpu.make_async_copy(source.at[2 * d + h], kept.at[i, slot], kept_sem.at[i, slot])

    def source(p):
        inner = jnp.minimum(s, n - 1 - s)
        near = lax.div(p + 1, 2)
        paired = jnp.where(lax.rem(p, 2) == 1, s - near, s + near)
        far = p - inner
        single = jnp.where(s < n - 1 - s, s + far, s - far)
        return jnp.where(p <= 2 * inner, paired, single)

    barrier = pltpu.get_barrier_semaphore()
    pl.semaphore_signal(barrier, inc=1, device_id=twin, device_id_type=MESH)

    @pl.when(s > 0)
    def _():
        pl.semaphore_signal(barrier, inc=1, device_id={"seq": s - 1}, device_id_type=MESH)

    @pl.when(s < n - 1)
    def _():
        pl.semaphore_signal(barrier, inc=1, device_id={"seq": s + 1}, device_id_type=MESH)

    pl.semaphore_wait(barrier, 1 + jnp.where(s > 0, 1, 0) + jnp.where(s < n - 1, 1, 0))

    for h in range(2):

        @pl.when(s < n - 1)
        def _():
            token_right(s, h, tokens.at[h]).start()

        @pl.when(s > 0)
        def _():
            token_left(s, h, tokens.at[h]).start()

        token_twin(s, h, tokens.at[h]).start()
        own_load(h).start()
    load_units = pltpu.make_async_copy(units, units_v, weight_sem.at[0])
    load_downs = pltpu.make_async_copy(downs, downs_v, weight_sem.at[1])
    load_units.start()
    load_downs.start()
    if backward:
        for i in range(2):
            kept_load(i, s, 0, 0).start()
    load_units.wait()
    load_downs.wait()

    def add_rows(d, h, into_own, use_line):
        step = 16

        def body(i, carry):
            rows = pl.ds(pl.multiple_of(i * step, step), step)
            total = own_sum[d, h, rows, :] + twin_sum[d, h, rows, :].astype(jnp.float32)
            for slot in use_line:
                total = total + line[slot, h, rows, :].astype(jnp.float32)
            if into_own:
                own_sum[d, h, rows, :] = total
            else:
                twin_sum[d, h, rows, :] = total.astype(twin_sum.dtype)
            return carry

        lax.fori_loop(0, piece_len // step, body, 0)

    def combine(d, h):
        to_left = d < s
        slot = jnp.where(to_left, d, d + 1)
        more = jnp.where(to_left, s < n - 1, s > 0)
        part_twin(d, h).wait_recv()

        @pl.when(more)
        def _():
            line_arrival(slot, h).wait_recv()
            add_rows(d, h, False, (slot,))

        @pl.when(jnp.logical_not(more))
        def _():
            add_rows(d, h, False, ())

        part_line(d, h).start()

    columns = width // 3
    chunk = n_units // 3

    def compute_forward(d, h, slot):
        rows = held[d, h].reshape(2 * piece_len, width)
        for c in range(3):
            cols = slice(c * chunk, (c + 1) * chunk)
            gate = times_rows(rows, units_v[cols, :width])
            up = times_rows(rows, units_v[cols, width:])
            value, unused = gelu_pieces(gate)
            stage[0, slot, :, cols] = gate.astype(stage.dtype)
            stage[1, slot, :, cols] = up.astype(stage.dtype)
            stage[2, slot, :, cols] = (value * up).astype(stage.dtype)
        for c in range(3):
            cols = slice(c * columns, (c + 1) * columns)
            part = add_slice(stage[2, slot], downs_v[:, cols])
            own_sum[d, h, :, cols] = part[:piece_len]
            twin_out[d, h, :, cols] = part[piece_len:].astype(twin_out.dtype)

    def compute_backward(d, h, slot):
        rows = held[d, h].reshape(2 * piece_len, width)
        for c in range(3):
            cols = slice(c * chunk, (c + 1) * chunk)
            grad = times_rows(rows, downs_v[cols, :])
            value, slope = gelu_pieces(kept[0, slot, :, cols].astype(jnp.float32))
            up = kept[1, slot, :, cols].astype(jnp.float32)
            stage[0, slot, :, cols] = (grad * up * slope).astype(stage.dtype)
            stage[1, slot, :, cols] = (grad * value).astype(stage.dtype)
        for c in range(3):
            cols = slice(c * columns, (c + 1) * columns)
            later = slice(width + c * columns, width + (c + 1) * columns)
            part = add_slice(stage[0, slot], units_v[:, cols])
            part = part + add_slice(stage[1, slot], units_v[:, later])
            own_sum[d, h, :, cols] = part[:piece_len]
            twin_out[d, h, :, cols] = part[piece_len:].astype(twin_out.dtype)

    def unit(t, carry):
        d = source(lax.div(t, 2))
        h = lax.rem(t, 2)
        slot = lax.rem(t, 2)

        @pl.when(t < 2)
        def _():
            own_load(h).wait()

        @pl.when(t >= 2)
        def _():
            piece = held.at[d, h, 0]
            token_left(d, h, piece).wait_recv()

            @pl.when((d < s) & (s < n - 1))
            def _():
                token_right(d, h, piece).start()

            @pl.when((d > s) & (s > 0))
            def _():
                token_left(d, h, piece).start()

            token_twin(d, h, piece).start()
            for i in range(len(stage_outs)):
                stage_store(i, d, h, slot).wait()

        if backward:

            @pl.when(t < 2 * n - 1)
            def _():
                for i in range(2):
                    kept_load(
                        i, source(lax.div(t + 1, 2)), lax.rem(t + 1, 2), 1 - slot
                    ).start()

            for i in range(2):
                kept_load(i, d, h, slot).wait()
        token_twin(d, h, held.at[d, h, 0]).wait_recv()
        if backward:
            compute_backward(d, h, slot)
        else:
            compute_forward(d, h, slot)
        part_twin(d, h).start()
        all_store(d, h).start()
        for i in range(len(stage_outs)):
            stage_store(i, d, h, slot).start()

        @pl.when(at_end & (t >= 3))
        def _():
            combine(source(lax.div(t - 1, 2)), lax.rem(t - 1, 2))

        return carry

    lax.fori_loop(0, 2 * n, unit, 0)

    @pl.when(at_end)
    def _():
        combine(source(n - 1), 1)

    @pl.when(jnp.logical_not(at_end))
    def _():
        right_first = 2 * s < n - 1

        def middle(i, carry):
            h = lax.rem(i, 2)
            j = lax.rem(lax.div(i, 2), n - 1) + 1
            to_right = jnp.where(i < 2 * (n - 1), right_first, jnp.logical_not(right_first))
            d = jnp.where(to_right, s + j, s - j)

            @pl.when((d >= 0) & (d <= n - 1))
            def _():
                combine(d, h)

            return carry

        lax.fori_loop(0, 4 * (n - 1), middle, 0)

    def finish(h, carry):
        part_twin(s, h).wait_recv()

        @pl.when(s < n - 1)
        def _():
            line_arrival(s, h).wait_recv()

        @pl.when(s > 0)
        def _():
            line_arrival(s + 1, h).wait_recv()

        @pl.when(s == 0)
        def _():
            add_rows(s, h, True, (s,))

        @pl.when(s == n - 1)
        def _():
            add_rows(s, h, True, (s + 1,))

        @pl.when(jnp.logical_not(at_end))
        def _():
            add_rows(s, h, True, (s, s + 1))

        pltpu.make_async_copy(own_sum.at[s, h], out.at[h], out_sem.at[h]).start()
        return carry

    lax.fori_loop(0, 2, finish, 0)

    def drain(t, carry):
        d = lax.div(t, 2)
        h = lax.rem(t, 2)
        piece = held.at[d, h, 0]

        @pl.when((d <= s) & (s < n - 1))
        def _():
            token_right(d, h, piece).wait_send()

        @pl.when((d >= s) & (s > 0))
        def _():
            token_left(d, h, piece).wait_send()

        token_twin(d, h, piece).wait_send()
        part_twin(d, h).wait_send()

        @pl.when(d != s)
        def _():
            part_line(d, h).wait_send()

        all_store(d, h).wait()
        return carry

    lax.fori_loop(0, 2 * n, drain, 0)
    for h in range(2):
        for i in range(len(stage_outs)):
            stage_store(i, 0, h, h).wait()
        pltpu.make_async_copy(own_sum.at[s, h], out.at[h], out_sem.at[h]).wait()


def run_units(n_seq, tokens, units, downs, kept=None):
    backward = kept is not None
    low = tokens.dtype
    n_units = downs.shape[0]
    halves, piece_len, width = tokens.shape
    n_stage = 2 if backward else 3
    held = (n_seq, halves, 2, piece_len, width)
    unit_rows = (2 * n_seq, 2 * piece_len, n_units)
    sums = (n_seq, halves, piece_len, width)
    scratch = [
        pltpu.VMEM(units.shape, low),
        pltpu.VMEM(downs.shape, low),
        pltpu.VMEM(held, low),
        pltpu.VMEM(sums, jnp.float32),
        pltpu.VMEM(sums, low),
        pltpu.VMEM(sums, low),
        pltpu.VMEM((n_seq + 1,) + sums[1:], low),
        pltpu.VMEM((n_stage, 2) + unit_rows[1:], low),
    ]
    if backward:
        scratch += [pltpu.VMEM((2, 2) + unit_rows[1:], low), DMA((2, 2))]
    pairs = DMA((n_seq, halves))
    scratch += [DMA((2,)), DMA((halves,))] + [pairs] * 8
    scratch += [DMA((n_seq + 1, halves)), DMA((n_stage, 2)), pairs, DMA((halves,))]
    operands = (tokens, units, downs) + (tuple(kept) if backward else ())
    return pl.pallas_call(
        partial(units_kernel, n_seq, backward),
        out_shape=[
            jax.ShapeDtypeStruct(tokens.shape, jnp.float32),
            jax.ShapeDtypeStruct(held, low),
        ]
        + [jax.ShapeDtypeStruct(unit_rows, low)] * n_stage,
        in_specs=[ANY] * len(operands),
        out_specs=[ANY] * (2 + n_stage),
        scratch_shapes=scratch,
        compiler_params=pltpu.CompilerParams(
            collective_id=6 if backward else 5,
            has_side_effects=True,
            vmem_limit_bytes=62 * 1024 * 1024,
        ),
    )(*operands)


def per_device_general(
    hidden_in,
    norm_gains,
    qkv_weight,
    out_weight,
    gate_up_weight,
    down_weight,
    output_cotangent,
    segment_ids,
    padding,
    positions,
):
    everyone = ("seq", "chip", "core")
    plane = ("chip", "core")
    column = ("seq", "core")
    groups = hidden_in.shape[0]
    piece_len = hidden_in.shape[1]
    model_width = hidden_in.shape[2]
    row_count = groups * piece_len
    seq_len = segment_ids.shape[1]
    group_size = HEADS // KV_HEADS
    query_width = HEADS * HEAD_DIM
    key_width = KV_HEADS * HEAD_DIM
    proj_width = qkv_weight.shape[1]

    residual = hidden_in.reshape(row_count, model_width).astype(jnp.float32)
    factor = lax.rsqrt(jnp.mean(residual * residual, axis=-1, keepdims=True) + EPSILON)
    gain_cols = lax.all_gather(norm_gains, everyone, axis=0, tiled=True).astype(jnp.float32)
    qkv_full = lax.all_gather(qkv_weight, everyone, axis=0, tiled=True)
    attn_input = (residual * factor * gain_cols[:, 0]).astype(jnp.bfloat16)
    projected = add_slice(attn_input, qkv_full)
    cosine, sine_part = rotary_tables(positions.reshape(row_count), HEAD_DIM)
    queries = (
        rotate(projected[:, :query_width].reshape(row_count, HEADS, HEAD_DIM), cosine, sine_part)
        .astype(jnp.bfloat16)
        .reshape(row_count, query_width)
    )
    keys_here = (
        rotate(
            projected[:, query_width : query_width + key_width].reshape(
                row_count, KV_HEADS, HEAD_DIM
            ),
            cosine,
            sine_part,
        )
        .astype(jnp.bfloat16)
        .reshape(groups, piece_len, key_width)
    )
    values_here = (
        projected[:, query_width + key_width :]
        .astype(jnp.bfloat16)
        .reshape(groups, piece_len, key_width)
    )
    both_all = lax.all_gather(
        jnp.concatenate([keys_here, values_here], axis=2), plane, axis=1, tiled=True
    )
    keys_all = both_all[:, :, :key_width]
    values_all = both_all[:, :, key_width:]
    first_query = (lax.axis_index("chip") * 2 + lax.axis_index("core")) * piece_len
    query_rows = first_query + jnp.arange(piece_len, dtype=jnp.int32)
    key_rows = jnp.arange(seq_len, dtype=jnp.int32)
    segment_query = lax.dynamic_slice_in_dim(segment_ids, first_query, piece_len, 1)
    allowed = (segment_query[:, :, None] == segment_ids[:, None, :]) & (
        key_rows[None, None, :] <= query_rows[None, :, None]
    ) & (padding[:, None, :] == 1) | (key_rows[None, None, :] == query_rows[None, :, None])
    allowed = allowed[:, None, None]
    probs = soft_probs(score_block(queries, keys_all), allowed)
    attn_out = mix_values(probs.astype(jnp.bfloat16), values_all)
    out_full = lax.all_gather(out_weight, everyone, axis=0, tiled=True)
    attn_proj = times_rows(attn_out, out_full)
    after_attn = residual + rms_norm(attn_proj, gain_cols[:, 1])
    ffn_input = rms_norm(after_attn, gain_cols[:, 2]).astype(jnp.bfloat16)

    unit_weights = lax.all_gather(gate_up_weight, "chip", axis=0, tiled=True)
    down_units = lax.all_gather(down_weight, "chip", axis=0, tiled=True)
    ffn_all = lax.all_gather(ffn_input, column, axis=0, tiled=True)
    gate_part = times_rows(ffn_all, unit_weights[:, :model_width])
    up_part = times_rows(ffn_all, unit_weights[:, model_width:])
    hidden_part = geglu_parts(gate_part, up_part).astype(jnp.bfloat16)
    down_part = add_slice(hidden_part, down_units).astype(jnp.bfloat16)
    down_out = lax.psum_scatter(down_part, column, scatter_dimension=0, tiled=True).astype(
        jnp.float32
    )
    layer_out = after_attn + rms_norm(down_out, gain_cols[:, 3])
    layer_output = layer_out.astype(jnp.bfloat16).reshape(groups, piece_len, model_width)

    cotangent = output_cotangent.reshape(row_count, model_width).astype(jnp.float32)
    unused_last, pull_last = jax.vjp(rms_norm, down_out, gain_cols[:, 3])
    grad_down, grad_gain_last = pull_last(cotangent)
    grad_down_low = grad_down.astype(jnp.bfloat16)
    grad_down_all = lax.all_gather(grad_down_low, column, axis=0, tiled=True)
    grad_part = times_rows(grad_down_all, down_units)
    unused_units, pull_units = jax.vjp(geglu_parts, gate_part, up_part)
    grad_gate_part, grad_up_part = pull_units(grad_part)
    gate_low = grad_gate_part.astype(jnp.bfloat16)
    up_low = grad_up_part.astype(jnp.bfloat16)
    grad_ffn_part = add_slice(gate_low, unit_weights[:, :model_width]) + add_slice(
        up_low, unit_weights[:, model_width:]
    )
    grad_ffn_in = lax.psum_scatter(
        grad_ffn_part.astype(jnp.bfloat16), column, scatter_dimension=0, tiled=True
    ).astype(jnp.float32)
    gate_up_rows = jnp.concatenate(
        [
            outer_rows(gate_low, ffn_all).astype(jnp.bfloat16),
            outer_rows(up_low, ffn_all).astype(jnp.bfloat16),
        ],
        axis=1,
    )
    down_rows = outer_rows(hidden_part, grad_down_all).astype(jnp.bfloat16)
    gate_up_grad = lax.psum_scatter(
        gate_up_rows, "chip", scatter_dimension=0, tiled=True
    ).astype(jnp.float32)
    down_grad = lax.psum_scatter(down_rows, "chip", scatter_dimension=0, tiled=True).astype(
        jnp.float32
    )

    unused_mid, pull_mid = jax.vjp(rms_norm, after_attn, gain_cols[:, 2])
    grad_after_ffn, grad_gain_mid = pull_mid(grad_ffn_in)
    grad_after = cotangent + grad_after_ffn
    unused_post, pull_post = jax.vjp(rms_norm, attn_proj, gain_cols[:, 1])
    grad_proj, grad_gain_post = pull_post(grad_after)
    grad_proj_low = grad_proj.astype(jnp.bfloat16)
    grad_attn = add_slice(grad_proj_low, out_full).astype(jnp.bfloat16)
    scaled = score_block(queries, keys_all)
    probs, pull_probs = jax.vjp(partial(soft_probs, allowed=allowed), scaled)
    grad_heads = grad_attn.reshape(groups, piece_len, KV_HEADS, group_size, HEAD_DIM)
    query_heads = queries.reshape(groups, piece_len, KV_HEADS, group_size, HEAD_DIM)
    key_heads = keys_all.reshape(groups, seq_len, KV_HEADS, HEAD_DIM)
    value_heads = values_all.reshape(groups, seq_len, KV_HEADS, HEAD_DIM)
    grad_probs = jnp.einsum(
        "spkgd,slkd->skgpl", grad_heads, value_heads, preferred_element_type=jnp.float32
    )
    (grad_scaled,) = pull_probs(grad_probs)
    grad_scaled_low = grad_scaled.astype(jnp.bfloat16)
    inverse_root = 1.0 / math.sqrt(HEAD_DIM)
    grad_query_rot = (
        jnp.einsum(
            "skgpl,slkd->spkgd", grad_scaled_low, key_heads, preferred_element_type=jnp.float32
        )
        * inverse_root
    )
    grad_key_rot = (
        jnp.einsum(
            "skgpl,spkgd->slkd", grad_scaled_low, query_heads, preferred_element_type=jnp.float32
        )
        * inverse_root
    )
    grad_value_part = jnp.einsum(
        "skgpl,spkgd->slkd",
        probs.astype(jnp.bfloat16),
        grad_heads,
        preferred_element_type=jnp.float32,
    )
    both_grads = jnp.concatenate(
        [
            grad_key_rot.reshape(groups, seq_len, key_width),
            grad_value_part.reshape(groups, seq_len, key_width),
        ],
        axis=2,
    ).astype(jnp.bfloat16)
    both_summed = lax.psum_scatter(both_grads, plane, scatter_dimension=1, tiled=True)
    both_summed = both_summed.astype(jnp.float32).reshape(row_count, 2 * key_width)
    key_summed = both_summed[:, :key_width]
    value_summed = both_summed[:, key_width:]
    grad_queries = rotate_back(
        grad_query_rot.reshape(row_count, HEADS, HEAD_DIM), cosine, sine_part
    ).reshape(row_count, query_width)
    grad_keys = rotate_back(
        key_summed.reshape(row_count, KV_HEADS, HEAD_DIM), cosine, sine_part
    ).reshape(row_count, key_width)
    grad_projected = jnp.concatenate([grad_queries, grad_keys, value_summed], axis=1).astype(
        jnp.bfloat16
    )
    grad_attn_in = times_rows(grad_projected, qkv_full)
    unused_first, pull_first = jax.vjp(rms_norm, residual, gain_cols[:, 0])
    grad_res_first, grad_gain_first = pull_first(grad_attn_in)
    input_grad = (grad_after + grad_res_first).reshape(groups, piece_len, model_width)
    gain_terms = jnp.stack([grad_gain_first, grad_gain_post, grad_gain_mid, grad_gain_last], axis=1)
    qkv_part = outer_rows(attn_input, grad_projected).astype(jnp.bfloat16)
    out_part = outer_rows(grad_proj_low, attn_out).astype(jnp.bfloat16)
    qkv_grad = lax.psum_scatter(qkv_part, everyone, scatter_dimension=0, tiled=True).astype(
        jnp.float32
    )
    out_proj_grad = lax.psum_scatter(out_part, everyone, scatter_dimension=0, tiled=True).astype(
        jnp.float32
    )
    gain_grad = lax.psum_scatter(gain_terms, everyone, scatter_dimension=0, tiled=True)
    return (layer_output, input_grad, gain_grad, qkv_grad, out_proj_grad, gate_up_grad, down_grad)


def per_device_by_heads(
    n_seq,
    hidden_in,
    norm_gains,
    qkv_weight,
    out_weight,
    gate_up_weight,
    down_weight,
    output_cotangent,
    segment_ids,
    padding,
    positions,
):
    groups, piece_len, model_width = hidden_in.shape
    row_count = groups * piece_len
    seq_len = segment_ids.shape[1]
    n_chip = KV_HEADS
    n_plane = 2 * n_chip
    group_size = HEADS // KV_HEADS
    query_width = HEADS * HEAD_DIM
    key_width = KV_HEADS * HEAD_DIM
    own_width = group_size * HEAD_DIM
    part_width = own_width + 2 * HEAD_DIM
    block_width = part_width + own_width
    weight_rows = qkv_weight.shape[0]
    extra_rows = 16 - weight_rows % 16
    block_rows = weight_rows + extra_rows
    core = lax.axis_index("core")

    gain_rows = jnp.pad(
        norm_gains.T, ((0, extra_rows - norm_gains.shape[1]), (0, block_width - weight_rows))
    )
    blocks = jnp.stack(
        [
            jnp.concatenate(
                [
                    jnp.concatenate(
                        [
                            qkv_weight[:, c * own_width : (c + 1) * own_width],
                            qkv_weight[
                                :, query_width + c * HEAD_DIM : query_width + (c + 1) * HEAD_DIM
                            ],
                            qkv_weight[
                                :,
                                query_width + key_width + c * HEAD_DIM : query_width
                                + key_width
                                + (c + 1) * HEAD_DIM,
                            ],
                            out_weight[:, c * own_width : (c + 1) * own_width],
                        ],
                        axis=1,
                    ),
                    gain_rows,
                ],
                axis=0,
            )
            for c in range(n_chip)
        ]
    )
    hidden_all, blocks_all = gather_first(n_seq, hidden_in, blocks)
    unit_weights = lax.all_gather(gate_up_weight, "chip", axis=0, tiled=True)
    down_units = lax.all_gather(down_weight, "chip", axis=0, tiled=True)
    blocks_all = blocks_all.transpose(0, 2, 1, 3, 4)
    own_weights = blocks_all[:, :, :, :weight_rows].reshape(model_width, block_width)
    own_qkv = own_weights[:, :part_width]
    own_out = own_weights[:, part_width:]
    gain_cols = (
        blocks_all[:, :, :, weight_rows : weight_rows + norm_gains.shape[1], :weight_rows]
        .transpose(0, 1, 2, 4, 3)
        .reshape(model_width, norm_gains.shape[1])
        .astype(jnp.float32)
    )

    seq_rows = hidden_all.reshape(seq_len, model_width).astype(jnp.float32)
    seq_factor = lax.rsqrt(jnp.mean(seq_rows * seq_rows, axis=-1, keepdims=True) + EPSILON)
    attn_input = (seq_rows * seq_factor * gain_cols[:, 0]).astype(jnp.bfloat16)
    projected = add_slice(attn_input, own_qkv)
    segment = lax.dynamic_index_in_dim(segment_ids, core, 0, keepdims=False)
    valid = lax.dynamic_index_in_dim(padding, core, 0, keepdims=False)
    token = jnp.arange(seq_len, dtype=jnp.int32)
    document_start = jnp.min(
        jnp.where(segment[:, None] == segment[None, :], token[None, :], seq_len), axis=1
    )
    cosine, sine_part = rotary_tables(token - document_start, HEAD_DIM)
    queries = (
        rotate(projected[:, :own_width].reshape(seq_len, group_size, HEAD_DIM), cosine, sine_part)
        .astype(jnp.bfloat16)
        .reshape(seq_len, own_width)
    )
    keys = (
        rotate(
            projected[:, own_width : own_width + HEAD_DIM].reshape(seq_len, 1, HEAD_DIM),
            cosine,
            sine_part,
        )
        .astype(jnp.bfloat16)
        .reshape(seq_len, HEAD_DIM)
    )
    values = projected[:, own_width + HEAD_DIM :].astype(jnp.bfloat16)
    segment_col = segment[:, None]
    segment_row = jnp.where(valid == 1, segment, -1)[None, :]
    attn_out = attend(queries, keys, values, segment_col, segment_row)
    proj_parts = times_rows(attn_out, own_out).astype(jnp.bfloat16)
    proj_parts = plane_exchange(
        proj_parts.reshape(n_plane, piece_len, model_width), False, 2
    )

    def sum_parts(parts):
        parts = parts.reshape(n_chip, groups, piece_len, model_width).astype(jnp.float32)
        return jnp.sum(parts, axis=0).reshape(row_count, model_width)

    attn_proj = sum_parts(proj_parts)
    residual = hidden_in.reshape(row_count, model_width).astype(jnp.float32)
    after_attn = residual + rms_norm(attn_proj, gain_cols[:, 1])
    ffn_input = rms_norm(after_attn, gain_cols[:, 2]).astype(jnp.bfloat16)

    pieces = (groups, piece_len, model_width)
    down_out, ffn_all, gate_part, up_part, hidden_part = run_units(
        n_seq, ffn_input.reshape(pieces), unit_weights, down_units
    )
    down_out = down_out.reshape(row_count, model_width)
    layer_out = after_attn + rms_norm(down_out, gain_cols[:, 3])
    layer_output = layer_out.astype(jnp.bfloat16).reshape(pieces)

    cotangent = output_cotangent.reshape(row_count, model_width).astype(jnp.float32)
    unused_last, pull_last = jax.vjp(rms_norm, down_out, gain_cols[:, 3])
    grad_down, grad_gain_last = pull_last(cotangent)
    grad_ffn_in, grad_down_all, gate_low, up_low = run_units(
        n_seq,
        grad_down.astype(jnp.bfloat16).reshape(pieces),
        unit_weights,
        down_units,
        (gate_part, up_part),
    )
    grad_ffn_in = grad_ffn_in.reshape(row_count, model_width)
    ffn_all = ffn_all.reshape(-1, model_width)
    grad_down_all = grad_down_all.reshape(-1, model_width)
    n_units = down_units.shape[0]
    gate_low, up_low, hidden_part = (
        array.reshape(-1, n_units) for array in (gate_low, up_low, hidden_part)
    )
    gate_up_rows = jnp.concatenate(
        [
            outer_rows(gate_low, ffn_all).astype(jnp.bfloat16),
            outer_rows(up_low, ffn_all).astype(jnp.bfloat16),
        ],
        axis=1,
    )
    down_rows = outer_rows(hidden_part, grad_down_all).astype(jnp.bfloat16)
    gate_up_grad = lax.psum_scatter(
        gate_up_rows, "chip", scatter_dimension=0, tiled=True
    ).astype(jnp.float32)
    down_grad = lax.psum_scatter(down_rows, "chip", scatter_dimension=0, tiled=True).astype(
        jnp.float32
    )

    unused_mid, pull_mid = jax.vjp(rms_norm, after_attn, gain_cols[:, 2])
    grad_after_ffn, grad_gain_mid = pull_mid(grad_ffn_in)
    grad_after = cotangent + grad_after_ffn
    unused_post, pull_post = jax.vjp(rms_norm, attn_proj, gain_cols[:, 1])
    grad_proj, grad_gain_post = pull_post(grad_after)
    grad_proj_low = grad_proj.astype(jnp.bfloat16)

    grad_proj_all = plane_exchange(
        grad_proj_low.reshape(groups, piece_len, model_width), True, 3
    ).reshape(seq_len, model_width)
    grad_attn = add_slice(grad_proj_all, own_out).astype(jnp.bfloat16)
    grad_query_rot, grad_key_rot, grad_values = attend_back(
        queries, keys, values, segment_col, segment_row, grad_attn
    )
    grad_queries = rotate_back(
        grad_query_rot.reshape(seq_len, group_size, HEAD_DIM), cosine, sine_part
    ).reshape(seq_len, own_width)
    grad_keys = rotate_back(
        grad_key_rot.reshape(seq_len, 1, HEAD_DIM), cosine, sine_part
    ).reshape(seq_len, HEAD_DIM)
    grad_projected = jnp.concatenate([grad_queries, grad_keys, grad_values], axis=1).astype(
        jnp.bfloat16
    )
    grad_in_part = times_rows(grad_projected, own_qkv)
    grad_gain_first = jnp.sum(grad_in_part * seq_rows * seq_factor, axis=0)
    weight_part = jnp.concatenate(
        [
            outer_rows(attn_input, grad_projected).astype(jnp.bfloat16),
            outer_rows(grad_proj_all, attn_out).astype(jnp.bfloat16),
        ],
        axis=1,
    ).reshape(n_seq, n_chip, 2, weight_rows, block_width)
    gain_terms = (
        jnp.stack([grad_gain_first, grad_gain_post, grad_gain_mid, grad_gain_last])
        .astype(jnp.bfloat16)
        .reshape(-1, n_seq, n_chip, 2, weight_rows)
        .transpose(1, 2, 3, 0, 4)
    )
    gain_terms = jnp.pad(
        gain_terms,
        ((0, 0),) * 3
        + ((0, extra_rows - gain_terms.shape[3]), (0, block_width - weight_rows)),
    )
    grad_blocks = jnp.concatenate([weight_part, gain_terms], axis=3).transpose(0, 2, 1, 3, 4)
    grad_in_parts, grad_sums = sum_last(
        n_seq,
        grad_in_part.astype(jnp.bfloat16).reshape(n_plane, piece_len, model_width),
        grad_blocks,
    )
    grad_attn_in = sum_parts(grad_in_parts)
    factor = lax.rsqrt(jnp.mean(residual * residual, axis=-1, keepdims=True) + EPSILON)
    unused_first, pull_first = jax.vjp(rms_norm, residual, gain_cols[:, 0])
    grad_res_first, unused_gain = pull_first(grad_attn_in)
    input_grad = (grad_after + grad_res_first).reshape(groups, piece_len, model_width)

    weight_sums = grad_sums[:, :weight_rows].astype(jnp.float32)
    qkv_grad = jnp.concatenate(
        [weight_sums[c, :, :own_width] for c in range(n_chip)]
        + [weight_sums[c, :, own_width : own_width + HEAD_DIM] for c in range(n_chip)]
        + [weight_sums[c, :, own_width + HEAD_DIM : part_width] for c in range(n_chip)],
        axis=1,
    )
    out_proj_grad = jnp.concatenate(
        [weight_sums[c, :, part_width:] for c in range(n_chip)], axis=1
    )
    gain_grad = jnp.sum(
        grad_sums[:, weight_rows : weight_rows + norm_gains.shape[1], :weight_rows].astype(
            jnp.float32
        ),
        axis=0,
    ).T
    return (layer_output, input_grad, gain_grad, qkv_grad, out_proj_grad, gate_up_grad, down_grad)


def solution(mesh):
    n_seq = mesh.shape["seq"]
    n_ctx = mesh.shape["ctx"]
    split_mesh = jax.sharding.Mesh(
        mesh.devices.reshape(n_seq, n_ctx // 2, 2), ("seq", "chip", "core")
    )
    plane = ("chip", "core")
    rows = P(("seq", "chip", "core"), None)
    tokens = P("seq", plane, None)
    placed = (
        tokens,
        rows,
        rows,
        rows,
        rows,
        rows,
        tokens,
        P("seq", None),
        P("seq", None),
        P("seq", plane),
    )

    def step(*arrays):
        groups = arrays[0].shape[0]
        if n_ctx // 2 == KV_HEADS and groups == 2:
            return per_device_by_heads(n_seq, *arrays)
        return per_device_general(*arrays)

    return jax.shard_map(
        step,
        mesh=split_mesh,
        in_specs=placed,
        out_specs=(tokens, tokens, rows, rows, rows, rows, rows),
        check_vma=False,
    )
```

```python
from functools import partial
import math

import jax
import jax.numpy as jnp
from jax import lax
from jax.experimental import pallas as pl
from jax.experimental.pallas import tpu as pltpu
from jax.sharding import PartitionSpec as P

HEADS = 8
KV_HEADS = 4
HEAD_DIM = 256


EPSILON = 1e-06
SOFT_CAP = 50.0
MASKED = -1e30


def rms_norm(matrix, gain_col):
    factor = lax.rsqrt(jnp.mean(matrix * matrix, axis=-1, keepdims=True) + EPSILON)
    return matrix * factor * gain_col


def rotary_tables(positions, head_dim):
    half_dim = head_dim // 2
    frequency = jnp.exp(
        jnp.arange(half_dim, dtype=jnp.float32) * (-2.0 * math.log(10000.0) / head_dim)
    )
    phase_angle = positions.astype(jnp.float32)[:, None] * frequency[None, :]
    return (jnp.cos(phase_angle)[:, None, :], jnp.sin(phase_angle)[:, None, :])


def rotate(vectors, cosine, sine_part):
    half_dim = vectors.shape[-1] // 2
    first_half = vectors[..., :half_dim]
    second_half = vectors[..., half_dim:]
    return jnp.concatenate(
        [
            first_half * cosine - second_half * sine_part,
            second_half * cosine + first_half * sine_part,
        ],
        axis=-1,
    )


def rotate_back(grads, cosine, sine_part):
    half_dim = grads.shape[-1] // 2
    first_half = grads[..., :half_dim]
    second_half = grads[..., half_dim:]
    return jnp.concatenate(
        [
            first_half * cosine + second_half * sine_part,
            second_half * cosine - first_half * sine_part,
        ],
        axis=-1,
    )


def soft_probs(scaled, allowed):
    capped = SOFT_CAP * jnp.tanh(scaled / SOFT_CAP)
    capped = jnp.where(allowed, capped, MASKED)
    return jax.nn.softmax(capped, axis=-1)


def geglu_parts(gate_part, up_part):
    return jax.nn.gelu(gate_part, approximate=True) * up_part


def score_block(queries, keys_all):
    groups = keys_all.shape[0]
    seq_len = keys_all.shape[1]
    piece_len = queries.shape[0] // groups
    query_heads = queries.reshape(groups, piece_len, KV_HEADS, HEADS // KV_HEADS, HEAD_DIM)
    key_heads = keys_all.reshape(groups, seq_len, KV_HEADS, HEAD_DIM)
    raw_score = jnp.einsum(
        "spkgd,slkd->skgpl", query_heads, key_heads, preferred_element_type=jnp.float32
    )
    return raw_score * (1.0 / math.sqrt(HEAD_DIM))


def mix_values(weights_low, values_all):
    groups = values_all.shape[0]
    seq_len = values_all.shape[1]
    piece_len = weights_low.shape[3]
    value_heads = values_all.reshape(groups, seq_len, KV_HEADS, HEAD_DIM)
    mixed = jnp.einsum(
        "skgpl,slkd->spkgd", weights_low, value_heads, preferred_element_type=jnp.float32
    )
    return mixed.reshape(groups * piece_len, HEADS * HEAD_DIM).astype(jnp.bfloat16)


def add_slice(left, weight_piece):
    return jnp.dot(left, weight_piece, preferred_element_type=jnp.float32)


def times_rows(left, weight_piece):
    return lax.dot_general(
        left, weight_piece, (((1,), (1,)), ((), ())), preferred_element_type=jnp.float32
    )


def outer_rows(left, right):
    return lax.dot_general(
        left, right, (((0,), (0,)), ((), ())), preferred_element_type=jnp.float32
    )


MESH = pl.DeviceIdType.MESH
ANY = pl.BlockSpec(memory_space=pl.ANY)
DMA = pltpu.SemaphoreType.DMA


def remote(source, target, send_sem, recv_sem, device):
    return pltpu.make_async_remote_copy(
        src_ref=source,
        dst_ref=target,
        send_sem=send_sem,
        recv_sem=recv_sem,
        device_id=device,
        device_id_type=MESH,
    )


def plane_device(index):
    return {"chip": index // 2, "core": lax.rem(index, 2)}


def greet(n_plane, n_seq):
    me = lax.axis_index("chip") * 2 + lax.axis_index("core")
    barrier = pltpu.get_barrier_semaphore()
    for step in range(1, n_plane):
        pl.semaphore_signal(
            barrier,
            inc=1,
            device_id=plane_device(lax.rem(me + step, n_plane)),
            device_id_type=MESH,
        )
    count = n_plane - 1
    if n_seq > 1:
        s = lax.axis_index("seq")

        @pl.when(s > 0)
        def _():
            pl.semaphore_signal(barrier, inc=1, device_id={"seq": s - 1}, device_id_type=MESH)

        @pl.when(s < n_seq - 1)
        def _():
            pl.semaphore_signal(barrier, inc=1, device_id={"seq": s + 1}, device_id_type=MESH)

        count = count + jnp.where(s > 0, 1, 0) + jnp.where(s < n_seq - 1, 1, 0)
    pl.semaphore_wait(barrier, count)


def start_exchange(n_plane, by_core, source, target, send_sems, recv_sems, local_sem):
    me = lax.axis_index("chip") * 2 + lax.axis_index("core")
    copies = []
    for step in (4, 2, 6, 3, 5, 1, 7):
        to = lax.rem(me + step, n_plane)
        block = lax.rem(to, 2) if by_core else to
        copy = remote(
            source.at[block],
            target.at[me],
            send_sems.at[step],
            recv_sems.at[step],
            plane_device(to),
        )
        copy.start()
        copies.append(copy)
    block = lax.rem(me, 2) if by_core else me
    own = pltpu.make_async_copy(source.at[block], target.at[me], local_sem.at[0])
    own.start()
    copies.append(own)
    return copies


def exchange_kernel(n_plane, by_core, source, target, send_sems, recv_sems, local_sem):
    greet(n_plane, 1)
    for copy in start_exchange(
        n_plane, by_core, source, target, send_sems, recv_sems, local_sem
    ):
        copy.wait()


def plane_exchange(blocks, by_core, collective_id):
    n_plane = 2 * KV_HEADS
    return pl.pallas_call(
        partial(exchange_kernel, n_plane, by_core),
        out_shape=jax.ShapeDtypeStruct((n_plane,) + blocks.shape[1:], blocks.dtype),
        in_specs=[ANY],
        out_specs=ANY,
        scratch_shapes=[DMA((n_plane,)), DMA((n_plane,)), DMA((1,))],
        compiler_params=pltpu.CompilerParams(
            collective_id=collective_id, has_side_effects=True
        ),
    )(blocks)


def gather_kernel(
    n_seq,
    n_plane,
    hidden,
    blocks,
    hidden_all,
    blocks_all,
    hid_send,
    hid_recv,
    hid_local,
    chip_send,
    chip_recv,
    chip_local,
    left_send,
    right_send,
    line_recv,
    twin_send,
    twin_recv,
):
    n_chip = n_plane // 2
    s = lax.axis_index("seq")
    q = lax.axis_index("chip")
    k = lax.axis_index("core")
    greet(n_plane, n_seq)
    swaps = []
    for step in range(1, n_chip):
        to = lax.rem(q + step, n_chip)
        copy = remote(
            blocks.at[to],
            blocks_all.at[s, k, q],
            chip_send.at[step],
            chip_recv.at[step],
            {"chip": to},
        )
        copy.start()
        swaps.append(copy)
    own = pltpu.make_async_copy(blocks.at[q], blocks_all.at[s, k, q], chip_local.at[0])
    own.start()
    hidden_copies = start_exchange(
        n_plane, True, hidden, hidden_all, hid_send, hid_recv, hid_local
    )
    for copy in swaps:
        copy.wait_recv()
    own.wait()

    def to_left(d):
        return remote(
            blocks_all.at[d, k], blocks_all.at[d, k], left_send.at[d], line_recv.at[d], {"seq": s - 1}
        )

    def to_right(d):
        return remote(
            blocks_all.at[d, k], blocks_all.at[d, k], right_send.at[d], line_recv.at[d], {"seq": s + 1}
        )

    def to_twin(d):
        return remote(
            blocks_all.at[d, k], blocks_all.at[d, k], twin_send.at[d], twin_recv.at[d], {"core": 1 - k}
        )

    def from_twin(d):
        return remote(
            blocks_all.at[d, 1 - k],
            blocks_all.at[d, 1 - k],
            twin_send.at[d],
            twin_recv.at[d],
            {"core": 1 - k},
        )

    @pl.when(s > 0)
    def _():
        to_left(s).start()

    @pl.when(s < n_seq - 1)
    def _():
        to_right(s).start()

    to_twin(s).start()
    for hop in range(1, n_seq):
        from_left = s - hop
        from_right = s + hop

        @pl.when(from_left >= 0)
        def _():
            to_left(from_left).wait_recv()

            @pl.when(s < n_seq - 1)
            def _():
                to_right(from_left).start()

            to_twin(from_left).start()

        @pl.when(from_right < n_seq)
        def _():
            to_right(from_right).wait_recv()

            @pl.when(s > 0)
            def _():
                to_left(from_right).start()

            to_twin(from_right).start()

    for d in range(n_seq):

        @pl.when((d >= s) & (s > 0))
        def _():
            to_left(d).wait_send()

        @pl.when((d <= s) & (s < n_seq - 1))
        def _():
            to_right(d).wait_send()

        to_twin(d).wait_send()
        from_twin(d).wait_recv()
    for copy in swaps:
        copy.wait_send()
    for copy in hidden_copies:
        copy.wait()


def gather_first(n_seq, hidden, blocks):
    n_plane = 2 * KV_HEADS
    n_chip = KV_HEADS
    return pl.pallas_call(
        partial(gather_kernel, n_seq, n_plane),
        out_shape=[
            jax.ShapeDtypeStruct((n_plane,) + hidden.shape[1:], hidden.dtype),
            jax.ShapeDtypeStruct((n_seq, 2) + blocks.shape, blocks.dtype),
        ],
        in_specs=[ANY, ANY],
        out_specs=[ANY, ANY],
        scratch_shapes=[
            DMA((n_plane,)),
            DMA((n_plane,)),
            DMA((1,)),
            DMA((n_chip,)),
            DMA((n_chip,)),
            DMA((1,)),
            DMA((n_seq,)),
            DMA((n_seq,)),
            DMA((n_seq,)),
            DMA((n_seq,)),
            DMA((n_seq,)),
        ],
        compiler_params=pltpu.CompilerParams(collective_id=1, has_side_effects=True),
    )(hidden, blocks)


def last_kernel(
    n_seq,
    n_plane,
    parts,
    blocks,
    parts_all,
    sums,
    held,
    twin,
    line,
    part_send,
    part_recv,
    part_local,
    held_sem,
    twin_send,
    twin_recv,
    line_send,
    line_recv,
    chip_send,
    chip_recv,
    chip_local,
):
    n_chip = n_plane // 2
    s = lax.axis_index("seq")
    q = lax.axis_index("chip")
    k = lax.axis_index("core")
    greet(n_plane, n_seq)

    def load(d):
        return pltpu.make_async_copy(blocks.at[d, k], held.at[d], held_sem.at[d])

    def to_twin(d):
        return remote(
            blocks.at[d, 1 - k], twin.at[d], twin_send.at[d], twin_recv.at[d], {"core": 1 - k}
        )

    def to_left(d):
        return remote(held.at[d], line.at[d], line_send.at[d], line_recv.at[d], {"seq": s - 1})

    def to_right(d):
        return remote(
            held.at[d], line.at[d + 1], line_send.at[d], line_recv.at[d + 1], {"seq": s + 1}
        )

    def gather_terms(d, with_left, with_right):
        load(d).wait()
        to_twin(d).wait_recv()

        @pl.when(with_right)
        def _():
            to_left(d).wait_recv()

        @pl.when(with_left)
        def _():
            to_right(d).wait_recv()

        def body(i, carry):
            held[d, i] = (held[d, i].astype(jnp.float32) + twin[d, i].astype(jnp.float32)).astype(
                held.dtype
            )
            return carry

        def body_right(i, carry):
            total = held[d, i].astype(jnp.float32) + twin[d, i].astype(jnp.float32)
            held[d, i] = (total + line[d, i].astype(jnp.float32)).astype(held.dtype)
            return carry

        def body_left(i, carry):
            total = held[d, i].astype(jnp.float32) + twin[d, i].astype(jnp.float32)
            held[d, i] = (total + line[d + 1, i].astype(jnp.float32)).astype(held.dtype)
            return carry

        def body_both(i, carry):
            total = held[d, i].astype(jnp.float32) + twin[d, i].astype(jnp.float32)
            total = total + line[d, i].astype(jnp.float32)
            held[d, i] = (total + line[d + 1, i].astype(jnp.float32)).astype(held.dtype)
            return carry

        @pl.when(jnp.logical_not(with_left) & jnp.logical_not(with_right))
        def _():
            lax.fori_loop(0, n_chip, body, 0)

        @pl.when(jnp.logical_not(with_left) & with_right)
        def _():
            lax.fori_loop(0, n_chip, body_right, 0)

        @pl.when(with_left & jnp.logical_not(with_right))
        def _():
            lax.fori_loop(0, n_chip, body_left, 0)

        @pl.when(with_left & with_right)
        def _():
            lax.fori_loop(0, n_chip, body_both, 0)

    for d in range(n_seq):
        to_twin(d).start()
        load(d).start()
    part_copies = start_exchange(
        n_plane, False, parts, parts_all, part_send, part_recv, part_local
    )
    never = s < 0
    for hop in range(1, n_seq):
        left = hop - n_seq + s
        right = n_seq - hop + s

        @pl.when(left >= 0)
        def _():
            gather_terms(left, never, s < n_seq - 1)
            to_left(left).start()

        @pl.when(right <= n_seq - 1)
        def _():
            gather_terms(right, s > 0, never)
            to_right(right).start()

    gather_terms(s, s > 0, s < n_seq - 1)
    swaps = []
    for step in range(1, n_chip):
        to = lax.rem(q + step, n_chip)
        copy = remote(
            held.at[s, to], sums.at[q], chip_send.at[step], chip_recv.at[step], {"chip": to}
        )
        copy.start()
        swaps.append(copy)
    own = pltpu.make_async_copy(held.at[s, q], sums.at[q], chip_local.at[0])
    own.start()
    for d in range(n_seq):
        to_twin(d).wait_send()

        @pl.when(d < s)
        def _():
            to_left(d).wait_send()

        @pl.when(d > s)
        def _():
            to_right(d).wait_send()

    for copy in part_copies:
        copy.wait()
    for copy in swaps:
        copy.wait()
    own.wait()


def sum_last(n_seq, parts, blocks):
    n_plane = 2 * KV_HEADS
    n_chip = KV_HEADS
    block = blocks.shape[2:]
    return pl.pallas_call(
        partial(last_kernel, n_seq, n_plane),
        out_shape=[
            jax.ShapeDtypeStruct(parts.shape, parts.dtype),
            jax.ShapeDtypeStruct(block, blocks.dtype),
        ],
        in_specs=[ANY, ANY],
        out_specs=[ANY, ANY],
        scratch_shapes=[
            pltpu.VMEM((n_seq,) + block, blocks.dtype),
            pltpu.VMEM((n_seq,) + block, blocks.dtype),
            pltpu.VMEM((n_seq + 1,) + block, blocks.dtype),
            DMA((n_plane,)),
            DMA((n_plane,)),
            DMA((1,)),
            DMA((n_seq,)),
            DMA((n_seq,)),
            DMA((n_seq,)),
            DMA((n_seq,)),
            DMA((n_seq + 1,)),
            DMA((n_chip,)),
            DMA((n_chip,)),
            DMA((1,)),
        ],
        compiler_params=pltpu.CompilerParams(
            collective_id=4, has_side_effects=True, vmem_limit_bytes=32 * 1024 * 1024
        ),
    )(parts, blocks)


QUERY_BLOCK = 256


def block_probs(query, keys, segment_col, segment_row, first):
    rows, width = query.shape[0], keys.shape[0]
    scaled = times_rows(query, keys) * (1.0 / math.sqrt(HEAD_DIM))
    bent = jnp.tanh(scaled / SOFT_CAP)
    row = first + lax.broadcasted_iota(jnp.int32, (rows, width), 0)
    col = lax.broadcasted_iota(jnp.int32, (rows, width), 1)
    allowed = ((segment_col == segment_row) & (col <= row)) | (col == row)
    capped = jnp.where(allowed, SOFT_CAP * bent, MASKED)
    raised = jnp.exp(capped - jnp.max(capped, axis=-1, keepdims=True))
    return raised / jnp.sum(raised, axis=-1, keepdims=True), bent


def attend_kernel(group_size, queries, keys, values, segment_col, segment_row, out):
    seq_len = keys.shape[0]
    for first in range(0, seq_len, QUERY_BLOCK):
        rows = slice(first, first + QUERY_BLOCK)
        width = first + QUERY_BLOCK
        for head in range(group_size):
            cols = slice(head * HEAD_DIM, (head + 1) * HEAD_DIM)
            probs, unused = block_probs(
                queries[rows, cols],
                keys[:width],
                segment_col[rows, :],
                segment_row[:, :width],
                first,
            )
            out[rows, cols] = add_slice(probs.astype(jnp.bfloat16), values[:width]).astype(
                out.dtype
            )


def attend(queries, keys, values, segment_col, segment_row):
    return pl.pallas_call(
        partial(attend_kernel, queries.shape[1] // HEAD_DIM),
        out_shape=jax.ShapeDtypeStruct(queries.shape, jnp.bfloat16),
        compiler_params=pltpu.CompilerParams(vmem_limit_bytes=40 * 1024 * 1024),
    )(queries, keys, values, segment_col, segment_row)


def attend_back_kernel(
    group_size,
    queries,
    keys,
    values,
    segment_col,
    segment_row,
    grads,
    grad_queries,
    grad_keys,
    grad_values,
):
    seq_len = keys.shape[0]
    inverse_root = 1.0 / math.sqrt(HEAD_DIM)
    grad_keys[...] = jnp.zeros_like(grad_keys)
    grad_values[...] = jnp.zeros_like(grad_values)
    for first in range(0, seq_len, QUERY_BLOCK):
        rows = slice(first, first + QUERY_BLOCK)
        width = first + QUERY_BLOCK
        for head in range(group_size):
            cols = slice(head * HEAD_DIM, (head + 1) * HEAD_DIM)
            query = queries[rows, cols]
            probs, bent = block_probs(
                query, keys[:width], segment_col[rows, :], segment_row[:, :width], first
            )
            grad = grads[rows, cols]
            grad_probs = times_rows(grad, values[:width])
            mean = jnp.sum(probs * grad_probs, axis=-1, keepdims=True)
            grad_scaled = (probs * (grad_probs - mean) * (1.0 - bent * bent)).astype(jnp.bfloat16)
            grad_queries[rows, cols] = add_slice(grad_scaled, keys[:width]) * inverse_root
            grad_keys[:width, :] += outer_rows(grad_scaled, query) * inverse_root
            grad_values[:width, :] += outer_rows(probs.astype(jnp.bfloat16), grad)


def attend_back(queries, keys, values, segment_col, segment_row, grads):
    return pl.pallas_call(
        partial(attend_back_kernel, queries.shape[1] // HEAD_DIM),
        out_shape=[
            jax.ShapeDtypeStruct(queries.shape, jnp.float32),
            jax.ShapeDtypeStruct(keys.shape, jnp.float32),
            jax.ShapeDtypeStruct(values.shape, jnp.float32),
        ],
        compiler_params=pltpu.CompilerParams(vmem_limit_bytes=40 * 1024 * 1024),
    )(queries, keys, values, segment_col, segment_row, grads)


def unit_orders(n):
    units, sums = [], []
    for s in range(n):
        keyed = []
        for d in range(n):
            if d != s:
                near = abs(s - d)
                behind, past = (s, d) if d < s else (n - 1 - s, n - 1 - d)
                keyed += [(near, d, 0), (behind + past + 1, d, 1)]
        order = [(s, 0), (s, 1)] + [(d, h) for unused, d, h in sorted(keyed)]
        units.append([2 * d + h for d, h in order])
        if s in (0, n - 1):
            sums.append(units[-1][2:])
            continue
        keyed = []
        for d in range(n):
            if d != s:
                hops, place = (n - 2 - s, d) if d < s else (s - 1, n - 1 - d)
                keyed += [(n - 2 - place + hops, d, 0), (n - 1 + place + hops, d, 1)]
        sums.append([2 * d + h for unused, d, h in sorted(keyed)])
    return units, sums


def pick(table, s, i):
    width = len(table[0])
    place = s * width + i
    value = 0
    for k, entry in enumerate(entry for row in table for entry in row):
        value = jnp.where(place == k, entry, value)
    return value


SUBS = 1
SUM_TURNS = (0, 1, 5, 6, 11, 12)
GELU_SCALE = math.sqrt(2.0 / math.pi)


def gelu_pieces(gate):
    bend = jnp.tanh(GELU_SCALE * (gate + 0.044715 * gate * gate * gate))
    value = 0.5 * gate * (1.0 + bend)
    slope = 0.5 * (1.0 + bend) + 0.5 * gate * (1.0 - bend * bend) * GELU_SCALE * (
        1.0 + 3.0 * 0.044715 * gate * gate
    )
    return value, slope


def units_kernel(n_seq, backward, *refs):
    if backward:
        tokens, units, downs, kept_gate, kept_up, kept_hidden, inputs = refs[:7]
        out, first_out, second_out, unit_grads, down_grads = refs[7:12]
        stage_outs = (first_out, second_out)
        scratch = refs[12:]
    else:
        tokens, units, downs = refs[:3]
        out, tokens_all, first_out, second_out, third_out = refs[3:8]
        stage_outs = (first_out, second_out, third_out)
        scratch = refs[8:]
    units_v, downs_v, held, own_sum, twin_sum, twin_out, line, stage = scratch[:8]
    scratch = scratch[8:]
    if backward:
        kept, kept_sem, tile, tile_sem, load_sem, rows_sem = scratch[:6]
        scratch = scratch[6:]
    (
        weight_sem,
        own_sem,
        left_send,
        right_send,
        token_recv,
        twin_send,
        twin_recv,
        part_send,
        part_recv,
        line_send,
        line_recv,
        stage_sem,
        all_sem,
        out_sem,
    ) = scratch
    n = n_seq
    s = lax.axis_index("seq")
    k = lax.axis_index("core")
    twin = {"core": 1 - k}
    n_units, width = downs_v.shape
    piece_len = tokens.shape[1]
    at_end = (s == 0) | (s == n - 1)

    def token_left(d, h, source):
        return remote(
            source, held.at[d, h, 0], left_send.at[d, h], token_recv.at[d, h], {"seq": s - 1}
        )

    def token_right(d, h, source):
        return remote(
            source, held.at[d, h, 0], right_send.at[d, h], token_recv.at[d, h], {"seq": s + 1}
        )

    def token_twin(d, h, source):
        return remote(source, held.at[d, h, 1], twin_send.at[d, h], twin_recv.at[d, h], twin)

    def part_twin(d, h):
        return remote(
            twin_out.at[d, h], twin_sum.at[d, h], part_send.at[d, h], part_recv.at[d, h], twin
        )

    sub_len = piece_len // SUBS

    def part_line(d, h, sub):
        to_left = d < s
        slot = jnp.where(to_left, d, d + 1)
        rows = pl.ds(sub * sub_len, sub_len)
        return remote(
            twin_sum.at[d, h, rows],
            line.at[slot, h, rows],
            line_send.at[d, h, sub],
            line_recv.at[slot, h, sub],
            {"seq": jnp.where(to_left, s - 1, s + 1)},
        )

    def line_arrival(slot, h, sub):
        rows = pl.ds(sub * sub_len, sub_len)
        return remote(
            twin_sum.at[0, h, rows],
            line.at[slot, h, rows],
            line_send.at[0, h, sub],
            line_recv.at[slot, h, sub],
            {"seq": s},
        )

    def own_load(h):
        return pltpu.make_async_copy(tokens.at[h], held.at[s, h, 0], own_sem.at[h])

    def all_store(d, h):
        return pltpu.make_async_copy(held.at[d, h], tokens_all.at[d, h], all_sem.at[d, h])

    def stage_store(i, d, h, slot):
        return pltpu.make_async_copy(
            stage.at[i, slot], stage_outs[i].at[2 * d + h], stage_sem.at[i, slot]
        )

    def kept_load(i, d, h, slot):
        source = (kept_gate, kept_up)[i]
        return pltpu.make_async_copy(source.at[2 * d + h], kept.at[i, slot], kept_sem.at[i, slot])

    unit_table, sum_table = unit_orders(n)
    right_table = [
        [2 if d == 0 else unit_table[d].index(2 * (d - 1) + 1) + 1 for d in range(n)]
    ]
    left_table = [
        [2 if d == n - 1 else unit_table[d].index(2 * (d + 1) + 1) + 1 for d in range(n)]
    ]

    def source(t):
        unit = pick(unit_table, s, t)
        return lax.div(unit, 2), lax.rem(unit, 2)

    barrier = pltpu.get_barrier_semaphore()
    pl.semaphore_signal(barrier, inc=1, device_id=twin, device_id_type=MESH)

    @pl.when(s > 0)
    def _():
        pl.semaphore_signal(barrier, inc=1, device_id={"seq": s - 1}, device_id_type=MESH)

    @pl.when(s < n - 1)
    def _():
        pl.semaphore_signal(barrier, inc=1, device_id={"seq": s + 1}, device_id_type=MESH)

    pl.semaphore_wait(barrier, 1 + jnp.where(s > 0, 1, 0) + jnp.where(s < n - 1, 1, 0))

    def second_half(t):
        @pl.when((s < n - 1) & (t == pick(right_table, 0, s)))
        def _():
            d, h = jnp.maximum(s - 1, 0), jnp.where(s > 0, 1, 0)
            token_right(d, h, held.at[d, h, 0]).wait_send()
            token_right(s, 1, tokens.at[1]).start()

        @pl.when((s > 0) & (t == pick(left_table, 0, s)))
        def _():
            d, h = jnp.minimum(s + 1, n - 1), jnp.where(s < n - 1, 1, 0)
            token_left(d, h, held.at[d, h, 0]).wait_send()
            token_left(s, 1, tokens.at[1]).start()

    @pl.when(s < n - 1)
    def _():
        token_right(s, 0, tokens.at[0]).start()

    @pl.when(s > 0)
    def _():
        token_left(s, 0, tokens.at[0]).start()

    for h in range(2):
        token_twin(s, h, tokens.at[h]).start()
        own_load(h).start()
    load_units = pltpu.make_async_copy(units, units_v, weight_sem.at[0])
    load_downs = pltpu.make_async_copy(downs, downs_v, weight_sem.at[1])
    load_units.start()
    load_downs.start()
    if backward:
        for i in range(2):
            kept_load(i, s, 0, 0).start()
    load_units.wait()
    load_downs.wait()

    def add_rows(d, h, sub, into_own, use_line):
        step = 16

        def body(i, carry):
            rows = pl.ds(pl.multiple_of(sub * sub_len + i * step, step), step)
            total = own_sum[d, h, rows, :] + twin_sum[d, h, rows, :].astype(jnp.float32)
            for slot in use_line:
                total = total + line[slot, h, rows, :].astype(jnp.float32)
            if into_own:
                own_sum[d, h, rows, :] = total
            else:
                twin_sum[d, h, rows, :] = total.astype(twin_sum.dtype)
            return carry

        lax.fori_loop(0, sub_len // step, body, 0)

    def combine(d, h):
        to_left = d < s
        slot = jnp.where(to_left, d, d + 1)
        more = jnp.where(to_left, s < n - 1, s > 0)
        part_twin(d, h).wait_recv()

        @pl.when(more)
        def _():
            for sub in range(SUBS):
                line_arrival(slot, h, sub).wait_recv()
                add_rows(d, h, sub, False, (slot,))
                part_line(d, h, sub).start()

        @pl.when(jnp.logical_not(more))
        def _():
            for sub in range(SUBS):
                add_rows(d, h, sub, False, ())
                part_line(d, h, sub).start()

    columns = width // 3
    chunk = n_units // 3

    def compute_forward(d, h, slot):
        rows = held[d, h].reshape(2 * piece_len, width)
        for c in range(3):
            cols = slice(c * chunk, (c + 1) * chunk)
            gate = times_rows(rows, units_v[cols, :width])
            up = times_rows(rows, units_v[cols, width:])
            value, unused = gelu_pieces(gate)
            stage[0, slot, :, cols] = gate.astype(stage.dtype)
            stage[1, slot, :, cols] = up.astype(stage.dtype)
            stage[2, slot, :, cols] = (value * up).astype(stage.dtype)
        for c in range(3):
            cols = slice(c * columns, (c + 1) * columns)
            part = add_slice(stage[2, slot], downs_v[:, cols])
            own_sum[d, h, :, cols] = part[:piece_len]
            twin_out[d, h, :, cols] = part[piece_len:].astype(twin_out.dtype)

    def compute_backward(d, h, slot):
        rows = held[d, h].reshape(2 * piece_len, width)
        for c in range(3):
            cols = slice(c * chunk, (c + 1) * chunk)
            grad = times_rows(rows, downs_v[cols, :])
            value, slope = gelu_pieces(kept[0, slot, :, cols].astype(jnp.float32))
            up = kept[1, slot, :, cols].astype(jnp.float32)
            stage[0, slot, :, cols] = (grad * up * slope).astype(stage.dtype)
            stage[1, slot, :, cols] = (grad * value).astype(stage.dtype)
        for c in range(3):
            cols = slice(c * columns, (c + 1) * columns)
            later = slice(width + c * columns, width + (c + 1) * columns)
            part = add_slice(stage[0, slot], units_v[:, cols])
            part = part + add_slice(stage[1, slot], units_v[:, later])
            own_sum[d, h, :, cols] = part[:piece_len]
            twin_out[d, h, :, cols] = part[piece_len:].astype(twin_out.dtype)

    row_tile, col_tile = n_units // 3, width // 3

    def weight_gradients(between):
        unit_rows = 2 * piece_len

        def left_load(i, u):
            source = (kept_hidden, first_out, second_out)[i].at[u]
            if i == 1:
                place = kept.at[u // 2, u % 2] if u < n else stage.at[(u - n) // 2, u % 2]
            else:
                place = downs_v.at[
                    pl.ds((u % n) * unit_rows, unit_rows), pl.ds((u // n) * n_units, n_units)
                ]
            return pltpu.make_async_copy(source, place, load_sem.at[i, u])

        def input_load(u):
            place = units_v.at[
                pl.ds((u % n) * unit_rows, unit_rows), pl.ds((u // n) * width, width)
            ]
            source = inputs.at[u // 2, u % 2]
            return [
                pltpu.make_async_copy(
                    source.at[half],
                    place.at[pl.ds(half * piece_len, piece_len)],
                    rows_sem.at[u, half],
                )
                for half in range(2)
            ]

        def left_rows(i, u, cols):
            if i == 1:
                return kept[u // 2, u % 2, :, cols] if u < n else stage[(u - n) // 2, u % 2, :, cols]
            return downs_v[
                (u % n) * unit_rows : (u % n + 1) * unit_rows,
                pl.ds(pl.multiple_of((u // n) * n_units + cols.start, 128), row_tile),
            ]

        def right_rows(i, u, cols):
            if i == 0:
                return held[u // 2, u % 2, :, :, cols].reshape(unit_rows, col_tile)
            return units_v[
                (u % n) * unit_rows : (u % n + 1) * unit_rows,
                pl.ds(pl.multiple_of((u // n) * width + cols.start, 128), col_tile),
            ]

        def tile_store(i, r, c, slot):
            rows = pl.ds(pl.multiple_of(r * row_tile, 16), row_tile)
            if i == 0:
                cols = pl.ds(pl.multiple_of(c * col_tile, 128), col_tile)
                place = down_grads.at[rows, cols]
            else:
                cols = pl.ds(pl.multiple_of((i - 1) * width + c * col_tile, 128), col_tile)
                place = unit_grads.at[rows, cols]
            return pltpu.make_async_copy(tile.at[slot], place, tile_sem.at[slot])

        for u in range(2 * n):
            left_load(0, u).start()
        for h in range(2):
            for i in range(2):
                stage_store(i, 0, h, h).wait()
        for u in range(2 * n):
            for load in input_load(u):
                load.start()
            left_load(1, u).start()
        for i in range(3):
            for u in range(2 * n):
                left_load(i, u).wait()
            if i == 1:
                for u in range(2 * n):
                    for load in input_load(u):
                        load.wait()
                for u in range(2 * n):
                    left_load(2, u).start()

            def one_tile(j, carry, i=i):
                count = 9 * i + j
                slot = lax.rem(count, 2)
                r, c = lax.div(j, 3), lax.rem(j, 3)
                row_cols = pl.ds(pl.multiple_of(r * row_tile, 128), row_tile)
                col_cols = pl.ds(pl.multiple_of(c * col_tile, 128), col_tile)
                total = jnp.zeros((row_tile, col_tile), jnp.float32)
                for u in range(2 * n):
                    total = total + outer_rows(
                        left_rows(i, u, row_cols), right_rows(i, u, col_cols)
                    )

                @pl.when(count >= 2)
                def _():
                    tile_store(i, r, c, slot).wait()

                tile[slot] = total.astype(tile.dtype)
                tile_store(i, r, c, slot).start()

                for step, turn in enumerate(SUM_TURNS):

                    @pl.when(count == turn)
                    def _():
                        between(step)

                return carry

            lax.fori_loop(0, 9, one_tile, 0)
        for slot in range(2):
            tile_store(0, 0, 0, slot).wait()

    def unit(t, carry):
        d, h = source(t)
        slot = lax.rem(t, 2)

        @pl.when(at_end & (t >= 3))
        def _():
            combine(*source(t - 1))

        @pl.when(t < 2)
        def _():
            own_load(h).wait()

        @pl.when(t >= 2)
        def _():
            piece = held.at[d, h, 0]
            token_left(d, h, piece).wait_recv()

            @pl.when((d < s) & (s < n - 1))
            def _():
                token_right(d, h, piece).start()

            @pl.when((d > s) & (s > 0))
            def _():
                token_left(d, h, piece).start()

            token_twin(d, h, piece).start()
            for i in range(len(stage_outs)):
                stage_store(i, d, h, slot).wait()

        second_half(t)
        if backward:

            @pl.when(t < 2 * n - 1)
            def _():
                for i in range(2):
                    kept_load(i, *source(t + 1), 1 - slot).start()

            for i in range(2):
                kept_load(i, d, h, slot).wait()
        token_twin(d, h, held.at[d, h, 0]).wait_recv()
        if backward:
            compute_backward(d, h, slot)
        else:
            compute_forward(d, h, slot)
        part_twin(d, h).start()
        if not backward:
            all_store(d, h).start()
        for i in range(len(stage_outs)):
            stage_store(i, d, h, slot).start()

        return carry

    lax.fori_loop(0, 2 * n, unit, 0)

    second_half(2 * n)

    @pl.when(at_end)
    def _():
        combine(*source(2 * n - 1))

    n_sums = 2 * (n - 1)

    def middle(i):
        @pl.when(jnp.logical_not(at_end) & (i < n_sums))
        def _():
            unit = pick(sum_table, s, i)
            combine(lax.div(unit, 2), lax.rem(unit, 2))

    if backward:
        weight_gradients(middle)
    else:

        def one(i, carry):
            middle(i)
            return carry

        lax.fori_loop(0, n_sums, one, 0)

    def finish(h, carry):
        part_twin(s, h).wait_recv()
        for sub in range(SUBS):

            @pl.when(s < n - 1)
            def _():
                line_arrival(s, h, sub).wait_recv()

            @pl.when(s > 0)
            def _():
                line_arrival(s + 1, h, sub).wait_recv()

            @pl.when(s == 0)
            def _():
                add_rows(s, h, sub, True, (s,))

            @pl.when(s == n - 1)
            def _():
                add_rows(s, h, sub, True, (s + 1,))

            @pl.when(jnp.logical_not(at_end))
            def _():
                add_rows(s, h, sub, True, (s, s + 1))

        pltpu.make_async_copy(own_sum.at[s, h], out.at[h], out_sem.at[h]).start()
        return carry

    lax.fori_loop(0, 2, finish, 0)

    def drain(t, carry):
        d = lax.div(t, 2)
        h = lax.rem(t, 2)
        piece = held.at[d, h, 0]

        right_seen = (d == jnp.maximum(s - 1, 0)) & (h == jnp.where(s > 0, 1, 0))
        left_seen = (d == jnp.minimum(s + 1, n - 1)) & (h == jnp.where(s < n - 1, 1, 0))

        @pl.when((d <= s) & (s < n - 1) & jnp.logical_not(right_seen))
        def _():
            token_right(d, h, piece).wait_send()

        @pl.when((d >= s) & (s > 0) & jnp.logical_not(left_seen))
        def _():
            token_left(d, h, piece).wait_send()

        token_twin(d, h, piece).wait_send()
        part_twin(d, h).wait_send()

        @pl.when(d != s)
        def _():
            for sub in range(SUBS):
                part_line(d, h, sub).wait_send()

        if not backward:
            all_store(d, h).wait()
        return carry

    lax.fori_loop(0, 2 * n, drain, 0)
    for h in range(2):
        if not backward:
            for i in range(len(stage_outs)):
                stage_store(i, 0, h, h).wait()
        pltpu.make_async_copy(own_sum.at[s, h], out.at[h], out_sem.at[h]).wait()


def run_units(n_seq, tokens, units, downs, kept=None):
    backward = kept is not None
    low = tokens.dtype
    n_units = downs.shape[0]
    halves, piece_len, width = tokens.shape
    n_stage = 2 if backward else 3
    held = (n_seq, halves, 2, piece_len, width)
    unit_rows = (2 * n_seq, 2 * piece_len, n_units)
    sums = (n_seq, halves, piece_len, width)
    scratch = [
        pltpu.VMEM(units.shape, low),
        pltpu.VMEM(downs.shape, low),
        pltpu.VMEM(held, low),
        pltpu.VMEM(sums, jnp.float32),
        pltpu.VMEM(sums, low),
        pltpu.VMEM(sums, low),
        pltpu.VMEM((n_seq + 1,) + sums[1:], low),
        pltpu.VMEM((n_stage, 2) + unit_rows[1:], low),
    ]
    outs = [jax.ShapeDtypeStruct(tokens.shape, jnp.float32)]
    if backward:
        scratch += [
            pltpu.VMEM((2, 2) + unit_rows[1:], low),
            DMA((2, 2)),
            pltpu.VMEM((2, n_units // 3, width // 3), low),
            DMA((2,)),
            DMA((3, 2 * n_seq)),
            DMA((2 * n_seq, 2)),
        ]
    else:
        outs += [jax.ShapeDtypeStruct(held, low)]
    outs += [jax.ShapeDtypeStruct(unit_rows, low)] * n_stage
    if backward:
        outs += [jax.ShapeDtypeStruct(units.shape, low), jax.ShapeDtypeStruct(downs.shape, low)]
    pairs = DMA((n_seq, halves))
    scratch += [DMA((2,)), DMA((halves,))] + [pairs] * 7
    scratch += [DMA((n_seq, halves, SUBS)), DMA((n_seq + 1, halves, SUBS))]
    scratch += [DMA((n_stage, 2)), pairs, DMA((halves,))]
    operands = (tokens, units, downs) + (tuple(kept) if backward else ())
    return pl.pallas_call(
        partial(units_kernel, n_seq, backward),
        out_shape=outs,
        in_specs=[ANY] * len(operands),
        out_specs=[ANY] * len(outs),
        scratch_shapes=scratch,
        compiler_params=pltpu.CompilerParams(
            collective_id=6 if backward else 5,
            has_side_effects=True,
            vmem_limit_bytes=63 * 1024 * 1024,
        ),
    )(*operands)


def per_device_general(
    hidden_in,
    norm_gains,
    qkv_weight,
    out_weight,
    gate_up_weight,
    down_weight,
    output_cotangent,
    segment_ids,
    padding,
    positions,
):
    everyone = ("seq", "chip", "core")
    plane = ("chip", "core")
    column = ("seq", "core")
    groups = hidden_in.shape[0]
    piece_len = hidden_in.shape[1]
    model_width = hidden_in.shape[2]
    row_count = groups * piece_len
    seq_len = segment_ids.shape[1]
    group_size = HEADS // KV_HEADS
    query_width = HEADS * HEAD_DIM
    key_width = KV_HEADS * HEAD_DIM
    proj_width = qkv_weight.shape[1]

    residual = hidden_in.reshape(row_count, model_width).astype(jnp.float32)
    factor = lax.rsqrt(jnp.mean(residual * residual, axis=-1, keepdims=True) + EPSILON)
    gain_cols = lax.all_gather(norm_gains, everyone, axis=0, tiled=True).astype(jnp.float32)
    qkv_full = lax.all_gather(qkv_weight, everyone, axis=0, tiled=True)
    attn_input = (residual * factor * gain_cols[:, 0]).astype(jnp.bfloat16)
    projected = add_slice(attn_input, qkv_full)
    cosine, sine_part = rotary_tables(positions.reshape(row_count), HEAD_DIM)
    queries = (
        rotate(projected[:, :query_width].reshape(row_count, HEADS, HEAD_DIM), cosine, sine_part)
        .astype(jnp.bfloat16)
        .reshape(row_count, query_width)
    )
    keys_here = (
        rotate(
            projected[:, query_width : query_width + key_width].reshape(
                row_count, KV_HEADS, HEAD_DIM
            ),
            cosine,
            sine_part,
        )
        .astype(jnp.bfloat16)
        .reshape(groups, piece_len, key_width)
    )
    values_here = (
        projected[:, query_width + key_width :]
        .astype(jnp.bfloat16)
        .reshape(groups, piece_len, key_width)
    )
    both_all = lax.all_gather(
        jnp.concatenate([keys_here, values_here], axis=2), plane, axis=1, tiled=True
    )
    keys_all = both_all[:, :, :key_width]
    values_all = both_all[:, :, key_width:]
    first_query = (lax.axis_index("chip") * 2 + lax.axis_index("core")) * piece_len
    query_rows = first_query + jnp.arange(piece_len, dtype=jnp.int32)
    key_rows = jnp.arange(seq_len, dtype=jnp.int32)
    segment_query = lax.dynamic_slice_in_dim(segment_ids, first_query, piece_len, 1)
    allowed = (segment_query[:, :, None] == segment_ids[:, None, :]) & (
        key_rows[None, None, :] <= query_rows[None, :, None]
    ) & (padding[:, None, :] == 1) | (key_rows[None, None, :] == query_rows[None, :, None])
    allowed = allowed[:, None, None]
    probs = soft_probs(score_block(queries, keys_all), allowed)
    attn_out = mix_values(probs.astype(jnp.bfloat16), values_all)
    out_full = lax.all_gather(out_weight, everyone, axis=0, tiled=True)
    attn_proj = times_rows(attn_out, out_full)
    after_attn = residual + rms_norm(attn_proj, gain_cols[:, 1])
    ffn_input = rms_norm(after_attn, gain_cols[:, 2]).astype(jnp.bfloat16)

    unit_weights = lax.all_gather(gate_up_weight, "chip", axis=0, tiled=True)
    down_units = lax.all_gather(down_weight, "chip", axis=0, tiled=True)
    ffn_all = lax.all_gather(ffn_input, column, axis=0, tiled=True)
    gate_part = times_rows(ffn_all, unit_weights[:, :model_width])
    up_part = times_rows(ffn_all, unit_weights[:, model_width:])
    hidden_part = geglu_parts(gate_part, up_part).astype(jnp.bfloat16)
    down_part = add_slice(hidden_part, down_units).astype(jnp.bfloat16)
    down_out = lax.psum_scatter(down_part, column, scatter_dimension=0, tiled=True).astype(
        jnp.float32
    )
    layer_out = after_attn + rms_norm(down_out, gain_cols[:, 3])
    layer_output = layer_out.astype(jnp.bfloat16).reshape(groups, piece_len, model_width)

    cotangent = output_cotangent.reshape(row_count, model_width).astype(jnp.float32)
    unused_last, pull_last = jax.vjp(rms_norm, down_out, gain_cols[:, 3])
    grad_down, grad_gain_last = pull_last(cotangent)
    grad_down_low = grad_down.astype(jnp.bfloat16)
    grad_down_all = lax.all_gather(grad_down_low, column, axis=0, tiled=True)
    grad_part = times_rows(grad_down_all, down_units)
    unused_units, pull_units = jax.vjp(geglu_parts, gate_part, up_part)
    grad_gate_part, grad_up_part = pull_units(grad_part)
    gate_low = grad_gate_part.astype(jnp.bfloat16)
    up_low = grad_up_part.astype(jnp.bfloat16)
    grad_ffn_part = add_slice(gate_low, unit_weights[:, :model_width]) + add_slice(
        up_low, unit_weights[:, model_width:]
    )
    grad_ffn_in = lax.psum_scatter(
        grad_ffn_part.astype(jnp.bfloat16), column, scatter_dimension=0, tiled=True
    ).astype(jnp.float32)
    gate_up_rows = jnp.concatenate(
        [
            outer_rows(gate_low, ffn_all).astype(jnp.bfloat16),
            outer_rows(up_low, ffn_all).astype(jnp.bfloat16),
        ],
        axis=1,
    )
    down_rows = outer_rows(hidden_part, grad_down_all).astype(jnp.bfloat16)
    gate_up_grad = lax.psum_scatter(
        gate_up_rows, "chip", scatter_dimension=0, tiled=True
    ).astype(jnp.float32)
    down_grad = lax.psum_scatter(down_rows, "chip", scatter_dimension=0, tiled=True).astype(
        jnp.float32
    )

    unused_mid, pull_mid = jax.vjp(rms_norm, after_attn, gain_cols[:, 2])
    grad_after_ffn, grad_gain_mid = pull_mid(grad_ffn_in)
    grad_after = cotangent + grad_after_ffn
    unused_post, pull_post = jax.vjp(rms_norm, attn_proj, gain_cols[:, 1])
    grad_proj, grad_gain_post = pull_post(grad_after)
    grad_proj_low = grad_proj.astype(jnp.bfloat16)
    grad_attn = add_slice(grad_proj_low, out_full).astype(jnp.bfloat16)
    scaled = score_block(queries, keys_all)
    probs, pull_probs = jax.vjp(partial(soft_probs, allowed=allowed), scaled)
    grad_heads = grad_attn.reshape(groups, piece_len, KV_HEADS, group_size, HEAD_DIM)
    query_heads = queries.reshape(groups, piece_len, KV_HEADS, group_size, HEAD_DIM)
    key_heads = keys_all.reshape(groups, seq_len, KV_HEADS, HEAD_DIM)
    value_heads = values_all.reshape(groups, seq_len, KV_HEADS, HEAD_DIM)
    grad_probs = jnp.einsum(
        "spkgd,slkd->skgpl", grad_heads, value_heads, preferred_element_type=jnp.float32
    )
    (grad_scaled,) = pull_probs(grad_probs)
    grad_scaled_low = grad_scaled.astype(jnp.bfloat16)
    inverse_root = 1.0 / math.sqrt(HEAD_DIM)
    grad_query_rot = (
        jnp.einsum(
            "skgpl,slkd->spkgd", grad_scaled_low, key_heads, preferred_element_type=jnp.float32
        )
        * inverse_root
    )
    grad_key_rot = (
        jnp.einsum(
            "skgpl,spkgd->slkd", grad_scaled_low, query_heads, preferred_element_type=jnp.float32
        )
        * inverse_root
    )
    grad_value_part = jnp.einsum(
        "skgpl,spkgd->slkd",
        probs.astype(jnp.bfloat16),
        grad_heads,
        preferred_element_type=jnp.float32,
    )
    both_grads = jnp.concatenate(
        [
            grad_key_rot.reshape(groups, seq_len, key_width),
            grad_value_part.reshape(groups, seq_len, key_width),
        ],
        axis=2,
    ).astype(jnp.bfloat16)
    both_summed = lax.psum_scatter(both_grads, plane, scatter_dimension=1, tiled=True)
    both_summed = both_summed.astype(jnp.float32).reshape(row_count, 2 * key_width)
    key_summed = both_summed[:, :key_width]
    value_summed = both_summed[:, key_width:]
    grad_queries = rotate_back(
        grad_query_rot.reshape(row_count, HEADS, HEAD_DIM), cosine, sine_part
    ).reshape(row_count, query_width)
    grad_keys = rotate_back(
        key_summed.reshape(row_count, KV_HEADS, HEAD_DIM), cosine, sine_part
    ).reshape(row_count, key_width)
    grad_projected = jnp.concatenate([grad_queries, grad_keys, value_summed], axis=1).astype(
        jnp.bfloat16
    )
    grad_attn_in = times_rows(grad_projected, qkv_full)
    unused_first, pull_first = jax.vjp(rms_norm, residual, gain_cols[:, 0])
    grad_res_first, grad_gain_first = pull_first(grad_attn_in)
    input_grad = (grad_after + grad_res_first).reshape(groups, piece_len, model_width)
    gain_terms = jnp.stack([grad_gain_first, grad_gain_post, grad_gain_mid, grad_gain_last], axis=1)
    qkv_part = outer_rows(attn_input, grad_projected).astype(jnp.bfloat16)
    out_part = outer_rows(grad_proj_low, attn_out).astype(jnp.bfloat16)
    qkv_grad = lax.psum_scatter(qkv_part, everyone, scatter_dimension=0, tiled=True).astype(
        jnp.float32
    )
    out_proj_grad = lax.psum_scatter(out_part, everyone, scatter_dimension=0, tiled=True).astype(
        jnp.float32
    )
    gain_grad = lax.psum_scatter(gain_terms, everyone, scatter_dimension=0, tiled=True)
    return (layer_output, input_grad, gain_grad, qkv_grad, out_proj_grad, gate_up_grad, down_grad)


def per_device_by_heads(
    n_seq,
    hidden_in,
    norm_gains,
    qkv_weight,
    out_weight,
    gate_up_weight,
    down_weight,
    output_cotangent,
    segment_ids,
    padding,
    positions,
):
    groups, piece_len, model_width = hidden_in.shape
    row_count = groups * piece_len
    seq_len = segment_ids.shape[1]
    n_chip = KV_HEADS
    n_plane = 2 * n_chip
    group_size = HEADS // KV_HEADS
    query_width = HEADS * HEAD_DIM
    key_width = KV_HEADS * HEAD_DIM
    own_width = group_size * HEAD_DIM
    part_width = own_width + 2 * HEAD_DIM
    block_width = part_width + own_width
    weight_rows = qkv_weight.shape[0]
    extra_rows = 16 - weight_rows % 16
    block_rows = weight_rows + extra_rows
    core = lax.axis_index("core")

    gain_rows = jnp.pad(
        norm_gains.T, ((0, extra_rows - norm_gains.shape[1]), (0, block_width - weight_rows))
    )
    blocks = jnp.stack(
        [
            jnp.concatenate(
                [
                    jnp.concatenate(
                        [
                            qkv_weight[:, c * own_width : (c + 1) * own_width],
                            qkv_weight[
                                :, query_width + c * HEAD_DIM : query_width + (c + 1) * HEAD_DIM
                            ],
                            qkv_weight[
                                :,
                                query_width + key_width + c * HEAD_DIM : query_width
                                + key_width
                                + (c + 1) * HEAD_DIM,
                            ],
                            out_weight[:, c * own_width : (c + 1) * own_width],
                        ],
                        axis=1,
                    ),
                    gain_rows,
                ],
                axis=0,
            )
            for c in range(n_chip)
        ]
    )
    hidden_all, blocks_all = gather_first(n_seq, hidden_in, blocks)
    unit_weights = lax.all_gather(gate_up_weight, "chip", axis=0, tiled=True)
    down_units = lax.all_gather(down_weight, "chip", axis=0, tiled=True)
    blocks_all = blocks_all.transpose(0, 2, 1, 3, 4)
    own_weights = blocks_all[:, :, :, :weight_rows].reshape(model_width, block_width)
    own_qkv = own_weights[:, :part_width]
    own_out = own_weights[:, part_width:]
    gain_cols = (
        blocks_all[:, :, :, weight_rows : weight_rows + norm_gains.shape[1], :weight_rows]
        .transpose(0, 1, 2, 4, 3)
        .reshape(model_width, norm_gains.shape[1])
        .astype(jnp.float32)
    )

    seq_rows = hidden_all.reshape(seq_len, model_width).astype(jnp.float32)
    seq_factor = lax.rsqrt(jnp.mean(seq_rows * seq_rows, axis=-1, keepdims=True) + EPSILON)
    attn_input = (seq_rows * seq_factor * gain_cols[:, 0]).astype(jnp.bfloat16)
    projected = add_slice(attn_input, own_qkv)
    segment = lax.dynamic_index_in_dim(segment_ids, core, 0, keepdims=False)
    valid = lax.dynamic_index_in_dim(padding, core, 0, keepdims=False)
    token = jnp.arange(seq_len, dtype=jnp.int32)
    document_start = jnp.min(
        jnp.where(segment[:, None] == segment[None, :], token[None, :], seq_len), axis=1
    )
    cosine, sine_part = rotary_tables(token - document_start, HEAD_DIM)
    queries = (
        rotate(projected[:, :own_width].reshape(seq_len, group_size, HEAD_DIM), cosine, sine_part)
        .astype(jnp.bfloat16)
        .reshape(seq_len, own_width)
    )
    keys = (
        rotate(
            projected[:, own_width : own_width + HEAD_DIM].reshape(seq_len, 1, HEAD_DIM),
            cosine,
            sine_part,
        )
        .astype(jnp.bfloat16)
        .reshape(seq_len, HEAD_DIM)
    )
    values = projected[:, own_width + HEAD_DIM :].astype(jnp.bfloat16)
    segment_col = segment[:, None]
    segment_row = jnp.where(valid == 1, segment, -1)[None, :]
    attn_out = attend(queries, keys, values, segment_col, segment_row)
    proj_parts = times_rows(attn_out, own_out).astype(jnp.bfloat16)
    proj_parts = plane_exchange(
        proj_parts.reshape(n_plane, piece_len, model_width), False, 2
    )

    def sum_parts(parts):
        parts = parts.reshape(n_chip, groups, piece_len, model_width).astype(jnp.float32)
        return jnp.sum(parts, axis=0).reshape(row_count, model_width)

    attn_proj = sum_parts(proj_parts)
    residual = hidden_in.reshape(row_count, model_width).astype(jnp.float32)
    after_attn = residual + rms_norm(attn_proj, gain_cols[:, 1])
    ffn_input = rms_norm(after_attn, gain_cols[:, 2]).astype(jnp.bfloat16)

    pieces = (groups, piece_len, model_width)
    down_out, ffn_all, gate_part, up_part, hidden_part = run_units(
        n_seq, ffn_input.reshape(pieces), unit_weights, down_units
    )
    down_out = down_out.reshape(row_count, model_width)
    layer_out = after_attn + rms_norm(down_out, gain_cols[:, 3])
    layer_output = layer_out.astype(jnp.bfloat16).reshape(pieces)

    cotangent = output_cotangent.reshape(row_count, model_width).astype(jnp.float32)
    unused_last, pull_last = jax.vjp(rms_norm, down_out, gain_cols[:, 3])
    grad_down, grad_gain_last = pull_last(cotangent)
    grad_ffn_in, unused_gate, unused_up, gate_up_rows, down_rows = run_units(
        n_seq,
        grad_down.astype(jnp.bfloat16).reshape(pieces),
        unit_weights,
        down_units,
        (gate_part, up_part, hidden_part, ffn_all),
    )
    grad_ffn_in = grad_ffn_in.reshape(row_count, model_width)
    gate_up_grad = lax.psum_scatter(
        gate_up_rows, "chip", scatter_dimension=0, tiled=True
    ).astype(jnp.float32)
    down_grad = lax.psum_scatter(down_rows, "chip", scatter_dimension=0, tiled=True).astype(
        jnp.float32
    )

    unused_mid, pull_mid = jax.vjp(rms_norm, after_attn, gain_cols[:, 2])
    grad_after_ffn, grad_gain_mid = pull_mid(grad_ffn_in)
    grad_after = cotangent + grad_after_ffn
    unused_post, pull_post = jax.vjp(rms_norm, attn_proj, gain_cols[:, 1])
    grad_proj, grad_gain_post = pull_post(grad_after)
    grad_proj_low = grad_proj.astype(jnp.bfloat16)

    grad_proj_all = plane_exchange(
        grad_proj_low.reshape(groups, piece_len, model_width), True, 3
    ).reshape(seq_len, model_width)
    grad_attn = add_slice(grad_proj_all, own_out).astype(jnp.bfloat16)
    grad_query_rot, grad_key_rot, grad_values = attend_back(
        queries, keys, values, segment_col, segment_row, grad_attn
    )
    grad_queries = rotate_back(
        grad_query_rot.reshape(seq_len, group_size, HEAD_DIM), cosine, sine_part
    ).reshape(seq_len, own_width)
    grad_keys = rotate_back(
        grad_key_rot.reshape(seq_len, 1, HEAD_DIM), cosine, sine_part
    ).reshape(seq_len, HEAD_DIM)
    grad_projected = jnp.concatenate([grad_queries, grad_keys, grad_values], axis=1).astype(
        jnp.bfloat16
    )
    grad_in_part = times_rows(grad_projected, own_qkv)
    grad_gain_first = jnp.sum(grad_in_part * seq_rows * seq_factor, axis=0)
    weight_part = jnp.concatenate(
        [
            outer_rows(attn_input, grad_projected).astype(jnp.bfloat16),
            outer_rows(grad_proj_all, attn_out).astype(jnp.bfloat16),
        ],
        axis=1,
    ).reshape(n_seq, n_chip, 2, weight_rows, block_width)
    gain_terms = (
        jnp.stack([grad_gain_first, grad_gain_post, grad_gain_mid, grad_gain_last])
        .astype(jnp.bfloat16)
        .reshape(-1, n_seq, n_chip, 2, weight_rows)
        .transpose(1, 2, 3, 0, 4)
    )
    gain_terms = jnp.pad(
        gain_terms,
        ((0, 0),) * 3
        + ((0, extra_rows - gain_terms.shape[3]), (0, block_width - weight_rows)),
    )
    grad_blocks = jnp.concatenate([weight_part, gain_terms], axis=3).transpose(0, 2, 1, 3, 4)
    grad_in_parts, grad_sums = sum_last(
        n_seq,
        grad_in_part.astype(jnp.bfloat16).reshape(n_plane, piece_len, model_width),
        grad_blocks,
    )
    grad_attn_in = sum_parts(grad_in_parts)
    factor = lax.rsqrt(jnp.mean(residual * residual, axis=-1, keepdims=True) + EPSILON)
    unused_first, pull_first = jax.vjp(rms_norm, residual, gain_cols[:, 0])
    grad_res_first, unused_gain = pull_first(grad_attn_in)
    input_grad = (grad_after + grad_res_first).reshape(groups, piece_len, model_width)

    weight_sums = grad_sums[:, :weight_rows].astype(jnp.float32)
    qkv_grad = jnp.concatenate(
        [weight_sums[c, :, :own_width] for c in range(n_chip)]
        + [weight_sums[c, :, own_width : own_width + HEAD_DIM] for c in range(n_chip)]
        + [weight_sums[c, :, own_width + HEAD_DIM : part_width] for c in range(n_chip)],
        axis=1,
    )
    out_proj_grad = jnp.concatenate(
        [weight_sums[c, :, part_width:] for c in range(n_chip)], axis=1
    )
    gain_grad = jnp.sum(
        grad_sums[:, weight_rows : weight_rows + norm_gains.shape[1], :weight_rows].astype(
            jnp.float32
        ),
        axis=0,
    ).T
    return (layer_output, input_grad, gain_grad, qkv_grad, out_proj_grad, gate_up_grad, down_grad)


def solution(mesh):
    n_seq = mesh.shape["seq"]
    n_ctx = mesh.shape["ctx"]
    split_mesh = jax.sharding.Mesh(
        mesh.devices.reshape(n_seq, n_ctx // 2, 2), ("seq", "chip", "core")
    )
    plane = ("chip", "core")
    rows = P(("seq", "chip", "core"), None)
    tokens = P("seq", plane, None)
    placed = (
        tokens,
        rows,
        rows,
        rows,
        rows,
        rows,
        tokens,
        P("seq", None),
        P("seq", None),
        P("seq", plane),
    )

    def step(*arrays):
        groups = arrays[0].shape[0]
        if n_ctx // 2 == KV_HEADS and groups == 2 and n_seq == 4:
            return per_device_by_heads(n_seq, *arrays)
        return per_device_general(*arrays)

    return jax.shard_map(
        step,
        mesh=split_mesh,
        in_specs=placed,
        out_specs=(tokens, tokens, rows, rows, rows, rows, rows),
        check_vma=False,
    )
```

```python
from functools import partial
import math

import jax
import jax.numpy as jnp
from jax import lax
from jax.experimental import pallas as pl
from jax.experimental.pallas import tpu as pltpu
from jax.sharding import PartitionSpec as P

HEADS = 8
KV_HEADS = 4
HEAD_DIM = 256


EPSILON = 1e-06
SOFT_CAP = 50.0
MASKED = -1e30


def rms_norm(matrix, gain_col):
    factor = lax.rsqrt(jnp.mean(matrix * matrix, axis=-1, keepdims=True) + EPSILON)
    return matrix * factor * gain_col


def rotary_tables(positions, head_dim):
    half_dim = head_dim // 2
    frequency = jnp.exp(
        jnp.arange(half_dim, dtype=jnp.float32) * (-2.0 * math.log(10000.0) / head_dim)
    )
    phase_angle = positions.astype(jnp.float32)[:, None] * frequency[None, :]
    return (jnp.cos(phase_angle)[:, None, :], jnp.sin(phase_angle)[:, None, :])


def rotate(vectors, cosine, sine_part):
    half_dim = vectors.shape[-1] // 2
    first_half = vectors[..., :half_dim]
    second_half = vectors[..., half_dim:]
    return jnp.concatenate(
        [
            first_half * cosine - second_half * sine_part,
            second_half * cosine + first_half * sine_part,
        ],
        axis=-1,
    )


def rotate_back(grads, cosine, sine_part):
    half_dim = grads.shape[-1] // 2
    first_half = grads[..., :half_dim]
    second_half = grads[..., half_dim:]
    return jnp.concatenate(
        [
            first_half * cosine + second_half * sine_part,
            second_half * cosine - first_half * sine_part,
        ],
        axis=-1,
    )


def soft_probs(scaled, allowed):
    capped = SOFT_CAP * jnp.tanh(scaled / SOFT_CAP)
    capped = jnp.where(allowed, capped, MASKED)
    return jax.nn.softmax(capped, axis=-1)


def geglu_parts(gate_part, up_part):
    return jax.nn.gelu(gate_part, approximate=True) * up_part


def score_block(queries, keys_all):
    groups = keys_all.shape[0]
    seq_len = keys_all.shape[1]
    piece_len = queries.shape[0] // groups
    query_heads = queries.reshape(groups, piece_len, KV_HEADS, HEADS // KV_HEADS, HEAD_DIM)
    key_heads = keys_all.reshape(groups, seq_len, KV_HEADS, HEAD_DIM)
    raw_score = jnp.einsum(
        "spkgd,slkd->skgpl", query_heads, key_heads, preferred_element_type=jnp.float32
    )
    return raw_score * (1.0 / math.sqrt(HEAD_DIM))


def mix_values(weights_low, values_all):
    groups = values_all.shape[0]
    seq_len = values_all.shape[1]
    piece_len = weights_low.shape[3]
    value_heads = values_all.reshape(groups, seq_len, KV_HEADS, HEAD_DIM)
    mixed = jnp.einsum(
        "skgpl,slkd->spkgd", weights_low, value_heads, preferred_element_type=jnp.float32
    )
    return mixed.reshape(groups * piece_len, HEADS * HEAD_DIM).astype(jnp.bfloat16)


def add_slice(left, weight_piece):
    return jnp.dot(left, weight_piece, preferred_element_type=jnp.float32)


def times_rows(left, weight_piece):
    return lax.dot_general(
        left, weight_piece, (((1,), (1,)), ((), ())), preferred_element_type=jnp.float32
    )


def outer_rows(left, right):
    return lax.dot_general(
        left, right, (((0,), (0,)), ((), ())), preferred_element_type=jnp.float32
    )


MESH = pl.DeviceIdType.MESH
ANY = pl.BlockSpec(memory_space=pl.ANY)
DMA = pltpu.SemaphoreType.DMA


def remote(source, target, send_sem, recv_sem, device):
    return pltpu.make_async_remote_copy(
        src_ref=source,
        dst_ref=target,
        send_sem=send_sem,
        recv_sem=recv_sem,
        device_id=device,
        device_id_type=MESH,
    )


def plane_device(index):
    return {"chip": index // 2, "core": lax.rem(index, 2)}


def greet(n_plane, n_seq):
    me = lax.axis_index("chip") * 2 + lax.axis_index("core")
    barrier = pltpu.get_barrier_semaphore()
    for step in range(1, n_plane):
        pl.semaphore_signal(
            barrier,
            inc=1,
            device_id=plane_device(lax.rem(me + step, n_plane)),
            device_id_type=MESH,
        )
    count = n_plane - 1
    if n_seq > 1:
        s = lax.axis_index("seq")

        @pl.when(s > 0)
        def _():
            pl.semaphore_signal(barrier, inc=1, device_id={"seq": s - 1}, device_id_type=MESH)

        @pl.when(s < n_seq - 1)
        def _():
            pl.semaphore_signal(barrier, inc=1, device_id={"seq": s + 1}, device_id_type=MESH)

        count = count + jnp.where(s > 0, 1, 0) + jnp.where(s < n_seq - 1, 1, 0)
    pl.semaphore_wait(barrier, count)


def start_exchange(n_plane, source, target, send_sems, recv_sems, local_sem):
    me = lax.axis_index("chip") * 2 + lax.axis_index("core")
    copies = []
    for step in (4, 2, 6, 3, 5, 1, 7):
        to = lax.rem(me + step, n_plane)
        copy = remote(
            source.at[to],
            target.at[me],
            send_sems.at[step],
            recv_sems.at[step],
            plane_device(to),
        )
        copy.start()
        copies.append(copy)
    own = pltpu.make_async_copy(source.at[me], target.at[me], local_sem.at[0])
    own.start()
    copies.append(own)
    return copies


class Spread:
    def __init__(self, source, target, send_sems, recv_sems, local_sem):
        self.source, self.target = source, target
        self.send_sems, self.recv_sems = send_sems, recv_sems
        self.local_sem = local_sem
        self.q = lax.axis_index("chip")
        self.k = lax.axis_index("core")
        self.half = source.shape[1] // 2

    def chip(self, flip):
        x, y = lax.rem(self.q, 2), self.q // 2
        x = 1 - x if flip in (1, 3) else x
        y = 1 - y if flip in (2, 3) else y
        return y * 2 + x

    def direct(self, flip, twin):
        core = 1 - self.k if twin else self.k
        slot = 2 * flip + twin
        return remote(
            self.source.at[core],
            self.target.at[2 * self.q + self.k],
            self.send_sems.at[slot],
            self.recv_sems.at[slot],
            {"chip": self.chip(flip), "core": core},
        )

    def passed(self, flip, twin):
        core = 1 - self.k if twin else self.k
        slot = 8 + 2 * (flip - 1) + twin
        rows = pl.ds(0 if flip == 1 else self.half, self.half)
        block = self.target.at[2 * self.chip(flip) + core, rows]
        return remote(
            block,
            block,
            self.send_sems.at[slot],
            self.recv_sems.at[slot],
            {"chip": self.chip(3 - flip)},
        )

    def own(self):
        return pltpu.make_async_copy(
            self.source.at[self.k],
            self.target.at[2 * self.q + self.k],
            self.local_sem.at[0],
        )

    def start(self):
        for twin in (0, 1):
            for flip in (1, 2):
                self.direct(flip, twin).start()
        self.direct(0, 1).start()
        self.own().start()

    def pass_on(self):
        for twin in (0, 1):
            for flip in (1, 2):
                self.direct(flip, twin).wait_recv()
                self.passed(flip, twin).start()

    def finish(self):
        for twin in (0, 1):
            for flip in (1, 2):
                self.passed(flip, twin).wait()
                self.direct(flip, twin).wait_send()
        self.direct(0, 1).wait()
        self.own().wait()


SPREAD_SLOTS = 12


def exchange_kernel(n_plane, source, target, send_sems, recv_sems, local_sem):
    greet(n_plane, 1)
    for copy in start_exchange(n_plane, source, target, send_sems, recv_sems, local_sem):
        copy.wait()


def plane_exchange(blocks, collective_id):
    n_plane = 2 * KV_HEADS
    return pl.pallas_call(
        partial(exchange_kernel, n_plane),
        out_shape=jax.ShapeDtypeStruct((n_plane,) + blocks.shape[1:], blocks.dtype),
        in_specs=[ANY],
        out_specs=ANY,
        scratch_shapes=[DMA((n_plane,)), DMA((n_plane,)), DMA((1,))],
        compiler_params=pltpu.CompilerParams(
            collective_id=collective_id, has_side_effects=True
        ),
    )(blocks)


def spread_kernel(
    n_plane,
    blocks,
    low_gate,
    low_up,
    tokens,
    target,
    grads,
    left,
    right,
    tile,
    send_sems,
    recv_sems,
    local_sem,
    load_sem,
    row_sem,
    tile_sem,
):
    greet(n_plane, 1)
    spread = Spread(blocks, target, send_sems, recv_sems, local_sem)
    spread.start()
    n_units, unit_rows, units = low_gate.shape
    width = right.shape[1]
    piece_len = tokens.shape[3]
    loads = []
    for i, source in enumerate((low_gate, low_up)):
        for u in range(n_units):
            place = left.at[i, pl.ds(u * unit_rows, unit_rows)]
            loads.append(pltpu.make_async_copy(source.at[u], place, load_sem.at[i, u]))
    for u in range(n_units):
        for half in range(2):
            place = right.at[pl.ds(u * unit_rows + half * piece_len, piece_len)]
            source = tokens.at[u // 2, u % 2, half]
            loads.append(pltpu.make_async_copy(source, place, row_sem.at[u, half]))
    for load in loads:
        load.start()
    for load in loads:
        load.wait()
    row_tile, col_tile = units // 3, width // 3

    def tile_store(i, r, c, slot):
        rows = pl.ds(pl.multiple_of(r * row_tile, 16), row_tile)
        cols = pl.ds(pl.multiple_of(i * width + c * col_tile, 128), col_tile)
        return pltpu.make_async_copy(tile.at[slot], grads.at[rows, cols], tile_sem.at[slot])

    def one_tile(j, carry):
        i, slot = lax.div(j, 9), lax.rem(j, 2)
        r, c = lax.div(lax.rem(j, 9), 3), lax.rem(j, 3)
        rows = pl.ds(pl.multiple_of(r * row_tile, 128), row_tile)
        cols = pl.ds(pl.multiple_of(c * col_tile, 128), col_tile)
        total = outer_rows(left[i, :, rows], right[:, cols])

        @pl.when(j >= 2)
        def _():
            tile_store(i, r, c, slot).wait()

        tile[slot] = total.astype(tile.dtype)
        tile_store(i, r, c, slot).start()
        return carry

    lax.fori_loop(0, PASS_TURN, one_tile, 0)
    spread.pass_on()
    lax.fori_loop(PASS_TURN, 18, one_tile, 0)
    for slot in range(2):
        tile_store(0, 0, 0, slot).wait()
    spread.finish()


PASS_TURN = 14


def spread_plane(blocks, low_gate, low_up, tokens):
    n_plane = 2 * KV_HEADS
    low = blocks.dtype
    n_units, unit_rows, units = low_gate.shape
    width = blocks.shape[2]
    return pl.pallas_call(
        partial(spread_kernel, n_plane),
        out_shape=[
            jax.ShapeDtypeStruct((n_plane,) + blocks.shape[1:], low),
            jax.ShapeDtypeStruct((units, 2 * width), low),
        ],
        in_specs=[ANY] * 4,
        out_specs=[ANY, ANY],
        scratch_shapes=[
            pltpu.VMEM((2, n_units * unit_rows, units), low),
            pltpu.VMEM((n_units * unit_rows, width), low),
            pltpu.VMEM((2, units // 3, width // 3), low),
            DMA((SPREAD_SLOTS,)),
            DMA((SPREAD_SLOTS,)),
            DMA((1,)),
            DMA((2, n_units)),
            DMA((n_units, 2)),
            DMA((2,)),
        ],
        compiler_params=pltpu.CompilerParams(
            collective_id=3, has_side_effects=True, vmem_limit_bytes=48 * 1024 * 1024
        ),
    )(blocks, low_gate, low_up, tokens)


def gather_kernel(
    n_seq,
    n_plane,
    hidden,
    blocks,
    hidden_all,
    blocks_all,
    hid_send,
    hid_recv,
    hid_local,
    chip_send,
    chip_recv,
    chip_local,
    left_send,
    right_send,
    line_recv,
    twin_send,
    twin_recv,
):
    n_chip = n_plane // 2
    s = lax.axis_index("seq")
    q = lax.axis_index("chip")
    k = lax.axis_index("core")
    greet(n_plane, n_seq)
    swaps = []
    for step in range(1, n_chip):
        to = lax.rem(q + step, n_chip)
        copy = remote(
            blocks.at[to],
            blocks_all.at[s, k, q],
            chip_send.at[step],
            chip_recv.at[step],
            {"chip": to},
        )
        copy.start()
        swaps.append(copy)
    own = pltpu.make_async_copy(blocks.at[q], blocks_all.at[s, k, q], chip_local.at[0])
    own.start()
    spread = Spread(hidden, hidden_all, hid_send, hid_recv, hid_local)
    for copy in swaps:
        copy.wait_recv()
    own.wait()
    spread.start()

    def to_left(d):
        return remote(
            blocks_all.at[d, k], blocks_all.at[d, k], left_send.at[d], line_recv.at[d], {"seq": s - 1}
        )

    def to_right(d):
        return remote(
            blocks_all.at[d, k], blocks_all.at[d, k], right_send.at[d], line_recv.at[d], {"seq": s + 1}
        )

    def to_twin(d):
        return remote(
            blocks_all.at[d, k], blocks_all.at[d, k], twin_send.at[d], twin_recv.at[d], {"core": 1 - k}
        )

    def from_twin(d):
        return remote(
            blocks_all.at[d, 1 - k],
            blocks_all.at[d, 1 - k],
            twin_send.at[d],
            twin_recv.at[d],
            {"core": 1 - k},
        )

    @pl.when(s > 0)
    def _():
        to_left(s).start()

    @pl.when(s < n_seq - 1)
    def _():
        to_right(s).start()

    to_twin(s).start()
    for hop in range(1, n_seq):
        if hop == 2:
            spread.pass_on()
        from_left = s - hop
        from_right = s + hop

        @pl.when(from_left >= 0)
        def _():
            to_left(from_left).wait_recv()

            @pl.when(s < n_seq - 1)
            def _():
                to_right(from_left).start()

            to_twin(from_left).start()

        @pl.when(from_right < n_seq)
        def _():
            to_right(from_right).wait_recv()

            @pl.when(s > 0)
            def _():
                to_left(from_right).start()

            to_twin(from_right).start()

    for d in range(n_seq):

        @pl.when((d >= s) & (s > 0))
        def _():
            to_left(d).wait_send()

        @pl.when((d <= s) & (s < n_seq - 1))
        def _():
            to_right(d).wait_send()

        to_twin(d).wait_send()
        from_twin(d).wait_recv()
    for copy in swaps:
        copy.wait_send()
    spread.finish()


def gather_first(n_seq, hidden, blocks):
    n_plane = 2 * KV_HEADS
    n_chip = KV_HEADS
    return pl.pallas_call(
        partial(gather_kernel, n_seq, n_plane),
        out_shape=[
            jax.ShapeDtypeStruct((n_plane,) + hidden.shape[1:], hidden.dtype),
            jax.ShapeDtypeStruct((n_seq, 2) + blocks.shape, blocks.dtype),
        ],
        in_specs=[ANY, ANY],
        out_specs=[ANY, ANY],
        scratch_shapes=[
            DMA((SPREAD_SLOTS,)),
            DMA((SPREAD_SLOTS,)),
            DMA((1,)),
            DMA((n_chip,)),
            DMA((n_chip,)),
            DMA((1,)),
            DMA((n_seq,)),
            DMA((n_seq,)),
            DMA((n_seq,)),
            DMA((n_seq,)),
            DMA((n_seq,)),
        ],
        compiler_params=pltpu.CompilerParams(collective_id=1, has_side_effects=True),
    )(hidden, blocks)


def last_kernel(
    n_seq,
    n_plane,
    parts,
    blocks,
    parts_all,
    sums,
    held,
    twin,
    line,
    part_send,
    part_recv,
    part_local,
    held_sem,
    twin_send,
    twin_recv,
    line_send,
    line_recv,
    chip_send,
    chip_recv,
    chip_local,
):
    n_chip = n_plane // 2
    s = lax.axis_index("seq")
    q = lax.axis_index("chip")
    k = lax.axis_index("core")
    greet(n_plane, n_seq)

    def load(d):
        return pltpu.make_async_copy(blocks.at[d, k], held.at[d], held_sem.at[d])

    def to_twin(d):
        return remote(
            blocks.at[d, 1 - k], twin.at[d], twin_send.at[d], twin_recv.at[d], {"core": 1 - k}
        )

    def to_left(d):
        return remote(held.at[d], line.at[d], line_send.at[d], line_recv.at[d], {"seq": s - 1})

    def to_right(d):
        return remote(
            held.at[d], line.at[d + 1], line_send.at[d], line_recv.at[d + 1], {"seq": s + 1}
        )

    def gather_terms(d, with_left, with_right):
        load(d).wait()
        to_twin(d).wait_recv()

        @pl.when(with_right)
        def _():
            to_left(d).wait_recv()

        @pl.when(with_left)
        def _():
            to_right(d).wait_recv()

        def body(i, carry):
            held[d, i] = (held[d, i].astype(jnp.float32) + twin[d, i].astype(jnp.float32)).astype(
                held.dtype
            )
            return carry

        def body_right(i, carry):
            total = held[d, i].astype(jnp.float32) + twin[d, i].astype(jnp.float32)
            held[d, i] = (total + line[d, i].astype(jnp.float32)).astype(held.dtype)
            return carry

        def body_left(i, carry):
            total = held[d, i].astype(jnp.float32) + twin[d, i].astype(jnp.float32)
            held[d, i] = (total + line[d + 1, i].astype(jnp.float32)).astype(held.dtype)
            return carry

        def body_both(i, carry):
            total = held[d, i].astype(jnp.float32) + twin[d, i].astype(jnp.float32)
            total = total + line[d, i].astype(jnp.float32)
            held[d, i] = (total + line[d + 1, i].astype(jnp.float32)).astype(held.dtype)
            return carry

        @pl.when(jnp.logical_not(with_left) & jnp.logical_not(with_right))
        def _():
            lax.fori_loop(0, n_chip, body, 0)

        @pl.when(jnp.logical_not(with_left) & with_right)
        def _():
            lax.fori_loop(0, n_chip, body_right, 0)

        @pl.when(with_left & jnp.logical_not(with_right))
        def _():
            lax.fori_loop(0, n_chip, body_left, 0)

        @pl.when(with_left & with_right)
        def _():
            lax.fori_loop(0, n_chip, body_both, 0)

    for d in range(n_seq):
        to_twin(d).start()
        load(d).start()
    part_copies = start_exchange(n_plane, parts, parts_all, part_send, part_recv, part_local)
    never = s < 0
    for hop in range(1, n_seq):
        left = hop - n_seq + s
        right = n_seq - hop + s

        @pl.when(left >= 0)
        def _():
            gather_terms(left, never, s < n_seq - 1)
            to_left(left).start()

        @pl.when(right <= n_seq - 1)
        def _():
            gather_terms(right, s > 0, never)
            to_right(right).start()

    gather_terms(s, s > 0, s < n_seq - 1)
    swaps = []
    for step in range(1, n_chip):
        to = lax.rem(q + step, n_chip)
        copy = remote(
            held.at[s, to], sums.at[q], chip_send.at[step], chip_recv.at[step], {"chip": to}
        )
        copy.start()
        swaps.append(copy)
    own = pltpu.make_async_copy(held.at[s, q], sums.at[q], chip_local.at[0])
    own.start()
    for d in range(n_seq):
        to_twin(d).wait_send()

        @pl.when(d < s)
        def _():
            to_left(d).wait_send()

        @pl.when(d > s)
        def _():
            to_right(d).wait_send()

    for copy in part_copies:
        copy.wait()
    for copy in swaps:
        copy.wait()
    own.wait()


def sum_last(n_seq, parts, blocks):
    n_plane = 2 * KV_HEADS
    n_chip = KV_HEADS
    block = blocks.shape[2:]
    return pl.pallas_call(
        partial(last_kernel, n_seq, n_plane),
        out_shape=[
            jax.ShapeDtypeStruct(parts.shape, parts.dtype),
            jax.ShapeDtypeStruct(block, blocks.dtype),
        ],
        in_specs=[ANY, ANY],
        out_specs=[ANY, ANY],
        scratch_shapes=[
            pltpu.VMEM((n_seq,) + block, blocks.dtype),
            pltpu.VMEM((n_seq,) + block, blocks.dtype),
            pltpu.VMEM((n_seq + 1,) + block, blocks.dtype),
            DMA((n_plane,)),
            DMA((n_plane,)),
            DMA((1,)),
            DMA((n_seq,)),
            DMA((n_seq,)),
            DMA((n_seq,)),
            DMA((n_seq,)),
            DMA((n_seq + 1,)),
            DMA((n_chip,)),
            DMA((n_chip,)),
            DMA((1,)),
        ],
        compiler_params=pltpu.CompilerParams(
            collective_id=4, has_side_effects=True, vmem_limit_bytes=32 * 1024 * 1024
        ),
    )(parts, blocks)


QUERY_BLOCK = 256


def block_probs(query, keys, segment_col, segment_row, first):
    rows, width = query.shape[0], keys.shape[0]
    scaled = times_rows(query, keys) * (1.0 / math.sqrt(HEAD_DIM))
    bent = jnp.tanh(scaled / SOFT_CAP)
    row = first + lax.broadcasted_iota(jnp.int32, (rows, width), 0)
    col = lax.broadcasted_iota(jnp.int32, (rows, width), 1)
    allowed = ((segment_col == segment_row) & (col <= row)) | (col == row)
    capped = jnp.where(allowed, SOFT_CAP * bent, MASKED)
    raised = jnp.exp(capped - jnp.max(capped, axis=-1, keepdims=True))
    return raised / jnp.sum(raised, axis=-1, keepdims=True), bent


def attend_kernel(group_size, queries, keys, values, segment_col, segment_row, out):
    seq_len = keys.shape[0]
    for first in range(0, seq_len, QUERY_BLOCK):
        rows = slice(first, first + QUERY_BLOCK)
        width = first + QUERY_BLOCK
        for head in range(group_size):
            cols = slice(head * HEAD_DIM, (head + 1) * HEAD_DIM)
            probs, unused = block_probs(
                queries[rows, cols],
                keys[:width],
                segment_col[rows, :],
                segment_row[:, :width],
                first,
            )
            out[rows, cols] = add_slice(probs.astype(jnp.bfloat16), values[:width]).astype(
                out.dtype
            )


def attend(queries, keys, values, segment_col, segment_row):
    return pl.pallas_call(
        partial(attend_kernel, queries.shape[1] // HEAD_DIM),
        out_shape=jax.ShapeDtypeStruct(queries.shape, jnp.bfloat16),
        compiler_params=pltpu.CompilerParams(vmem_limit_bytes=40 * 1024 * 1024),
    )(queries, keys, values, segment_col, segment_row)


def attend_back_kernel(
    group_size,
    queries,
    keys,
    values,
    segment_col,
    segment_row,
    grads,
    grad_queries,
    grad_keys,
    grad_values,
):
    seq_len = keys.shape[0]
    inverse_root = 1.0 / math.sqrt(HEAD_DIM)
    grad_keys[...] = jnp.zeros_like(grad_keys)
    grad_values[...] = jnp.zeros_like(grad_values)
    for first in range(0, seq_len, QUERY_BLOCK):
        rows = slice(first, first + QUERY_BLOCK)
        width = first + QUERY_BLOCK
        for head in range(group_size):
            cols = slice(head * HEAD_DIM, (head + 1) * HEAD_DIM)
            query = queries[rows, cols]
            probs, bent = block_probs(
                query, keys[:width], segment_col[rows, :], segment_row[:, :width], first
            )
            grad = grads[rows, cols]
            grad_probs = times_rows(grad, values[:width])
            mean = jnp.sum(probs * grad_probs, axis=-1, keepdims=True)
            grad_scaled = (probs * (grad_probs - mean) * (1.0 - bent * bent)).astype(jnp.bfloat16)
            grad_queries[rows, cols] = add_slice(grad_scaled, keys[:width]) * inverse_root
            grad_keys[:width, :] += outer_rows(grad_scaled, query) * inverse_root
            grad_values[:width, :] += outer_rows(probs.astype(jnp.bfloat16), grad)


def attend_back(queries, keys, values, segment_col, segment_row, grads):
    return pl.pallas_call(
        partial(attend_back_kernel, queries.shape[1] // HEAD_DIM),
        out_shape=[
            jax.ShapeDtypeStruct(queries.shape, jnp.float32),
            jax.ShapeDtypeStruct(keys.shape, jnp.float32),
            jax.ShapeDtypeStruct(values.shape, jnp.float32),
        ],
        compiler_params=pltpu.CompilerParams(vmem_limit_bytes=40 * 1024 * 1024),
    )(queries, keys, values, segment_col, segment_row, grads)


def unit_orders(n):
    units, sums = [], []
    for s in range(n):
        keyed = []
        for d in range(n):
            if d != s:
                near = abs(s - d)
                behind, past = (s, d) if d < s else (n - 1 - s, n - 1 - d)
                keyed += [(near, d, 0), (behind + past + 1, d, 1)]
        order = [(s, 0), (s, 1)] + [(d, h) for unused, d, h in sorted(keyed)]
        units.append([2 * d + h for d, h in order])
        if s in (0, n - 1):
            sums.append(units[-1][2:])
            continue
        keyed = []
        for d in range(n):
            if d != s:
                hops, place = (n - 2 - s, d) if d < s else (s - 1, n - 1 - d)
                keyed += [(n - 2 - place + hops, d, 0), (n - 1 + place + hops, d, 1)]
        sums.append([2 * d + h for unused, d, h in sorted(keyed)])
    return units, sums


def pick(table, s, i):
    width = len(table[0])
    place = s * width + i
    value = 0
    for k, entry in enumerate(entry for row in table for entry in row):
        value = jnp.where(place == k, entry, value)
    return value


SUBS = 1
SUM_TURNS = (0, 1, 4, 5, 8, 8)
GELU_SCALE = math.sqrt(2.0 / math.pi)


def gelu_pieces(gate):
    bend = jnp.tanh(GELU_SCALE * (gate + 0.044715 * gate * gate * gate))
    value = 0.5 * gate * (1.0 + bend)
    slope = 0.5 * (1.0 + bend) + 0.5 * gate * (1.0 - bend * bend) * GELU_SCALE * (
        1.0 + 3.0 * 0.044715 * gate * gate
    )
    return value, slope


def units_kernel(n_seq, backward, *refs):
    if backward:
        tokens, units, downs, kept_gate, kept_up, kept_hidden = refs[:6]
        out, first_out, second_out, down_grads = refs[6:10]
        stage_outs = (first_out, second_out)
        scratch = refs[10:]
    else:
        tokens, units, downs = refs[:3]
        out, tokens_all, first_out, second_out, third_out = refs[3:8]
        stage_outs = (first_out, second_out, third_out)
        scratch = refs[8:]
    units_v, downs_v, held, own_sum, twin_sum, twin_out, line, stage = scratch[:8]
    scratch = scratch[8:]
    if backward:
        kept, kept_sem, tile, tile_sem, load_sem = scratch[:5]
        scratch = scratch[5:]
    (
        weight_sem,
        own_sem,
        left_send,
        right_send,
        token_recv,
        twin_send,
        twin_recv,
        part_send,
        part_recv,
        line_send,
        line_recv,
        stage_sem,
        all_sem,
        out_sem,
    ) = scratch
    n = n_seq
    s = lax.axis_index("seq")
    k = lax.axis_index("core")
    twin = {"core": 1 - k}
    n_units, width = downs_v.shape
    piece_len = tokens.shape[1]
    at_end = (s == 0) | (s == n - 1)

    def token_left(d, h, source):
        return remote(
            source, held.at[d, h, 0], left_send.at[d, h], token_recv.at[d, h], {"seq": s - 1}
        )

    def token_right(d, h, source):
        return remote(
            source, held.at[d, h, 0], right_send.at[d, h], token_recv.at[d, h], {"seq": s + 1}
        )

    def token_twin(d, h, source):
        return remote(source, held.at[d, h, 1], twin_send.at[d, h], twin_recv.at[d, h], twin)

    def part_twin(d, h):
        return remote(
            twin_out.at[d, h], twin_sum.at[d, h], part_send.at[d, h], part_recv.at[d, h], twin
        )

    sub_len = piece_len // SUBS

    def part_line(d, h, sub):
        to_left = d < s
        slot = jnp.where(to_left, d, d + 1)
        rows = pl.ds(sub * sub_len, sub_len)
        return remote(
            twin_sum.at[d, h, rows],
            line.at[slot, h, rows],
            line_send.at[d, h, sub],
            line_recv.at[slot, h, sub],
            {"seq": jnp.where(to_left, s - 1, s + 1)},
        )

    def line_arrival(slot, h, sub):
        rows = pl.ds(sub * sub_len, sub_len)
        return remote(
            twin_sum.at[0, h, rows],
            line.at[slot, h, rows],
            line_send.at[0, h, sub],
            line_recv.at[slot, h, sub],
            {"seq": s},
        )

    def own_load(h):
        return pltpu.make_async_copy(tokens.at[h], held.at[s, h, 0], own_sem.at[h])

    def all_store(d, h):
        return pltpu.make_async_copy(held.at[d, h], tokens_all.at[d, h], all_sem.at[d, h])

    def stage_store(i, d, h, slot):
        return pltpu.make_async_copy(
            stage.at[i, slot], stage_outs[i].at[2 * d + h], stage_sem.at[i, slot]
        )

    def kept_load(i, d, h, slot):
        source = (kept_gate, kept_up)[i]
        return pltpu.make_async_copy(source.at[2 * d + h], kept.at[i, slot], kept_sem.at[i, slot])

    unit_table, sum_table = unit_orders(n)
    right_table = [
        [2 if d == 0 else unit_table[d].index(2 * (d - 1) + 1) + 1 for d in range(n)]
    ]
    left_table = [
        [2 if d == n - 1 else unit_table[d].index(2 * (d + 1) + 1) + 1 for d in range(n)]
    ]

    def source(t):
        unit = pick(unit_table, s, t)
        return lax.div(unit, 2), lax.rem(unit, 2)

    barrier = pltpu.get_barrier_semaphore()
    pl.semaphore_signal(barrier, inc=1, device_id=twin, device_id_type=MESH)

    @pl.when(s > 0)
    def _():
        pl.semaphore_signal(barrier, inc=1, device_id={"seq": s - 1}, device_id_type=MESH)

    @pl.when(s < n - 1)
    def _():
        pl.semaphore_signal(barrier, inc=1, device_id={"seq": s + 1}, device_id_type=MESH)

    pl.semaphore_wait(barrier, 1 + jnp.where(s > 0, 1, 0) + jnp.where(s < n - 1, 1, 0))

    def second_half(t):
        @pl.when((s < n - 1) & (t == pick(right_table, 0, s)))
        def _():
            d, h = jnp.maximum(s - 1, 0), jnp.where(s > 0, 1, 0)
            token_right(d, h, held.at[d, h, 0]).wait_send()
            token_right(s, 1, tokens.at[1]).start()

        @pl.when((s > 0) & (t == pick(left_table, 0, s)))
        def _():
            d, h = jnp.minimum(s + 1, n - 1), jnp.where(s < n - 1, 1, 0)
            token_left(d, h, held.at[d, h, 0]).wait_send()
            token_left(s, 1, tokens.at[1]).start()

    @pl.when(s < n - 1)
    def _():
        token_right(s, 0, tokens.at[0]).start()

    @pl.when(s > 0)
    def _():
        token_left(s, 0, tokens.at[0]).start()

    for h in range(2):
        token_twin(s, h, tokens.at[h]).start()
        own_load(h).start()
    load_units = pltpu.make_async_copy(units, units_v, weight_sem.at[0])
    load_downs = pltpu.make_async_copy(downs, downs_v, weight_sem.at[1])
    load_units.start()
    load_downs.start()
    if backward:
        for i in range(2):
            kept_load(i, s, 0, 0).start()
    load_units.wait()
    load_downs.wait()

    def add_rows(d, h, sub, into_own, use_line):
        step = 16

        def body(i, carry):
            rows = pl.ds(pl.multiple_of(sub * sub_len + i * step, step), step)
            total = own_sum[d, h, rows, :] + twin_sum[d, h, rows, :].astype(jnp.float32)
            for slot in use_line:
                total = total + line[slot, h, rows, :].astype(jnp.float32)
            if into_own:
                own_sum[d, h, rows, :] = total
            else:
                twin_sum[d, h, rows, :] = total.astype(twin_sum.dtype)
            return carry

        lax.fori_loop(0, sub_len // step, body, 0)

    def combine(d, h):
        to_left = d < s
        slot = jnp.where(to_left, d, d + 1)
        more = jnp.where(to_left, s < n - 1, s > 0)
        part_twin(d, h).wait_recv()

        @pl.when(more)
        def _():
            for sub in range(SUBS):
                line_arrival(slot, h, sub).wait_recv()
                add_rows(d, h, sub, False, (slot,))
                part_line(d, h, sub).start()

        @pl.when(jnp.logical_not(more))
        def _():
            for sub in range(SUBS):
                add_rows(d, h, sub, False, ())
                part_line(d, h, sub).start()

    columns = width // 3
    chunk = n_units // 3

    def compute_forward(d, h, slot):
        rows = held[d, h].reshape(2 * piece_len, width)
        for c in range(3):
            cols = slice(c * chunk, (c + 1) * chunk)
            gate = times_rows(rows, units_v[cols, :width])
            up = times_rows(rows, units_v[cols, width:])
            value, unused = gelu_pieces(gate)
            stage[0, slot, :, cols] = gate.astype(stage.dtype)
            stage[1, slot, :, cols] = up.astype(stage.dtype)
            stage[2, slot, :, cols] = (value * up).astype(stage.dtype)
        for c in range(3):
            cols = slice(c * columns, (c + 1) * columns)
            part = add_slice(stage[2, slot], downs_v[:, cols])
            own_sum[d, h, :, cols] = part[:piece_len]
            twin_out[d, h, :, cols] = part[piece_len:].astype(twin_out.dtype)

    def compute_backward(d, h, slot):
        rows = held[d, h].reshape(2 * piece_len, width)
        for c in range(3):
            cols = slice(c * chunk, (c + 1) * chunk)
            grad = times_rows(rows, downs_v[cols, :])
            value, slope = gelu_pieces(kept[0, slot, :, cols].astype(jnp.float32))
            up = kept[1, slot, :, cols].astype(jnp.float32)
            stage[0, slot, :, cols] = (grad * up * slope).astype(stage.dtype)
            stage[1, slot, :, cols] = (grad * value).astype(stage.dtype)
        for c in range(3):
            cols = slice(c * columns, (c + 1) * columns)
            later = slice(width + c * columns, width + (c + 1) * columns)
            part = add_slice(stage[0, slot], units_v[:, cols])
            part = part + add_slice(stage[1, slot], units_v[:, later])
            own_sum[d, h, :, cols] = part[:piece_len]
            twin_out[d, h, :, cols] = part[piece_len:].astype(twin_out.dtype)

    row_tile, col_tile = n_units // 3, width // 3

    def down_gradient(between):
        unit_rows = 2 * piece_len
        group_rows = n * unit_rows

        def left_load(u):
            place = downs_v.at[
                pl.ds((u % n) * unit_rows, unit_rows), pl.ds((u // n) * n_units, n_units)
            ]
            return pltpu.make_async_copy(kept_hidden.at[u], place, load_sem.at[u])

        def left_rows(g, first):
            return downs_v[
                :group_rows, pl.ds(pl.multiple_of(g * n_units + first, 128), row_tile)
            ]

        def right_rows(g, first):
            cols = pl.ds(pl.multiple_of(first, 128), col_tile)
            part = held[g * n // 2 : (g + 1) * n // 2, :, :, :, cols]
            return part.reshape(group_rows, col_tile)

        def tile_store(r, c, slot):
            rows = pl.ds(pl.multiple_of(r * row_tile, 16), row_tile)
            cols = pl.ds(pl.multiple_of(c * col_tile, 128), col_tile)
            return pltpu.make_async_copy(tile.at[slot], down_grads.at[rows, cols], tile_sem.at[slot])

        for u in range(2 * n):
            left_load(u).start()
        for u in range(2 * n):
            left_load(u).wait()

        def one_tile(j, carry):
            slot = lax.rem(j, 2)
            r, c = lax.div(j, 3), lax.rem(j, 3)
            total = sum(
                outer_rows(left_rows(g, r * row_tile), right_rows(g, c * col_tile))
                for g in range(2)
            )

            @pl.when(j >= 2)
            def _():
                tile_store(r, c, slot).wait()

            tile[slot] = total.astype(tile.dtype)
            tile_store(r, c, slot).start()
            for step, turn in enumerate(SUM_TURNS):

                @pl.when(j == turn)
                def _():
                    between(step)

            return carry

        lax.fori_loop(0, 9, one_tile, 0)
        for slot in range(2):
            tile_store(0, 0, slot).wait()

    def unit(t, carry):
        d, h = source(t)
        slot = lax.rem(t, 2)

        @pl.when(at_end & (t >= 3))
        def _():
            combine(*source(t - 1))

        @pl.when(t < 2)
        def _():
            own_load(h).wait()

        @pl.when(t >= 2)
        def _():
            piece = held.at[d, h, 0]
            token_left(d, h, piece).wait_recv()

            @pl.when((d < s) & (s < n - 1))
            def _():
                token_right(d, h, piece).start()

            @pl.when((d > s) & (s > 0))
            def _():
                token_left(d, h, piece).start()

            token_twin(d, h, piece).start()
            for i in range(len(stage_outs)):
                stage_store(i, d, h, slot).wait()

        second_half(t)
        if backward:

            @pl.when(t < 2 * n - 1)
            def _():
                for i in range(2):
                    kept_load(i, *source(t + 1), 1 - slot).start()

            for i in range(2):
                kept_load(i, d, h, slot).wait()
        token_twin(d, h, held.at[d, h, 0]).wait_recv()
        if backward:
            compute_backward(d, h, slot)
        else:
            compute_forward(d, h, slot)
        part_twin(d, h).start()
        if not backward:
            all_store(d, h).start()
        for i in range(len(stage_outs)):
            stage_store(i, d, h, slot).start()

        return carry

    lax.fori_loop(0, 2 * n, unit, 0)

    second_half(2 * n)

    @pl.when(at_end)
    def _():
        combine(*source(2 * n - 1))

    n_sums = 2 * (n - 1)

    def middle(i):
        @pl.when(jnp.logical_not(at_end) & (i < n_sums))
        def _():
            unit = pick(sum_table, s, i)
            combine(lax.div(unit, 2), lax.rem(unit, 2))

    if backward:
        down_gradient(middle)
    else:

        def one(i, carry):
            middle(i)
            return carry

        lax.fori_loop(0, n_sums, one, 0)

    def finish(h, carry):
        part_twin(s, h).wait_recv()
        for sub in range(SUBS):

            @pl.when(s < n - 1)
            def _():
                line_arrival(s, h, sub).wait_recv()

            @pl.when(s > 0)
            def _():
                line_arrival(s + 1, h, sub).wait_recv()

            @pl.when(s == 0)
            def _():
                add_rows(s, h, sub, True, (s,))

            @pl.when(s == n - 1)
            def _():
                add_rows(s, h, sub, True, (s + 1,))

            @pl.when(jnp.logical_not(at_end))
            def _():
                add_rows(s, h, sub, True, (s, s + 1))

        pltpu.make_async_copy(own_sum.at[s, h], out.at[h], out_sem.at[h]).start()
        return carry

    lax.fori_loop(0, 2, finish, 0)

    def drain(t, carry):
        d = lax.div(t, 2)
        h = lax.rem(t, 2)
        piece = held.at[d, h, 0]

        right_seen = (d == jnp.maximum(s - 1, 0)) & (h == jnp.where(s > 0, 1, 0))
        left_seen = (d == jnp.minimum(s + 1, n - 1)) & (h == jnp.where(s < n - 1, 1, 0))

        @pl.when((d <= s) & (s < n - 1) & jnp.logical_not(right_seen))
        def _():
            token_right(d, h, piece).wait_send()

        @pl.when((d >= s) & (s > 0) & jnp.logical_not(left_seen))
        def _():
            token_left(d, h, piece).wait_send()

        token_twin(d, h, piece).wait_send()
        part_twin(d, h).wait_send()

        @pl.when(d != s)
        def _():
            for sub in range(SUBS):
                part_line(d, h, sub).wait_send()

        if not backward:
            all_store(d, h).wait()
        return carry

    lax.fori_loop(0, 2 * n, drain, 0)
    for h in range(2):
        for i in range(len(stage_outs)):
            stage_store(i, 0, h, h).wait()
        pltpu.make_async_copy(own_sum.at[s, h], out.at[h], out_sem.at[h]).wait()


def run_units(n_seq, tokens, units, downs, kept=None):
    backward = kept is not None
    low = tokens.dtype
    n_units = downs.shape[0]
    halves, piece_len, width = tokens.shape
    n_stage = 2 if backward else 3
    held = (n_seq, halves, 2, piece_len, width)
    unit_rows = (2 * n_seq, 2 * piece_len, n_units)
    sums = (n_seq, halves, piece_len, width)
    scratch = [
        pltpu.VMEM(units.shape, low),
        pltpu.VMEM(downs.shape, low),
        pltpu.VMEM(held, low),
        pltpu.VMEM(sums, jnp.float32),
        pltpu.VMEM(sums, low),
        pltpu.VMEM(sums, low),
        pltpu.VMEM((n_seq + 1,) + sums[1:], low),
        pltpu.VMEM((n_stage, 2) + unit_rows[1:], low),
    ]
    outs = [jax.ShapeDtypeStruct(tokens.shape, jnp.float32)]
    if backward:
        scratch += [
            pltpu.VMEM((2, 2) + unit_rows[1:], low),
            DMA((2, 2)),
            pltpu.VMEM((2, n_units // 3, width // 3), low),
            DMA((2,)),
            DMA((2 * n_seq,)),
        ]
    else:
        outs += [jax.ShapeDtypeStruct(held, low)]
    outs += [jax.ShapeDtypeStruct(unit_rows, low)] * n_stage
    if backward:
        outs += [jax.ShapeDtypeStruct(downs.shape, low)]
    pairs = DMA((n_seq, halves))
    scratch += [DMA((2,)), DMA((halves,))] + [pairs] * 7
    scratch += [DMA((n_seq, halves, SUBS)), DMA((n_seq + 1, halves, SUBS))]
    scratch += [DMA((n_stage, 2)), pairs, DMA((halves,))]
    operands = (tokens, units, downs) + (tuple(kept) if backward else ())
    return pl.pallas_call(
        partial(units_kernel, n_seq, backward),
        out_shape=outs,
        in_specs=[ANY] * len(operands),
        out_specs=[ANY] * len(outs),
        scratch_shapes=scratch,
        compiler_params=pltpu.CompilerParams(
            collective_id=6 if backward else 5,
            has_side_effects=True,
            vmem_limit_bytes=63 * 1024 * 1024,
        ),
    )(*operands)


def per_device_general(
    hidden_in,
    norm_gains,
    qkv_weight,
    out_weight,
    gate_up_weight,
    down_weight,
    output_cotangent,
    segment_ids,
    padding,
    positions,
):
    everyone = ("seq", "chip", "core")
    plane = ("chip", "core")
    column = ("seq", "core")
    groups = hidden_in.shape[0]
    piece_len = hidden_in.shape[1]
    model_width = hidden_in.shape[2]
    row_count = groups * piece_len
    seq_len = segment_ids.shape[1]
    group_size = HEADS // KV_HEADS
    query_width = HEADS * HEAD_DIM
    key_width = KV_HEADS * HEAD_DIM
    proj_width = qkv_weight.shape[1]

    residual = hidden_in.reshape(row_count, model_width).astype(jnp.float32)
    factor = lax.rsqrt(jnp.mean(residual * residual, axis=-1, keepdims=True) + EPSILON)
    gain_cols = lax.all_gather(norm_gains, everyone, axis=0, tiled=True).astype(jnp.float32)
    qkv_full = lax.all_gather(qkv_weight, everyone, axis=0, tiled=True)
    attn_input = (residual * factor * gain_cols[:, 0]).astype(jnp.bfloat16)
    projected = add_slice(attn_input, qkv_full)
    cosine, sine_part = rotary_tables(positions.reshape(row_count), HEAD_DIM)
    queries = (
        rotate(projected[:, :query_width].reshape(row_count, HEADS, HEAD_DIM), cosine, sine_part)
        .astype(jnp.bfloat16)
        .reshape(row_count, query_width)
    )
    keys_here = (
        rotate(
            projected[:, query_width : query_width + key_width].reshape(
                row_count, KV_HEADS, HEAD_DIM
            ),
            cosine,
            sine_part,
        )
        .astype(jnp.bfloat16)
        .reshape(groups, piece_len, key_width)
    )
    values_here = (
        projected[:, query_width + key_width :]
        .astype(jnp.bfloat16)
        .reshape(groups, piece_len, key_width)
    )
    both_all = lax.all_gather(
        jnp.concatenate([keys_here, values_here], axis=2), plane, axis=1, tiled=True
    )
    keys_all = both_all[:, :, :key_width]
    values_all = both_all[:, :, key_width:]
    first_query = (lax.axis_index("chip") * 2 + lax.axis_index("core")) * piece_len
    query_rows = first_query + jnp.arange(piece_len, dtype=jnp.int32)
    key_rows = jnp.arange(seq_len, dtype=jnp.int32)
    segment_query = lax.dynamic_slice_in_dim(segment_ids, first_query, piece_len, 1)
    allowed = (segment_query[:, :, None] == segment_ids[:, None, :]) & (
        key_rows[None, None, :] <= query_rows[None, :, None]
    ) & (padding[:, None, :] == 1) | (key_rows[None, None, :] == query_rows[None, :, None])
    allowed = allowed[:, None, None]
    probs = soft_probs(score_block(queries, keys_all), allowed)
    attn_out = mix_values(probs.astype(jnp.bfloat16), values_all)
    out_full = lax.all_gather(out_weight, everyone, axis=0, tiled=True)
    attn_proj = times_rows(attn_out, out_full)
    after_attn = residual + rms_norm(attn_proj, gain_cols[:, 1])
    ffn_input = rms_norm(after_attn, gain_cols[:, 2]).astype(jnp.bfloat16)

    unit_weights = lax.all_gather(gate_up_weight, "chip", axis=0, tiled=True)
    down_units = lax.all_gather(down_weight, "chip", axis=0, tiled=True)
    ffn_all = lax.all_gather(ffn_input, column, axis=0, tiled=True)
    gate_part = times_rows(ffn_all, unit_weights[:, :model_width])
    up_part = times_rows(ffn_all, unit_weights[:, model_width:])
    hidden_part = geglu_parts(gate_part, up_part).astype(jnp.bfloat16)
    down_part = add_slice(hidden_part, down_units).astype(jnp.bfloat16)
    down_out = lax.psum_scatter(down_part, column, scatter_dimension=0, tiled=True).astype(
        jnp.float32
    )
    layer_out = after_attn + rms_norm(down_out, gain_cols[:, 3])
    layer_output = layer_out.astype(jnp.bfloat16).reshape(groups, piece_len, model_width)

    cotangent = output_cotangent.reshape(row_count, model_width).astype(jnp.float32)
    unused_last, pull_last = jax.vjp(rms_norm, down_out, gain_cols[:, 3])
    grad_down, grad_gain_last = pull_last(cotangent)
    grad_down_low = grad_down.astype(jnp.bfloat16)
    grad_down_all = lax.all_gather(grad_down_low, column, axis=0, tiled=True)
    grad_part = times_rows(grad_down_all, down_units)
    unused_units, pull_units = jax.vjp(geglu_parts, gate_part, up_part)
    grad_gate_part, grad_up_part = pull_units(grad_part)
    gate_low = grad_gate_part.astype(jnp.bfloat16)
    up_low = grad_up_part.astype(jnp.bfloat16)
    grad_ffn_part = add_slice(gate_low, unit_weights[:, :model_width]) + add_slice(
        up_low, unit_weights[:, model_width:]
    )
    grad_ffn_in = lax.psum_scatter(
        grad_ffn_part.astype(jnp.bfloat16), column, scatter_dimension=0, tiled=True
    ).astype(jnp.float32)
    gate_up_rows = jnp.concatenate(
        [
            outer_rows(gate_low, ffn_all).astype(jnp.bfloat16),
            outer_rows(up_low, ffn_all).astype(jnp.bfloat16),
        ],
        axis=1,
    )
    down_rows = outer_rows(hidden_part, grad_down_all).astype(jnp.bfloat16)
    gate_up_grad = lax.psum_scatter(
        gate_up_rows, "chip", scatter_dimension=0, tiled=True
    ).astype(jnp.float32)
    down_grad = lax.psum_scatter(down_rows, "chip", scatter_dimension=0, tiled=True).astype(
        jnp.float32
    )

    unused_mid, pull_mid = jax.vjp(rms_norm, after_attn, gain_cols[:, 2])
    grad_after_ffn, grad_gain_mid = pull_mid(grad_ffn_in)
    grad_after = cotangent + grad_after_ffn
    unused_post, pull_post = jax.vjp(rms_norm, attn_proj, gain_cols[:, 1])
    grad_proj, grad_gain_post = pull_post(grad_after)
    grad_proj_low = grad_proj.astype(jnp.bfloat16)
    grad_attn = add_slice(grad_proj_low, out_full).astype(jnp.bfloat16)
    scaled = score_block(queries, keys_all)
    probs, pull_probs = jax.vjp(partial(soft_probs, allowed=allowed), scaled)
    grad_heads = grad_attn.reshape(groups, piece_len, KV_HEADS, group_size, HEAD_DIM)
    query_heads = queries.reshape(groups, piece_len, KV_HEADS, group_size, HEAD_DIM)
    key_heads = keys_all.reshape(groups, seq_len, KV_HEADS, HEAD_DIM)
    value_heads = values_all.reshape(groups, seq_len, KV_HEADS, HEAD_DIM)
    grad_probs = jnp.einsum(
        "spkgd,slkd->skgpl", grad_heads, value_heads, preferred_element_type=jnp.float32
    )
    (grad_scaled,) = pull_probs(grad_probs)
    grad_scaled_low = grad_scaled.astype(jnp.bfloat16)
    inverse_root = 1.0 / math.sqrt(HEAD_DIM)
    grad_query_rot = (
        jnp.einsum(
            "skgpl,slkd->spkgd", grad_scaled_low, key_heads, preferred_element_type=jnp.float32
        )
        * inverse_root
    )
    grad_key_rot = (
        jnp.einsum(
            "skgpl,spkgd->slkd", grad_scaled_low, query_heads, preferred_element_type=jnp.float32
        )
        * inverse_root
    )
    grad_value_part = jnp.einsum(
        "skgpl,spkgd->slkd",
        probs.astype(jnp.bfloat16),
        grad_heads,
        preferred_element_type=jnp.float32,
    )
    both_grads = jnp.concatenate(
        [
            grad_key_rot.reshape(groups, seq_len, key_width),
            grad_value_part.reshape(groups, seq_len, key_width),
        ],
        axis=2,
    ).astype(jnp.bfloat16)
    both_summed = lax.psum_scatter(both_grads, plane, scatter_dimension=1, tiled=True)
    both_summed = both_summed.astype(jnp.float32).reshape(row_count, 2 * key_width)
    key_summed = both_summed[:, :key_width]
    value_summed = both_summed[:, key_width:]
    grad_queries = rotate_back(
        grad_query_rot.reshape(row_count, HEADS, HEAD_DIM), cosine, sine_part
    ).reshape(row_count, query_width)
    grad_keys = rotate_back(
        key_summed.reshape(row_count, KV_HEADS, HEAD_DIM), cosine, sine_part
    ).reshape(row_count, key_width)
    grad_projected = jnp.concatenate([grad_queries, grad_keys, value_summed], axis=1).astype(
        jnp.bfloat16
    )
    grad_attn_in = times_rows(grad_projected, qkv_full)
    unused_first, pull_first = jax.vjp(rms_norm, residual, gain_cols[:, 0])
    grad_res_first, grad_gain_first = pull_first(grad_attn_in)
    input_grad = (grad_after + grad_res_first).reshape(groups, piece_len, model_width)
    gain_terms = jnp.stack([grad_gain_first, grad_gain_post, grad_gain_mid, grad_gain_last], axis=1)
    qkv_part = outer_rows(attn_input, grad_projected).astype(jnp.bfloat16)
    out_part = outer_rows(grad_proj_low, attn_out).astype(jnp.bfloat16)
    qkv_grad = lax.psum_scatter(qkv_part, everyone, scatter_dimension=0, tiled=True).astype(
        jnp.float32
    )
    out_proj_grad = lax.psum_scatter(out_part, everyone, scatter_dimension=0, tiled=True).astype(
        jnp.float32
    )
    gain_grad = lax.psum_scatter(gain_terms, everyone, scatter_dimension=0, tiled=True)
    return (layer_output, input_grad, gain_grad, qkv_grad, out_proj_grad, gate_up_grad, down_grad)


def per_device_by_heads(
    n_seq,
    hidden_in,
    norm_gains,
    qkv_weight,
    out_weight,
    gate_up_weight,
    down_weight,
    output_cotangent,
    segment_ids,
    padding,
    positions,
):
    groups, piece_len, model_width = hidden_in.shape
    row_count = groups * piece_len
    seq_len = segment_ids.shape[1]
    n_chip = KV_HEADS
    n_plane = 2 * n_chip
    group_size = HEADS // KV_HEADS
    query_width = HEADS * HEAD_DIM
    key_width = KV_HEADS * HEAD_DIM
    own_width = group_size * HEAD_DIM
    part_width = own_width + 2 * HEAD_DIM
    block_width = part_width + own_width
    weight_rows = qkv_weight.shape[0]
    extra_rows = 16 - weight_rows % 16
    block_rows = weight_rows + extra_rows
    core = lax.axis_index("core")

    gain_rows = jnp.pad(
        norm_gains.T, ((0, extra_rows - norm_gains.shape[1]), (0, block_width - weight_rows))
    )
    blocks = jnp.stack(
        [
            jnp.concatenate(
                [
                    jnp.concatenate(
                        [
                            qkv_weight[:, c * own_width : (c + 1) * own_width],
                            qkv_weight[
                                :, query_width + c * HEAD_DIM : query_width + (c + 1) * HEAD_DIM
                            ],
                            qkv_weight[
                                :,
                                query_width + key_width + c * HEAD_DIM : query_width
                                + key_width
                                + (c + 1) * HEAD_DIM,
                            ],
                            out_weight[:, c * own_width : (c + 1) * own_width],
                        ],
                        axis=1,
                    ),
                    gain_rows,
                ],
                axis=0,
            )
            for c in range(n_chip)
        ]
    )
    hidden_all, blocks_all = gather_first(n_seq, hidden_in, blocks)
    unit_weights = lax.all_gather(gate_up_weight, "chip", axis=0, tiled=True)
    down_units = lax.all_gather(down_weight, "chip", axis=0, tiled=True)
    blocks_all = blocks_all.transpose(0, 2, 1, 3, 4)
    own_weights = blocks_all[:, :, :, :weight_rows].reshape(model_width, block_width)
    own_qkv = own_weights[:, :part_width]
    own_out = own_weights[:, part_width:]
    gain_cols = (
        blocks_all[:, :, :, weight_rows : weight_rows + norm_gains.shape[1], :weight_rows]
        .transpose(0, 1, 2, 4, 3)
        .reshape(model_width, norm_gains.shape[1])
        .astype(jnp.float32)
    )

    seq_rows = hidden_all.reshape(seq_len, model_width).astype(jnp.float32)
    seq_factor = lax.rsqrt(jnp.mean(seq_rows * seq_rows, axis=-1, keepdims=True) + EPSILON)
    attn_input = (seq_rows * seq_factor * gain_cols[:, 0]).astype(jnp.bfloat16)
    projected = add_slice(attn_input, own_qkv)
    segment = lax.dynamic_index_in_dim(segment_ids, core, 0, keepdims=False)
    valid = lax.dynamic_index_in_dim(padding, core, 0, keepdims=False)
    token = jnp.arange(seq_len, dtype=jnp.int32)
    document_start = jnp.min(
        jnp.where(segment[:, None] == segment[None, :], token[None, :], seq_len), axis=1
    )
    cosine, sine_part = rotary_tables(token - document_start, HEAD_DIM)
    queries = (
        rotate(projected[:, :own_width].reshape(seq_len, group_size, HEAD_DIM), cosine, sine_part)
        .astype(jnp.bfloat16)
        .reshape(seq_len, own_width)
    )
    keys = (
        rotate(
            projected[:, own_width : own_width + HEAD_DIM].reshape(seq_len, 1, HEAD_DIM),
            cosine,
            sine_part,
        )
        .astype(jnp.bfloat16)
        .reshape(seq_len, HEAD_DIM)
    )
    values = projected[:, own_width + HEAD_DIM :].astype(jnp.bfloat16)
    segment_col = segment[:, None]
    segment_row = jnp.where(valid == 1, segment, -1)[None, :]
    attn_out = attend(queries, keys, values, segment_col, segment_row)
    proj_parts = times_rows(attn_out, own_out).astype(jnp.bfloat16)
    proj_parts = plane_exchange(
        proj_parts.reshape(n_plane, piece_len, model_width), 2
    )

    def sum_parts(parts):
        parts = parts.reshape(n_chip, groups, piece_len, model_width).astype(jnp.float32)
        return jnp.sum(parts, axis=0).reshape(row_count, model_width)

    attn_proj = sum_parts(proj_parts)
    residual = hidden_in.reshape(row_count, model_width).astype(jnp.float32)
    after_attn = residual + rms_norm(attn_proj, gain_cols[:, 1])
    ffn_input = rms_norm(after_attn, gain_cols[:, 2]).astype(jnp.bfloat16)

    pieces = (groups, piece_len, model_width)
    down_out, ffn_all, gate_part, up_part, hidden_part = run_units(
        n_seq, ffn_input.reshape(pieces), unit_weights, down_units
    )
    down_out = down_out.reshape(row_count, model_width)
    layer_out = after_attn + rms_norm(down_out, gain_cols[:, 3])
    layer_output = layer_out.astype(jnp.bfloat16).reshape(pieces)

    cotangent = output_cotangent.reshape(row_count, model_width).astype(jnp.float32)
    unused_last, pull_last = jax.vjp(rms_norm, down_out, gain_cols[:, 3])
    grad_down, grad_gain_last = pull_last(cotangent)
    grad_ffn_in, gate_low, up_low, down_rows = run_units(
        n_seq,
        grad_down.astype(jnp.bfloat16).reshape(pieces),
        unit_weights,
        down_units,
        (gate_part, up_part, hidden_part),
    )
    grad_ffn_in = grad_ffn_in.reshape(row_count, model_width)
    down_grad = lax.psum_scatter(down_rows, "chip", scatter_dimension=0, tiled=True).astype(
        jnp.float32
    )

    unused_mid, pull_mid = jax.vjp(rms_norm, after_attn, gain_cols[:, 2])
    grad_after_ffn, grad_gain_mid = pull_mid(grad_ffn_in)
    grad_after = cotangent + grad_after_ffn
    unused_post, pull_post = jax.vjp(rms_norm, attn_proj, gain_cols[:, 1])
    grad_proj, grad_gain_post = pull_post(grad_after)
    grad_proj_low = grad_proj.astype(jnp.bfloat16)

    grad_proj_all, gate_up_rows = spread_plane(
        grad_proj_low.reshape(groups, piece_len, model_width), gate_low, up_low, ffn_all
    )
    gate_up_grad = lax.psum_scatter(
        gate_up_rows, "chip", scatter_dimension=0, tiled=True
    ).astype(jnp.float32)
    grad_proj_all = grad_proj_all.reshape(seq_len, model_width)
    grad_attn = add_slice(grad_proj_all, own_out).astype(jnp.bfloat16)
    grad_query_rot, grad_key_rot, grad_values = attend_back(
        queries, keys, values, segment_col, segment_row, grad_attn
    )
    grad_queries = rotate_back(
        grad_query_rot.reshape(seq_len, group_size, HEAD_DIM), cosine, sine_part
    ).reshape(seq_len, own_width)
    grad_keys = rotate_back(
        grad_key_rot.reshape(seq_len, 1, HEAD_DIM), cosine, sine_part
    ).reshape(seq_len, HEAD_DIM)
    grad_projected = jnp.concatenate([grad_queries, grad_keys, grad_values], axis=1).astype(
        jnp.bfloat16
    )
    grad_in_part = times_rows(grad_projected, own_qkv)
    grad_gain_first = jnp.sum(grad_in_part * seq_rows * seq_factor, axis=0)
    weight_part = jnp.concatenate(
        [
            outer_rows(attn_input, grad_projected).astype(jnp.bfloat16),
            outer_rows(grad_proj_all, attn_out).astype(jnp.bfloat16),
        ],
        axis=1,
    ).reshape(n_seq, n_chip, 2, weight_rows, block_width)
    gain_terms = (
        jnp.stack([grad_gain_first, grad_gain_post, grad_gain_mid, grad_gain_last])
        .astype(jnp.bfloat16)
        .reshape(-1, n_seq, n_chip, 2, weight_rows)
        .transpose(1, 2, 3, 0, 4)
    )
    gain_terms = jnp.pad(
        gain_terms,
        ((0, 0),) * 3
        + ((0, extra_rows - gain_terms.shape[3]), (0, block_width - weight_rows)),
    )
    grad_blocks = jnp.concatenate([weight_part, gain_terms], axis=3).transpose(0, 2, 1, 3, 4)
    grad_in_parts, grad_sums = sum_last(
        n_seq,
        grad_in_part.astype(jnp.bfloat16).reshape(n_plane, piece_len, model_width),
        grad_blocks,
    )
    grad_attn_in = sum_parts(grad_in_parts)
    factor = lax.rsqrt(jnp.mean(residual * residual, axis=-1, keepdims=True) + EPSILON)
    unused_first, pull_first = jax.vjp(rms_norm, residual, gain_cols[:, 0])
    grad_res_first, unused_gain = pull_first(grad_attn_in)
    input_grad = (grad_after + grad_res_first).reshape(groups, piece_len, model_width)

    weight_sums = grad_sums[:, :weight_rows].astype(jnp.float32)
    qkv_grad = jnp.concatenate(
        [weight_sums[c, :, :own_width] for c in range(n_chip)]
        + [weight_sums[c, :, own_width : own_width + HEAD_DIM] for c in range(n_chip)]
        + [weight_sums[c, :, own_width + HEAD_DIM : part_width] for c in range(n_chip)],
        axis=1,
    )
    out_proj_grad = jnp.concatenate(
        [weight_sums[c, :, part_width:] for c in range(n_chip)], axis=1
    )
    gain_grad = jnp.sum(
        grad_sums[:, weight_rows : weight_rows + norm_gains.shape[1], :weight_rows].astype(
            jnp.float32
        ),
        axis=0,
    ).T
    return (layer_output, input_grad, gain_grad, qkv_grad, out_proj_grad, gate_up_grad, down_grad)


def solution(mesh):
    n_seq = mesh.shape["seq"]
    n_ctx = mesh.shape["ctx"]
    split_mesh = jax.sharding.Mesh(
        mesh.devices.reshape(n_seq, n_ctx // 2, 2), ("seq", "chip", "core")
    )
    plane = ("chip", "core")
    rows = P(("seq", "chip", "core"), None)
    tokens = P("seq", plane, None)
    placed = (
        tokens,
        rows,
        rows,
        rows,
        rows,
        rows,
        tokens,
        P("seq", None),
        P("seq", None),
        P("seq", plane),
    )

    def step(*arrays):
        groups = arrays[0].shape[0]
        if n_ctx // 2 == KV_HEADS and groups == 2 and n_seq == 4:
            return per_device_by_heads(n_seq, *arrays)
        return per_device_general(*arrays)

    return jax.shard_map(
        step,
        mesh=split_mesh,
        in_specs=placed,
        out_specs=(tokens, tokens, rows, rows, rows, rows, rows),
        check_vma=False,
    )
```

```python
from functools import partial
import math

import jax
import jax.numpy as jnp
from jax import lax
from jax.experimental import pallas as pl
from jax.experimental.pallas import tpu as pltpu
from jax.sharding import PartitionSpec as P

HEADS = 8
KV_HEADS = 4
HEAD_DIM = 256


EPSILON = 1e-06
SOFT_CAP = 50.0
MASKED = -1e30


def rms_norm(matrix, gain_col):
    factor = lax.rsqrt(jnp.mean(matrix * matrix, axis=-1, keepdims=True) + EPSILON)
    return matrix * factor * gain_col


def rotary_tables(positions, head_dim):
    half_dim = head_dim // 2
    frequency = jnp.exp(
        jnp.arange(half_dim, dtype=jnp.float32) * (-2.0 * math.log(10000.0) / head_dim)
    )
    phase_angle = positions.astype(jnp.float32)[:, None] * frequency[None, :]
    return (jnp.cos(phase_angle)[:, None, :], jnp.sin(phase_angle)[:, None, :])


def rotate(vectors, cosine, sine_part):
    half_dim = vectors.shape[-1] // 2
    first_half = vectors[..., :half_dim]
    second_half = vectors[..., half_dim:]
    return jnp.concatenate(
        [
            first_half * cosine - second_half * sine_part,
            second_half * cosine + first_half * sine_part,
        ],
        axis=-1,
    )


def rotate_back(grads, cosine, sine_part):
    half_dim = grads.shape[-1] // 2
    first_half = grads[..., :half_dim]
    second_half = grads[..., half_dim:]
    return jnp.concatenate(
        [
            first_half * cosine + second_half * sine_part,
            second_half * cosine - first_half * sine_part,
        ],
        axis=-1,
    )


def soft_probs(scaled, allowed):
    capped = SOFT_CAP * jnp.tanh(scaled / SOFT_CAP)
    capped = jnp.where(allowed, capped, MASKED)
    return jax.nn.softmax(capped, axis=-1)


def geglu_parts(gate_part, up_part):
    return jax.nn.gelu(gate_part, approximate=True) * up_part


def score_block(queries, keys_all):
    groups = keys_all.shape[0]
    seq_len = keys_all.shape[1]
    piece_len = queries.shape[0] // groups
    query_heads = queries.reshape(groups, piece_len, KV_HEADS, HEADS // KV_HEADS, HEAD_DIM)
    key_heads = keys_all.reshape(groups, seq_len, KV_HEADS, HEAD_DIM)
    raw_score = jnp.einsum(
        "spkgd,slkd->skgpl", query_heads, key_heads, preferred_element_type=jnp.float32
    )
    return raw_score * (1.0 / math.sqrt(HEAD_DIM))


def mix_values(weights_low, values_all):
    groups = values_all.shape[0]
    seq_len = values_all.shape[1]
    piece_len = weights_low.shape[3]
    value_heads = values_all.reshape(groups, seq_len, KV_HEADS, HEAD_DIM)
    mixed = jnp.einsum(
        "skgpl,slkd->spkgd", weights_low, value_heads, preferred_element_type=jnp.float32
    )
    return mixed.reshape(groups * piece_len, HEADS * HEAD_DIM).astype(jnp.bfloat16)


def add_slice(left, weight_piece):
    return jnp.dot(left, weight_piece, preferred_element_type=jnp.float32)


def times_rows(left, weight_piece):
    return lax.dot_general(
        left, weight_piece, (((1,), (1,)), ((), ())), preferred_element_type=jnp.float32
    )


def outer_rows(left, right):
    return lax.dot_general(
        left, right, (((0,), (0,)), ((), ())), preferred_element_type=jnp.float32
    )


MESH = pl.DeviceIdType.MESH
ANY = pl.BlockSpec(memory_space=pl.ANY)
DMA = pltpu.SemaphoreType.DMA


def remote(source, target, send_sem, recv_sem, device):
    return pltpu.make_async_remote_copy(
        src_ref=source,
        dst_ref=target,
        send_sem=send_sem,
        recv_sem=recv_sem,
        device_id=device,
        device_id_type=MESH,
    )


def plane_device(index):
    return {"chip": index // 2, "core": lax.rem(index, 2)}


def greet(n_plane, n_seq):
    me = lax.axis_index("chip") * 2 + lax.axis_index("core")
    barrier = pltpu.get_barrier_semaphore()
    for step in range(1, n_plane):
        pl.semaphore_signal(
            barrier,
            inc=1,
            device_id=plane_device(lax.rem(me + step, n_plane)),
            device_id_type=MESH,
        )
    count = n_plane - 1
    if n_seq > 1:
        s = lax.axis_index("seq")

        @pl.when(s > 0)
        def _():
            pl.semaphore_signal(barrier, inc=1, device_id={"seq": s - 1}, device_id_type=MESH)

        @pl.when(s < n_seq - 1)
        def _():
            pl.semaphore_signal(barrier, inc=1, device_id={"seq": s + 1}, device_id_type=MESH)

        count = count + jnp.where(s > 0, 1, 0) + jnp.where(s < n_seq - 1, 1, 0)
    pl.semaphore_wait(barrier, count)


def start_exchange(n_plane, source, target, send_sems, recv_sems, local_sem):
    me = lax.axis_index("chip") * 2 + lax.axis_index("core")
    copies = []
    for step in (4, 2, 6, 3, 5, 1, 7):
        to = lax.rem(me + step, n_plane)
        copy = remote(
            source.at[to],
            target.at[me],
            send_sems.at[step],
            recv_sems.at[step],
            plane_device(to),
        )
        copy.start()
        copies.append(copy)
    own = pltpu.make_async_copy(source.at[me], target.at[me], local_sem.at[0])
    own.start()
    copies.append(own)
    return copies


class Spread:
    def __init__(self, source, target, send_sems, recv_sems, local_sem):
        self.source, self.target = source, target
        self.send_sems, self.recv_sems = send_sems, recv_sems
        self.local_sem = local_sem
        self.q = lax.axis_index("chip")
        self.k = lax.axis_index("core")
        self.half = source.shape[1] // 2

    def chip(self, flip):
        x, y = lax.rem(self.q, 2), self.q // 2
        x = 1 - x if flip in (1, 3) else x
        y = 1 - y if flip in (2, 3) else y
        return y * 2 + x

    def direct(self, flip, twin):
        core = 1 - self.k if twin else self.k
        slot = 2 * flip + twin
        return remote(
            self.source.at[core],
            self.target.at[2 * self.q + self.k],
            self.send_sems.at[slot],
            self.recv_sems.at[slot],
            {"chip": self.chip(flip), "core": core},
        )

    def passed(self, flip, twin):
        core = 1 - self.k if twin else self.k
        slot = 8 + 2 * (flip - 1) + twin
        rows = pl.ds(0 if flip == 1 else self.half, self.half)
        block = self.target.at[2 * self.chip(flip) + core, rows]
        return remote(
            block,
            block,
            self.send_sems.at[slot],
            self.recv_sems.at[slot],
            {"chip": self.chip(3 - flip)},
        )

    def own(self):
        return pltpu.make_async_copy(
            self.source.at[self.k],
            self.target.at[2 * self.q + self.k],
            self.local_sem.at[0],
        )

    def start(self):
        for twin in (0, 1):
            for flip in (1, 2):
                self.direct(flip, twin).start()
        self.direct(0, 1).start()
        self.own().start()

    def pass_on(self):
        for twin in (0, 1):
            for flip in (1, 2):
                self.direct(flip, twin).wait_recv()
                self.passed(flip, twin).start()

    def finish(self):
        for twin in (0, 1):
            for flip in (1, 2):
                self.passed(flip, twin).wait()
                self.direct(flip, twin).wait_send()
        self.direct(0, 1).wait()
        self.own().wait()


SPREAD_SLOTS = 12


def exchange_kernel(n_plane, source, target, send_sems, recv_sems, local_sem):
    greet(n_plane, 1)
    for copy in start_exchange(n_plane, source, target, send_sems, recv_sems, local_sem):
        copy.wait()


def plane_exchange(blocks, collective_id):
    n_plane = 2 * KV_HEADS
    return pl.pallas_call(
        partial(exchange_kernel, n_plane),
        out_shape=jax.ShapeDtypeStruct((n_plane,) + blocks.shape[1:], blocks.dtype),
        in_specs=[ANY],
        out_specs=ANY,
        scratch_shapes=[DMA((n_plane,)), DMA((n_plane,)), DMA((1,))],
        compiler_params=pltpu.CompilerParams(
            collective_id=collective_id, has_side_effects=True
        ),
    )(blocks)


def spread_kernel(
    n_plane,
    blocks,
    low_gate,
    low_up,
    tokens,
    target,
    grads,
    left,
    right,
    tile,
    send_sems,
    recv_sems,
    local_sem,
    load_sem,
    row_sem,
    tile_sem,
):
    greet(n_plane, 1)
    spread = Spread(blocks, target, send_sems, recv_sems, local_sem)
    spread.start()
    n_units, unit_rows, units = low_gate.shape
    width = right.shape[1]
    piece_len = tokens.shape[3]
    loads = []
    for i, source in enumerate((low_gate, low_up)):
        for u in range(n_units):
            place = left.at[i, pl.ds(u * unit_rows, unit_rows)]
            loads.append(pltpu.make_async_copy(source.at[u], place, load_sem.at[i, u]))
    for u in range(n_units):
        for half in range(2):
            place = right.at[pl.ds(u * unit_rows + half * piece_len, piece_len)]
            source = tokens.at[u // 2, u % 2, half]
            loads.append(pltpu.make_async_copy(source, place, row_sem.at[u, half]))
    for load in loads:
        load.start()
    for load in loads:
        load.wait()
    row_tile, col_tile = units // 3, width // 3

    def tile_store(i, r, c, slot):
        rows = pl.ds(pl.multiple_of(r * row_tile, 16), row_tile)
        cols = pl.ds(pl.multiple_of(i * width + c * col_tile, 128), col_tile)
        return pltpu.make_async_copy(tile.at[slot], grads.at[rows, cols], tile_sem.at[slot])

    def one_tile(j, carry):
        i, slot = lax.div(j, 9), lax.rem(j, 2)
        r, c = lax.div(lax.rem(j, 9), 3), lax.rem(j, 3)
        rows = pl.ds(pl.multiple_of(r * row_tile, 128), row_tile)
        cols = pl.ds(pl.multiple_of(c * col_tile, 128), col_tile)
        total = outer_rows(left[i, :, rows], right[:, cols])

        @pl.when(j >= 2)
        def _():
            tile_store(i, r, c, slot).wait()

        tile[slot] = total.astype(tile.dtype)
        tile_store(i, r, c, slot).start()
        return carry

    lax.fori_loop(0, PASS_TURN, one_tile, 0)
    spread.pass_on()
    lax.fori_loop(PASS_TURN, 18, one_tile, 0)
    for slot in range(2):
        tile_store(0, 0, 0, slot).wait()
    spread.finish()


PASS_TURN = 14


def spread_plane(blocks, low_gate, low_up, tokens):
    n_plane = 2 * KV_HEADS
    low = blocks.dtype
    n_units, unit_rows, units = low_gate.shape
    width = blocks.shape[2]
    return pl.pallas_call(
        partial(spread_kernel, n_plane),
        out_shape=[
            jax.ShapeDtypeStruct((n_plane,) + blocks.shape[1:], low),
            jax.ShapeDtypeStruct((units, 2 * width), low),
        ],
        in_specs=[ANY] * 4,
        out_specs=[ANY, ANY],
        scratch_shapes=[
            pltpu.VMEM((2, n_units * unit_rows, units), low),
            pltpu.VMEM((n_units * unit_rows, width), low),
            pltpu.VMEM((2, units // 3, width // 3), low),
            DMA((SPREAD_SLOTS,)),
            DMA((SPREAD_SLOTS,)),
            DMA((1,)),
            DMA((2, n_units)),
            DMA((n_units, 2)),
            DMA((2,)),
        ],
        compiler_params=pltpu.CompilerParams(
            collective_id=3, has_side_effects=True, vmem_limit_bytes=48 * 1024 * 1024
        ),
    )(blocks, low_gate, low_up, tokens)


def gather_kernel(
    n_seq,
    n_plane,
    hidden,
    blocks,
    hidden_all,
    blocks_all,
    hid_send,
    hid_recv,
    hid_local,
    chip_send,
    chip_recv,
    chip_local,
    left_send,
    right_send,
    line_recv,
    twin_send,
    twin_recv,
):
    n_chip = n_plane // 2
    s = lax.axis_index("seq")
    q = lax.axis_index("chip")
    k = lax.axis_index("core")
    greet(n_plane, n_seq)
    swaps = []
    for step in range(1, n_chip):
        to = lax.rem(q + step, n_chip)
        copy = remote(
            blocks.at[to],
            blocks_all.at[s, k, q],
            chip_send.at[step],
            chip_recv.at[step],
            {"chip": to},
        )
        copy.start()
        swaps.append(copy)
    own = pltpu.make_async_copy(blocks.at[q], blocks_all.at[s, k, q], chip_local.at[0])
    own.start()
    spread = Spread(hidden, hidden_all, hid_send, hid_recv, hid_local)
    for copy in swaps:
        copy.wait_recv()
    own.wait()
    spread.start()

    def to_left(d):
        return remote(
            blocks_all.at[d, k], blocks_all.at[d, k], left_send.at[d], line_recv.at[d], {"seq": s - 1}
        )

    def to_right(d):
        return remote(
            blocks_all.at[d, k], blocks_all.at[d, k], right_send.at[d], line_recv.at[d], {"seq": s + 1}
        )

    def to_twin(d):
        return remote(
            blocks_all.at[d, k], blocks_all.at[d, k], twin_send.at[d], twin_recv.at[d], {"core": 1 - k}
        )

    def from_twin(d):
        return remote(
            blocks_all.at[d, 1 - k],
            blocks_all.at[d, 1 - k],
            twin_send.at[d],
            twin_recv.at[d],
            {"core": 1 - k},
        )

    @pl.when(s > 0)
    def _():
        to_left(s).start()

    @pl.when(s < n_seq - 1)
    def _():
        to_right(s).start()

    to_twin(s).start()
    for hop in range(1, n_seq):
        if hop == 2:
            spread.pass_on()
        from_left = s - hop
        from_right = s + hop

        @pl.when(from_left >= 0)
        def _():
            to_left(from_left).wait_recv()

            @pl.when(s < n_seq - 1)
            def _():
                to_right(from_left).start()

            to_twin(from_left).start()

        @pl.when(from_right < n_seq)
        def _():
            to_right(from_right).wait_recv()

            @pl.when(s > 0)
            def _():
                to_left(from_right).start()

            to_twin(from_right).start()

    for d in range(n_seq):

        @pl.when((d >= s) & (s > 0))
        def _():
            to_left(d).wait_send()

        @pl.when((d <= s) & (s < n_seq - 1))
        def _():
            to_right(d).wait_send()

        to_twin(d).wait_send()
        from_twin(d).wait_recv()
    for copy in swaps:
        copy.wait_send()
    spread.finish()


def gather_first(n_seq, hidden, blocks):
    n_plane = 2 * KV_HEADS
    n_chip = KV_HEADS
    return pl.pallas_call(
        partial(gather_kernel, n_seq, n_plane),
        out_shape=[
            jax.ShapeDtypeStruct((n_plane,) + hidden.shape[1:], hidden.dtype),
            jax.ShapeDtypeStruct((n_seq, 2) + blocks.shape, blocks.dtype),
        ],
        in_specs=[ANY, ANY],
        out_specs=[ANY, ANY],
        scratch_shapes=[
            DMA((SPREAD_SLOTS,)),
            DMA((SPREAD_SLOTS,)),
            DMA((1,)),
            DMA((n_chip,)),
            DMA((n_chip,)),
            DMA((1,)),
            DMA((n_seq,)),
            DMA((n_seq,)),
            DMA((n_seq,)),
            DMA((n_seq,)),
            DMA((n_seq,)),
        ],
        compiler_params=pltpu.CompilerParams(collective_id=1, has_side_effects=True),
    )(hidden, blocks)


def last_kernel(
    n_seq,
    n_plane,
    parts,
    blocks,
    parts_all,
    sums,
    held,
    twin,
    line,
    part_send,
    part_recv,
    part_local,
    held_sem,
    twin_send,
    twin_recv,
    line_send,
    line_recv,
    chip_send,
    chip_recv,
    chip_local,
):
    n_chip = n_plane // 2
    s = lax.axis_index("seq")
    q = lax.axis_index("chip")
    k = lax.axis_index("core")
    greet(n_plane, n_seq)

    def load(d):
        return pltpu.make_async_copy(blocks.at[d, k], held.at[d], held_sem.at[d])

    def to_twin(d):
        return remote(
            blocks.at[d, 1 - k], twin.at[d], twin_send.at[d], twin_recv.at[d], {"core": 1 - k}
        )

    def to_left(d):
        return remote(held.at[d], line.at[d], line_send.at[d], line_recv.at[d], {"seq": s - 1})

    def to_right(d):
        return remote(
            held.at[d], line.at[d + 1], line_send.at[d], line_recv.at[d + 1], {"seq": s + 1}
        )

    def gather_terms(d, with_left, with_right):
        load(d).wait()
        to_twin(d).wait_recv()

        @pl.when(with_right)
        def _():
            to_left(d).wait_recv()

        @pl.when(with_left)
        def _():
            to_right(d).wait_recv()

        def body(i, carry):
            held[d, i] = (held[d, i].astype(jnp.float32) + twin[d, i].astype(jnp.float32)).astype(
                held.dtype
            )
            return carry

        def body_right(i, carry):
            total = held[d, i].astype(jnp.float32) + twin[d, i].astype(jnp.float32)
            held[d, i] = (total + line[d, i].astype(jnp.float32)).astype(held.dtype)
            return carry

        def body_left(i, carry):
            total = held[d, i].astype(jnp.float32) + twin[d, i].astype(jnp.float32)
            held[d, i] = (total + line[d + 1, i].astype(jnp.float32)).astype(held.dtype)
            return carry

        def body_both(i, carry):
            total = held[d, i].astype(jnp.float32) + twin[d, i].astype(jnp.float32)
            total = total + line[d, i].astype(jnp.float32)
            held[d, i] = (total + line[d + 1, i].astype(jnp.float32)).astype(held.dtype)
            return carry

        @pl.when(jnp.logical_not(with_left) & jnp.logical_not(with_right))
        def _():
            lax.fori_loop(0, n_chip, body, 0)

        @pl.when(jnp.logical_not(with_left) & with_right)
        def _():
            lax.fori_loop(0, n_chip, body_right, 0)

        @pl.when(with_left & jnp.logical_not(with_right))
        def _():
            lax.fori_loop(0, n_chip, body_left, 0)

        @pl.when(with_left & with_right)
        def _():
            lax.fori_loop(0, n_chip, body_both, 0)

    for d in range(n_seq):
        to_twin(d).start()
        load(d).start()
    part_copies = start_exchange(n_plane, parts, parts_all, part_send, part_recv, part_local)
    never = s < 0
    for hop in range(1, n_seq):
        left = hop - n_seq + s
        right = n_seq - hop + s

        @pl.when(left >= 0)
        def _():
            gather_terms(left, never, s < n_seq - 1)
            to_left(left).start()

        @pl.when(right <= n_seq - 1)
        def _():
            gather_terms(right, s > 0, never)
            to_right(right).start()

    gather_terms(s, s > 0, s < n_seq - 1)
    swaps = []
    for step in range(1, n_chip):
        to = lax.rem(q + step, n_chip)
        copy = remote(
            held.at[s, to], sums.at[q], chip_send.at[step], chip_recv.at[step], {"chip": to}
        )
        copy.start()
        swaps.append(copy)
    own = pltpu.make_async_copy(held.at[s, q], sums.at[q], chip_local.at[0])
    own.start()
    for d in range(n_seq):
        to_twin(d).wait_send()

        @pl.when(d < s)
        def _():
            to_left(d).wait_send()

        @pl.when(d > s)
        def _():
            to_right(d).wait_send()

    for copy in part_copies:
        copy.wait()
    for copy in swaps:
        copy.wait()
    own.wait()


def sum_last(n_seq, parts, blocks):
    n_plane = 2 * KV_HEADS
    n_chip = KV_HEADS
    block = blocks.shape[2:]
    return pl.pallas_call(
        partial(last_kernel, n_seq, n_plane),
        out_shape=[
            jax.ShapeDtypeStruct(parts.shape, parts.dtype),
            jax.ShapeDtypeStruct(block, blocks.dtype),
        ],
        in_specs=[ANY, ANY],
        out_specs=[ANY, ANY],
        scratch_shapes=[
            pltpu.VMEM((n_seq,) + block, blocks.dtype),
            pltpu.VMEM((n_seq,) + block, blocks.dtype),
            pltpu.VMEM((n_seq + 1,) + block, blocks.dtype),
            DMA((n_plane,)),
            DMA((n_plane,)),
            DMA((1,)),
            DMA((n_seq,)),
            DMA((n_seq,)),
            DMA((n_seq,)),
            DMA((n_seq,)),
            DMA((n_seq + 1,)),
            DMA((n_chip,)),
            DMA((n_chip,)),
            DMA((1,)),
        ],
        compiler_params=pltpu.CompilerParams(
            collective_id=4, has_side_effects=True, vmem_limit_bytes=32 * 1024 * 1024
        ),
    )(parts, blocks)


QUERY_BLOCK = 256


def block_probs(query, keys, segment_col, segment_row, first):
    rows, width = query.shape[0], keys.shape[0]
    scaled = times_rows(query, keys) * (1.0 / math.sqrt(HEAD_DIM))
    bent = jnp.tanh(scaled / SOFT_CAP)
    row = first + lax.broadcasted_iota(jnp.int32, (rows, width), 0)
    col = lax.broadcasted_iota(jnp.int32, (rows, width), 1)
    allowed = ((segment_col == segment_row) & (col <= row)) | (col == row)
    capped = jnp.where(allowed, SOFT_CAP * bent, MASKED)
    raised = jnp.exp(capped - jnp.max(capped, axis=-1, keepdims=True))
    return raised / jnp.sum(raised, axis=-1, keepdims=True), bent


def attend_kernel(group_size, queries, keys, values, segment_col, segment_row, out):
    seq_len = keys.shape[0]
    for first in range(0, seq_len, QUERY_BLOCK):
        rows = slice(first, first + QUERY_BLOCK)
        width = first + QUERY_BLOCK
        for head in range(group_size):
            cols = slice(head * HEAD_DIM, (head + 1) * HEAD_DIM)
            probs, unused = block_probs(
                queries[rows, cols],
                keys[:width],
                segment_col[rows, :],
                segment_row[:, :width],
                first,
            )
            out[rows, cols] = add_slice(probs.astype(jnp.bfloat16), values[:width]).astype(
                out.dtype
            )


def attend(queries, keys, values, segment_col, segment_row):
    return pl.pallas_call(
        partial(attend_kernel, queries.shape[1] // HEAD_DIM),
        out_shape=jax.ShapeDtypeStruct(queries.shape, jnp.bfloat16),
        compiler_params=pltpu.CompilerParams(vmem_limit_bytes=40 * 1024 * 1024),
    )(queries, keys, values, segment_col, segment_row)


def attend_back_kernel(
    group_size,
    queries,
    keys,
    values,
    segment_col,
    segment_row,
    grads,
    grad_queries,
    grad_keys,
    grad_values,
):
    seq_len = keys.shape[0]
    inverse_root = 1.0 / math.sqrt(HEAD_DIM)
    grad_keys[...] = jnp.zeros_like(grad_keys)
    grad_values[...] = jnp.zeros_like(grad_values)
    for first in range(0, seq_len, QUERY_BLOCK):
        rows = slice(first, first + QUERY_BLOCK)
        width = first + QUERY_BLOCK
        for head in range(group_size):
            cols = slice(head * HEAD_DIM, (head + 1) * HEAD_DIM)
            query = queries[rows, cols]
            probs, bent = block_probs(
                query, keys[:width], segment_col[rows, :], segment_row[:, :width], first
            )
            grad = grads[rows, cols]
            grad_probs = times_rows(grad, values[:width])
            mean = jnp.sum(probs * grad_probs, axis=-1, keepdims=True)
            grad_scaled = (probs * (grad_probs - mean) * (1.0 - bent * bent)).astype(jnp.bfloat16)
            grad_queries[rows, cols] = add_slice(grad_scaled, keys[:width]) * inverse_root
            grad_keys[:width, :] += outer_rows(grad_scaled, query) * inverse_root
            grad_values[:width, :] += outer_rows(probs.astype(jnp.bfloat16), grad)


def attend_back(queries, keys, values, segment_col, segment_row, grads):
    return pl.pallas_call(
        partial(attend_back_kernel, queries.shape[1] // HEAD_DIM),
        out_shape=[
            jax.ShapeDtypeStruct(queries.shape, jnp.float32),
            jax.ShapeDtypeStruct(keys.shape, jnp.float32),
            jax.ShapeDtypeStruct(values.shape, jnp.float32),
        ],
        compiler_params=pltpu.CompilerParams(vmem_limit_bytes=40 * 1024 * 1024),
    )(queries, keys, values, segment_col, segment_row, grads)


def chip_beside(c, flip):
    return c ^ flip


def chip_places(rows):
    q = lax.axis_index("chip")
    x, y = lax.rem(q, 2), lax.div(q, 2)
    across = (2 * (1 - y) + 1 - x) * rows
    return (q * rows, (2 * y + 1 - x) * rows, (2 * (1 - y) + x) * rows, across, across + rows // 2)


def send_beside(part, flip):
    return lax.ppermute(part, "chip", [(c, chip_beside(c, flip)) for c in range(KV_HEADS)])


def unit_orders(n):
    units, sums = [], []
    for s in range(n):
        keyed = []
        for d in range(n):
            if d != s:
                near = abs(s - d)
                behind, past = (s, d) if d < s else (n - 1 - s, n - 1 - d)
                keyed += [(near, d, 0), (behind + past + 1, d, 1)]
        order = [(s, 0), (s, 1)] + [(d, h) for unused, d, h in sorted(keyed)]
        units.append([2 * d + h for d, h in order])
        if s in (0, n - 1):
            sums.append(units[-1][2:])
            continue
        keyed = []
        for d in range(n):
            if d != s:
                hops, place = (n - 2 - s, d) if d < s else (s - 1, n - 1 - d)
                keyed += [(n - 2 - place + hops, d, 0), (n - 1 + place + hops, d, 1)]
        sums.append([2 * d + h for unused, d, h in sorted(keyed)])
    return units, sums


def pick(table, s, i):
    width = len(table[0])
    place = s * width + i
    value = 0
    for k, entry in enumerate(entry for row in table for entry in row):
        value = jnp.where(place == k, entry, value)
    return value


SUBS = 1
SUM_TURNS = (0, 1, 4, 5, 8, 8)
GELU_SCALE = math.sqrt(2.0 / math.pi)


def gelu_pieces(gate):
    bend = jnp.tanh(GELU_SCALE * (gate + 0.044715 * gate * gate * gate))
    value = 0.5 * gate * (1.0 + bend)
    slope = 0.5 * (1.0 + bend) + 0.5 * gate * (1.0 - bend * bend) * GELU_SCALE * (
        1.0 + 3.0 * 0.044715 * gate * gate
    )
    return value, slope


def units_kernel(n_seq, backward, *refs):
    if backward:
        tokens, units = refs[:2]
        downs = refs[2:7]
        kept_gate, kept_up, kept_hidden = refs[7:10]
        out, first_out, second_out, down_grads = refs[10:14]
        stage_outs = (first_out, second_out)
        scratch = refs[14:]
    else:
        tokens, units = refs[:2]
        downs = refs[2:7]
        out, tokens_all, first_out, second_out, third_out = refs[7:12]
        stage_outs = (first_out, second_out, third_out)
        scratch = refs[12:]
    units_v, downs_v, held, own_sum, twin_sum, twin_out, line, stage = scratch[:8]
    scratch = scratch[8:]
    if backward:
        kept, kept_sem, tile, tile_sem, load_sem = scratch[:5]
        scratch = scratch[5:]
    (
        weight_sem,
        own_sem,
        left_send,
        right_send,
        token_recv,
        twin_send,
        twin_recv,
        part_send,
        part_recv,
        line_send,
        line_recv,
        stage_sem,
        all_sem,
        out_sem,
    ) = scratch
    n = n_seq
    s = lax.axis_index("seq")
    k = lax.axis_index("core")
    twin = {"core": 1 - k}
    n_units, width = downs_v.shape
    piece_len = tokens.shape[1]
    at_end = (s == 0) | (s == n - 1)

    def token_left(d, h, source):
        return remote(
            source, held.at[d, h, 0], left_send.at[d, h], token_recv.at[d, h], {"seq": s - 1}
        )

    def token_right(d, h, source):
        return remote(
            source, held.at[d, h, 0], right_send.at[d, h], token_recv.at[d, h], {"seq": s + 1}
        )

    def token_twin(d, h, source):
        return remote(source, held.at[d, h, 1], twin_send.at[d, h], twin_recv.at[d, h], twin)

    def part_twin(d, h):
        return remote(
            twin_out.at[d, h], twin_sum.at[d, h], part_send.at[d, h], part_recv.at[d, h], twin
        )

    sub_len = piece_len // SUBS

    def part_line(d, h, sub):
        to_left = d < s
        slot = jnp.where(to_left, d, d + 1)
        rows = pl.ds(sub * sub_len, sub_len)
        return remote(
            twin_sum.at[d, h, rows],
            line.at[slot, h, rows],
            line_send.at[d, h, sub],
            line_recv.at[slot, h, sub],
            {"seq": jnp.where(to_left, s - 1, s + 1)},
        )

    def line_arrival(slot, h, sub):
        rows = pl.ds(sub * sub_len, sub_len)
        return remote(
            twin_sum.at[0, h, rows],
            line.at[slot, h, rows],
            line_send.at[0, h, sub],
            line_recv.at[slot, h, sub],
            {"seq": s},
        )

    def own_load(h):
        return pltpu.make_async_copy(tokens.at[h], held.at[s, h, 0], own_sem.at[h])

    def all_store(d, h):
        return pltpu.make_async_copy(held.at[d, h], tokens_all.at[d, h], all_sem.at[d, h])

    def stage_store(i, d, h, slot):
        return pltpu.make_async_copy(
            stage.at[i, slot], stage_outs[i].at[2 * d + h], stage_sem.at[i, slot]
        )

    def kept_load(i, d, h, slot):
        source = (kept_gate, kept_up)[i]
        return pltpu.make_async_copy(source.at[2 * d + h], kept.at[i, slot], kept_sem.at[i, slot])

    unit_table, sum_table = unit_orders(n)
    right_table = [
        [2 if d == 0 else unit_table[d].index(2 * (d - 1) + 1) + 1 for d in range(n)]
    ]
    left_table = [
        [2 if d == n - 1 else unit_table[d].index(2 * (d + 1) + 1) + 1 for d in range(n)]
    ]

    def source(t):
        unit = pick(unit_table, s, t)
        return lax.div(unit, 2), lax.rem(unit, 2)

    barrier = pltpu.get_barrier_semaphore()
    pl.semaphore_signal(barrier, inc=1, device_id=twin, device_id_type=MESH)

    @pl.when(s > 0)
    def _():
        pl.semaphore_signal(barrier, inc=1, device_id={"seq": s - 1}, device_id_type=MESH)

    @pl.when(s < n - 1)
    def _():
        pl.semaphore_signal(barrier, inc=1, device_id={"seq": s + 1}, device_id_type=MESH)

    pl.semaphore_wait(barrier, 1 + jnp.where(s > 0, 1, 0) + jnp.where(s < n - 1, 1, 0))

    def second_half(t):
        @pl.when((s < n - 1) & (t == pick(right_table, 0, s)))
        def _():
            d, h = jnp.maximum(s - 1, 0), jnp.where(s > 0, 1, 0)
            token_right(d, h, held.at[d, h, 0]).wait_send()
            token_right(s, 1, tokens.at[1]).start()

        @pl.when((s > 0) & (t == pick(left_table, 0, s)))
        def _():
            d, h = jnp.minimum(s + 1, n - 1), jnp.where(s < n - 1, 1, 0)
            token_left(d, h, held.at[d, h, 0]).wait_send()
            token_left(s, 1, tokens.at[1]).start()

    @pl.when(s < n - 1)
    def _():
        token_right(s, 0, tokens.at[0]).start()

    @pl.when(s > 0)
    def _():
        token_left(s, 0, tokens.at[0]).start()

    for h in range(2):
        token_twin(s, h, tokens.at[h]).start()
        own_load(h).start()
    load_units = pltpu.make_async_copy(units, units_v, weight_sem.at[0])
    load_downs = []
    for i, (first, part) in enumerate(zip(chip_places(downs[0].shape[0]), downs)):
        rows = pl.ds(pl.multiple_of(first, 16), part.shape[0])
        load_downs.append(pltpu.make_async_copy(part, downs_v.at[rows], weight_sem.at[1 + i]))
    load_units.start()
    for load in load_downs:
        load.start()
    if backward:
        for i in range(2):
            kept_load(i, s, 0, 0).start()
    load_units.wait()
    for load in load_downs:
        load.wait()

    def add_rows(d, h, sub, into_own, use_line):
        step = 16

        def body(i, carry):
            rows = pl.ds(pl.multiple_of(sub * sub_len + i * step, step), step)
            total = own_sum[d, h, rows, :] + twin_sum[d, h, rows, :].astype(jnp.float32)
            for slot in use_line:
                total = total + line[slot, h, rows, :].astype(jnp.float32)
            if into_own:
                own_sum[d, h, rows, :] = total
            else:
                twin_sum[d, h, rows, :] = total.astype(twin_sum.dtype)
            return carry

        lax.fori_loop(0, sub_len // step, body, 0)

    def combine(d, h):
        to_left = d < s
        slot = jnp.where(to_left, d, d + 1)
        more = jnp.where(to_left, s < n - 1, s > 0)
        part_twin(d, h).wait_recv()

        @pl.when(more)
        def _():
            for sub in range(SUBS):
                line_arrival(slot, h, sub).wait_recv()
                add_rows(d, h, sub, False, (slot,))
                part_line(d, h, sub).start()

        @pl.when(jnp.logical_not(more))
        def _():
            for sub in range(SUBS):
                add_rows(d, h, sub, False, ())
                part_line(d, h, sub).start()

    columns = width // 3
    chunk = n_units // 3

    def compute_forward(d, h, slot):
        rows = held[d, h].reshape(2 * piece_len, width)
        for c in range(3):
            cols = slice(c * chunk, (c + 1) * chunk)
            gate = times_rows(rows, units_v[cols, :width])
            up = times_rows(rows, units_v[cols, width:])
            value, unused = gelu_pieces(gate)
            stage[0, slot, :, cols] = gate.astype(stage.dtype)
            stage[1, slot, :, cols] = up.astype(stage.dtype)
            stage[2, slot, :, cols] = (value * up).astype(stage.dtype)
        for c in range(3):
            cols = slice(c * columns, (c + 1) * columns)
            part = add_slice(stage[2, slot], downs_v[:, cols])
            own_sum[d, h, :, cols] = part[:piece_len]
            twin_out[d, h, :, cols] = part[piece_len:].astype(twin_out.dtype)

    def compute_backward(d, h, slot):
        rows = held[d, h].reshape(2 * piece_len, width)
        for c in range(3):
            cols = slice(c * chunk, (c + 1) * chunk)
            grad = times_rows(rows, downs_v[cols, :])
            value, slope = gelu_pieces(kept[0, slot, :, cols].astype(jnp.float32))
            up = kept[1, slot, :, cols].astype(jnp.float32)
            stage[0, slot, :, cols] = (grad * up * slope).astype(stage.dtype)
            stage[1, slot, :, cols] = (grad * value).astype(stage.dtype)
        for c in range(3):
            cols = slice(c * columns, (c + 1) * columns)
            later = slice(width + c * columns, width + (c + 1) * columns)
            part = add_slice(stage[0, slot], units_v[:, cols])
            part = part + add_slice(stage[1, slot], units_v[:, later])
            own_sum[d, h, :, cols] = part[:piece_len]
            twin_out[d, h, :, cols] = part[piece_len:].astype(twin_out.dtype)

    row_tile, col_tile = n_units // 3, width // 3

    def down_gradient(between):
        unit_rows = 2 * piece_len
        group_rows = n * unit_rows

        def left_load(u):
            place = downs_v.at[
                pl.ds((u % n) * unit_rows, unit_rows), pl.ds((u // n) * n_units, n_units)
            ]
            return pltpu.make_async_copy(kept_hidden.at[u], place, load_sem.at[u])

        def left_rows(g, first):
            return downs_v[
                :group_rows, pl.ds(pl.multiple_of(g * n_units + first, 128), row_tile)
            ]

        def right_rows(g, first):
            cols = pl.ds(pl.multiple_of(first, 128), col_tile)
            part = held[g * n // 2 : (g + 1) * n // 2, :, :, :, cols]
            return part.reshape(group_rows, col_tile)

        def tile_store(r, c, slot):
            rows = pl.ds(pl.multiple_of(r * row_tile, 16), row_tile)
            cols = pl.ds(pl.multiple_of(c * col_tile, 128), col_tile)
            return pltpu.make_async_copy(tile.at[slot], down_grads.at[rows, cols], tile_sem.at[slot])

        for u in range(2 * n):
            left_load(u).start()
        for u in range(2 * n):
            left_load(u).wait()

        def one_tile(j, carry):
            slot = lax.rem(j, 2)
            r, c = lax.div(j, 3), lax.rem(j, 3)
            total = sum(
                outer_rows(left_rows(g, r * row_tile), right_rows(g, c * col_tile))
                for g in range(2)
            )

            @pl.when(j >= 2)
            def _():
                tile_store(r, c, slot).wait()

            tile[slot] = total.astype(tile.dtype)
            tile_store(r, c, slot).start()
            for step, turn in enumerate(SUM_TURNS):

                @pl.when(j == turn)
                def _():
                    between(step)

            return carry

        lax.fori_loop(0, 9, one_tile, 0)
        for slot in range(2):
            tile_store(0, 0, slot).wait()

    def unit(t, carry):
        d, h = source(t)
        slot = lax.rem(t, 2)

        @pl.when(at_end & (t >= 3))
        def _():
            combine(*source(t - 1))

        @pl.when(t < 2)
        def _():
            own_load(h).wait()

        @pl.when(t >= 2)
        def _():
            piece = held.at[d, h, 0]
            token_left(d, h, piece).wait_recv()

            @pl.when((d < s) & (s < n - 1))
            def _():
                token_right(d, h, piece).start()

            @pl.when((d > s) & (s > 0))
            def _():
                token_left(d, h, piece).start()

            token_twin(d, h, piece).start()
            for i in range(len(stage_outs)):
                stage_store(i, d, h, slot).wait()

        second_half(t)
        if backward:

            @pl.when(t < 2 * n - 1)
            def _():
                for i in range(2):
                    kept_load(i, *source(t + 1), 1 - slot).start()

            for i in range(2):
                kept_load(i, d, h, slot).wait()
        token_twin(d, h, held.at[d, h, 0]).wait_recv()
        if backward:
            compute_backward(d, h, slot)
        else:
            compute_forward(d, h, slot)
        part_twin(d, h).start()
        if not backward:
            all_store(d, h).start()
        for i in range(len(stage_outs)):
            stage_store(i, d, h, slot).start()

        return carry

    lax.fori_loop(0, 2 * n, unit, 0)

    second_half(2 * n)

    @pl.when(at_end)
    def _():
        combine(*source(2 * n - 1))

    n_sums = 2 * (n - 1)

    def middle(i):
        @pl.when(jnp.logical_not(at_end) & (i < n_sums))
        def _():
            unit = pick(sum_table, s, i)
            combine(lax.div(unit, 2), lax.rem(unit, 2))

    if backward:
        down_gradient(middle)
    else:

        def one(i, carry):
            middle(i)
            return carry

        lax.fori_loop(0, n_sums, one, 0)

    def finish(h, carry):
        part_twin(s, h).wait_recv()
        for sub in range(SUBS):

            @pl.when(s < n - 1)
            def _():
                line_arrival(s, h, sub).wait_recv()

            @pl.when(s > 0)
            def _():
                line_arrival(s + 1, h, sub).wait_recv()

            @pl.when(s == 0)
            def _():
                add_rows(s, h, sub, True, (s,))

            @pl.when(s == n - 1)
            def _():
                add_rows(s, h, sub, True, (s + 1,))

            @pl.when(jnp.logical_not(at_end))
            def _():
                add_rows(s, h, sub, True, (s, s + 1))

        pltpu.make_async_copy(own_sum.at[s, h], out.at[h], out_sem.at[h]).start()
        return carry

    lax.fori_loop(0, 2, finish, 0)

    def drain(t, carry):
        d = lax.div(t, 2)
        h = lax.rem(t, 2)
        piece = held.at[d, h, 0]

        right_seen = (d == jnp.maximum(s - 1, 0)) & (h == jnp.where(s > 0, 1, 0))
        left_seen = (d == jnp.minimum(s + 1, n - 1)) & (h == jnp.where(s < n - 1, 1, 0))

        @pl.when((d <= s) & (s < n - 1) & jnp.logical_not(right_seen))
        def _():
            token_right(d, h, piece).wait_send()

        @pl.when((d >= s) & (s > 0) & jnp.logical_not(left_seen))
        def _():
            token_left(d, h, piece).wait_send()

        token_twin(d, h, piece).wait_send()
        part_twin(d, h).wait_send()

        @pl.when(d != s)
        def _():
            for sub in range(SUBS):
                part_line(d, h, sub).wait_send()

        if not backward:
            all_store(d, h).wait()
        return carry

    lax.fori_loop(0, 2 * n, drain, 0)
    for h in range(2):
        for i in range(len(stage_outs)):
            stage_store(i, 0, h, h).wait()
        pltpu.make_async_copy(own_sum.at[s, h], out.at[h], out_sem.at[h]).wait()


def run_units(n_seq, tokens, units, downs, kept=None):
    backward = kept is not None
    low = tokens.dtype
    n_units = units.shape[0]
    halves, piece_len, width = tokens.shape
    n_stage = 2 if backward else 3
    held = (n_seq, halves, 2, piece_len, width)
    unit_rows = (2 * n_seq, 2 * piece_len, n_units)
    sums = (n_seq, halves, piece_len, width)
    scratch = [
        pltpu.VMEM(units.shape, low),
        pltpu.VMEM((n_units, width), low),
        pltpu.VMEM(held, low),
        pltpu.VMEM(sums, jnp.float32),
        pltpu.VMEM(sums, low),
        pltpu.VMEM(sums, low),
        pltpu.VMEM((n_seq + 1,) + sums[1:], low),
        pltpu.VMEM((n_stage, 2) + unit_rows[1:], low),
    ]
    outs = [jax.ShapeDtypeStruct(tokens.shape, jnp.float32)]
    if backward:
        scratch += [
            pltpu.VMEM((2, 2) + unit_rows[1:], low),
            DMA((2, 2)),
            pltpu.VMEM((2, n_units // 3, width // 3), low),
            DMA((2,)),
            DMA((2 * n_seq,)),
        ]
    else:
        outs += [jax.ShapeDtypeStruct(held, low)]
    outs += [jax.ShapeDtypeStruct(unit_rows, low)] * n_stage
    if backward:
        outs += [jax.ShapeDtypeStruct((n_units, width), low)]
    pairs = DMA((n_seq, halves))
    scratch += [DMA((1 + len(downs),)), DMA((halves,))] + [pairs] * 7
    scratch += [DMA((n_seq, halves, SUBS)), DMA((n_seq + 1, halves, SUBS))]
    scratch += [DMA((n_stage, 2)), pairs, DMA((halves,))]
    operands = (tokens, units) + tuple(downs) + (tuple(kept) if backward else ())
    return pl.pallas_call(
        partial(units_kernel, n_seq, backward),
        out_shape=outs,
        in_specs=[ANY] * len(operands),
        out_specs=[ANY] * len(outs),
        scratch_shapes=scratch,
        compiler_params=pltpu.CompilerParams(
            collective_id=6 if backward else 5,
            has_side_effects=True,
            vmem_limit_bytes=63 * 1024 * 1024,
        ),
    )(*operands)


def per_device_general(
    hidden_in,
    norm_gains,
    qkv_weight,
    out_weight,
    gate_up_weight,
    down_weight,
    output_cotangent,
    segment_ids,
    padding,
    positions,
):
    everyone = ("seq", "chip", "core")
    plane = ("chip", "core")
    column = ("seq", "core")
    groups = hidden_in.shape[0]
    piece_len = hidden_in.shape[1]
    model_width = hidden_in.shape[2]
    row_count = groups * piece_len
    seq_len = segment_ids.shape[1]
    group_size = HEADS // KV_HEADS
    query_width = HEADS * HEAD_DIM
    key_width = KV_HEADS * HEAD_DIM
    proj_width = qkv_weight.shape[1]

    residual = hidden_in.reshape(row_count, model_width).astype(jnp.float32)
    factor = lax.rsqrt(jnp.mean(residual * residual, axis=-1, keepdims=True) + EPSILON)
    gain_cols = lax.all_gather(norm_gains, everyone, axis=0, tiled=True).astype(jnp.float32)
    qkv_full = lax.all_gather(qkv_weight, everyone, axis=0, tiled=True)
    attn_input = (residual * factor * gain_cols[:, 0]).astype(jnp.bfloat16)
    projected = add_slice(attn_input, qkv_full)
    cosine, sine_part = rotary_tables(positions.reshape(row_count), HEAD_DIM)
    queries = (
        rotate(projected[:, :query_width].reshape(row_count, HEADS, HEAD_DIM), cosine, sine_part)
        .astype(jnp.bfloat16)
        .reshape(row_count, query_width)
    )
    keys_here = (
        rotate(
            projected[:, query_width : query_width + key_width].reshape(
                row_count, KV_HEADS, HEAD_DIM
            ),
            cosine,
            sine_part,
        )
        .astype(jnp.bfloat16)
        .reshape(groups, piece_len, key_width)
    )
    values_here = (
        projected[:, query_width + key_width :]
        .astype(jnp.bfloat16)
        .reshape(groups, piece_len, key_width)
    )
    both_all = lax.all_gather(
        jnp.concatenate([keys_here, values_here], axis=2), plane, axis=1, tiled=True
    )
    keys_all = both_all[:, :, :key_width]
    values_all = both_all[:, :, key_width:]
    first_query = (lax.axis_index("chip") * 2 + lax.axis_index("core")) * piece_len
    query_rows = first_query + jnp.arange(piece_len, dtype=jnp.int32)
    key_rows = jnp.arange(seq_len, dtype=jnp.int32)
    segment_query = lax.dynamic_slice_in_dim(segment_ids, first_query, piece_len, 1)
    allowed = (segment_query[:, :, None] == segment_ids[:, None, :]) & (
        key_rows[None, None, :] <= query_rows[None, :, None]
    ) & (padding[:, None, :] == 1) | (key_rows[None, None, :] == query_rows[None, :, None])
    allowed = allowed[:, None, None]
    probs = soft_probs(score_block(queries, keys_all), allowed)
    attn_out = mix_values(probs.astype(jnp.bfloat16), values_all)
    out_full = lax.all_gather(out_weight, everyone, axis=0, tiled=True)
    attn_proj = times_rows(attn_out, out_full)
    after_attn = residual + rms_norm(attn_proj, gain_cols[:, 1])
    ffn_input = rms_norm(after_attn, gain_cols[:, 2]).astype(jnp.bfloat16)

    unit_weights = lax.all_gather(gate_up_weight, "chip", axis=0, tiled=True)
    down_units = lax.all_gather(down_weight, "chip", axis=0, tiled=True)
    ffn_all = lax.all_gather(ffn_input, column, axis=0, tiled=True)
    gate_part = times_rows(ffn_all, unit_weights[:, :model_width])
    up_part = times_rows(ffn_all, unit_weights[:, model_width:])
    hidden_part = geglu_parts(gate_part, up_part).astype(jnp.bfloat16)
    down_part = add_slice(hidden_part, down_units).astype(jnp.bfloat16)
    down_out = lax.psum_scatter(down_part, column, scatter_dimension=0, tiled=True).astype(
        jnp.float32
    )
    layer_out = after_attn + rms_norm(down_out, gain_cols[:, 3])
    layer_output = layer_out.astype(jnp.bfloat16).reshape(groups, piece_len, model_width)

    cotangent = output_cotangent.reshape(row_count, model_width).astype(jnp.float32)
    unused_last, pull_last = jax.vjp(rms_norm, down_out, gain_cols[:, 3])
    grad_down, grad_gain_last = pull_last(cotangent)
    grad_down_low = grad_down.astype(jnp.bfloat16)
    grad_down_all = lax.all_gather(grad_down_low, column, axis=0, tiled=True)
    grad_part = times_rows(grad_down_all, down_units)
    unused_units, pull_units = jax.vjp(geglu_parts, gate_part, up_part)
    grad_gate_part, grad_up_part = pull_units(grad_part)
    gate_low = grad_gate_part.astype(jnp.bfloat16)
    up_low = grad_up_part.astype(jnp.bfloat16)
    grad_ffn_part = add_slice(gate_low, unit_weights[:, :model_width]) + add_slice(
        up_low, unit_weights[:, model_width:]
    )
    grad_ffn_in = lax.psum_scatter(
        grad_ffn_part.astype(jnp.bfloat16), column, scatter_dimension=0, tiled=True
    ).astype(jnp.float32)
    gate_up_rows = jnp.concatenate(
        [
            outer_rows(gate_low, ffn_all).astype(jnp.bfloat16),
            outer_rows(up_low, ffn_all).astype(jnp.bfloat16),
        ],
        axis=1,
    )
    down_rows = outer_rows(hidden_part, grad_down_all).astype(jnp.bfloat16)
    gate_up_grad = lax.psum_scatter(
        gate_up_rows, "chip", scatter_dimension=0, tiled=True
    ).astype(jnp.float32)
    down_grad = lax.psum_scatter(down_rows, "chip", scatter_dimension=0, tiled=True).astype(
        jnp.float32
    )

    unused_mid, pull_mid = jax.vjp(rms_norm, after_attn, gain_cols[:, 2])
    grad_after_ffn, grad_gain_mid = pull_mid(grad_ffn_in)
    grad_after = cotangent + grad_after_ffn
    unused_post, pull_post = jax.vjp(rms_norm, attn_proj, gain_cols[:, 1])
    grad_proj, grad_gain_post = pull_post(grad_after)
    grad_proj_low = grad_proj.astype(jnp.bfloat16)
    grad_attn = add_slice(grad_proj_low, out_full).astype(jnp.bfloat16)
    scaled = score_block(queries, keys_all)
    probs, pull_probs = jax.vjp(partial(soft_probs, allowed=allowed), scaled)
    grad_heads = grad_attn.reshape(groups, piece_len, KV_HEADS, group_size, HEAD_DIM)
    query_heads = queries.reshape(groups, piece_len, KV_HEADS, group_size, HEAD_DIM)
    key_heads = keys_all.reshape(groups, seq_len, KV_HEADS, HEAD_DIM)
    value_heads = values_all.reshape(groups, seq_len, KV_HEADS, HEAD_DIM)
    grad_probs = jnp.einsum(
        "spkgd,slkd->skgpl", grad_heads, value_heads, preferred_element_type=jnp.float32
    )
    (grad_scaled,) = pull_probs(grad_probs)
    grad_scaled_low = grad_scaled.astype(jnp.bfloat16)
    inverse_root = 1.0 / math.sqrt(HEAD_DIM)
    grad_query_rot = (
        jnp.einsum(
            "skgpl,slkd->spkgd", grad_scaled_low, key_heads, preferred_element_type=jnp.float32
        )
        * inverse_root
    )
    grad_key_rot = (
        jnp.einsum(
            "skgpl,spkgd->slkd", grad_scaled_low, query_heads, preferred_element_type=jnp.float32
        )
        * inverse_root
    )
    grad_value_part = jnp.einsum(
        "skgpl,spkgd->slkd",
        probs.astype(jnp.bfloat16),
        grad_heads,
        preferred_element_type=jnp.float32,
    )
    both_grads = jnp.concatenate(
        [
            grad_key_rot.reshape(groups, seq_len, key_width),
            grad_value_part.reshape(groups, seq_len, key_width),
        ],
        axis=2,
    ).astype(jnp.bfloat16)
    both_summed = lax.psum_scatter(both_grads, plane, scatter_dimension=1, tiled=True)
    both_summed = both_summed.astype(jnp.float32).reshape(row_count, 2 * key_width)
    key_summed = both_summed[:, :key_width]
    value_summed = both_summed[:, key_width:]
    grad_queries = rotate_back(
        grad_query_rot.reshape(row_count, HEADS, HEAD_DIM), cosine, sine_part
    ).reshape(row_count, query_width)
    grad_keys = rotate_back(
        key_summed.reshape(row_count, KV_HEADS, HEAD_DIM), cosine, sine_part
    ).reshape(row_count, key_width)
    grad_projected = jnp.concatenate([grad_queries, grad_keys, value_summed], axis=1).astype(
        jnp.bfloat16
    )
    grad_attn_in = times_rows(grad_projected, qkv_full)
    unused_first, pull_first = jax.vjp(rms_norm, residual, gain_cols[:, 0])
    grad_res_first, grad_gain_first = pull_first(grad_attn_in)
    input_grad = (grad_after + grad_res_first).reshape(groups, piece_len, model_width)
    gain_terms = jnp.stack([grad_gain_first, grad_gain_post, grad_gain_mid, grad_gain_last], axis=1)
    qkv_part = outer_rows(attn_input, grad_projected).astype(jnp.bfloat16)
    out_part = outer_rows(grad_proj_low, attn_out).astype(jnp.bfloat16)
    qkv_grad = lax.psum_scatter(qkv_part, everyone, scatter_dimension=0, tiled=True).astype(
        jnp.float32
    )
    out_proj_grad = lax.psum_scatter(out_part, everyone, scatter_dimension=0, tiled=True).astype(
        jnp.float32
    )
    gain_grad = lax.psum_scatter(gain_terms, everyone, scatter_dimension=0, tiled=True)
    return (layer_output, input_grad, gain_grad, qkv_grad, out_proj_grad, gate_up_grad, down_grad)


def per_device_by_heads(
    n_seq,
    hidden_in,
    norm_gains,
    qkv_weight,
    out_weight,
    gate_up_weight,
    down_weight,
    output_cotangent,
    segment_ids,
    padding,
    positions,
):
    groups, piece_len, model_width = hidden_in.shape
    row_count = groups * piece_len
    seq_len = segment_ids.shape[1]
    n_chip = KV_HEADS
    n_plane = 2 * n_chip
    group_size = HEADS // KV_HEADS
    query_width = HEADS * HEAD_DIM
    key_width = KV_HEADS * HEAD_DIM
    own_width = group_size * HEAD_DIM
    part_width = own_width + 2 * HEAD_DIM
    block_width = part_width + own_width
    weight_rows = qkv_weight.shape[0]
    extra_rows = 16 - weight_rows % 16
    block_rows = weight_rows + extra_rows
    core = lax.axis_index("core")

    gain_rows = jnp.pad(
        norm_gains.T, ((0, extra_rows - norm_gains.shape[1]), (0, block_width - weight_rows))
    )
    blocks = jnp.stack(
        [
            jnp.concatenate(
                [
                    jnp.concatenate(
                        [
                            qkv_weight[:, c * own_width : (c + 1) * own_width],
                            qkv_weight[
                                :, query_width + c * HEAD_DIM : query_width + (c + 1) * HEAD_DIM
                            ],
                            qkv_weight[
                                :,
                                query_width + key_width + c * HEAD_DIM : query_width
                                + key_width
                                + (c + 1) * HEAD_DIM,
                            ],
                            out_weight[:, c * own_width : (c + 1) * own_width],
                        ],
                        axis=1,
                    ),
                    gain_rows,
                ],
                axis=0,
            )
            for c in range(n_chip)
        ]
    )
    hidden_all, blocks_all = gather_first(n_seq, hidden_in, blocks)
    unit_weights = lax.all_gather(gate_up_weight, "chip", axis=0, tiled=True)
    blocks_all, down_weight = lax.optimization_barrier((blocks_all, down_weight))
    down_x, down_y = send_beside(down_weight, 1), send_beside(down_weight, 2)
    blocks_all = blocks_all.transpose(0, 2, 1, 3, 4)
    own_weights = blocks_all[:, :, :, :weight_rows].reshape(model_width, block_width)
    own_qkv = own_weights[:, :part_width]
    own_out = own_weights[:, part_width:]
    gain_cols = (
        blocks_all[:, :, :, weight_rows : weight_rows + norm_gains.shape[1], :weight_rows]
        .transpose(0, 1, 2, 4, 3)
        .reshape(model_width, norm_gains.shape[1])
        .astype(jnp.float32)
    )

    seq_rows = hidden_all.reshape(seq_len, model_width).astype(jnp.float32)
    seq_factor = lax.rsqrt(jnp.mean(seq_rows * seq_rows, axis=-1, keepdims=True) + EPSILON)
    attn_input = (seq_rows * seq_factor * gain_cols[:, 0]).astype(jnp.bfloat16)
    projected = add_slice(attn_input, own_qkv)
    segment = lax.dynamic_index_in_dim(segment_ids, core, 0, keepdims=False)
    valid = lax.dynamic_index_in_dim(padding, core, 0, keepdims=False)
    token = jnp.arange(seq_len, dtype=jnp.int32)
    document_start = jnp.min(
        jnp.where(segment[:, None] == segment[None, :], token[None, :], seq_len), axis=1
    )
    cosine, sine_part = rotary_tables(token - document_start, HEAD_DIM)
    queries = (
        rotate(projected[:, :own_width].reshape(seq_len, group_size, HEAD_DIM), cosine, sine_part)
        .astype(jnp.bfloat16)
        .reshape(seq_len, own_width)
    )
    keys = (
        rotate(
            projected[:, own_width : own_width + HEAD_DIM].reshape(seq_len, 1, HEAD_DIM),
            cosine,
            sine_part,
        )
        .astype(jnp.bfloat16)
        .reshape(seq_len, HEAD_DIM)
    )
    values = projected[:, own_width + HEAD_DIM :].astype(jnp.bfloat16)
    segment_col = segment[:, None]
    segment_row = jnp.where(valid == 1, segment, -1)[None, :]
    attn_out = attend(queries, keys, values, segment_col, segment_row)
    proj_parts = times_rows(attn_out, own_out).astype(jnp.bfloat16)
    proj_parts, down_x, down_y = lax.optimization_barrier((proj_parts, down_x, down_y))
    half = down_weight.shape[0] // 2
    down_units = (
        down_weight,
        down_x,
        down_y,
        send_beside(down_x[:half], 2),
        send_beside(down_y[half:], 1),
    )
    proj_parts = plane_exchange(
        proj_parts.reshape(n_plane, piece_len, model_width), 2
    )

    def sum_parts(parts):
        parts = parts.reshape(n_chip, groups, piece_len, model_width).astype(jnp.float32)
        return jnp.sum(parts, axis=0).reshape(row_count, model_width)

    attn_proj = sum_parts(proj_parts)
    residual = hidden_in.reshape(row_count, model_width).astype(jnp.float32)
    after_attn = residual + rms_norm(attn_proj, gain_cols[:, 1])
    ffn_input = rms_norm(after_attn, gain_cols[:, 2]).astype(jnp.bfloat16)

    pieces = (groups, piece_len, model_width)
    down_out, ffn_all, gate_part, up_part, hidden_part = run_units(
        n_seq, ffn_input.reshape(pieces), unit_weights, down_units
    )
    down_out = down_out.reshape(row_count, model_width)
    layer_out = after_attn + rms_norm(down_out, gain_cols[:, 3])
    layer_output = layer_out.astype(jnp.bfloat16).reshape(pieces)

    cotangent = output_cotangent.reshape(row_count, model_width).astype(jnp.float32)
    unused_last, pull_last = jax.vjp(rms_norm, down_out, gain_cols[:, 3])
    grad_down, grad_gain_last = pull_last(cotangent)
    grad_ffn_in, gate_low, up_low, down_rows = run_units(
        n_seq,
        grad_down.astype(jnp.bfloat16).reshape(pieces),
        unit_weights,
        down_units,
        (gate_part, up_part, hidden_part),
    )
    grad_ffn_in = grad_ffn_in.reshape(row_count, model_width)
    down_grad = lax.psum_scatter(down_rows, "chip", scatter_dimension=0, tiled=True).astype(
        jnp.float32
    )

    unused_mid, pull_mid = jax.vjp(rms_norm, after_attn, gain_cols[:, 2])
    grad_after_ffn, grad_gain_mid = pull_mid(grad_ffn_in)
    grad_after = cotangent + grad_after_ffn
    unused_post, pull_post = jax.vjp(rms_norm, attn_proj, gain_cols[:, 1])
    grad_proj, grad_gain_post = pull_post(grad_after)
    grad_proj_low = grad_proj.astype(jnp.bfloat16)

    grad_proj_all, gate_up_rows = spread_plane(
        grad_proj_low.reshape(groups, piece_len, model_width), gate_low, up_low, ffn_all
    )
    gate_up_grad = lax.psum_scatter(
        gate_up_rows, "chip", scatter_dimension=0, tiled=True
    ).astype(jnp.float32)
    grad_proj_all = grad_proj_all.reshape(seq_len, model_width)
    grad_attn = add_slice(grad_proj_all, own_out).astype(jnp.bfloat16)
    grad_query_rot, grad_key_rot, grad_values = attend_back(
        queries, keys, values, segment_col, segment_row, grad_attn
    )
    grad_queries = rotate_back(
        grad_query_rot.reshape(seq_len, group_size, HEAD_DIM), cosine, sine_part
    ).reshape(seq_len, own_width)
    grad_keys = rotate_back(
        grad_key_rot.reshape(seq_len, 1, HEAD_DIM), cosine, sine_part
    ).reshape(seq_len, HEAD_DIM)
    grad_projected = jnp.concatenate([grad_queries, grad_keys, grad_values], axis=1).astype(
        jnp.bfloat16
    )
    grad_in_part = times_rows(grad_projected, own_qkv)
    grad_gain_first = jnp.sum(grad_in_part * seq_rows * seq_factor, axis=0)
    weight_part = jnp.concatenate(
        [
            outer_rows(attn_input, grad_projected).astype(jnp.bfloat16),
            outer_rows(grad_proj_all, attn_out).astype(jnp.bfloat16),
        ],
        axis=1,
    ).reshape(n_seq, n_chip, 2, weight_rows, block_width)
    gain_terms = (
        jnp.stack([grad_gain_first, grad_gain_post, grad_gain_mid, grad_gain_last])
        .astype(jnp.bfloat16)
        .reshape(-1, n_seq, n_chip, 2, weight_rows)
        .transpose(1, 2, 3, 0, 4)
    )
    gain_terms = jnp.pad(
        gain_terms,
        ((0, 0),) * 3
        + ((0, extra_rows - gain_terms.shape[3]), (0, block_width - weight_rows)),
    )
    grad_blocks = jnp.concatenate([weight_part, gain_terms], axis=3).transpose(0, 2, 1, 3, 4)
    grad_in_parts, grad_sums = sum_last(
        n_seq,
        grad_in_part.astype(jnp.bfloat16).reshape(n_plane, piece_len, model_width),
        grad_blocks,
    )
    grad_attn_in = sum_parts(grad_in_parts)
    factor = lax.rsqrt(jnp.mean(residual * residual, axis=-1, keepdims=True) + EPSILON)
    unused_first, pull_first = jax.vjp(rms_norm, residual, gain_cols[:, 0])
    grad_res_first, unused_gain = pull_first(grad_attn_in)
    input_grad = (grad_after + grad_res_first).reshape(groups, piece_len, model_width)

    weight_sums = grad_sums[:, :weight_rows].astype(jnp.float32)
    qkv_grad = jnp.concatenate(
        [weight_sums[c, :, :own_width] for c in range(n_chip)]
        + [weight_sums[c, :, own_width : own_width + HEAD_DIM] for c in range(n_chip)]
        + [weight_sums[c, :, own_width + HEAD_DIM : part_width] for c in range(n_chip)],
        axis=1,
    )
    out_proj_grad = jnp.concatenate(
        [weight_sums[c, :, part_width:] for c in range(n_chip)], axis=1
    )
    gain_grad = jnp.sum(
        grad_sums[:, weight_rows : weight_rows + norm_gains.shape[1], :weight_rows].astype(
            jnp.float32
        ),
        axis=0,
    ).T
    return (layer_output, input_grad, gain_grad, qkv_grad, out_proj_grad, gate_up_grad, down_grad)


def solution(mesh):
    n_seq = mesh.shape["seq"]
    n_ctx = mesh.shape["ctx"]
    split_mesh = jax.sharding.Mesh(
        mesh.devices.reshape(n_seq, n_ctx // 2, 2), ("seq", "chip", "core")
    )
    plane = ("chip", "core")
    rows = P(("seq", "chip", "core"), None)
    tokens = P("seq", plane, None)
    placed = (
        tokens,
        rows,
        rows,
        rows,
        rows,
        rows,
        tokens,
        P("seq", None),
        P("seq", None),
        P("seq", plane),
    )

    def step(*arrays):
        groups = arrays[0].shape[0]
        if n_ctx // 2 == KV_HEADS and groups == 2 and n_seq == 4:
            return per_device_by_heads(n_seq, *arrays)
        return per_device_general(*arrays)

    return jax.shard_map(
        step,
        mesh=split_mesh,
        in_specs=placed,
        out_specs=(tokens, tokens, rows, rows, rows, rows, rows),
        check_vma=False,
    )
```

```python
from functools import partial
import math

import jax
import jax.numpy as jnp
from jax import lax
from jax.experimental import pallas as pl
from jax.experimental.pallas import tpu as pltpu
from jax.sharding import PartitionSpec as P

HEADS = 8
KV_HEADS = 4
HEAD_DIM = 256


EPSILON = 1e-06
SOFT_CAP = 50.0
MASKED = -1e30


def rms_norm(matrix, gain_col):
    factor = lax.rsqrt(jnp.mean(matrix * matrix, axis=-1, keepdims=True) + EPSILON)
    return matrix * factor * gain_col


def rotary_tables(positions, head_dim):
    half_dim = head_dim // 2
    frequency = jnp.exp(
        jnp.arange(half_dim, dtype=jnp.float32) * (-2.0 * math.log(10000.0) / head_dim)
    )
    phase_angle = positions.astype(jnp.float32)[:, None] * frequency[None, :]
    return (jnp.cos(phase_angle)[:, None, :], jnp.sin(phase_angle)[:, None, :])


def rotate(vectors, cosine, sine_part):
    half_dim = vectors.shape[-1] // 2
    first_half = vectors[..., :half_dim]
    second_half = vectors[..., half_dim:]
    return jnp.concatenate(
        [
            first_half * cosine - second_half * sine_part,
            second_half * cosine + first_half * sine_part,
        ],
        axis=-1,
    )


def rotate_back(grads, cosine, sine_part):
    half_dim = grads.shape[-1] // 2
    first_half = grads[..., :half_dim]
    second_half = grads[..., half_dim:]
    return jnp.concatenate(
        [
            first_half * cosine + second_half * sine_part,
            second_half * cosine - first_half * sine_part,
        ],
        axis=-1,
    )


def soft_probs(scaled, allowed):
    capped = SOFT_CAP * jnp.tanh(scaled / SOFT_CAP)
    capped = jnp.where(allowed, capped, MASKED)
    return jax.nn.softmax(capped, axis=-1)


def geglu_parts(gate_part, up_part):
    return jax.nn.gelu(gate_part, approximate=True) * up_part


def score_block(queries, keys_all):
    groups = keys_all.shape[0]
    seq_len = keys_all.shape[1]
    piece_len = queries.shape[0] // groups
    query_heads = queries.reshape(groups, piece_len, KV_HEADS, HEADS // KV_HEADS, HEAD_DIM)
    key_heads = keys_all.reshape(groups, seq_len, KV_HEADS, HEAD_DIM)
    raw_score = jnp.einsum(
        "spkgd,slkd->skgpl", query_heads, key_heads, preferred_element_type=jnp.float32
    )
    return raw_score * (1.0 / math.sqrt(HEAD_DIM))


def mix_values(weights_low, values_all):
    groups = values_all.shape[0]
    seq_len = values_all.shape[1]
    piece_len = weights_low.shape[3]
    value_heads = values_all.reshape(groups, seq_len, KV_HEADS, HEAD_DIM)
    mixed = jnp.einsum(
        "skgpl,slkd->spkgd", weights_low, value_heads, preferred_element_type=jnp.float32
    )
    return mixed.reshape(groups * piece_len, HEADS * HEAD_DIM).astype(jnp.bfloat16)


def add_slice(left, weight_piece):
    return jnp.dot(left, weight_piece, preferred_element_type=jnp.float32)


def times_rows(left, weight_piece):
    return lax.dot_general(
        left, weight_piece, (((1,), (1,)), ((), ())), preferred_element_type=jnp.float32
    )


def outer_rows(left, right):
    return lax.dot_general(
        left, right, (((0,), (0,)), ((), ())), preferred_element_type=jnp.float32
    )


MESH = pl.DeviceIdType.MESH
ANY = pl.BlockSpec(memory_space=pl.ANY)
DMA = pltpu.SemaphoreType.DMA


def remote(source, target, send_sem, recv_sem, device):
    return pltpu.make_async_remote_copy(
        src_ref=source,
        dst_ref=target,
        send_sem=send_sem,
        recv_sem=recv_sem,
        device_id=device,
        device_id_type=MESH,
    )


def plane_device(index):
    return {"chip": index // 2, "core": lax.rem(index, 2)}


def greet(n_plane, n_seq):
    me = lax.axis_index("chip") * 2 + lax.axis_index("core")
    barrier = pltpu.get_barrier_semaphore()
    for step in range(1, n_plane):
        pl.semaphore_signal(
            barrier,
            inc=1,
            device_id=plane_device(lax.rem(me + step, n_plane)),
            device_id_type=MESH,
        )
    count = n_plane - 1
    if n_seq > 1:
        s = lax.axis_index("seq")

        @pl.when(s > 0)
        def _():
            pl.semaphore_signal(barrier, inc=1, device_id={"seq": s - 1}, device_id_type=MESH)

        @pl.when(s < n_seq - 1)
        def _():
            pl.semaphore_signal(barrier, inc=1, device_id={"seq": s + 1}, device_id_type=MESH)

        count = count + jnp.where(s > 0, 1, 0) + jnp.where(s < n_seq - 1, 1, 0)
    pl.semaphore_wait(barrier, count)


def chip_at(q, flip):
    x, y = lax.rem(q, 2), q // 2
    x = 1 - x if flip in (1, 3) else x
    y = 1 - y if flip in (2, 3) else y
    return y * 2 + x


class Merge:
    def __init__(self, source, target, added, own_part, sems):
        self.source, self.target, self.added, self.own_part = source, target, added, own_part
        self.send_sems, self.recv_sems, self.load_sems, self.local_sems = sems
        self.q = lax.axis_index("chip")
        self.k = lax.axis_index("core")
        self.half = source.shape[1] // 2

    def rows(self, flip):
        return pl.ds(0 if flip == 1 else self.half, self.half)

    def direct(self, flip, core):
        chip = chip_at(self.q, flip)
        slot = 6 * (flip - 1) + core
        return remote(
            self.source.at[2 * chip + core, self.rows(flip)],
            self.target.at[1, self.k, self.rows(flip)],
            self.send_sems.at[slot],
            self.recv_sems.at[6 * (flip - 1) + self.k],
            {"chip": chip, "core": core},
        )

    def arrival(self, flip, core):
        return remote(
            self.source.at[0, self.rows(flip)],
            self.target.at[1, core, self.rows(flip)],
            self.send_sems.at[0],
            self.recv_sems.at[6 * (flip - 1) + core],
            {"chip": chip_at(self.q, flip)},
        )

    def across(self, flip, core):
        slot = 6 * (flip - 1) + 2 + core
        return remote(
            self.source.at[2 * chip_at(self.q, 3) + core, self.rows(flip)],
            self.added.at[flip - 1, core],
            self.send_sems.at[slot],
            self.recv_sems.at[slot],
            {"chip": chip_at(self.q, flip)},
        )

    def load(self, flip, core):
        return pltpu.make_async_copy(
            self.source.at[2 * chip_at(self.q, 3 - flip) + core, self.rows(flip)],
            self.own_part.at[flip - 1, core],
            self.load_sems.at[flip - 1, core],
        )

    def summed(self, flip, core):
        slot = 6 * (flip - 1) + 4 + core
        return remote(
            self.own_part.at[flip - 1, core],
            self.target.at[2, self.k, self.rows(flip)],
            self.send_sems.at[slot],
            self.recv_sems.at[6 * (flip - 1) + 4 + self.k],
            {"chip": chip_at(self.q, 3 - flip), "core": core},
        )

    def summed_arrival(self, flip, core):
        return remote(
            self.own_part.at[flip - 1, 0],
            self.target.at[2, core, self.rows(flip)],
            self.send_sems.at[0],
            self.recv_sems.at[6 * (flip - 1) + 4 + core],
            {"chip": chip_at(self.q, 3 - flip)},
        )

    def twin(self):
        return remote(
            self.source.at[2 * self.q + 1 - self.k],
            self.target.at[0, self.k],
            self.send_sems.at[12],
            self.recv_sems.at[12],
            {"core": 1 - self.k},
        )

    def twin_arrival(self):
        return remote(
            self.source.at[0],
            self.target.at[0, 1 - self.k],
            self.send_sems.at[12],
            self.recv_sems.at[12],
            {"core": 1 - self.k},
        )

    def own(self):
        return pltpu.make_async_copy(
            self.source.at[2 * self.q + self.k], self.target.at[0, self.k], self.local_sems.at[0]
        )

    def start(self):
        pairs = [(flip, core) for core in (0, 1) for flip in (1, 2)]
        for flip, core in pairs:
            self.across(flip, core).start()
        for flip, core in pairs:
            self.load(flip, core).start()
        for flip, core in pairs:
            self.direct(flip, core).start()
        self.twin().start()
        self.own().start()

    def pass_on(self):
        step = 16
        for core in (0, 1):
            for flip in (1, 2):
                self.load(flip, core).wait()
                self.across(flip, core).wait_recv()

                def body(i, carry, flip=flip, core=core):
                    rows = pl.ds(pl.multiple_of(i * step, step), step)
                    total = self.own_part[flip - 1, core, rows, :].astype(jnp.float32)
                    total = total + self.added[flip - 1, core, rows, :].astype(jnp.float32)
                    self.own_part[flip - 1, core, rows, :] = total.astype(self.own_part.dtype)
                    return carry

                lax.fori_loop(0, self.half // step, body, 0)
                self.summed(flip, core).start()

    def finish(self):
        for core in (0, 1):
            for flip in (1, 2):
                self.across(flip, core).wait_send()
                self.direct(flip, core).wait_send()
                self.arrival(flip, core).wait_recv()
                self.summed(flip, core).wait_send()
                self.summed_arrival(flip, core).wait_recv()
        self.twin().wait_send()
        self.twin_arrival().wait_recv()
        self.own().wait()


def merge_scratch(blocks):
    part = (2, 2, blocks.shape[1] // 2, blocks.shape[2])
    return [
        pltpu.VMEM(part, blocks.dtype),
        pltpu.VMEM(part, blocks.dtype),
        DMA((13,)),
        DMA((13,)),
        DMA((2, 2)),
        DMA((1,)),
    ]


def merged_shape(blocks):
    return jax.ShapeDtypeStruct((3, 2) + blocks.shape[1:], blocks.dtype)


class Spread:
    def __init__(self, source, target, send_sems, recv_sems, local_sem):
        self.source, self.target = source, target
        self.send_sems, self.recv_sems = send_sems, recv_sems
        self.local_sem = local_sem
        self.q = lax.axis_index("chip")
        self.k = lax.axis_index("core")
        self.half = source.shape[1] // 2

    def chip(self, flip):
        return chip_at(self.q, flip)

    def direct(self, flip, twin):
        core = 1 - self.k if twin else self.k
        slot = 2 * flip + twin
        return remote(
            self.source.at[core],
            self.target.at[2 * self.q + self.k],
            self.send_sems.at[slot],
            self.recv_sems.at[slot],
            {"chip": self.chip(flip), "core": core},
        )

    def passed(self, flip, twin):
        core = 1 - self.k if twin else self.k
        slot = 8 + 2 * (flip - 1) + twin
        rows = pl.ds(0 if flip == 1 else self.half, self.half)
        block = self.target.at[2 * self.chip(flip) + core, rows]
        return remote(
            block,
            block,
            self.send_sems.at[slot],
            self.recv_sems.at[slot],
            {"chip": self.chip(3 - flip)},
        )

    def own(self):
        return pltpu.make_async_copy(
            self.source.at[self.k],
            self.target.at[2 * self.q + self.k],
            self.local_sem.at[0],
        )

    def start(self):
        for twin in (0, 1):
            for flip in (1, 2):
                self.direct(flip, twin).start()
        self.direct(0, 1).start()
        self.own().start()

    def pass_on(self):
        for twin in (0, 1):
            for flip in (1, 2):
                self.direct(flip, twin).wait_recv()
                self.passed(flip, twin).start()

    def finish(self):
        for twin in (0, 1):
            for flip in (1, 2):
                self.passed(flip, twin).wait()
                self.direct(flip, twin).wait_send()
        self.direct(0, 1).wait()
        self.own().wait()


SPREAD_SLOTS = 12


def merge_kernel(n_plane, source, rows_x, rows_y, target, across, added, own_part, *sems):
    greet(n_plane, 1)
    merge = Merge(source, target, added, own_part, sems[:4])
    pass_send, pass_recv = sems[4:]
    merge.start()
    half = rows_x.shape[0] // 2
    passed = [
        remote(
            rows.at[pl.ds(i * half, half)],
            across.at[i],
            pass_send.at[i],
            pass_recv.at[i],
            {"chip": chip_at(merge.q, 2 - i)},
        )
        for i, rows in enumerate((rows_x, rows_y))
    ]
    for copy in passed:
        copy.start()
    merge.pass_on()
    merge.finish()
    for copy in passed:
        copy.wait()


def merge_plane(blocks, rows_x, rows_y, collective_id):
    half = (2, rows_x.shape[0] // 2, rows_x.shape[1])
    return pl.pallas_call(
        partial(merge_kernel, 2 * KV_HEADS),
        out_shape=[merged_shape(blocks), jax.ShapeDtypeStruct(half, rows_x.dtype)],
        in_specs=[ANY] * 3,
        out_specs=[ANY] * 2,
        scratch_shapes=merge_scratch(blocks) + [DMA((2,)), DMA((2,))],
        compiler_params=pltpu.CompilerParams(
            collective_id=collective_id, has_side_effects=True
        ),
    )(blocks, rows_x, rows_y)


def spread_kernel(
    n_plane,
    blocks,
    low_gate,
    low_up,
    tokens,
    target,
    grads,
    left,
    right,
    tile,
    send_sems,
    recv_sems,
    local_sem,
    load_sem,
    row_sem,
    tile_sem,
):
    greet(n_plane, 1)
    spread = Spread(blocks, target, send_sems, recv_sems, local_sem)
    spread.start()
    n_units, unit_rows, units = low_gate.shape
    width = right.shape[1]
    piece_len = tokens.shape[3]
    loads = []
    for i, source in enumerate((low_gate, low_up)):
        for u in range(n_units):
            place = left.at[i, pl.ds(u * unit_rows, unit_rows)]
            loads.append(pltpu.make_async_copy(source.at[u], place, load_sem.at[i, u]))
    for u in range(n_units):
        for half in range(2):
            place = right.at[pl.ds(u * unit_rows + half * piece_len, piece_len)]
            source = tokens.at[u // 2, u % 2, half]
            loads.append(pltpu.make_async_copy(source, place, row_sem.at[u, half]))
    for load in loads:
        load.start()
    for load in loads:
        load.wait()
    row_tile, col_tile = units // 3, width // 3

    def tile_store(i, r, c, slot):
        rows = pl.ds(pl.multiple_of(r * row_tile, 16), row_tile)
        cols = pl.ds(pl.multiple_of(i * width + c * col_tile, 128), col_tile)
        return pltpu.make_async_copy(tile.at[slot], grads.at[rows, cols], tile_sem.at[slot])

    def one_tile(j, carry):
        i, slot = lax.div(j, 9), lax.rem(j, 2)
        r, c = lax.div(lax.rem(j, 9), 3), lax.rem(j, 3)
        rows = pl.ds(pl.multiple_of(r * row_tile, 128), row_tile)
        cols = pl.ds(pl.multiple_of(c * col_tile, 128), col_tile)
        total = outer_rows(left[i, :, rows], right[:, cols])

        @pl.when(j >= 2)
        def _():
            tile_store(i, r, c, slot).wait()

        tile[slot] = total.astype(tile.dtype)
        tile_store(i, r, c, slot).start()
        return carry

    lax.fori_loop(0, PASS_TURN, one_tile, 0)
    spread.pass_on()
    lax.fori_loop(PASS_TURN, 18, one_tile, 0)
    for slot in range(2):
        tile_store(0, 0, 0, slot).wait()
    spread.finish()


PASS_TURN = 14


def spread_plane(blocks, low_gate, low_up, tokens):
    n_plane = 2 * KV_HEADS
    low = blocks.dtype
    n_units, unit_rows, units = low_gate.shape
    width = blocks.shape[2]
    return pl.pallas_call(
        partial(spread_kernel, n_plane),
        out_shape=[
            jax.ShapeDtypeStruct((n_plane,) + blocks.shape[1:], low),
            jax.ShapeDtypeStruct((units, 2 * width), low),
        ],
        in_specs=[ANY] * 4,
        out_specs=[ANY, ANY],
        scratch_shapes=[
            pltpu.VMEM((2, n_units * unit_rows, units), low),
            pltpu.VMEM((n_units * unit_rows, width), low),
            pltpu.VMEM((2, units // 3, width // 3), low),
            DMA((SPREAD_SLOTS,)),
            DMA((SPREAD_SLOTS,)),
            DMA((1,)),
            DMA((2, n_units)),
            DMA((n_units, 2)),
            DMA((2,)),
        ],
        compiler_params=pltpu.CompilerParams(
            collective_id=3, has_side_effects=True, vmem_limit_bytes=48 * 1024 * 1024
        ),
    )(blocks, low_gate, low_up, tokens)


def gather_kernel(
    n_seq,
    n_plane,
    hidden,
    blocks,
    hidden_all,
    blocks_all,
    hid_send,
    hid_recv,
    hid_local,
    chip_send,
    chip_recv,
    chip_local,
    left_send,
    right_send,
    line_recv,
    twin_send,
    twin_recv,
):
    n_chip = n_plane // 2
    s = lax.axis_index("seq")
    q = lax.axis_index("chip")
    k = lax.axis_index("core")
    greet(n_plane, n_seq)
    swaps = []
    for step in range(1, n_chip):
        to = lax.rem(q + step, n_chip)
        copy = remote(
            blocks.at[to],
            blocks_all.at[s, k, q],
            chip_send.at[step],
            chip_recv.at[step],
            {"chip": to},
        )
        copy.start()
        swaps.append(copy)
    own = pltpu.make_async_copy(blocks.at[q], blocks_all.at[s, k, q], chip_local.at[0])
    own.start()
    spread = Spread(hidden, hidden_all, hid_send, hid_recv, hid_local)
    for copy in swaps:
        copy.wait_recv()
    own.wait()
    spread.start()

    def to_left(d):
        return remote(
            blocks_all.at[d, k], blocks_all.at[d, k], left_send.at[d], line_recv.at[d], {"seq": s - 1}
        )

    def to_right(d):
        return remote(
            blocks_all.at[d, k], blocks_all.at[d, k], right_send.at[d], line_recv.at[d], {"seq": s + 1}
        )

    def to_twin(d):
        return remote(
            blocks_all.at[d, k], blocks_all.at[d, k], twin_send.at[d], twin_recv.at[d], {"core": 1 - k}
        )

    def from_twin(d):
        return remote(
            blocks_all.at[d, 1 - k],
            blocks_all.at[d, 1 - k],
            twin_send.at[d],
            twin_recv.at[d],
            {"core": 1 - k},
        )

    @pl.when(s > 0)
    def _():
        to_left(s).start()

    @pl.when(s < n_seq - 1)
    def _():
        to_right(s).start()

    to_twin(s).start()
    for hop in range(1, n_seq):
        if hop == 2:
            spread.pass_on()
        from_left = s - hop
        from_right = s + hop

        @pl.when(from_left >= 0)
        def _():
            to_left(from_left).wait_recv()

            @pl.when(s < n_seq - 1)
            def _():
                to_right(from_left).start()

            to_twin(from_left).start()

        @pl.when(from_right < n_seq)
        def _():
            to_right(from_right).wait_recv()

            @pl.when(s > 0)
            def _():
                to_left(from_right).start()

            to_twin(from_right).start()

    for d in range(n_seq):

        @pl.when((d >= s) & (s > 0))
        def _():
            to_left(d).wait_send()

        @pl.when((d <= s) & (s < n_seq - 1))
        def _():
            to_right(d).wait_send()

        to_twin(d).wait_send()
        from_twin(d).wait_recv()
    for copy in swaps:
        copy.wait_send()
    spread.finish()


def gather_first(n_seq, hidden, blocks):
    n_plane = 2 * KV_HEADS
    n_chip = KV_HEADS
    return pl.pallas_call(
        partial(gather_kernel, n_seq, n_plane),
        out_shape=[
            jax.ShapeDtypeStruct((n_plane,) + hidden.shape[1:], hidden.dtype),
            jax.ShapeDtypeStruct((n_seq, 2) + blocks.shape, blocks.dtype),
        ],
        in_specs=[ANY, ANY],
        out_specs=[ANY, ANY],
        scratch_shapes=[
            DMA((SPREAD_SLOTS,)),
            DMA((SPREAD_SLOTS,)),
            DMA((1,)),
            DMA((n_chip,)),
            DMA((n_chip,)),
            DMA((1,)),
            DMA((n_seq,)),
            DMA((n_seq,)),
            DMA((n_seq,)),
            DMA((n_seq,)),
            DMA((n_seq,)),
        ],
        compiler_params=pltpu.CompilerParams(collective_id=1, has_side_effects=True),
    )(hidden, blocks)


def last_kernel(
    n_seq,
    n_plane,
    parts,
    blocks,
    parts_all,
    sums,
    held,
    twin,
    line,
    part_added,
    part_own,
    part_send,
    part_recv,
    part_load,
    part_local,
    held_sem,
    twin_send,
    twin_recv,
    line_send,
    line_recv,
    chip_send,
    chip_recv,
    chip_local,
):
    n_chip = n_plane // 2
    s = lax.axis_index("seq")
    q = lax.axis_index("chip")
    k = lax.axis_index("core")
    greet(n_plane, n_seq)

    def load(d):
        return pltpu.make_async_copy(blocks.at[d, k], held.at[d], held_sem.at[d])

    def to_twin(d):
        return remote(
            blocks.at[d, 1 - k], twin.at[d], twin_send.at[d], twin_recv.at[d], {"core": 1 - k}
        )

    def to_left(d):
        return remote(held.at[d], line.at[d], line_send.at[d], line_recv.at[d], {"seq": s - 1})

    def to_right(d):
        return remote(
            held.at[d], line.at[d + 1], line_send.at[d], line_recv.at[d + 1], {"seq": s + 1}
        )

    def gather_terms(d, with_left, with_right):
        load(d).wait()
        to_twin(d).wait_recv()

        @pl.when(with_right)
        def _():
            to_left(d).wait_recv()

        @pl.when(with_left)
        def _():
            to_right(d).wait_recv()

        def body(i, carry):
            held[d, i] = (held[d, i].astype(jnp.float32) + twin[d, i].astype(jnp.float32)).astype(
                held.dtype
            )
            return carry

        def body_right(i, carry):
            total = held[d, i].astype(jnp.float32) + twin[d, i].astype(jnp.float32)
            held[d, i] = (total + line[d, i].astype(jnp.float32)).astype(held.dtype)
            return carry

        def body_left(i, carry):
            total = held[d, i].astype(jnp.float32) + twin[d, i].astype(jnp.float32)
            held[d, i] = (total + line[d + 1, i].astype(jnp.float32)).astype(held.dtype)
            return carry

        def body_both(i, carry):
            total = held[d, i].astype(jnp.float32) + twin[d, i].astype(jnp.float32)
            total = total + line[d, i].astype(jnp.float32)
            held[d, i] = (total + line[d + 1, i].astype(jnp.float32)).astype(held.dtype)
            return carry

        @pl.when(jnp.logical_not(with_left) & jnp.logical_not(with_right))
        def _():
            lax.fori_loop(0, n_chip, body, 0)

        @pl.when(jnp.logical_not(with_left) & with_right)
        def _():
            lax.fori_loop(0, n_chip, body_right, 0)

        @pl.when(with_left & jnp.logical_not(with_right))
        def _():
            lax.fori_loop(0, n_chip, body_left, 0)

        @pl.when(with_left & with_right)
        def _():
            lax.fori_loop(0, n_chip, body_both, 0)

    for d in range(n_seq):
        to_twin(d).start()
        load(d).start()
    part_sems = (part_send, part_recv, part_load, part_local)
    merge = Merge(parts, parts_all, part_added, part_own, part_sems)
    merge.start()
    never = s < 0
    for hop in range(1, n_seq):
        if hop == 2:
            merge.pass_on()
        left = hop - n_seq + s
        right = n_seq - hop + s

        @pl.when(left >= 0)
        def _():
            gather_terms(left, never, s < n_seq - 1)
            to_left(left).start()

        @pl.when(right <= n_seq - 1)
        def _():
            gather_terms(right, s > 0, never)
            to_right(right).start()

    gather_terms(s, s > 0, s < n_seq - 1)
    swaps = []
    for step in range(1, n_chip):
        to = lax.rem(q + step, n_chip)
        copy = remote(
            held.at[s, to], sums.at[q], chip_send.at[step], chip_recv.at[step], {"chip": to}
        )
        copy.start()
        swaps.append(copy)
    own = pltpu.make_async_copy(held.at[s, q], sums.at[q], chip_local.at[0])
    own.start()
    for d in range(n_seq):
        to_twin(d).wait_send()

        @pl.when(d < s)
        def _():
            to_left(d).wait_send()

        @pl.when(d > s)
        def _():
            to_right(d).wait_send()

    merge.finish()
    for copy in swaps:
        copy.wait()
    own.wait()


def sum_last(n_seq, parts, blocks):
    n_plane = 2 * KV_HEADS
    n_chip = KV_HEADS
    block = blocks.shape[2:]
    return pl.pallas_call(
        partial(last_kernel, n_seq, n_plane),
        out_shape=[
            merged_shape(parts),
            jax.ShapeDtypeStruct(block, blocks.dtype),
        ],
        in_specs=[ANY, ANY],
        out_specs=[ANY, ANY],
        scratch_shapes=[
            pltpu.VMEM((n_seq,) + block, blocks.dtype),
            pltpu.VMEM((n_seq,) + block, blocks.dtype),
            pltpu.VMEM((n_seq + 1,) + block, blocks.dtype),
            *merge_scratch(parts),
            DMA((n_seq,)),
            DMA((n_seq,)),
            DMA((n_seq,)),
            DMA((n_seq,)),
            DMA((n_seq + 1,)),
            DMA((n_chip,)),
            DMA((n_chip,)),
            DMA((1,)),
        ],
        compiler_params=pltpu.CompilerParams(
            collective_id=4, has_side_effects=True, vmem_limit_bytes=32 * 1024 * 1024
        ),
    )(parts, blocks)


QUERY_BLOCK = 256


def block_probs(query, keys, segment_col, segment_row, first):
    rows, width = query.shape[0], keys.shape[0]
    scaled = times_rows(query, keys) * (1.0 / math.sqrt(HEAD_DIM))
    bent = jnp.tanh(scaled / SOFT_CAP)
    row = first + lax.broadcasted_iota(jnp.int32, (rows, width), 0)
    col = lax.broadcasted_iota(jnp.int32, (rows, width), 1)
    allowed = ((segment_col == segment_row) & (col <= row)) | (col == row)
    capped = jnp.where(allowed, SOFT_CAP * bent, MASKED)
    raised = jnp.exp(capped - jnp.max(capped, axis=-1, keepdims=True))
    return raised / jnp.sum(raised, axis=-1, keepdims=True), bent


def attend_kernel(group_size, queries, keys, values, segment_col, segment_row, out):
    seq_len = keys.shape[0]
    for first in range(0, seq_len, QUERY_BLOCK):
        rows = slice(first, first + QUERY_BLOCK)
        width = first + QUERY_BLOCK
        for head in range(group_size):
            cols = slice(head * HEAD_DIM, (head + 1) * HEAD_DIM)
            probs, unused = block_probs(
                queries[rows, cols],
                keys[:width],
                segment_col[rows, :],
                segment_row[:, :width],
                first,
            )
            out[rows, cols] = add_slice(probs.astype(jnp.bfloat16), values[:width]).astype(
                out.dtype
            )


def attend(queries, keys, values, segment_col, segment_row):
    return pl.pallas_call(
        partial(attend_kernel, queries.shape[1] // HEAD_DIM),
        out_shape=jax.ShapeDtypeStruct(queries.shape, jnp.bfloat16),
        compiler_params=pltpu.CompilerParams(vmem_limit_bytes=40 * 1024 * 1024),
    )(queries, keys, values, segment_col, segment_row)


def attend_back_kernel(
    group_size,
    queries,
    keys,
    values,
    segment_col,
    segment_row,
    grads,
    grad_queries,
    grad_keys,
    grad_values,
):
    seq_len = keys.shape[0]
    inverse_root = 1.0 / math.sqrt(HEAD_DIM)
    grad_keys[...] = jnp.zeros_like(grad_keys)
    grad_values[...] = jnp.zeros_like(grad_values)
    for first in range(0, seq_len, QUERY_BLOCK):
        rows = slice(first, first + QUERY_BLOCK)
        width = first + QUERY_BLOCK
        for head in range(group_size):
            cols = slice(head * HEAD_DIM, (head + 1) * HEAD_DIM)
            query = queries[rows, cols]
            probs, bent = block_probs(
                query, keys[:width], segment_col[rows, :], segment_row[:, :width], first
            )
            grad = grads[rows, cols]
            grad_probs = times_rows(grad, values[:width])
            mean = jnp.sum(probs * grad_probs, axis=-1, keepdims=True)
            grad_scaled = (probs * (grad_probs - mean) * (1.0 - bent * bent)).astype(jnp.bfloat16)
            grad_queries[rows, cols] = add_slice(grad_scaled, keys[:width]) * inverse_root
            grad_keys[:width, :] += outer_rows(grad_scaled, query) * inverse_root
            grad_values[:width, :] += outer_rows(probs.astype(jnp.bfloat16), grad)


def attend_back(queries, keys, values, segment_col, segment_row, grads):
    return pl.pallas_call(
        partial(attend_back_kernel, queries.shape[1] // HEAD_DIM),
        out_shape=[
            jax.ShapeDtypeStruct(queries.shape, jnp.float32),
            jax.ShapeDtypeStruct(keys.shape, jnp.float32),
            jax.ShapeDtypeStruct(values.shape, jnp.float32),
        ],
        compiler_params=pltpu.CompilerParams(vmem_limit_bytes=40 * 1024 * 1024),
    )(queries, keys, values, segment_col, segment_row, grads)


def chip_beside(c, flip):
    return c ^ flip


LATE = 3


def chip_places(rows, late_rows):
    q = lax.axis_index("chip")
    x, y = lax.rem(q, 2), lax.div(q, 2)
    across = (2 * (1 - y) + 1 - x) * rows
    half = (rows - late_rows) // 2
    return (q * rows, (2 * y + 1 - x) * rows, (2 * (1 - y) + x) * rows, across, across + half)


def send_beside(part, flip):
    return lax.ppermute(part, "chip", [(c, chip_beside(c, flip)) for c in range(KV_HEADS)])


def unit_orders(n):
    units, sums = [], []
    for s in range(n):
        keyed = []
        for d in range(n):
            if d != s:
                near = abs(s - d)
                behind, past = (s, d) if d < s else (n - 1 - s, n - 1 - d)
                keyed += [(near, d, 0), (behind + past + 1, d, 1)]
        order = [(s, 0), (s, 1)] + [(d, h) for unused, d, h in sorted(keyed)]
        units.append([2 * d + h for d, h in order])
        if s in (0, n - 1):
            sums.append(units[-1][2:])
            continue
        keyed = []
        for d in range(n):
            if d != s:
                hops, place = (n - 2 - s, d) if d < s else (s - 1, n - 1 - d)
                keyed += [(n - 2 - place + hops, d, 0), (n - 1 + place + hops, d, 1)]
        sums.append([2 * d + h for unused, d, h in sorted(keyed)])
    return units, sums


def pick(table, s, i):
    width = len(table[0])
    place = s * width + i
    value = 0
    for k, entry in enumerate(entry for row in table for entry in row):
        value = jnp.where(place == k, entry, value)
    return value


SUBS = 1
SUM_TURNS = (0, 1, 4, 5, 8, 8)
GELU_SCALE = math.sqrt(2.0 / math.pi)


def gelu_pieces(gate):
    bend = jnp.tanh(GELU_SCALE * (gate + 0.044715 * gate * gate * gate))
    value = 0.5 * gate * (1.0 + bend)
    slope = 0.5 * (1.0 + bend) + 0.5 * gate * (1.0 - bend * bend) * GELU_SCALE * (
        1.0 + 3.0 * 0.044715 * gate * gate
    )
    return value, slope


def units_kernel(n_seq, backward, *refs):
    if backward:
        tokens, units = refs[:2]
        downs, late = refs[2:7], refs[7]
        kept_gate, kept_up, kept_hidden = refs[8:11]
        out, first_out, second_out, down_grads = refs[11:15]
        stage_outs = (first_out, second_out)
        scratch = refs[15:]
    else:
        tokens, units = refs[:2]
        downs = refs[2:7]
        out, tokens_all, late, first_out, second_out, third_out = refs[7:13]
        stage_outs = (first_out, second_out, third_out)
        scratch = refs[13:]
    units_v, downs_v, held, own_sum, twin_sum, twin_out, line, stage = scratch[:8]
    scratch = scratch[8:]
    if backward:
        kept, kept_sem, tile, tile_sem, load_sem = scratch[:5]
        scratch = scratch[5:]
    else:
        own_hidden, late_send, late_recv = scratch[:3]
        scratch = scratch[3:]
    (
        weight_sem,
        late_sem,
        own_sem,
        left_send,
        right_send,
        token_recv,
        twin_send,
        twin_recv,
        part_send,
        part_recv,
        line_send,
        line_recv,
        stage_sem,
        all_sem,
        out_sem,
    ) = scratch
    n = n_seq
    s = lax.axis_index("seq")
    k = lax.axis_index("core")
    twin = {"core": 1 - k}
    n_units, width = downs_v.shape
    piece_len = tokens.shape[1]
    at_end = (s == 0) | (s == n - 1)

    def token_left(d, h, source):
        return remote(
            source, held.at[d, h, 0], left_send.at[d, h], token_recv.at[d, h], {"seq": s - 1}
        )

    def token_right(d, h, source):
        return remote(
            source, held.at[d, h, 0], right_send.at[d, h], token_recv.at[d, h], {"seq": s + 1}
        )

    def token_twin(d, h, source):
        return remote(source, held.at[d, h, 1], twin_send.at[d, h], twin_recv.at[d, h], twin)

    def part_twin(d, h):
        return remote(
            twin_out.at[d, h], twin_sum.at[d, h], part_send.at[d, h], part_recv.at[d, h], twin
        )

    sub_len = piece_len // SUBS

    def part_line(d, h, sub):
        to_left = d < s
        slot = jnp.where(to_left, d, d + 1)
        rows = pl.ds(sub * sub_len, sub_len)
        return remote(
            twin_sum.at[d, h, rows],
            line.at[slot, h, rows],
            line_send.at[d, h, sub],
            line_recv.at[slot, h, sub],
            {"seq": jnp.where(to_left, s - 1, s + 1)},
        )

    def line_arrival(slot, h, sub):
        rows = pl.ds(sub * sub_len, sub_len)
        return remote(
            twin_sum.at[0, h, rows],
            line.at[slot, h, rows],
            line_send.at[0, h, sub],
            line_recv.at[slot, h, sub],
            {"seq": s},
        )

    def own_load(h):
        return pltpu.make_async_copy(tokens.at[h], held.at[s, h, 0], own_sem.at[h])

    def all_store(d, h):
        return pltpu.make_async_copy(held.at[d, h], tokens_all.at[d, h], all_sem.at[d, h])

    def stage_store(i, d, h, slot):
        return pltpu.make_async_copy(
            stage.at[i, slot], stage_outs[i].at[2 * d + h], stage_sem.at[i, slot]
        )

    def kept_load(i, d, h, slot):
        source = (kept_gate, kept_up)[i]
        return pltpu.make_async_copy(source.at[2 * d + h], kept.at[i, slot], kept_sem.at[i, slot])

    unit_table, sum_table = unit_orders(n)
    right_table = [
        [2 if d == 0 else unit_table[d].index(2 * (d - 1) + 1) + 1 for d in range(n)]
    ]
    left_table = [
        [2 if d == n - 1 else unit_table[d].index(2 * (d + 1) + 1) + 1 for d in range(n)]
    ]

    def source(t):
        unit = pick(unit_table, s, t)
        return lax.div(unit, 2), lax.rem(unit, 2)

    barrier = pltpu.get_barrier_semaphore()
    pl.semaphore_signal(barrier, inc=1, device_id=twin, device_id_type=MESH)

    @pl.when(s > 0)
    def _():
        pl.semaphore_signal(barrier, inc=1, device_id={"seq": s - 1}, device_id_type=MESH)

    @pl.when(s < n - 1)
    def _():
        pl.semaphore_signal(barrier, inc=1, device_id={"seq": s + 1}, device_id_type=MESH)

    greeted = 1 + jnp.where(s > 0, 1, 0) + jnp.where(s < n - 1, 1, 0)
    n_chip, late_rows = late.shape[:2]
    chip_rows = n_units // n_chip
    q = lax.axis_index("chip")
    if not backward:
        for step in range(1, n_chip):
            pl.semaphore_signal(
                barrier,
                inc=1,
                device_id={"chip": lax.rem(q + step, n_chip)},
                device_id_type=MESH,
            )
        greeted = greeted + n_chip - 1
    pl.semaphore_wait(barrier, greeted)

    def late_place(chip):
        first = chip * chip_rows + chip_rows - late_rows
        return downs_v.at[pl.ds(pl.multiple_of(first, 16), late_rows)]

    def late_copy(step):
        return remote(
            downs[0].at[pl.ds(chip_rows - late_rows, late_rows)],
            late_place(q),
            late_send.at[step],
            late_recv.at[step],
            {"chip": lax.rem(q + step, n_chip)},
        )

    def late_store(chip):
        return pltpu.make_async_copy(late_place(chip), late.at[chip], late_sem.at[chip])

    def late_load(chip):
        return pltpu.make_async_copy(late.at[chip], late_place(chip), late_sem.at[chip])

    def second_half(t):
        @pl.when((s < n - 1) & (t == pick(right_table, 0, s)))
        def _():
            d, h = jnp.maximum(s - 1, 0), jnp.where(s > 0, 1, 0)
            token_right(d, h, held.at[d, h, 0]).wait_send()
            token_right(s, 1, tokens.at[1]).start()

        @pl.when((s > 0) & (t == pick(left_table, 0, s)))
        def _():
            d, h = jnp.minimum(s + 1, n - 1), jnp.where(s < n - 1, 1, 0)
            token_left(d, h, held.at[d, h, 0]).wait_send()
            token_left(s, 1, tokens.at[1]).start()

    @pl.when(s < n - 1)
    def _():
        token_right(s, 0, tokens.at[0]).start()

    @pl.when(s > 0)
    def _():
        token_left(s, 0, tokens.at[0]).start()

    for h in range(2):
        token_twin(s, h, tokens.at[h]).start()
        own_load(h).start()
    load_units = pltpu.make_async_copy(units, units_v, weight_sem.at[0])
    load_downs = []
    for i, (first, part) in enumerate(zip(chip_places(chip_rows, late_rows), downs)):
        count = chip_rows - late_rows if i == 0 and backward else part.shape[0]
        load_downs.append(
            pltpu.make_async_copy(
                part.at[pl.ds(0, count)],
                downs_v.at[pl.ds(pl.multiple_of(first, 16), count)],
                weight_sem.at[1 + i],
            )
        )
    if backward:
        load_downs += [late_load(chip) for chip in range(n_chip)]
    else:
        for step in (2, 1, 3):
            late_copy(step).start()
    load_units.start()
    for load in load_downs:
        load.start()
    if backward:
        for i in range(2):
            kept_load(i, s, 0, 0).start()
    load_units.wait()
    for load in load_downs:
        load.wait()

    def add_rows(d, h, sub, into_own, use_line):
        step = 16

        def body(i, carry):
            rows = pl.ds(pl.multiple_of(sub * sub_len + i * step, step), step)
            total = own_sum[d, h, rows, :] + twin_sum[d, h, rows, :].astype(jnp.float32)
            for slot in use_line:
                total = total + line[slot, h, rows, :].astype(jnp.float32)
            if into_own:
                own_sum[d, h, rows, :] = total
            else:
                twin_sum[d, h, rows, :] = total.astype(twin_sum.dtype)
            return carry

        lax.fori_loop(0, sub_len // step, body, 0)

    def combine(d, h):
        to_left = d < s
        slot = jnp.where(to_left, d, d + 1)
        more = jnp.where(to_left, s < n - 1, s > 0)
        part_twin(d, h).wait_recv()

        @pl.when(more)
        def _():
            for sub in range(SUBS):
                line_arrival(slot, h, sub).wait_recv()
                add_rows(d, h, sub, False, (slot,))
                part_line(d, h, sub).start()

        @pl.when(jnp.logical_not(more))
        def _():
            for sub in range(SUBS):
                add_rows(d, h, sub, False, ())
                part_line(d, h, sub).start()

    columns = width // 3
    chunk = n_units // 3

    def hidden_forward(d, h, slot):
        rows = held[d, h].reshape(2 * piece_len, width)
        for c in range(3):
            cols = slice(c * chunk, (c + 1) * chunk)
            gate = times_rows(rows, units_v[cols, :width])
            up = times_rows(rows, units_v[cols, width:])
            value, unused = gelu_pieces(gate)
            stage[0, slot, :, cols] = gate.astype(stage.dtype)
            stage[1, slot, :, cols] = up.astype(stage.dtype)
            stage[2, slot, :, cols] = (value * up).astype(stage.dtype)

    def down_forward(d, h, hidden):
        for c in range(3):
            cols = slice(c * columns, (c + 1) * columns)
            part = add_slice(hidden[...], downs_v[:, cols])
            own_sum[d, h, :, cols] = part[:piece_len]
            twin_out[d, h, :, cols] = part[piece_len:].astype(twin_out.dtype)
        part_twin(d, h).start()

    def own_forward(h):
        down_forward(s, h, own_hidden.at[h])

    def compute_backward(d, h, slot):
        rows = held[d, h].reshape(2 * piece_len, width)
        for c in range(3):
            cols = slice(c * chunk, (c + 1) * chunk)
            grad = times_rows(rows, downs_v[cols, :])
            value, slope = gelu_pieces(kept[0, slot, :, cols].astype(jnp.float32))
            up = kept[1, slot, :, cols].astype(jnp.float32)
            stage[0, slot, :, cols] = (grad * up * slope).astype(stage.dtype)
            stage[1, slot, :, cols] = (grad * value).astype(stage.dtype)
        for c in range(3):
            cols = slice(c * columns, (c + 1) * columns)
            later = slice(width + c * columns, width + (c + 1) * columns)
            part = add_slice(stage[0, slot], units_v[:, cols])
            part = part + add_slice(stage[1, slot], units_v[:, later])
            own_sum[d, h, :, cols] = part[:piece_len]
            twin_out[d, h, :, cols] = part[piece_len:].astype(twin_out.dtype)

    row_tile, col_tile = n_units // 3, width // 3

    def down_gradient(between):
        unit_rows = 2 * piece_len
        group_rows = n * unit_rows

        def left_load(u):
            place = downs_v.at[
                pl.ds((u % n) * unit_rows, unit_rows), pl.ds((u // n) * n_units, n_units)
            ]
            return pltpu.make_async_copy(kept_hidden.at[u], place, load_sem.at[u])

        def left_rows(g, first):
            return downs_v[
                :group_rows, pl.ds(pl.multiple_of(g * n_units + first, 128), row_tile)
            ]

        def right_rows(g, first):
            cols = pl.ds(pl.multiple_of(first, 128), col_tile)
            part = held[g * n // 2 : (g + 1) * n // 2, :, :, :, cols]
            return part.reshape(group_rows, col_tile)

        def tile_store(r, c, slot):
            rows = pl.ds(pl.multiple_of(r * row_tile, 16), row_tile)
            cols = pl.ds(pl.multiple_of(c * col_tile, 128), col_tile)
            return pltpu.make_async_copy(tile.at[slot], down_grads.at[rows, cols], tile_sem.at[slot])

        for u in range(2 * n):
            left_load(u).start()
        for u in range(2 * n):
            left_load(u).wait()

        def one_tile(j, carry):
            slot = lax.rem(j, 2)
            r, c = lax.div(j, 3), lax.rem(j, 3)
            total = sum(
                outer_rows(left_rows(g, r * row_tile), right_rows(g, c * col_tile))
                for g in range(2)
            )

            @pl.when(j >= 2)
            def _():
                tile_store(r, c, slot).wait()

            tile[slot] = total.astype(tile.dtype)
            tile_store(r, c, slot).start()
            for step, turn in enumerate(SUM_TURNS):

                @pl.when(j == turn)
                def _():
                    between(step)

            return carry

        lax.fori_loop(0, 9, one_tile, 0)
        for slot in range(2):
            tile_store(0, 0, slot).wait()

    def unit(t, carry):
        d, h = source(t)
        slot = lax.rem(t, 2)

        @pl.when(at_end & (t >= 3))
        def _():
            combine(*source(t - 1))

        @pl.when(t < 2)
        def _():
            own_load(h).wait()

        @pl.when(t >= 2)
        def _():
            piece = held.at[d, h, 0]
            token_left(d, h, piece).wait_recv()

            @pl.when((d < s) & (s < n - 1))
            def _():
                token_right(d, h, piece).start()

            @pl.when((d > s) & (s > 0))
            def _():
                token_left(d, h, piece).start()

            token_twin(d, h, piece).start()
            for i in range(len(stage_outs)):
                stage_store(i, d, h, slot).wait()

        second_half(t)
        if backward:

            @pl.when(t < 2 * n - 1)
            def _():
                for i in range(2):
                    kept_load(i, *source(t + 1), 1 - slot).start()

            for i in range(2):
                kept_load(i, d, h, slot).wait()
        token_twin(d, h, held.at[d, h, 0]).wait_recv()
        if backward:
            compute_backward(d, h, slot)
            part_twin(d, h).start()
        else:
            hidden_forward(d, h, slot)

            @pl.when(t < 2)
            def _():
                own_hidden[slot] = stage[2, slot]

            @pl.when(t == 2)
            def _():
                for step in range(1, n_chip):
                    late_copy(step).wait_recv()

            @pl.when(t >= 2)
            def _():
                down_forward(d, h, stage.at[2, slot])

        if not backward:
            all_store(d, h).start()
        for i in range(len(stage_outs)):
            stage_store(i, d, h, slot).start()

        return carry

    lax.fori_loop(0, 2 * n, unit, 0)

    second_half(2 * n)

    @pl.when(at_end)
    def _():
        combine(*source(2 * n - 1))

    n_sums = 2 * (n - 1)

    def middle(i):
        @pl.when(jnp.logical_not(at_end) & (i < n_sums))
        def _():
            unit = pick(sum_table, s, i)
            combine(lax.div(unit, 2), lax.rem(unit, 2))

    if backward:
        down_gradient(middle)
    else:

        for chip in range(n_chip):
            late_store(chip).start()

        def one(i, carry):
            middle(i)

            @pl.when((i == 1) | (i == 2))
            def _():
                own_forward(i - 1)

            return carry

        lax.fori_loop(0, n_sums, one, 0)

    def finish(h, carry):
        part_twin(s, h).wait_recv()
        for sub in range(SUBS):

            @pl.when(s < n - 1)
            def _():
                line_arrival(s, h, sub).wait_recv()

            @pl.when(s > 0)
            def _():
                line_arrival(s + 1, h, sub).wait_recv()

            @pl.when(s == 0)
            def _():
                add_rows(s, h, sub, True, (s,))

            @pl.when(s == n - 1)
            def _():
                add_rows(s, h, sub, True, (s + 1,))

            @pl.when(jnp.logical_not(at_end))
            def _():
                add_rows(s, h, sub, True, (s, s + 1))

        pltpu.make_async_copy(own_sum.at[s, h], out.at[h], out_sem.at[h]).start()
        return carry

    lax.fori_loop(0, 2, finish, 0)

    def drain(t, carry):
        d = lax.div(t, 2)
        h = lax.rem(t, 2)
        piece = held.at[d, h, 0]

        right_seen = (d == jnp.maximum(s - 1, 0)) & (h == jnp.where(s > 0, 1, 0))
        left_seen = (d == jnp.minimum(s + 1, n - 1)) & (h == jnp.where(s < n - 1, 1, 0))

        @pl.when((d <= s) & (s < n - 1) & jnp.logical_not(right_seen))
        def _():
            token_right(d, h, piece).wait_send()

        @pl.when((d >= s) & (s > 0) & jnp.logical_not(left_seen))
        def _():
            token_left(d, h, piece).wait_send()

        token_twin(d, h, piece).wait_send()
        part_twin(d, h).wait_send()

        @pl.when(d != s)
        def _():
            for sub in range(SUBS):
                part_line(d, h, sub).wait_send()

        if not backward:
            all_store(d, h).wait()
        return carry

    lax.fori_loop(0, 2 * n, drain, 0)
    if not backward:
        for step in range(1, n_chip):
            late_copy(step).wait_send()
        for chip in range(n_chip):
            late_store(chip).wait()
    for h in range(2):
        for i in range(len(stage_outs)):
            stage_store(i, 0, h, h).wait()
        pltpu.make_async_copy(own_sum.at[s, h], out.at[h], out_sem.at[h]).wait()


def run_units(n_seq, tokens, units, downs, kept=None):
    backward = kept is not None
    low = tokens.dtype
    n_units = units.shape[0]
    halves, piece_len, width = tokens.shape
    n_stage = 2 if backward else 3
    held = (n_seq, halves, 2, piece_len, width)
    unit_rows = (2 * n_seq, 2 * piece_len, n_units)
    sums = (n_seq, halves, piece_len, width)
    scratch = [
        pltpu.VMEM(units.shape, low),
        pltpu.VMEM((n_units, width), low),
        pltpu.VMEM(held, low),
        pltpu.VMEM(sums, jnp.float32),
        pltpu.VMEM(sums, low),
        pltpu.VMEM(sums, low),
        pltpu.VMEM((n_seq + 1,) + sums[1:], low),
        pltpu.VMEM((n_stage, 2) + unit_rows[1:], low),
    ]
    outs = [jax.ShapeDtypeStruct(tokens.shape, jnp.float32)]
    late_shape = (KV_HEADS, downs[0].shape[0] // LATE, width)
    if backward:
        scratch += [
            pltpu.VMEM((2, 2) + unit_rows[1:], low),
            DMA((2, 2)),
            pltpu.VMEM((2, n_units // 3, width // 3), low),
            DMA((2,)),
            DMA((2 * n_seq,)),
        ]
    else:
        scratch += [pltpu.VMEM((2,) + unit_rows[1:], low), DMA((KV_HEADS,)), DMA((KV_HEADS,))]
        outs += [jax.ShapeDtypeStruct(held, low), jax.ShapeDtypeStruct(late_shape, low)]
    outs += [jax.ShapeDtypeStruct(unit_rows, low)] * n_stage
    if backward:
        outs += [jax.ShapeDtypeStruct((n_units, width), low)]
    pairs = DMA((n_seq, halves))
    scratch += [DMA((6,)), DMA((KV_HEADS,)), DMA((halves,))] + [pairs] * 7
    scratch += [DMA((n_seq, halves, SUBS)), DMA((n_seq + 1, halves, SUBS))]
    scratch += [DMA((n_stage, 2)), pairs, DMA((halves,))]
    operands = (tokens, units) + tuple(downs) + (tuple(kept) if backward else ())
    return pl.pallas_call(
        partial(units_kernel, n_seq, backward),
        out_shape=outs,
        in_specs=[ANY] * len(operands),
        out_specs=[ANY] * len(outs),
        scratch_shapes=scratch,
        compiler_params=pltpu.CompilerParams(
            collective_id=6 if backward else 5,
            has_side_effects=True,
            vmem_limit_bytes=63 * 1024 * 1024,
        ),
    )(*operands)


def per_device_general(
    hidden_in,
    norm_gains,
    qkv_weight,
    out_weight,
    gate_up_weight,
    down_weight,
    output_cotangent,
    segment_ids,
    padding,
    positions,
):
    everyone = ("seq", "chip", "core")
    plane = ("chip", "core")
    column = ("seq", "core")
    groups = hidden_in.shape[0]
    piece_len = hidden_in.shape[1]
    model_width = hidden_in.shape[2]
    row_count = groups * piece_len
    seq_len = segment_ids.shape[1]
    group_size = HEADS // KV_HEADS
    query_width = HEADS * HEAD_DIM
    key_width = KV_HEADS * HEAD_DIM
    proj_width = qkv_weight.shape[1]

    residual = hidden_in.reshape(row_count, model_width).astype(jnp.float32)
    factor = lax.rsqrt(jnp.mean(residual * residual, axis=-1, keepdims=True) + EPSILON)
    gain_cols = lax.all_gather(norm_gains, everyone, axis=0, tiled=True).astype(jnp.float32)
    qkv_full = lax.all_gather(qkv_weight, everyone, axis=0, tiled=True)
    attn_input = (residual * factor * gain_cols[:, 0]).astype(jnp.bfloat16)
    projected = add_slice(attn_input, qkv_full)
    cosine, sine_part = rotary_tables(positions.reshape(row_count), HEAD_DIM)
    queries = (
        rotate(projected[:, :query_width].reshape(row_count, HEADS, HEAD_DIM), cosine, sine_part)
        .astype(jnp.bfloat16)
        .reshape(row_count, query_width)
    )
    keys_here = (
        rotate(
            projected[:, query_width : query_width + key_width].reshape(
                row_count, KV_HEADS, HEAD_DIM
            ),
            cosine,
            sine_part,
        )
        .astype(jnp.bfloat16)
        .reshape(groups, piece_len, key_width)
    )
    values_here = (
        projected[:, query_width + key_width :]
        .astype(jnp.bfloat16)
        .reshape(groups, piece_len, key_width)
    )
    both_all = lax.all_gather(
        jnp.concatenate([keys_here, values_here], axis=2), plane, axis=1, tiled=True
    )
    keys_all = both_all[:, :, :key_width]
    values_all = both_all[:, :, key_width:]
    first_query = (lax.axis_index("chip") * 2 + lax.axis_index("core")) * piece_len
    query_rows = first_query + jnp.arange(piece_len, dtype=jnp.int32)
    key_rows = jnp.arange(seq_len, dtype=jnp.int32)
    segment_query = lax.dynamic_slice_in_dim(segment_ids, first_query, piece_len, 1)
    allowed = (segment_query[:, :, None] == segment_ids[:, None, :]) & (
        key_rows[None, None, :] <= query_rows[None, :, None]
    ) & (padding[:, None, :] == 1) | (key_rows[None, None, :] == query_rows[None, :, None])
    allowed = allowed[:, None, None]
    probs = soft_probs(score_block(queries, keys_all), allowed)
    attn_out = mix_values(probs.astype(jnp.bfloat16), values_all)
    out_full = lax.all_gather(out_weight, everyone, axis=0, tiled=True)
    attn_proj = times_rows(attn_out, out_full)
    after_attn = residual + rms_norm(attn_proj, gain_cols[:, 1])
    ffn_input = rms_norm(after_attn, gain_cols[:, 2]).astype(jnp.bfloat16)

    unit_weights = lax.all_gather(gate_up_weight, "chip", axis=0, tiled=True)
    down_units = lax.all_gather(down_weight, "chip", axis=0, tiled=True)
    ffn_all = lax.all_gather(ffn_input, column, axis=0, tiled=True)
    gate_part = times_rows(ffn_all, unit_weights[:, :model_width])
    up_part = times_rows(ffn_all, unit_weights[:, model_width:])
    hidden_part = geglu_parts(gate_part, up_part).astype(jnp.bfloat16)
    down_part = add_slice(hidden_part, down_units).astype(jnp.bfloat16)
    down_out = lax.psum_scatter(down_part, column, scatter_dimension=0, tiled=True).astype(
        jnp.float32
    )
    layer_out = after_attn + rms_norm(down_out, gain_cols[:, 3])
    layer_output = layer_out.astype(jnp.bfloat16).reshape(groups, piece_len, model_width)

    cotangent = output_cotangent.reshape(row_count, model_width).astype(jnp.float32)
    unused_last, pull_last = jax.vjp(rms_norm, down_out, gain_cols[:, 3])
    grad_down, grad_gain_last = pull_last(cotangent)
    grad_down_low = grad_down.astype(jnp.bfloat16)
    grad_down_all = lax.all_gather(grad_down_low, column, axis=0, tiled=True)
    grad_part = times_rows(grad_down_all, down_units)
    unused_units, pull_units = jax.vjp(geglu_parts, gate_part, up_part)
    grad_gate_part, grad_up_part = pull_units(grad_part)
    gate_low = grad_gate_part.astype(jnp.bfloat16)
    up_low = grad_up_part.astype(jnp.bfloat16)
    grad_ffn_part = add_slice(gate_low, unit_weights[:, :model_width]) + add_slice(
        up_low, unit_weights[:, model_width:]
    )
    grad_ffn_in = lax.psum_scatter(
        grad_ffn_part.astype(jnp.bfloat16), column, scatter_dimension=0, tiled=True
    ).astype(jnp.float32)
    gate_up_rows = jnp.concatenate(
        [
            outer_rows(gate_low, ffn_all).astype(jnp.bfloat16),
            outer_rows(up_low, ffn_all).astype(jnp.bfloat16),
        ],
        axis=1,
    )
    down_rows = outer_rows(hidden_part, grad_down_all).astype(jnp.bfloat16)
    gate_up_grad = lax.psum_scatter(
        gate_up_rows, "chip", scatter_dimension=0, tiled=True
    ).astype(jnp.float32)
    down_grad = lax.psum_scatter(down_rows, "chip", scatter_dimension=0, tiled=True).astype(
        jnp.float32
    )

    unused_mid, pull_mid = jax.vjp(rms_norm, after_attn, gain_cols[:, 2])
    grad_after_ffn, grad_gain_mid = pull_mid(grad_ffn_in)
    grad_after = cotangent + grad_after_ffn
    unused_post, pull_post = jax.vjp(rms_norm, attn_proj, gain_cols[:, 1])
    grad_proj, grad_gain_post = pull_post(grad_after)
    grad_proj_low = grad_proj.astype(jnp.bfloat16)
    grad_attn = add_slice(grad_proj_low, out_full).astype(jnp.bfloat16)
    scaled = score_block(queries, keys_all)
    probs, pull_probs = jax.vjp(partial(soft_probs, allowed=allowed), scaled)
    grad_heads = grad_attn.reshape(groups, piece_len, KV_HEADS, group_size, HEAD_DIM)
    query_heads = queries.reshape(groups, piece_len, KV_HEADS, group_size, HEAD_DIM)
    key_heads = keys_all.reshape(groups, seq_len, KV_HEADS, HEAD_DIM)
    value_heads = values_all.reshape(groups, seq_len, KV_HEADS, HEAD_DIM)
    grad_probs = jnp.einsum(
        "spkgd,slkd->skgpl", grad_heads, value_heads, preferred_element_type=jnp.float32
    )
    (grad_scaled,) = pull_probs(grad_probs)
    grad_scaled_low = grad_scaled.astype(jnp.bfloat16)
    inverse_root = 1.0 / math.sqrt(HEAD_DIM)
    grad_query_rot = (
        jnp.einsum(
            "skgpl,slkd->spkgd", grad_scaled_low, key_heads, preferred_element_type=jnp.float32
        )
        * inverse_root
    )
    grad_key_rot = (
        jnp.einsum(
            "skgpl,spkgd->slkd", grad_scaled_low, query_heads, preferred_element_type=jnp.float32
        )
        * inverse_root
    )
    grad_value_part = jnp.einsum(
        "skgpl,spkgd->slkd",
        probs.astype(jnp.bfloat16),
        grad_heads,
        preferred_element_type=jnp.float32,
    )
    both_grads = jnp.concatenate(
        [
            grad_key_rot.reshape(groups, seq_len, key_width),
            grad_value_part.reshape(groups, seq_len, key_width),
        ],
        axis=2,
    ).astype(jnp.bfloat16)
    both_summed = lax.psum_scatter(both_grads, plane, scatter_dimension=1, tiled=True)
    both_summed = both_summed.astype(jnp.float32).reshape(row_count, 2 * key_width)
    key_summed = both_summed[:, :key_width]
    value_summed = both_summed[:, key_width:]
    grad_queries = rotate_back(
        grad_query_rot.reshape(row_count, HEADS, HEAD_DIM), cosine, sine_part
    ).reshape(row_count, query_width)
    grad_keys = rotate_back(
        key_summed.reshape(row_count, KV_HEADS, HEAD_DIM), cosine, sine_part
    ).reshape(row_count, key_width)
    grad_projected = jnp.concatenate([grad_queries, grad_keys, value_summed], axis=1).astype(
        jnp.bfloat16
    )
    grad_attn_in = times_rows(grad_projected, qkv_full)
    unused_first, pull_first = jax.vjp(rms_norm, residual, gain_cols[:, 0])
    grad_res_first, grad_gain_first = pull_first(grad_attn_in)
    input_grad = (grad_after + grad_res_first).reshape(groups, piece_len, model_width)
    gain_terms = jnp.stack([grad_gain_first, grad_gain_post, grad_gain_mid, grad_gain_last], axis=1)
    qkv_part = outer_rows(attn_input, grad_projected).astype(jnp.bfloat16)
    out_part = outer_rows(grad_proj_low, attn_out).astype(jnp.bfloat16)
    qkv_grad = lax.psum_scatter(qkv_part, everyone, scatter_dimension=0, tiled=True).astype(
        jnp.float32
    )
    out_proj_grad = lax.psum_scatter(out_part, everyone, scatter_dimension=0, tiled=True).astype(
        jnp.float32
    )
    gain_grad = lax.psum_scatter(gain_terms, everyone, scatter_dimension=0, tiled=True)
    return (layer_output, input_grad, gain_grad, qkv_grad, out_proj_grad, gate_up_grad, down_grad)


def per_device_by_heads(
    n_seq,
    hidden_in,
    norm_gains,
    qkv_weight,
    out_weight,
    gate_up_weight,
    down_weight,
    output_cotangent,
    segment_ids,
    padding,
    positions,
):
    groups, piece_len, model_width = hidden_in.shape
    row_count = groups * piece_len
    seq_len = segment_ids.shape[1]
    n_chip = KV_HEADS
    n_plane = 2 * n_chip
    group_size = HEADS // KV_HEADS
    query_width = HEADS * HEAD_DIM
    key_width = KV_HEADS * HEAD_DIM
    own_width = group_size * HEAD_DIM
    part_width = own_width + 2 * HEAD_DIM
    block_width = part_width + own_width
    weight_rows = qkv_weight.shape[0]
    extra_rows = 16 - weight_rows % 16
    block_rows = weight_rows + extra_rows
    core = lax.axis_index("core")

    gain_rows = jnp.pad(
        norm_gains.T, ((0, extra_rows - norm_gains.shape[1]), (0, block_width - weight_rows))
    )
    blocks = jnp.stack(
        [
            jnp.concatenate(
                [
                    jnp.concatenate(
                        [
                            qkv_weight[:, c * own_width : (c + 1) * own_width],
                            qkv_weight[
                                :, query_width + c * HEAD_DIM : query_width + (c + 1) * HEAD_DIM
                            ],
                            qkv_weight[
                                :,
                                query_width + key_width + c * HEAD_DIM : query_width
                                + key_width
                                + (c + 1) * HEAD_DIM,
                            ],
                            out_weight[:, c * own_width : (c + 1) * own_width],
                        ],
                        axis=1,
                    ),
                    gain_rows,
                ],
                axis=0,
            )
            for c in range(n_chip)
        ]
    )
    hidden_all, blocks_all = gather_first(n_seq, hidden_in, blocks)
    unit_weights = lax.all_gather(gate_up_weight, "chip", axis=0, tiled=True)
    blocks_all, down_weight = lax.optimization_barrier((blocks_all, down_weight))
    early = down_weight.shape[0] - down_weight.shape[0] // LATE
    down_x, down_y = send_beside(down_weight[:early], 1), send_beside(down_weight[:early], 2)
    blocks_all = blocks_all.transpose(0, 2, 1, 3, 4)
    own_weights = blocks_all[:, :, :, :weight_rows].reshape(model_width, block_width)
    own_qkv = own_weights[:, :part_width]
    own_out = own_weights[:, part_width:]
    gain_cols = (
        blocks_all[:, :, :, weight_rows : weight_rows + norm_gains.shape[1], :weight_rows]
        .transpose(0, 1, 2, 4, 3)
        .reshape(model_width, norm_gains.shape[1])
        .astype(jnp.float32)
    )

    seq_rows = hidden_all.reshape(seq_len, model_width).astype(jnp.float32)
    seq_factor = lax.rsqrt(jnp.mean(seq_rows * seq_rows, axis=-1, keepdims=True) + EPSILON)
    attn_input = (seq_rows * seq_factor * gain_cols[:, 0]).astype(jnp.bfloat16)
    projected = add_slice(attn_input, own_qkv)
    segment = lax.dynamic_index_in_dim(segment_ids, core, 0, keepdims=False)
    valid = lax.dynamic_index_in_dim(padding, core, 0, keepdims=False)
    token = jnp.arange(seq_len, dtype=jnp.int32)
    document_start = jnp.min(
        jnp.where(segment[:, None] == segment[None, :], token[None, :], seq_len), axis=1
    )
    cosine, sine_part = rotary_tables(token - document_start, HEAD_DIM)
    queries = (
        rotate(projected[:, :own_width].reshape(seq_len, group_size, HEAD_DIM), cosine, sine_part)
        .astype(jnp.bfloat16)
        .reshape(seq_len, own_width)
    )
    keys = (
        rotate(
            projected[:, own_width : own_width + HEAD_DIM].reshape(seq_len, 1, HEAD_DIM),
            cosine,
            sine_part,
        )
        .astype(jnp.bfloat16)
        .reshape(seq_len, HEAD_DIM)
    )
    values = projected[:, own_width + HEAD_DIM :].astype(jnp.bfloat16)
    segment_col = segment[:, None]
    segment_row = jnp.where(valid == 1, segment, -1)[None, :]
    attn_out = attend(queries, keys, values, segment_col, segment_row)
    proj_parts = times_rows(attn_out, own_out).astype(jnp.bfloat16)
    proj_parts, down_across = merge_plane(
        proj_parts.reshape(n_plane, piece_len, model_width), down_x, down_y, 2
    )
    down_units = (down_weight, down_x, down_y, down_across[0], down_across[1])

    def sum_parts(parts):
        return jnp.sum(parts.astype(jnp.float32), axis=0).reshape(row_count, model_width)

    attn_proj = sum_parts(proj_parts)
    residual = hidden_in.reshape(row_count, model_width).astype(jnp.float32)
    after_attn = residual + rms_norm(attn_proj, gain_cols[:, 1])
    ffn_input = rms_norm(after_attn, gain_cols[:, 2]).astype(jnp.bfloat16)

    pieces = (groups, piece_len, model_width)
    down_out, ffn_all, down_late, gate_part, up_part, hidden_part = run_units(
        n_seq, ffn_input.reshape(pieces), unit_weights, down_units
    )
    down_out = down_out.reshape(row_count, model_width)
    layer_out = after_attn + rms_norm(down_out, gain_cols[:, 3])
    layer_output = layer_out.astype(jnp.bfloat16).reshape(pieces)

    cotangent = output_cotangent.reshape(row_count, model_width).astype(jnp.float32)
    unused_last, pull_last = jax.vjp(rms_norm, down_out, gain_cols[:, 3])
    grad_down, grad_gain_last = pull_last(cotangent)
    grad_ffn_in, gate_low, up_low, down_rows = run_units(
        n_seq,
        grad_down.astype(jnp.bfloat16).reshape(pieces),
        unit_weights,
        down_units,
        (down_late, gate_part, up_part, hidden_part),
    )
    grad_ffn_in = grad_ffn_in.reshape(row_count, model_width)
    down_grad = lax.psum_scatter(down_rows, "chip", scatter_dimension=0, tiled=True).astype(
        jnp.float32
    )

    unused_mid, pull_mid = jax.vjp(rms_norm, after_attn, gain_cols[:, 2])
    grad_after_ffn, grad_gain_mid = pull_mid(grad_ffn_in)
    grad_after = cotangent + grad_after_ffn
    unused_post, pull_post = jax.vjp(rms_norm, attn_proj, gain_cols[:, 1])
    grad_proj, grad_gain_post = pull_post(grad_after)
    grad_proj_low = grad_proj.astype(jnp.bfloat16)

    grad_proj_all, gate_up_rows = spread_plane(
        grad_proj_low.reshape(groups, piece_len, model_width), gate_low, up_low, ffn_all
    )
    gate_up_grad = lax.psum_scatter(
        gate_up_rows, "chip", scatter_dimension=0, tiled=True
    ).astype(jnp.float32)
    grad_proj_all = grad_proj_all.reshape(seq_len, model_width)
    grad_attn = add_slice(grad_proj_all, own_out).astype(jnp.bfloat16)
    grad_query_rot, grad_key_rot, grad_values = attend_back(
        queries, keys, values, segment_col, segment_row, grad_attn
    )
    grad_queries = rotate_back(
        grad_query_rot.reshape(seq_len, group_size, HEAD_DIM), cosine, sine_part
    ).reshape(seq_len, own_width)
    grad_keys = rotate_back(
        grad_key_rot.reshape(seq_len, 1, HEAD_DIM), cosine, sine_part
    ).reshape(seq_len, HEAD_DIM)
    grad_projected = jnp.concatenate([grad_queries, grad_keys, grad_values], axis=1).astype(
        jnp.bfloat16
    )
    grad_in_part = times_rows(grad_projected, own_qkv)
    grad_gain_first = jnp.sum(grad_in_part * seq_rows * seq_factor, axis=0)
    weight_part = jnp.concatenate(
        [
            outer_rows(attn_input, grad_projected).astype(jnp.bfloat16),
            outer_rows(grad_proj_all, attn_out).astype(jnp.bfloat16),
        ],
        axis=1,
    ).reshape(n_seq, n_chip, 2, weight_rows, block_width)
    gain_terms = (
        jnp.stack([grad_gain_first, grad_gain_post, grad_gain_mid, grad_gain_last])
        .astype(jnp.bfloat16)
        .reshape(-1, n_seq, n_chip, 2, weight_rows)
        .transpose(1, 2, 3, 0, 4)
    )
    gain_terms = jnp.pad(
        gain_terms,
        ((0, 0),) * 3
        + ((0, extra_rows - gain_terms.shape[3]), (0, block_width - weight_rows)),
    )
    grad_blocks = jnp.concatenate([weight_part, gain_terms], axis=3).transpose(0, 2, 1, 3, 4)
    grad_in_parts, grad_sums = sum_last(
        n_seq,
        grad_in_part.astype(jnp.bfloat16).reshape(n_plane, piece_len, model_width),
        grad_blocks,
    )
    grad_attn_in = sum_parts(grad_in_parts)
    factor = lax.rsqrt(jnp.mean(residual * residual, axis=-1, keepdims=True) + EPSILON)
    unused_first, pull_first = jax.vjp(rms_norm, residual, gain_cols[:, 0])
    grad_res_first, unused_gain = pull_first(grad_attn_in)
    input_grad = (grad_after + grad_res_first).reshape(groups, piece_len, model_width)

    weight_sums = grad_sums[:, :weight_rows].astype(jnp.float32)
    qkv_grad = jnp.concatenate(
        [weight_sums[c, :, :own_width] for c in range(n_chip)]
        + [weight_sums[c, :, own_width : own_width + HEAD_DIM] for c in range(n_chip)]
        + [weight_sums[c, :, own_width + HEAD_DIM : part_width] for c in range(n_chip)],
        axis=1,
    )
    out_proj_grad = jnp.concatenate(
        [weight_sums[c, :, part_width:] for c in range(n_chip)], axis=1
    )
    gain_grad = jnp.sum(
        grad_sums[:, weight_rows : weight_rows + norm_gains.shape[1], :weight_rows].astype(
            jnp.float32
        ),
        axis=0,
    ).T
    return (layer_output, input_grad, gain_grad, qkv_grad, out_proj_grad, gate_up_grad, down_grad)


def solution(mesh):
    n_seq = mesh.shape["seq"]
    n_ctx = mesh.shape["ctx"]
    split_mesh = jax.sharding.Mesh(
        mesh.devices.reshape(n_seq, n_ctx // 2, 2), ("seq", "chip", "core")
    )
    plane = ("chip", "core")
    rows = P(("seq", "chip", "core"), None)
    tokens = P("seq", plane, None)
    placed = (
        tokens,
        rows,
        rows,
        rows,
        rows,
        rows,
        tokens,
        P("seq", None),
        P("seq", None),
        P("seq", plane),
    )

    def step(*arrays):
        groups = arrays[0].shape[0]
        if n_ctx // 2 == KV_HEADS and groups == 2 and n_seq == 4:
            return per_device_by_heads(n_seq, *arrays)
        return per_device_general(*arrays)

    return jax.shard_map(
        step,
        mesh=split_mesh,
        in_specs=placed,
        out_specs=(tokens, tokens, rows, rows, rows, rows, rows),
        check_vma=False,
    )
```

```python
from functools import partial
import math

import jax
import jax.numpy as jnp
from jax import lax
from jax.experimental import pallas as pl
from jax.experimental.pallas import tpu as pltpu
from jax.sharding import PartitionSpec as P

HEADS = 8
KV_HEADS = 4
HEAD_DIM = 256


EPSILON = 1e-06
SOFT_CAP = 50.0
MASKED = -1e30


def rms_norm(matrix, gain_col):
    factor = lax.rsqrt(jnp.mean(matrix * matrix, axis=-1, keepdims=True) + EPSILON)
    return matrix * factor * gain_col


def rotary_tables(positions, head_dim):
    half_dim = head_dim // 2
    frequency = jnp.exp(
        jnp.arange(half_dim, dtype=jnp.float32) * (-2.0 * math.log(10000.0) / head_dim)
    )
    phase_angle = positions.astype(jnp.float32)[:, None] * frequency[None, :]
    return (jnp.cos(phase_angle)[:, None, :], jnp.sin(phase_angle)[:, None, :])


def rotate(vectors, cosine, sine_part):
    half_dim = vectors.shape[-1] // 2
    first_half = vectors[..., :half_dim]
    second_half = vectors[..., half_dim:]
    return jnp.concatenate(
        [
            first_half * cosine - second_half * sine_part,
            second_half * cosine + first_half * sine_part,
        ],
        axis=-1,
    )


def rotate_back(grads, cosine, sine_part):
    half_dim = grads.shape[-1] // 2
    first_half = grads[..., :half_dim]
    second_half = grads[..., half_dim:]
    return jnp.concatenate(
        [
            first_half * cosine + second_half * sine_part,
            second_half * cosine - first_half * sine_part,
        ],
        axis=-1,
    )


def soft_probs(scaled, allowed):
    capped = SOFT_CAP * jnp.tanh(scaled / SOFT_CAP)
    capped = jnp.where(allowed, capped, MASKED)
    return jax.nn.softmax(capped, axis=-1)


def geglu_parts(gate_part, up_part):
    return jax.nn.gelu(gate_part, approximate=True) * up_part


def score_block(queries, keys_all):
    groups = keys_all.shape[0]
    seq_len = keys_all.shape[1]
    piece_len = queries.shape[0] // groups
    query_heads = queries.reshape(groups, piece_len, KV_HEADS, HEADS // KV_HEADS, HEAD_DIM)
    key_heads = keys_all.reshape(groups, seq_len, KV_HEADS, HEAD_DIM)
    raw_score = jnp.einsum(
        "spkgd,slkd->skgpl", query_heads, key_heads, preferred_element_type=jnp.float32
    )
    return raw_score * (1.0 / math.sqrt(HEAD_DIM))


def mix_values(weights_low, values_all):
    groups = values_all.shape[0]
    seq_len = values_all.shape[1]
    piece_len = weights_low.shape[3]
    value_heads = values_all.reshape(groups, seq_len, KV_HEADS, HEAD_DIM)
    mixed = jnp.einsum(
        "skgpl,slkd->spkgd", weights_low, value_heads, preferred_element_type=jnp.float32
    )
    return mixed.reshape(groups * piece_len, HEADS * HEAD_DIM).astype(jnp.bfloat16)


def add_slice(left, weight_piece):
    return jnp.dot(left, weight_piece, preferred_element_type=jnp.float32)


def times_rows(left, weight_piece):
    return lax.dot_general(
        left, weight_piece, (((1,), (1,)), ((), ())), preferred_element_type=jnp.float32
    )


def outer_rows(left, right):
    return lax.dot_general(
        left, right, (((0,), (0,)), ((), ())), preferred_element_type=jnp.float32
    )


MESH = pl.DeviceIdType.MESH
ANY = pl.BlockSpec(memory_space=pl.ANY)
DMA = pltpu.SemaphoreType.DMA


def remote(source, target, send_sem, recv_sem, device):
    return pltpu.make_async_remote_copy(
        src_ref=source,
        dst_ref=target,
        send_sem=send_sem,
        recv_sem=recv_sem,
        device_id=device,
        device_id_type=MESH,
    )


def plane_device(index):
    return {"chip": index // 2, "core": lax.rem(index, 2)}


def greet(n_plane, n_seq):
    me = lax.axis_index("chip") * 2 + lax.axis_index("core")
    barrier = pltpu.get_barrier_semaphore()
    for step in range(1, n_plane):
        pl.semaphore_signal(
            barrier,
            inc=1,
            device_id=plane_device(lax.rem(me + step, n_plane)),
            device_id_type=MESH,
        )
    count = n_plane - 1
    if n_seq > 1:
        s = lax.axis_index("seq")

        @pl.when(s > 0)
        def _():
            pl.semaphore_signal(barrier, inc=1, device_id={"seq": s - 1}, device_id_type=MESH)

        @pl.when(s < n_seq - 1)
        def _():
            pl.semaphore_signal(barrier, inc=1, device_id={"seq": s + 1}, device_id_type=MESH)

        count = count + jnp.where(s > 0, 1, 0) + jnp.where(s < n_seq - 1, 1, 0)
    pl.semaphore_wait(barrier, count)


def chip_at(q, flip):
    x, y = lax.rem(q, 2), q // 2
    x = 1 - x if flip in (1, 3) else x
    y = 1 - y if flip in (2, 3) else y
    return y * 2 + x


class Merge:
    def __init__(self, source, target, added, own_part, sems):
        self.source, self.target, self.added, self.own_part = source, target, added, own_part
        self.send_sems, self.recv_sems, self.load_sems, self.local_sems = sems
        self.q = lax.axis_index("chip")
        self.k = lax.axis_index("core")
        self.half = source.shape[1] // 2

    def rows(self, flip):
        return pl.ds(0 if flip == 1 else self.half, self.half)

    def direct(self, flip, core):
        chip = chip_at(self.q, flip)
        slot = 6 * (flip - 1) + core
        return remote(
            self.source.at[2 * chip + core, self.rows(flip)],
            self.target.at[1, self.k, self.rows(flip)],
            self.send_sems.at[slot],
            self.recv_sems.at[6 * (flip - 1) + self.k],
            {"chip": chip, "core": core},
        )

    def arrival(self, flip, core):
        return remote(
            self.source.at[0, self.rows(flip)],
            self.target.at[1, core, self.rows(flip)],
            self.send_sems.at[0],
            self.recv_sems.at[6 * (flip - 1) + core],
            {"chip": chip_at(self.q, flip)},
        )

    def across(self, flip, core):
        slot = 6 * (flip - 1) + 2 + core
        return remote(
            self.source.at[2 * chip_at(self.q, 3) + core, self.rows(flip)],
            self.added.at[flip - 1, core],
            self.send_sems.at[slot],
            self.recv_sems.at[slot],
            {"chip": chip_at(self.q, flip)},
        )

    def load(self, flip, core):
        return pltpu.make_async_copy(
            self.source.at[2 * chip_at(self.q, 3 - flip) + core, self.rows(flip)],
            self.own_part.at[flip - 1, core],
            self.load_sems.at[flip - 1, core],
        )

    def summed(self, flip, core):
        slot = 6 * (flip - 1) + 4 + core
        return remote(
            self.own_part.at[flip - 1, core],
            self.target.at[2, self.k, self.rows(flip)],
            self.send_sems.at[slot],
            self.recv_sems.at[6 * (flip - 1) + 4 + self.k],
            {"chip": chip_at(self.q, 3 - flip), "core": core},
        )

    def summed_arrival(self, flip, core):
        return remote(
            self.own_part.at[flip - 1, 0],
            self.target.at[2, core, self.rows(flip)],
            self.send_sems.at[0],
            self.recv_sems.at[6 * (flip - 1) + 4 + core],
            {"chip": chip_at(self.q, 3 - flip)},
        )

    def twin(self):
        return remote(
            self.source.at[2 * self.q + 1 - self.k],
            self.target.at[0, self.k],
            self.send_sems.at[12],
            self.recv_sems.at[12],
            {"core": 1 - self.k},
        )

    def twin_arrival(self):
        return remote(
            self.source.at[0],
            self.target.at[0, 1 - self.k],
            self.send_sems.at[12],
            self.recv_sems.at[12],
            {"core": 1 - self.k},
        )

    def own(self):
        return pltpu.make_async_copy(
            self.source.at[2 * self.q + self.k], self.target.at[0, self.k], self.local_sems.at[0]
        )

    def start(self):
        pairs = [(flip, core) for core in (0, 1) for flip in (1, 2)]
        for flip, core in pairs:
            self.across(flip, core).start()
        for flip, core in pairs:
            self.load(flip, core).start()
        for flip, core in pairs:
            self.direct(flip, core).start()
        self.twin().start()
        self.own().start()

    def pass_on(self):
        step = 16
        for core in (0, 1):
            for flip in (1, 2):
                self.load(flip, core).wait()
                self.across(flip, core).wait_recv()

                def body(i, carry, flip=flip, core=core):
                    rows = pl.ds(pl.multiple_of(i * step, step), step)
                    total = self.own_part[flip - 1, core, rows, :].astype(jnp.float32)
                    total = total + self.added[flip - 1, core, rows, :].astype(jnp.float32)
                    self.own_part[flip - 1, core, rows, :] = total.astype(self.own_part.dtype)
                    return carry

                lax.fori_loop(0, self.half // step, body, 0)
                self.summed(flip, core).start()

    def finish(self):
        for core in (0, 1):
            for flip in (1, 2):
                self.across(flip, core).wait_send()
                self.direct(flip, core).wait_send()
                self.arrival(flip, core).wait_recv()
                self.summed(flip, core).wait_send()
                self.summed_arrival(flip, core).wait_recv()
        self.twin().wait_send()
        self.twin_arrival().wait_recv()
        self.own().wait()


def merge_scratch(blocks):
    part = (2, 2, blocks.shape[1] // 2, blocks.shape[2])
    return [
        pltpu.VMEM(part, blocks.dtype),
        pltpu.VMEM(part, blocks.dtype),
        DMA((13,)),
        DMA((13,)),
        DMA((2, 2)),
        DMA((1,)),
    ]


def merged_shape(blocks):
    return jax.ShapeDtypeStruct((3, 2) + blocks.shape[1:], blocks.dtype)


class Spread:
    def __init__(self, source, target, send_sems, recv_sems, local_sem):
        self.source, self.target = source, target
        self.send_sems, self.recv_sems = send_sems, recv_sems
        self.local_sem = local_sem
        self.q = lax.axis_index("chip")
        self.k = lax.axis_index("core")
        self.half = source.shape[1] // 2

    def chip(self, flip):
        return chip_at(self.q, flip)

    def direct(self, flip, twin):
        core = 1 - self.k if twin else self.k
        slot = 2 * flip + twin
        return remote(
            self.source.at[core],
            self.target.at[2 * self.q + self.k],
            self.send_sems.at[slot],
            self.recv_sems.at[slot],
            {"chip": self.chip(flip), "core": core},
        )

    def passed(self, flip, twin):
        core = 1 - self.k if twin else self.k
        slot = 8 + 2 * (flip - 1) + twin
        rows = pl.ds(0 if flip == 1 else self.half, self.half)
        block = self.target.at[2 * self.chip(flip) + core, rows]
        return remote(
            block,
            block,
            self.send_sems.at[slot],
            self.recv_sems.at[slot],
            {"chip": self.chip(3 - flip)},
        )

    def own(self):
        return pltpu.make_async_copy(
            self.source.at[self.k],
            self.target.at[2 * self.q + self.k],
            self.local_sem.at[0],
        )

    def start(self):
        for twin in (0, 1):
            for flip in (1, 2):
                self.direct(flip, twin).start()
        self.direct(0, 1).start()
        self.own().start()

    def pass_on(self):
        for twin in (0, 1):
            for flip in (1, 2):
                self.direct(flip, twin).wait_recv()
                self.passed(flip, twin).start()

    def finish(self):
        for twin in (0, 1):
            for flip in (1, 2):
                self.passed(flip, twin).wait()
                self.direct(flip, twin).wait_send()
        self.direct(0, 1).wait()
        self.own().wait()


SPREAD_SLOTS = 12


def merge_kernel(n_plane, source, rows_x, rows_y, target, across, added, own_part, *sems):
    greet(n_plane, 1)
    merge = Merge(source, target, added, own_part, sems[:4])
    pass_send, pass_recv = sems[4:]
    merge.start()
    half = rows_x.shape[0] // 2
    passed = [
        remote(
            rows.at[pl.ds(i * half, half)],
            across.at[i],
            pass_send.at[i],
            pass_recv.at[i],
            {"chip": chip_at(merge.q, 2 - i)},
        )
        for i, rows in enumerate((rows_x, rows_y))
    ]
    for copy in passed:
        copy.start()
    merge.pass_on()
    merge.finish()
    for copy in passed:
        copy.wait()


def merge_plane(blocks, rows_x, rows_y, collective_id):
    half = (2, rows_x.shape[0] // 2, rows_x.shape[1])
    return pl.pallas_call(
        partial(merge_kernel, 2 * KV_HEADS),
        out_shape=[merged_shape(blocks), jax.ShapeDtypeStruct(half, rows_x.dtype)],
        in_specs=[ANY] * 3,
        out_specs=[ANY] * 2,
        scratch_shapes=merge_scratch(blocks) + [DMA((2,)), DMA((2,))],
        compiler_params=pltpu.CompilerParams(
            collective_id=collective_id, has_side_effects=True
        ),
    )(blocks, rows_x, rows_y)


def spread_kernel(
    n_plane,
    blocks,
    low_gate,
    low_up,
    tokens,
    target,
    grads,
    left,
    right,
    tile,
    send_sems,
    recv_sems,
    local_sem,
    load_sem,
    row_sem,
    tile_sem,
):
    greet(n_plane, 1)
    spread = Spread(blocks, target, send_sems, recv_sems, local_sem)
    spread.start()
    n_units, unit_rows, units = low_gate.shape
    width = right.shape[1]
    piece_len = tokens.shape[3]
    loads = []
    for i, source in enumerate((low_gate, low_up)):
        for u in range(n_units):
            place = left.at[i, pl.ds(u * unit_rows, unit_rows)]
            loads.append(pltpu.make_async_copy(source.at[u], place, load_sem.at[i, u]))
    for u in range(n_units):
        for half in range(2):
            place = right.at[pl.ds(u * unit_rows + half * piece_len, piece_len)]
            source = tokens.at[u // 2, u % 2, half]
            loads.append(pltpu.make_async_copy(source, place, row_sem.at[u, half]))
    for load in loads:
        load.start()
    for load in loads:
        load.wait()
    row_tile, col_tile = units // 3, width // 3

    def tile_store(i, r, c, slot):
        rows = pl.ds(pl.multiple_of(r * row_tile, 16), row_tile)
        cols = pl.ds(pl.multiple_of(i * width + c * col_tile, 128), col_tile)
        return pltpu.make_async_copy(tile.at[slot], grads.at[rows, cols], tile_sem.at[slot])

    def one_tile(j, carry):
        i, slot = lax.div(j, 9), lax.rem(j, 2)
        r, c = lax.div(lax.rem(j, 9), 3), lax.rem(j, 3)
        rows = pl.ds(pl.multiple_of(r * row_tile, 128), row_tile)
        cols = pl.ds(pl.multiple_of(c * col_tile, 128), col_tile)
        total = outer_rows(left[i, :, rows], right[:, cols])

        @pl.when(j >= 2)
        def _():
            tile_store(i, r, c, slot).wait()

        tile[slot] = total.astype(tile.dtype)
        tile_store(i, r, c, slot).start()
        return carry

    lax.fori_loop(0, PASS_TURN, one_tile, 0)
    spread.pass_on()
    lax.fori_loop(PASS_TURN, 18, one_tile, 0)
    for slot in range(2):
        tile_store(0, 0, 0, slot).wait()
    spread.finish()


PASS_TURN = 14


def spread_plane(blocks, low_gate, low_up, tokens):
    n_plane = 2 * KV_HEADS
    low = blocks.dtype
    n_units, unit_rows, units = low_gate.shape
    width = blocks.shape[2]
    return pl.pallas_call(
        partial(spread_kernel, n_plane),
        out_shape=[
            jax.ShapeDtypeStruct((n_plane,) + blocks.shape[1:], low),
            jax.ShapeDtypeStruct((units, 2 * width), low),
        ],
        in_specs=[ANY] * 4,
        out_specs=[ANY, ANY],
        scratch_shapes=[
            pltpu.VMEM((2, n_units * unit_rows, units), low),
            pltpu.VMEM((n_units * unit_rows, width), low),
            pltpu.VMEM((2, units // 3, width // 3), low),
            DMA((SPREAD_SLOTS,)),
            DMA((SPREAD_SLOTS,)),
            DMA((1,)),
            DMA((2, n_units)),
            DMA((n_units, 2)),
            DMA((2,)),
        ],
        compiler_params=pltpu.CompilerParams(
            collective_id=3, has_side_effects=True, vmem_limit_bytes=48 * 1024 * 1024
        ),
    )(blocks, low_gate, low_up, tokens)


def gather_kernel(
    n_seq,
    n_plane,
    hidden,
    blocks,
    hidden_all,
    blocks_all,
    hid_send,
    hid_recv,
    hid_local,
    chip_send,
    chip_recv,
    chip_local,
    left_send,
    right_send,
    line_recv,
    twin_send,
    twin_recv,
):
    n_chip = n_plane // 2
    s = lax.axis_index("seq")
    q = lax.axis_index("chip")
    k = lax.axis_index("core")
    greet(n_plane, n_seq)
    swaps = []
    for step in range(1, n_chip):
        to = lax.rem(q + step, n_chip)
        copy = remote(
            blocks.at[to],
            blocks_all.at[s, k, q],
            chip_send.at[step],
            chip_recv.at[step],
            {"chip": to},
        )
        copy.start()
        swaps.append(copy)
    own = pltpu.make_async_copy(blocks.at[q], blocks_all.at[s, k, q], chip_local.at[0])
    own.start()
    spread = Spread(hidden, hidden_all, hid_send, hid_recv, hid_local)
    for copy in swaps:
        copy.wait_recv()
    own.wait()
    spread.start()

    def to_left(d):
        return remote(
            blocks_all.at[d, k], blocks_all.at[d, k], left_send.at[d], line_recv.at[d], {"seq": s - 1}
        )

    def to_right(d):
        return remote(
            blocks_all.at[d, k], blocks_all.at[d, k], right_send.at[d], line_recv.at[d], {"seq": s + 1}
        )

    def to_twin(d):
        return remote(
            blocks_all.at[d, k], blocks_all.at[d, k], twin_send.at[d], twin_recv.at[d], {"core": 1 - k}
        )

    def from_twin(d):
        return remote(
            blocks_all.at[d, 1 - k],
            blocks_all.at[d, 1 - k],
            twin_send.at[d],
            twin_recv.at[d],
            {"core": 1 - k},
        )

    @pl.when(s > 0)
    def _():
        to_left(s).start()

    @pl.when(s < n_seq - 1)
    def _():
        to_right(s).start()

    to_twin(s).start()
    for hop in range(1, n_seq):
        if hop == 2:
            spread.pass_on()
        from_left = s - hop
        from_right = s + hop

        @pl.when(from_left >= 0)
        def _():
            to_left(from_left).wait_recv()

            @pl.when(s < n_seq - 1)
            def _():
                to_right(from_left).start()

            to_twin(from_left).start()

        @pl.when(from_right < n_seq)
        def _():
            to_right(from_right).wait_recv()

            @pl.when(s > 0)
            def _():
                to_left(from_right).start()

            to_twin(from_right).start()

    for d in range(n_seq):

        @pl.when((d >= s) & (s > 0))
        def _():
            to_left(d).wait_send()

        @pl.when((d <= s) & (s < n_seq - 1))
        def _():
            to_right(d).wait_send()

        to_twin(d).wait_send()
        from_twin(d).wait_recv()
    for copy in swaps:
        copy.wait_send()
    spread.finish()


def gather_first(n_seq, hidden, blocks):
    n_plane = 2 * KV_HEADS
    n_chip = KV_HEADS
    return pl.pallas_call(
        partial(gather_kernel, n_seq, n_plane),
        out_shape=[
            jax.ShapeDtypeStruct((n_plane,) + hidden.shape[1:], hidden.dtype),
            jax.ShapeDtypeStruct((n_seq, 2) + blocks.shape, blocks.dtype),
        ],
        in_specs=[ANY, ANY],
        out_specs=[ANY, ANY],
        scratch_shapes=[
            DMA((SPREAD_SLOTS,)),
            DMA((SPREAD_SLOTS,)),
            DMA((1,)),
            DMA((n_chip,)),
            DMA((n_chip,)),
            DMA((1,)),
            DMA((n_seq,)),
            DMA((n_seq,)),
            DMA((n_seq,)),
            DMA((n_seq,)),
            DMA((n_seq,)),
        ],
        compiler_params=pltpu.CompilerParams(collective_id=1, has_side_effects=True),
    )(hidden, blocks)


def last_kernel(
    n_seq,
    n_plane,
    parts,
    blocks,
    parts_all,
    sums,
    held,
    twin,
    line,
    part_added,
    part_own,
    part_send,
    part_recv,
    part_load,
    part_local,
    held_sem,
    twin_send,
    twin_recv,
    line_send,
    line_recv,
    chip_send,
    chip_recv,
    chip_local,
):
    n_chip = n_plane // 2
    s = lax.axis_index("seq")
    q = lax.axis_index("chip")
    k = lax.axis_index("core")
    greet(n_plane, n_seq)

    def load(d):
        return pltpu.make_async_copy(blocks.at[d, k], held.at[d], held_sem.at[d])

    def to_twin(d):
        return remote(
            blocks.at[d, 1 - k], twin.at[d], twin_send.at[d], twin_recv.at[d], {"core": 1 - k}
        )

    def to_left(d):
        return remote(held.at[d], line.at[d], line_send.at[d], line_recv.at[d], {"seq": s - 1})

    def to_right(d):
        return remote(
            held.at[d], line.at[d + 1], line_send.at[d], line_recv.at[d + 1], {"seq": s + 1}
        )

    def gather_terms(d, with_left, with_right):
        load(d).wait()
        to_twin(d).wait_recv()

        @pl.when(with_right)
        def _():
            to_left(d).wait_recv()

        @pl.when(with_left)
        def _():
            to_right(d).wait_recv()

        def body(i, carry):
            held[d, i] = (held[d, i].astype(jnp.float32) + twin[d, i].astype(jnp.float32)).astype(
                held.dtype
            )
            return carry

        def body_right(i, carry):
            total = held[d, i].astype(jnp.float32) + twin[d, i].astype(jnp.float32)
            held[d, i] = (total + line[d, i].astype(jnp.float32)).astype(held.dtype)
            return carry

        def body_left(i, carry):
            total = held[d, i].astype(jnp.float32) + twin[d, i].astype(jnp.float32)
            held[d, i] = (total + line[d + 1, i].astype(jnp.float32)).astype(held.dtype)
            return carry

        def body_both(i, carry):
            total = held[d, i].astype(jnp.float32) + twin[d, i].astype(jnp.float32)
            total = total + line[d, i].astype(jnp.float32)
            held[d, i] = (total + line[d + 1, i].astype(jnp.float32)).astype(held.dtype)
            return carry

        @pl.when(jnp.logical_not(with_left) & jnp.logical_not(with_right))
        def _():
            lax.fori_loop(0, n_chip, body, 0)

        @pl.when(jnp.logical_not(with_left) & with_right)
        def _():
            lax.fori_loop(0, n_chip, body_right, 0)

        @pl.when(with_left & jnp.logical_not(with_right))
        def _():
            lax.fori_loop(0, n_chip, body_left, 0)

        @pl.when(with_left & with_right)
        def _():
            lax.fori_loop(0, n_chip, body_both, 0)

    for d in range(n_seq):
        to_twin(d).start()
        load(d).start()
    part_sems = (part_send, part_recv, part_load, part_local)
    merge = Merge(parts, parts_all, part_added, part_own, part_sems)
    merge.start()
    never = s < 0
    for hop in range(1, n_seq):
        if hop == 2:
            merge.pass_on()
        left = hop - n_seq + s
        right = n_seq - hop + s

        @pl.when(left >= 0)
        def _():
            gather_terms(left, never, s < n_seq - 1)
            to_left(left).start()

        @pl.when(right <= n_seq - 1)
        def _():
            gather_terms(right, s > 0, never)
            to_right(right).start()

    gather_terms(s, s > 0, s < n_seq - 1)
    swaps = []
    for step in range(1, n_chip):
        to = lax.rem(q + step, n_chip)
        copy = remote(
            held.at[s, to], sums.at[q], chip_send.at[step], chip_recv.at[step], {"chip": to}
        )
        copy.start()
        swaps.append(copy)
    own = pltpu.make_async_copy(held.at[s, q], sums.at[q], chip_local.at[0])
    own.start()
    for d in range(n_seq):
        to_twin(d).wait_send()

        @pl.when(d < s)
        def _():
            to_left(d).wait_send()

        @pl.when(d > s)
        def _():
            to_right(d).wait_send()

    merge.finish()
    for copy in swaps:
        copy.wait()
    own.wait()


def sum_last(n_seq, parts, blocks):
    n_plane = 2 * KV_HEADS
    n_chip = KV_HEADS
    block = blocks.shape[2:]
    return pl.pallas_call(
        partial(last_kernel, n_seq, n_plane),
        out_shape=[
            merged_shape(parts),
            jax.ShapeDtypeStruct(block, blocks.dtype),
        ],
        in_specs=[ANY, ANY],
        out_specs=[ANY, ANY],
        scratch_shapes=[
            pltpu.VMEM((n_seq,) + block, blocks.dtype),
            pltpu.VMEM((n_seq,) + block, blocks.dtype),
            pltpu.VMEM((n_seq + 1,) + block, blocks.dtype),
            *merge_scratch(parts),
            DMA((n_seq,)),
            DMA((n_seq,)),
            DMA((n_seq,)),
            DMA((n_seq,)),
            DMA((n_seq + 1,)),
            DMA((n_chip,)),
            DMA((n_chip,)),
            DMA((1,)),
        ],
        compiler_params=pltpu.CompilerParams(
            collective_id=4, has_side_effects=True, vmem_limit_bytes=32 * 1024 * 1024
        ),
    )(parts, blocks)


QUERY_BLOCK = 256


def block_probs(query, keys, segment_col, segment_row, first):
    rows, width = query.shape[0], keys.shape[0]
    scaled = times_rows(query, keys) * (1.0 / math.sqrt(HEAD_DIM))
    bent = jnp.tanh(scaled / SOFT_CAP)
    row = first + lax.broadcasted_iota(jnp.int32, (rows, width), 0)
    col = lax.broadcasted_iota(jnp.int32, (rows, width), 1)
    allowed = ((segment_col == segment_row) & (col <= row)) | (col == row)
    capped = jnp.where(allowed, SOFT_CAP * bent, MASKED)
    raised = jnp.exp(capped - jnp.max(capped, axis=-1, keepdims=True))
    return raised / jnp.sum(raised, axis=-1, keepdims=True), bent


def attend_kernel(group_size, queries, keys, values, segment_col, segment_row, out):
    seq_len = keys.shape[0]
    for first in range(0, seq_len, QUERY_BLOCK):
        rows = slice(first, first + QUERY_BLOCK)
        width = first + QUERY_BLOCK
        for head in range(group_size):
            cols = slice(head * HEAD_DIM, (head + 1) * HEAD_DIM)
            probs, unused = block_probs(
                queries[rows, cols],
                keys[:width],
                segment_col[rows, :],
                segment_row[:, :width],
                first,
            )
            out[rows, cols] = add_slice(probs.astype(jnp.bfloat16), values[:width]).astype(
                out.dtype
            )


def attend(queries, keys, values, segment_col, segment_row):
    return pl.pallas_call(
        partial(attend_kernel, queries.shape[1] // HEAD_DIM),
        out_shape=jax.ShapeDtypeStruct(queries.shape, jnp.bfloat16),
        compiler_params=pltpu.CompilerParams(vmem_limit_bytes=40 * 1024 * 1024),
    )(queries, keys, values, segment_col, segment_row)


def turn_back(grads, cosine, sine_part):
    half = grads.shape[1] // 2
    first, second = grads[:, :half], grads[:, half:]
    return jnp.concatenate(
        [first * cosine + second * sine_part, second * cosine - first * sine_part], axis=1
    )


def attend_back_kernel(
    group_size,
    queries,
    keys,
    values,
    segment_col,
    segment_row,
    grads,
    cosine,
    sine_part,
    out,
    grad_keys,
    grad_values,
):
    seq_len = keys.shape[0]
    inverse_root = 1.0 / math.sqrt(HEAD_DIM)
    key_cols = slice(group_size * HEAD_DIM, (group_size + 1) * HEAD_DIM)
    value_cols = slice((group_size + 1) * HEAD_DIM, (group_size + 2) * HEAD_DIM)
    grad_keys[...] = jnp.zeros_like(grad_keys)
    grad_values[...] = jnp.zeros_like(grad_values)
    for first in range(0, seq_len, QUERY_BLOCK):
        rows = slice(first, first + QUERY_BLOCK)
        width = first + QUERY_BLOCK
        for head in range(group_size):
            cols = slice(head * HEAD_DIM, (head + 1) * HEAD_DIM)
            query = queries[rows, cols]
            probs, bent = block_probs(
                query, keys[:width], segment_col[rows, :], segment_row[:, :width], first
            )
            grad = grads[rows, cols]
            grad_probs = times_rows(grad, values[:width])
            mean = jnp.sum(probs * grad_probs, axis=-1, keepdims=True)
            grad_scaled = (probs * (grad_probs - mean) * (1.0 - bent * bent)).astype(jnp.bfloat16)
            grad_query = add_slice(grad_scaled, keys[:width]) * inverse_root
            out[rows, cols] = turn_back(grad_query, cosine[rows, :], sine_part[rows, :]).astype(
                out.dtype
            )
            grad_keys[:width, :] += outer_rows(grad_scaled, query) * inverse_root
            grad_values[:width, :] += outer_rows(probs.astype(jnp.bfloat16), grad)
    for first in range(0, seq_len, QUERY_BLOCK):
        rows = slice(first, first + QUERY_BLOCK)
        out[rows, key_cols] = turn_back(
            grad_keys[rows, :], cosine[rows, :], sine_part[rows, :]
        ).astype(out.dtype)
        out[rows, value_cols] = grad_values[rows, :].astype(out.dtype)


def attend_back(queries, keys, values, segment_col, segment_row, grads, cosine, sine_part):
    seq_len, own_width = queries.shape
    return pl.pallas_call(
        partial(attend_back_kernel, own_width // HEAD_DIM),
        out_shape=jax.ShapeDtypeStruct((seq_len, own_width + 2 * HEAD_DIM), jnp.bfloat16),
        scratch_shapes=[
            pltpu.VMEM((seq_len, HEAD_DIM), jnp.float32),
            pltpu.VMEM((seq_len, HEAD_DIM), jnp.float32),
        ],
        compiler_params=pltpu.CompilerParams(vmem_limit_bytes=40 * 1024 * 1024),
    )(queries, keys, values, segment_col, segment_row, grads, cosine, sine_part)


def weight_blocks_kernel(weight_rows, inputs, grads, grad_outs, outs, gains, blocks):
    n_first, n_core, n_chip, block_rows = blocks.shape[:4]
    columns = outs.shape[1]
    for c in range(blocks.shape[4] // columns):
        cols = slice(c * columns, (c + 1) * columns)
        if c * columns < grads.shape[1]:
            total = outer_rows(inputs[...], grads[:, cols])
        else:
            total = outer_rows(grad_outs[...], outs[...])
        for d in range(n_first):
            for q in range(n_chip):
                for core in range(n_core):
                    b = (d * n_chip + q) * n_core + core
                    part = total[b * weight_rows : (b + 1) * weight_rows]
                    part = jnp.concatenate([part, gains[b, :, cols]], axis=0)
                    blocks[d, core, q, :, cols] = part.astype(blocks.dtype)


def weight_blocks(n_seq, inputs, grads, grad_outs, outs, gains):
    seq_len, model_width = inputs.shape
    n_blocks, extra_rows, block_width = gains.shape
    weight_rows = model_width // n_blocks
    steps = 2
    part = model_width // steps
    block = (n_seq // steps, 2, KV_HEADS, weight_rows + extra_rows, block_width)
    whole = lambda i: (0, 0)
    return pl.pallas_call(
        partial(weight_blocks_kernel, weight_rows),
        grid=(steps,),
        out_shape=jax.ShapeDtypeStruct((n_seq,) + block[1:], jnp.bfloat16),
        in_specs=[
            pl.BlockSpec((seq_len, part), lambda i: (0, i)),
            pl.BlockSpec(grads.shape, whole),
            pl.BlockSpec((seq_len, part), lambda i: (0, i)),
            pl.BlockSpec(outs.shape, whole),
            pl.BlockSpec((n_blocks // steps, extra_rows, block_width), lambda i: (i, 0, 0)),
        ],
        out_specs=pl.BlockSpec(block, lambda i: (i, 0, 0, 0, 0)),
        compiler_params=pltpu.CompilerParams(vmem_limit_bytes=56 * 1024 * 1024),
    )(inputs, grads, grad_outs, outs, gains)


def chip_beside(c, flip):
    return c ^ flip


LATE = 3
LATE_COLUMNS = 2


def chip_places(rows, late_rows):
    q = lax.axis_index("chip")
    x, y = lax.rem(q, 2), lax.div(q, 2)
    across = (2 * (1 - y) + 1 - x) * rows
    half = (rows - late_rows) // 2
    return (q * rows, (2 * y + 1 - x) * rows, (2 * (1 - y) + x) * rows, across, across + half)


def send_beside(part, flip):
    return lax.ppermute(part, "chip", [(c, chip_beside(c, flip)) for c in range(KV_HEADS)])


def unit_orders(n):
    units, sums = [], []
    for s in range(n):
        keyed = []
        for d in range(n):
            if d != s:
                near = abs(s - d)
                behind, past = (s, d) if d < s else (n - 1 - s, n - 1 - d)
                keyed += [(near, d, 0), (behind + past + 1, d, 1)]
        order = [(s, 0), (s, 1)] + [(d, h) for unused, d, h in sorted(keyed)]
        units.append([2 * d + h for d, h in order])
        if s in (0, n - 1):
            sums.append(units[-1][2:])
            continue
        keyed = []
        for d in range(n):
            if d != s:
                hops, place = (n - 2 - s, d) if d < s else (s - 1, n - 1 - d)
                keyed += [(n - 2 - place + hops, d, 0), (n - 1 + place + hops, d, 1)]
        sums.append([2 * d + h for unused, d, h in sorted(keyed)])
    return units, sums


def pick(table, s, i):
    width = len(table[0])
    place = s * width + i
    value = 0
    for k, entry in enumerate(entry for row in table for entry in row):
        value = jnp.where(place == k, entry, value)
    return value


SUBS = 1
SUM_TURNS = (0, 1, 4, 5, 8, 8)
GELU_SCALE = math.sqrt(2.0 / math.pi)


def gelu_pieces(gate):
    bend = jnp.tanh(GELU_SCALE * (gate + 0.044715 * gate * gate * gate))
    value = 0.5 * gate * (1.0 + bend)
    slope = 0.5 * (1.0 + bend) + 0.5 * gate * (1.0 - bend * bend) * GELU_SCALE * (
        1.0 + 3.0 * 0.044715 * gate * gate
    )
    return value, slope


def units_kernel(n_seq, backward, *refs):
    if backward:
        tokens, units = refs[:2]
        downs, late = refs[2:7], refs[7]
        kept_gate, kept_up, kept_hidden = refs[8:11]
        out, first_out, second_out, early_grads = refs[11:15]
        late_grads = refs[15 : 15 + LATE_COLUMNS]
        late_parts = refs[15 + LATE_COLUMNS : 15 + 2 * LATE_COLUMNS]
        stage_outs = (first_out, second_out)
        scratch = refs[15 + 2 * LATE_COLUMNS :]
    else:
        tokens, units = refs[:2]
        downs = refs[2:7]
        out, tokens_all, late, first_out, second_out, third_out = refs[7:13]
        stage_outs = (first_out, second_out, third_out)
        scratch = refs[13:]
    units_v, downs_v, held, own_sum, twin_sum, twin_out, line, stage = scratch[:8]
    scratch = scratch[8:]
    if backward:
        kept, kept_sem, tile, tile_sem, load_sem = scratch[:5]
        scratch = scratch[5:]
    else:
        own_hidden = scratch[0]
        scratch = scratch[1:]
    late_send, late_recv = scratch[:2]
    scratch = scratch[2:]
    (
        weight_sem,
        late_sem,
        own_sem,
        left_send,
        right_send,
        token_recv,
        twin_send,
        twin_recv,
        part_send,
        part_recv,
        line_send,
        line_recv,
        stage_sem,
        all_sem,
        out_sem,
    ) = scratch
    n = n_seq
    s = lax.axis_index("seq")
    k = lax.axis_index("core")
    twin = {"core": 1 - k}
    n_units, width = downs_v.shape
    piece_len = tokens.shape[1]
    at_end = (s == 0) | (s == n - 1)

    def token_left(d, h, source):
        return remote(
            source, held.at[d, h, 0], left_send.at[d, h], token_recv.at[d, h], {"seq": s - 1}
        )

    def token_right(d, h, source):
        return remote(
            source, held.at[d, h, 0], right_send.at[d, h], token_recv.at[d, h], {"seq": s + 1}
        )

    def token_twin(d, h, source):
        return remote(source, held.at[d, h, 1], twin_send.at[d, h], twin_recv.at[d, h], twin)

    def part_twin(d, h):
        return remote(
            twin_out.at[d, h], twin_sum.at[d, h], part_send.at[d, h], part_recv.at[d, h], twin
        )

    sub_len = piece_len // SUBS

    def part_line(d, h, sub):
        to_left = d < s
        slot = jnp.where(to_left, d, d + 1)
        rows = pl.ds(sub * sub_len, sub_len)
        return remote(
            twin_sum.at[d, h, rows],
            line.at[slot, h, rows],
            line_send.at[d, h, sub],
            line_recv.at[slot, h, sub],
            {"seq": jnp.where(to_left, s - 1, s + 1)},
        )

    def line_arrival(slot, h, sub):
        rows = pl.ds(sub * sub_len, sub_len)
        return remote(
            twin_sum.at[0, h, rows],
            line.at[slot, h, rows],
            line_send.at[0, h, sub],
            line_recv.at[slot, h, sub],
            {"seq": s},
        )

    def own_load(h):
        return pltpu.make_async_copy(tokens.at[h], held.at[s, h, 0], own_sem.at[h])

    def all_store(d, h):
        return pltpu.make_async_copy(held.at[d, h], tokens_all.at[d, h], all_sem.at[d, h])

    def stage_store(i, d, h, slot):
        return pltpu.make_async_copy(
            stage.at[i, slot], stage_outs[i].at[2 * d + h], stage_sem.at[i, slot]
        )

    def kept_load(i, d, h, slot):
        source = (kept_gate, kept_up)[i]
        return pltpu.make_async_copy(source.at[2 * d + h], kept.at[i, slot], kept_sem.at[i, slot])

    unit_table, sum_table = unit_orders(n)
    right_table = [
        [2 if d == 0 else unit_table[d].index(2 * (d - 1) + 1) + 1 for d in range(n)]
    ]
    left_table = [
        [2 if d == n - 1 else unit_table[d].index(2 * (d + 1) + 1) + 1 for d in range(n)]
    ]

    def source(t):
        unit = pick(unit_table, s, t)
        return lax.div(unit, 2), lax.rem(unit, 2)

    barrier = pltpu.get_barrier_semaphore()
    pl.semaphore_signal(barrier, inc=1, device_id=twin, device_id_type=MESH)

    @pl.when(s > 0)
    def _():
        pl.semaphore_signal(barrier, inc=1, device_id={"seq": s - 1}, device_id_type=MESH)

    @pl.when(s < n - 1)
    def _():
        pl.semaphore_signal(barrier, inc=1, device_id={"seq": s + 1}, device_id_type=MESH)

    greeted = 1 + jnp.where(s > 0, 1, 0) + jnp.where(s < n - 1, 1, 0)
    n_chip, late_rows = late.shape[:2]
    chip_rows = n_units // n_chip
    q = lax.axis_index("chip")
    for step in range(1, n_chip):
        pl.semaphore_signal(
            barrier,
            inc=1,
            device_id={"chip": lax.rem(q + step, n_chip)},
            device_id_type=MESH,
        )
    pl.semaphore_wait(barrier, greeted + n_chip - 1)

    def late_place(chip):
        first = chip * chip_rows + chip_rows - late_rows
        return downs_v.at[pl.ds(pl.multiple_of(first, 16), late_rows)]

    def late_copy(step):
        return remote(
            downs[0].at[pl.ds(chip_rows - late_rows, late_rows)],
            late_place(q),
            late_send.at[step],
            late_recv.at[step],
            {"chip": lax.rem(q + step, n_chip)},
        )

    def late_grad(i, step):
        chip = lax.rem(q + step, n_chip)
        return remote(
            late_grads[i].at[pl.ds(pl.multiple_of(chip * chip_rows, 16), chip_rows)],
            late_parts[i].at[q],
            late_send.at[n_chip * i + step],
            late_recv.at[n_chip * i + step],
            {"chip": chip},
        )

    def late_store(chip):
        return pltpu.make_async_copy(late_place(chip), late.at[chip], late_sem.at[chip])

    def late_load(chip):
        return pltpu.make_async_copy(late.at[chip], late_place(chip), late_sem.at[chip])

    def second_half(t):
        @pl.when((s < n - 1) & (t == pick(right_table, 0, s)))
        def _():
            d, h = jnp.maximum(s - 1, 0), jnp.where(s > 0, 1, 0)
            token_right(d, h, held.at[d, h, 0]).wait_send()
            token_right(s, 1, tokens.at[1]).start()

        @pl.when((s > 0) & (t == pick(left_table, 0, s)))
        def _():
            d, h = jnp.minimum(s + 1, n - 1), jnp.where(s < n - 1, 1, 0)
            token_left(d, h, held.at[d, h, 0]).wait_send()
            token_left(s, 1, tokens.at[1]).start()

    @pl.when(s < n - 1)
    def _():
        token_right(s, 0, tokens.at[0]).start()

    @pl.when(s > 0)
    def _():
        token_left(s, 0, tokens.at[0]).start()

    for h in range(2):
        token_twin(s, h, tokens.at[h]).start()
        own_load(h).start()
    load_units = pltpu.make_async_copy(units, units_v, weight_sem.at[0])
    load_downs = []
    for i, (first, part) in enumerate(zip(chip_places(chip_rows, late_rows), downs)):
        count = chip_rows - late_rows if i == 0 and backward else part.shape[0]
        load_downs.append(
            pltpu.make_async_copy(
                part.at[pl.ds(0, count)],
                downs_v.at[pl.ds(pl.multiple_of(first, 16), count)],
                weight_sem.at[1 + i],
            )
        )
    if backward:
        load_downs += [late_load(chip) for chip in range(n_chip)]
    else:
        for step in (2, 1, 3):
            late_copy(step).start()
    load_units.start()
    for load in load_downs:
        load.start()
    if backward:
        for i in range(2):
            kept_load(i, s, 0, 0).start()
    load_units.wait()
    for load in load_downs:
        load.wait()

    def add_rows(d, h, sub, into_own, use_line):
        step = 16

        def body(i, carry):
            rows = pl.ds(pl.multiple_of(sub * sub_len + i * step, step), step)
            total = own_sum[d, h, rows, :] + twin_sum[d, h, rows, :].astype(jnp.float32)
            for slot in use_line:
                total = total + line[slot, h, rows, :].astype(jnp.float32)
            if into_own:
                own_sum[d, h, rows, :] = total
            else:
                twin_sum[d, h, rows, :] = total.astype(twin_sum.dtype)
            return carry

        lax.fori_loop(0, sub_len // step, body, 0)

    def combine(d, h):
        to_left = d < s
        slot = jnp.where(to_left, d, d + 1)
        more = jnp.where(to_left, s < n - 1, s > 0)
        part_twin(d, h).wait_recv()

        @pl.when(more)
        def _():
            for sub in range(SUBS):
                line_arrival(slot, h, sub).wait_recv()
                add_rows(d, h, sub, False, (slot,))
                part_line(d, h, sub).start()

        @pl.when(jnp.logical_not(more))
        def _():
            for sub in range(SUBS):
                add_rows(d, h, sub, False, ())
                part_line(d, h, sub).start()

    columns = width // 3
    chunk = n_units // 3

    def hidden_forward(d, h, slot):
        rows = held[d, h].reshape(2 * piece_len, width)
        for c in range(3):
            cols = slice(c * chunk, (c + 1) * chunk)
            gate = times_rows(rows, units_v[cols, :width])
            up = times_rows(rows, units_v[cols, width:])
            value, unused = gelu_pieces(gate)
            stage[0, slot, :, cols] = gate.astype(stage.dtype)
            stage[1, slot, :, cols] = up.astype(stage.dtype)
            stage[2, slot, :, cols] = (value * up).astype(stage.dtype)

    def down_forward(d, h, hidden):
        for c in range(3):
            cols = slice(c * columns, (c + 1) * columns)
            part = add_slice(hidden[...], downs_v[:, cols])
            own_sum[d, h, :, cols] = part[:piece_len]
            twin_out[d, h, :, cols] = part[piece_len:].astype(twin_out.dtype)
        part_twin(d, h).start()

    def own_forward(h):
        down_forward(s, h, own_hidden.at[h])

    def compute_backward(d, h, slot):
        rows = held[d, h].reshape(2 * piece_len, width)
        for c in range(3):
            cols = slice(c * chunk, (c + 1) * chunk)
            grad = times_rows(rows, downs_v[cols, :])
            value, slope = gelu_pieces(kept[0, slot, :, cols].astype(jnp.float32))
            up = kept[1, slot, :, cols].astype(jnp.float32)
            stage[0, slot, :, cols] = (grad * up * slope).astype(stage.dtype)
            stage[1, slot, :, cols] = (grad * value).astype(stage.dtype)
        for c in range(3):
            cols = slice(c * columns, (c + 1) * columns)
            later = slice(width + c * columns, width + (c + 1) * columns)
            part = add_slice(stage[0, slot], units_v[:, cols])
            part = part + add_slice(stage[1, slot], units_v[:, later])
            own_sum[d, h, :, cols] = part[:piece_len]
            twin_out[d, h, :, cols] = part[piece_len:].astype(twin_out.dtype)

    row_tile, col_tile = n_units // 3, width // 3

    def down_gradient(between):
        unit_rows = 2 * piece_len
        group_rows = n * unit_rows

        def left_load(u):
            place = downs_v.at[
                pl.ds((u % n) * unit_rows, unit_rows), pl.ds((u // n) * n_units, n_units)
            ]
            return pltpu.make_async_copy(kept_hidden.at[u], place, load_sem.at[u])

        def left_rows(g, first):
            return downs_v[
                :group_rows, pl.ds(pl.multiple_of(g * n_units + first, 128), row_tile)
            ]

        def right_rows(g, first):
            cols = pl.ds(pl.multiple_of(first, 128), col_tile)
            part = held[g * n // 2 : (g + 1) * n // 2, :, :, :, cols]
            return part.reshape(group_rows, col_tile)

        def tile_store(r, c, slot):
            rows = pl.ds(pl.multiple_of(r * row_tile, 16), row_tile)
            if c < LATE_COLUMNS:
                place = late_grads[c].at[rows]
            else:
                place = early_grads.at[rows, pl.ds((c - LATE_COLUMNS) * col_tile, col_tile)]
            return pltpu.make_async_copy(tile.at[slot], place, tile_sem.at[slot])

        for u in range(2 * n):
            left_load(u).start()
        for u in range(2 * n):
            left_load(u).wait()

        def one_tile(c, r, carry):
            slot = lax.rem(r, 2)
            total = sum(
                outer_rows(left_rows(g, r * row_tile), right_rows(g, c * col_tile))
                for g in range(2)
            )

            @pl.when(r >= 2)
            def _():
                tile_store(r, c, slot).wait()

            tile[slot] = total.astype(tile.dtype)
            tile_store(r, c, slot).start()
            for step, turn in enumerate(SUM_TURNS):

                @pl.when(3 * c + r == turn)
                def _():
                    between(step)

            return carry

        for c in range(3):
            lax.fori_loop(0, 3, partial(one_tile, c), 0)
            for slot in range(2):
                tile_store(0, c, slot).wait()
            if c < LATE_COLUMNS:
                for step in (2, 1, 3):
                    late_grad(c, step).start()

    def unit(t, carry):
        d, h = source(t)
        slot = lax.rem(t, 2)

        @pl.when(at_end & (t >= 3))
        def _():
            combine(*source(t - 1))

        @pl.when(t < 2)
        def _():
            own_load(h).wait()

        @pl.when(t >= 2)
        def _():
            piece = held.at[d, h, 0]
            token_left(d, h, piece).wait_recv()

            @pl.when((d < s) & (s < n - 1))
            def _():
                token_right(d, h, piece).start()

            @pl.when((d > s) & (s > 0))
            def _():
                token_left(d, h, piece).start()

            token_twin(d, h, piece).start()
            for i in range(len(stage_outs)):
                stage_store(i, d, h, slot).wait()

        second_half(t)
        if backward:

            @pl.when(t < 2 * n - 1)
            def _():
                for i in range(2):
                    kept_load(i, *source(t + 1), 1 - slot).start()

            for i in range(2):
                kept_load(i, d, h, slot).wait()
        token_twin(d, h, held.at[d, h, 0]).wait_recv()
        if backward:
            compute_backward(d, h, slot)
            part_twin(d, h).start()
        else:
            hidden_forward(d, h, slot)

            @pl.when(t < 2)
            def _():
                own_hidden[slot] = stage[2, slot]

            @pl.when(t == 2)
            def _():
                for step in range(1, n_chip):
                    late_copy(step).wait_recv()

            @pl.when(t >= 2)
            def _():
                down_forward(d, h, stage.at[2, slot])

        if not backward:
            all_store(d, h).start()
        for i in range(len(stage_outs)):
            stage_store(i, d, h, slot).start()

        return carry

    lax.fori_loop(0, 2 * n, unit, 0)

    second_half(2 * n)

    @pl.when(at_end)
    def _():
        combine(*source(2 * n - 1))

    n_sums = 2 * (n - 1)

    def middle(i):
        @pl.when(jnp.logical_not(at_end) & (i < n_sums))
        def _():
            unit = pick(sum_table, s, i)
            combine(lax.div(unit, 2), lax.rem(unit, 2))

    if backward:
        down_gradient(middle)
    else:

        for chip in range(n_chip):
            late_store(chip).start()

        def one(i, carry):
            middle(i)

            @pl.when((i == 1) | (i == 2))
            def _():
                own_forward(i - 1)

            return carry

        lax.fori_loop(0, n_sums, one, 0)

    def finish(h, carry):
        part_twin(s, h).wait_recv()
        for sub in range(SUBS):

            @pl.when(s < n - 1)
            def _():
                line_arrival(s, h, sub).wait_recv()

            @pl.when(s > 0)
            def _():
                line_arrival(s + 1, h, sub).wait_recv()

            @pl.when(s == 0)
            def _():
                add_rows(s, h, sub, True, (s,))

            @pl.when(s == n - 1)
            def _():
                add_rows(s, h, sub, True, (s + 1,))

            @pl.when(jnp.logical_not(at_end))
            def _():
                add_rows(s, h, sub, True, (s, s + 1))

        pltpu.make_async_copy(own_sum.at[s, h], out.at[h], out_sem.at[h]).start()
        return carry

    lax.fori_loop(0, 2, finish, 0)

    def drain(t, carry):
        d = lax.div(t, 2)
        h = lax.rem(t, 2)
        piece = held.at[d, h, 0]

        right_seen = (d == jnp.maximum(s - 1, 0)) & (h == jnp.where(s > 0, 1, 0))
        left_seen = (d == jnp.minimum(s + 1, n - 1)) & (h == jnp.where(s < n - 1, 1, 0))

        @pl.when((d <= s) & (s < n - 1) & jnp.logical_not(right_seen))
        def _():
            token_right(d, h, piece).wait_send()

        @pl.when((d >= s) & (s > 0) & jnp.logical_not(left_seen))
        def _():
            token_left(d, h, piece).wait_send()

        token_twin(d, h, piece).wait_send()
        part_twin(d, h).wait_send()

        @pl.when(d != s)
        def _():
            for sub in range(SUBS):
                part_line(d, h, sub).wait_send()

        if not backward:
            all_store(d, h).wait()
        return carry

    lax.fori_loop(0, 2 * n, drain, 0)
    if backward:
        for i in range(LATE_COLUMNS):
            for step in range(1, n_chip):
                late_grad(i, step).wait()
    else:
        for step in range(1, n_chip):
            late_copy(step).wait_send()
        for chip in range(n_chip):
            late_store(chip).wait()
    for h in range(2):
        for i in range(len(stage_outs)):
            stage_store(i, 0, h, h).wait()
        pltpu.make_async_copy(own_sum.at[s, h], out.at[h], out_sem.at[h]).wait()


def run_units(n_seq, tokens, units, downs, kept=None):
    backward = kept is not None
    low = tokens.dtype
    n_units = units.shape[0]
    halves, piece_len, width = tokens.shape
    n_stage = 2 if backward else 3
    held = (n_seq, halves, 2, piece_len, width)
    unit_rows = (2 * n_seq, 2 * piece_len, n_units)
    sums = (n_seq, halves, piece_len, width)
    scratch = [
        pltpu.VMEM(units.shape, low),
        pltpu.VMEM((n_units, width), low),
        pltpu.VMEM(held, low),
        pltpu.VMEM(sums, jnp.float32),
        pltpu.VMEM(sums, low),
        pltpu.VMEM(sums, low),
        pltpu.VMEM((n_seq + 1,) + sums[1:], low),
        pltpu.VMEM((n_stage, 2) + unit_rows[1:], low),
    ]
    outs = [jax.ShapeDtypeStruct(tokens.shape, jnp.float32)]
    late_shape = (KV_HEADS, downs[0].shape[0] // LATE, width)
    if backward:
        scratch += [
            pltpu.VMEM((2, 2) + unit_rows[1:], low),
            DMA((2, 2)),
            pltpu.VMEM((2, n_units // 3, width // 3), low),
            DMA((2,)),
            DMA((2 * n_seq,)),
        ]
    else:
        scratch += [pltpu.VMEM((2,) + unit_rows[1:], low)]
        outs += [jax.ShapeDtypeStruct(held, low), jax.ShapeDtypeStruct(late_shape, low)]
    outs += [jax.ShapeDtypeStruct(unit_rows, low)] * n_stage
    if backward:
        column = width // 3
        outs += [jax.ShapeDtypeStruct((n_units, (3 - LATE_COLUMNS) * column), low)]
        outs += [jax.ShapeDtypeStruct((n_units, column), low)] * LATE_COLUMNS
        parts = (KV_HEADS, n_units // KV_HEADS, column)
        outs += [jax.ShapeDtypeStruct(parts, low)] * LATE_COLUMNS
    scratch += [DMA((KV_HEADS * LATE_COLUMNS,)), DMA((KV_HEADS * LATE_COLUMNS,))]
    pairs = DMA((n_seq, halves))
    scratch += [DMA((6,)), DMA((KV_HEADS,)), DMA((halves,))] + [pairs] * 7
    scratch += [DMA((n_seq, halves, SUBS)), DMA((n_seq + 1, halves, SUBS))]
    scratch += [DMA((n_stage, 2)), pairs, DMA((halves,))]
    operands = (tokens, units) + tuple(downs) + (tuple(kept) if backward else ())
    return pl.pallas_call(
        partial(units_kernel, n_seq, backward),
        out_shape=outs,
        in_specs=[ANY] * len(operands),
        out_specs=[ANY] * len(outs),
        scratch_shapes=scratch,
        compiler_params=pltpu.CompilerParams(
            collective_id=6 if backward else 5,
            has_side_effects=True,
            vmem_limit_bytes=63 * 1024 * 1024,
        ),
    )(*operands)


def per_device_general(
    hidden_in,
    norm_gains,
    qkv_weight,
    out_weight,
    gate_up_weight,
    down_weight,
    output_cotangent,
    segment_ids,
    padding,
    positions,
):
    everyone = ("seq", "chip", "core")
    plane = ("chip", "core")
    column = ("seq", "core")
    groups = hidden_in.shape[0]
    piece_len = hidden_in.shape[1]
    model_width = hidden_in.shape[2]
    row_count = groups * piece_len
    seq_len = segment_ids.shape[1]
    group_size = HEADS // KV_HEADS
    query_width = HEADS * HEAD_DIM
    key_width = KV_HEADS * HEAD_DIM
    proj_width = qkv_weight.shape[1]

    residual = hidden_in.reshape(row_count, model_width).astype(jnp.float32)
    factor = lax.rsqrt(jnp.mean(residual * residual, axis=-1, keepdims=True) + EPSILON)
    gain_cols = lax.all_gather(norm_gains, everyone, axis=0, tiled=True).astype(jnp.float32)
    qkv_full = lax.all_gather(qkv_weight, everyone, axis=0, tiled=True)
    attn_input = (residual * factor * gain_cols[:, 0]).astype(jnp.bfloat16)
    projected = add_slice(attn_input, qkv_full)
    cosine, sine_part = rotary_tables(positions.reshape(row_count), HEAD_DIM)
    queries = (
        rotate(projected[:, :query_width].reshape(row_count, HEADS, HEAD_DIM), cosine, sine_part)
        .astype(jnp.bfloat16)
        .reshape(row_count, query_width)
    )
    keys_here = (
        rotate(
            projected[:, query_width : query_width + key_width].reshape(
                row_count, KV_HEADS, HEAD_DIM
            ),
            cosine,
            sine_part,
        )
        .astype(jnp.bfloat16)
        .reshape(groups, piece_len, key_width)
    )
    values_here = (
        projected[:, query_width + key_width :]
        .astype(jnp.bfloat16)
        .reshape(groups, piece_len, key_width)
    )
    both_all = lax.all_gather(
        jnp.concatenate([keys_here, values_here], axis=2), plane, axis=1, tiled=True
    )
    keys_all = both_all[:, :, :key_width]
    values_all = both_all[:, :, key_width:]
    first_query = (lax.axis_index("chip") * 2 + lax.axis_index("core")) * piece_len
    query_rows = first_query + jnp.arange(piece_len, dtype=jnp.int32)
    key_rows = jnp.arange(seq_len, dtype=jnp.int32)
    segment_query = lax.dynamic_slice_in_dim(segment_ids, first_query, piece_len, 1)
    allowed = (segment_query[:, :, None] == segment_ids[:, None, :]) & (
        key_rows[None, None, :] <= query_rows[None, :, None]
    ) & (padding[:, None, :] == 1) | (key_rows[None, None, :] == query_rows[None, :, None])
    allowed = allowed[:, None, None]
    probs = soft_probs(score_block(queries, keys_all), allowed)
    attn_out = mix_values(probs.astype(jnp.bfloat16), values_all)
    out_full = lax.all_gather(out_weight, everyone, axis=0, tiled=True)
    attn_proj = times_rows(attn_out, out_full)
    after_attn = residual + rms_norm(attn_proj, gain_cols[:, 1])
    ffn_input = rms_norm(after_attn, gain_cols[:, 2]).astype(jnp.bfloat16)

    unit_weights = lax.all_gather(gate_up_weight, "chip", axis=0, tiled=True)
    down_units = lax.all_gather(down_weight, "chip", axis=0, tiled=True)
    ffn_all = lax.all_gather(ffn_input, column, axis=0, tiled=True)
    gate_part = times_rows(ffn_all, unit_weights[:, :model_width])
    up_part = times_rows(ffn_all, unit_weights[:, model_width:])
    hidden_part = geglu_parts(gate_part, up_part).astype(jnp.bfloat16)
    down_part = add_slice(hidden_part, down_units).astype(jnp.bfloat16)
    down_out = lax.psum_scatter(down_part, column, scatter_dimension=0, tiled=True).astype(
        jnp.float32
    )
    layer_out = after_attn + rms_norm(down_out, gain_cols[:, 3])
    layer_output = layer_out.astype(jnp.bfloat16).reshape(groups, piece_len, model_width)

    cotangent = output_cotangent.reshape(row_count, model_width).astype(jnp.float32)
    unused_last, pull_last = jax.vjp(rms_norm, down_out, gain_cols[:, 3])
    grad_down, grad_gain_last = pull_last(cotangent)
    grad_down_low = grad_down.astype(jnp.bfloat16)
    grad_down_all = lax.all_gather(grad_down_low, column, axis=0, tiled=True)
    grad_part = times_rows(grad_down_all, down_units)
    unused_units, pull_units = jax.vjp(geglu_parts, gate_part, up_part)
    grad_gate_part, grad_up_part = pull_units(grad_part)
    gate_low = grad_gate_part.astype(jnp.bfloat16)
    up_low = grad_up_part.astype(jnp.bfloat16)
    grad_ffn_part = add_slice(gate_low, unit_weights[:, :model_width]) + add_slice(
        up_low, unit_weights[:, model_width:]
    )
    grad_ffn_in = lax.psum_scatter(
        grad_ffn_part.astype(jnp.bfloat16), column, scatter_dimension=0, tiled=True
    ).astype(jnp.float32)
    gate_up_rows = jnp.concatenate(
        [
            outer_rows(gate_low, ffn_all).astype(jnp.bfloat16),
            outer_rows(up_low, ffn_all).astype(jnp.bfloat16),
        ],
        axis=1,
    )
    down_rows = outer_rows(hidden_part, grad_down_all).astype(jnp.bfloat16)
    gate_up_grad = lax.psum_scatter(
        gate_up_rows, "chip", scatter_dimension=0, tiled=True
    ).astype(jnp.float32)
    down_grad = lax.psum_scatter(down_rows, "chip", scatter_dimension=0, tiled=True).astype(
        jnp.float32
    )

    unused_mid, pull_mid = jax.vjp(rms_norm, after_attn, gain_cols[:, 2])
    grad_after_ffn, grad_gain_mid = pull_mid(grad_ffn_in)
    grad_after = cotangent + grad_after_ffn
    unused_post, pull_post = jax.vjp(rms_norm, attn_proj, gain_cols[:, 1])
    grad_proj, grad_gain_post = pull_post(grad_after)
    grad_proj_low = grad_proj.astype(jnp.bfloat16)
    grad_attn = add_slice(grad_proj_low, out_full).astype(jnp.bfloat16)
    scaled = score_block(queries, keys_all)
    probs, pull_probs = jax.vjp(partial(soft_probs, allowed=allowed), scaled)
    grad_heads = grad_attn.reshape(groups, piece_len, KV_HEADS, group_size, HEAD_DIM)
    query_heads = queries.reshape(groups, piece_len, KV_HEADS, group_size, HEAD_DIM)
    key_heads = keys_all.reshape(groups, seq_len, KV_HEADS, HEAD_DIM)
    value_heads = values_all.reshape(groups, seq_len, KV_HEADS, HEAD_DIM)
    grad_probs = jnp.einsum(
        "spkgd,slkd->skgpl", grad_heads, value_heads, preferred_element_type=jnp.float32
    )
    (grad_scaled,) = pull_probs(grad_probs)
    grad_scaled_low = grad_scaled.astype(jnp.bfloat16)
    inverse_root = 1.0 / math.sqrt(HEAD_DIM)
    grad_query_rot = (
        jnp.einsum(
            "skgpl,slkd->spkgd", grad_scaled_low, key_heads, preferred_element_type=jnp.float32
        )
        * inverse_root
    )
    grad_key_rot = (
        jnp.einsum(
            "skgpl,spkgd->slkd", grad_scaled_low, query_heads, preferred_element_type=jnp.float32
        )
        * inverse_root
    )
    grad_value_part = jnp.einsum(
        "skgpl,spkgd->slkd",
        probs.astype(jnp.bfloat16),
        grad_heads,
        preferred_element_type=jnp.float32,
    )
    both_grads = jnp.concatenate(
        [
            grad_key_rot.reshape(groups, seq_len, key_width),
            grad_value_part.reshape(groups, seq_len, key_width),
        ],
        axis=2,
    ).astype(jnp.bfloat16)
    both_summed = lax.psum_scatter(both_grads, plane, scatter_dimension=1, tiled=True)
    both_summed = both_summed.astype(jnp.float32).reshape(row_count, 2 * key_width)
    key_summed = both_summed[:, :key_width]
    value_summed = both_summed[:, key_width:]
    grad_queries = rotate_back(
        grad_query_rot.reshape(row_count, HEADS, HEAD_DIM), cosine, sine_part
    ).reshape(row_count, query_width)
    grad_keys = rotate_back(
        key_summed.reshape(row_count, KV_HEADS, HEAD_DIM), cosine, sine_part
    ).reshape(row_count, key_width)
    grad_projected = jnp.concatenate([grad_queries, grad_keys, value_summed], axis=1).astype(
        jnp.bfloat16
    )
    grad_attn_in = times_rows(grad_projected, qkv_full)
    unused_first, pull_first = jax.vjp(rms_norm, residual, gain_cols[:, 0])
    grad_res_first, grad_gain_first = pull_first(grad_attn_in)
    input_grad = (grad_after + grad_res_first).reshape(groups, piece_len, model_width)
    gain_terms = jnp.stack([grad_gain_first, grad_gain_post, grad_gain_mid, grad_gain_last], axis=1)
    qkv_part = outer_rows(attn_input, grad_projected).astype(jnp.bfloat16)
    out_part = outer_rows(grad_proj_low, attn_out).astype(jnp.bfloat16)
    qkv_grad = lax.psum_scatter(qkv_part, everyone, scatter_dimension=0, tiled=True).astype(
        jnp.float32
    )
    out_proj_grad = lax.psum_scatter(out_part, everyone, scatter_dimension=0, tiled=True).astype(
        jnp.float32
    )
    gain_grad = lax.psum_scatter(gain_terms, everyone, scatter_dimension=0, tiled=True)
    return (layer_output, input_grad, gain_grad, qkv_grad, out_proj_grad, gate_up_grad, down_grad)


def per_device_by_heads(
    n_seq,
    hidden_in,
    norm_gains,
    qkv_weight,
    out_weight,
    gate_up_weight,
    down_weight,
    output_cotangent,
    segment_ids,
    padding,
    positions,
):
    groups, piece_len, model_width = hidden_in.shape
    row_count = groups * piece_len
    seq_len = segment_ids.shape[1]
    n_chip = KV_HEADS
    n_plane = 2 * n_chip
    group_size = HEADS // KV_HEADS
    query_width = HEADS * HEAD_DIM
    key_width = KV_HEADS * HEAD_DIM
    own_width = group_size * HEAD_DIM
    part_width = own_width + 2 * HEAD_DIM
    block_width = part_width + own_width
    weight_rows = qkv_weight.shape[0]
    extra_rows = 16 - weight_rows % 16
    block_rows = weight_rows + extra_rows
    core = lax.axis_index("core")

    gain_rows = jnp.pad(
        norm_gains.T, ((0, extra_rows - norm_gains.shape[1]), (0, block_width - weight_rows))
    )
    blocks = jnp.stack(
        [
            jnp.concatenate(
                [
                    jnp.concatenate(
                        [
                            qkv_weight[:, c * own_width : (c + 1) * own_width],
                            qkv_weight[
                                :, query_width + c * HEAD_DIM : query_width + (c + 1) * HEAD_DIM
                            ],
                            qkv_weight[
                                :,
                                query_width + key_width + c * HEAD_DIM : query_width
                                + key_width
                                + (c + 1) * HEAD_DIM,
                            ],
                            out_weight[:, c * own_width : (c + 1) * own_width],
                        ],
                        axis=1,
                    ),
                    gain_rows,
                ],
                axis=0,
            )
            for c in range(n_chip)
        ]
    )
    hidden_all, blocks_all = gather_first(n_seq, hidden_in, blocks)
    unit_weights = lax.all_gather(gate_up_weight, "chip", axis=0, tiled=True)
    blocks_all, down_weight = lax.optimization_barrier((blocks_all, down_weight))
    early = down_weight.shape[0] - down_weight.shape[0] // LATE
    down_x, down_y = send_beside(down_weight[:early], 1), send_beside(down_weight[:early], 2)
    blocks_all = blocks_all.transpose(0, 2, 1, 3, 4)
    own_weights = blocks_all[:, :, :, :weight_rows].reshape(model_width, block_width)
    own_qkv = own_weights[:, :part_width]
    own_out = own_weights[:, part_width:]
    gain_cols = (
        blocks_all[:, :, :, weight_rows : weight_rows + norm_gains.shape[1], :weight_rows]
        .transpose(0, 1, 2, 4, 3)
        .reshape(model_width, norm_gains.shape[1])
        .astype(jnp.float32)
    )

    seq_rows = hidden_all.reshape(seq_len, model_width).astype(jnp.float32)
    seq_factor = lax.rsqrt(jnp.mean(seq_rows * seq_rows, axis=-1, keepdims=True) + EPSILON)
    attn_input = (seq_rows * seq_factor * gain_cols[:, 0]).astype(jnp.bfloat16)
    projected = add_slice(attn_input, own_qkv)
    segment = lax.dynamic_index_in_dim(segment_ids, core, 0, keepdims=False)
    valid = lax.dynamic_index_in_dim(padding, core, 0, keepdims=False)
    token = jnp.arange(seq_len, dtype=jnp.int32)
    document_start = jnp.min(
        jnp.where(segment[:, None] == segment[None, :], token[None, :], seq_len), axis=1
    )
    cosine, sine_part = rotary_tables(token - document_start, HEAD_DIM)
    queries = (
        rotate(projected[:, :own_width].reshape(seq_len, group_size, HEAD_DIM), cosine, sine_part)
        .astype(jnp.bfloat16)
        .reshape(seq_len, own_width)
    )
    keys = (
        rotate(
            projected[:, own_width : own_width + HEAD_DIM].reshape(seq_len, 1, HEAD_DIM),
            cosine,
            sine_part,
        )
        .astype(jnp.bfloat16)
        .reshape(seq_len, HEAD_DIM)
    )
    values = projected[:, own_width + HEAD_DIM :].astype(jnp.bfloat16)
    segment_col = segment[:, None]
    segment_row = jnp.where(valid == 1, segment, -1)[None, :]
    attn_out = attend(queries, keys, values, segment_col, segment_row)
    proj_parts = times_rows(attn_out, own_out).astype(jnp.bfloat16)
    proj_parts, down_across = merge_plane(
        proj_parts.reshape(n_plane, piece_len, model_width), down_x, down_y, 2
    )
    down_units = (down_weight, down_x, down_y, down_across[0], down_across[1])

    def sum_parts(parts):
        return jnp.sum(parts.astype(jnp.float32), axis=0).reshape(row_count, model_width)

    attn_proj = sum_parts(proj_parts)
    residual = hidden_in.reshape(row_count, model_width).astype(jnp.float32)
    after_attn = residual + rms_norm(attn_proj, gain_cols[:, 1])
    ffn_input = rms_norm(after_attn, gain_cols[:, 2]).astype(jnp.bfloat16)

    pieces = (groups, piece_len, model_width)
    down_out, ffn_all, down_late, gate_part, up_part, hidden_part = run_units(
        n_seq, ffn_input.reshape(pieces), unit_weights, down_units
    )
    down_out = down_out.reshape(row_count, model_width)
    layer_out = after_attn + rms_norm(down_out, gain_cols[:, 3])
    layer_output = layer_out.astype(jnp.bfloat16).reshape(pieces)

    cotangent = output_cotangent.reshape(row_count, model_width).astype(jnp.float32)
    unused_last, pull_last = jax.vjp(rms_norm, down_out, gain_cols[:, 3])
    grad_down, grad_gain_last = pull_last(cotangent)
    grad_ffn_in, gate_low, up_low, early_rows, *late = run_units(
        n_seq,
        grad_down.astype(jnp.bfloat16).reshape(pieces),
        unit_weights,
        down_units,
        (down_late, gate_part, up_part, hidden_part),
    )
    grad_ffn_in = grad_ffn_in.reshape(row_count, model_width)
    chip = lax.axis_index("chip")
    chips = jnp.arange(n_chip, dtype=jnp.int32)[:, None, None]
    down_columns = []
    for grads, parts in zip(late[:LATE_COLUMNS], late[LATE_COLUMNS:]):
        own = lax.dynamic_slice_in_dim(grads, chip * parts.shape[1], parts.shape[1], 0)
        parts = jnp.where(chips == chip, own[None], parts)
        down_columns.append(jnp.sum(parts.astype(jnp.float32), axis=0))
    if LATE_COLUMNS < 3:
        early_grad = lax.psum_scatter(early_rows, "chip", scatter_dimension=0, tiled=True)
        down_columns.append(early_grad.astype(jnp.float32))
    down_grad = jnp.concatenate(down_columns, axis=1)

    unused_mid, pull_mid = jax.vjp(rms_norm, after_attn, gain_cols[:, 2])
    grad_after_ffn, grad_gain_mid = pull_mid(grad_ffn_in)
    grad_after = cotangent + grad_after_ffn
    unused_post, pull_post = jax.vjp(rms_norm, attn_proj, gain_cols[:, 1])
    grad_proj, grad_gain_post = pull_post(grad_after)
    grad_proj_low = grad_proj.astype(jnp.bfloat16)

    grad_proj_all, gate_up_rows = spread_plane(
        grad_proj_low.reshape(groups, piece_len, model_width), gate_low, up_low, ffn_all
    )
    gate_up_grad = lax.psum_scatter(
        gate_up_rows, "chip", scatter_dimension=0, tiled=True
    ).astype(jnp.float32)
    grad_proj_all = grad_proj_all.reshape(seq_len, model_width)
    grad_attn = add_slice(grad_proj_all, own_out).astype(jnp.bfloat16)
    grad_projected = attend_back(
        queries,
        keys,
        values,
        segment_col,
        segment_row,
        grad_attn,
        cosine[:, 0],
        sine_part[:, 0],
    )
    grad_in_part = times_rows(grad_projected, own_qkv)
    grad_gain_first = jnp.sum(grad_in_part * seq_rows * seq_factor, axis=0)
    gain_terms = (
        jnp.stack([grad_gain_first, grad_gain_post, grad_gain_mid, grad_gain_last])
        .reshape(-1, n_seq * n_plane, weight_rows)
        .transpose(1, 0, 2)
    )
    gain_terms = jnp.pad(
        gain_terms,
        ((0, 0), (0, extra_rows - gain_terms.shape[1]), (0, block_width - weight_rows)),
    )
    grad_blocks = weight_blocks(
        n_seq, attn_input, grad_projected, grad_proj_all, attn_out, gain_terms
    )
    grad_in_parts, grad_sums = sum_last(
        n_seq,
        grad_in_part.astype(jnp.bfloat16).reshape(n_plane, piece_len, model_width),
        grad_blocks,
    )
    grad_attn_in = sum_parts(grad_in_parts)
    factor = lax.rsqrt(jnp.mean(residual * residual, axis=-1, keepdims=True) + EPSILON)
    unused_first, pull_first = jax.vjp(rms_norm, residual, gain_cols[:, 0])
    grad_res_first, unused_gain = pull_first(grad_attn_in)
    input_grad = (grad_after + grad_res_first).reshape(groups, piece_len, model_width)

    weight_sums = grad_sums[:, :weight_rows].astype(jnp.float32)
    qkv_grad = jnp.concatenate(
        [weight_sums[c, :, :own_width] for c in range(n_chip)]
        + [weight_sums[c, :, own_width : own_width + HEAD_DIM] for c in range(n_chip)]
        + [weight_sums[c, :, own_width + HEAD_DIM : part_width] for c in range(n_chip)],
        axis=1,
    )
    out_proj_grad = jnp.concatenate(
        [weight_sums[c, :, part_width:] for c in range(n_chip)], axis=1
    )
    gain_grad = jnp.sum(
        grad_sums[:, weight_rows : weight_rows + norm_gains.shape[1], :weight_rows].astype(
            jnp.float32
        ),
        axis=0,
    ).T
    return (layer_output, input_grad, gain_grad, qkv_grad, out_proj_grad, gate_up_grad, down_grad)


def solution(mesh):
    n_seq = mesh.shape["seq"]
    n_ctx = mesh.shape["ctx"]
    split_mesh = jax.sharding.Mesh(
        mesh.devices.reshape(n_seq, n_ctx // 2, 2), ("seq", "chip", "core")
    )
    plane = ("chip", "core")
    rows = P(("seq", "chip", "core"), None)
    tokens = P("seq", plane, None)
    placed = (
        tokens,
        rows,
        rows,
        rows,
        rows,
        rows,
        tokens,
        P("seq", None),
        P("seq", None),
        P("seq", plane),
    )

    def step(*arrays):
        groups = arrays[0].shape[0]
        if n_ctx // 2 == KV_HEADS and groups == 2 and n_seq == 4:
            return per_device_by_heads(n_seq, *arrays)
        return per_device_general(*arrays)

    return jax.shard_map(
        step,
        mesh=split_mesh,
        in_specs=placed,
        out_specs=(tokens, tokens, rows, rows, rows, rows, rows),
        check_vma=False,
    )
```

```python
from functools import partial
import math

import jax
import jax.numpy as jnp
from jax import lax
from jax.experimental import pallas as pl
from jax.experimental.pallas import tpu as pltpu
from jax.sharding import PartitionSpec as P

HEADS = 8
KV_HEADS = 4
HEAD_DIM = 256


EPSILON = 1e-06
SOFT_CAP = 50.0
MASKED = -1e30


def rms_norm(matrix, gain_col):
    factor = lax.rsqrt(jnp.mean(matrix * matrix, axis=-1, keepdims=True) + EPSILON)
    return matrix * factor * gain_col


def rotary_tables(positions, head_dim):
    half_dim = head_dim // 2
    frequency = jnp.exp(
        jnp.arange(half_dim, dtype=jnp.float32) * (-2.0 * math.log(10000.0) / head_dim)
    )
    phase_angle = positions.astype(jnp.float32)[:, None] * frequency[None, :]
    return (jnp.cos(phase_angle)[:, None, :], jnp.sin(phase_angle)[:, None, :])


def rotate(vectors, cosine, sine_part):
    half_dim = vectors.shape[-1] // 2
    first_half = vectors[..., :half_dim]
    second_half = vectors[..., half_dim:]
    return jnp.concatenate(
        [
            first_half * cosine - second_half * sine_part,
            second_half * cosine + first_half * sine_part,
        ],
        axis=-1,
    )


def rotate_back(grads, cosine, sine_part):
    half_dim = grads.shape[-1] // 2
    first_half = grads[..., :half_dim]
    second_half = grads[..., half_dim:]
    return jnp.concatenate(
        [
            first_half * cosine + second_half * sine_part,
            second_half * cosine - first_half * sine_part,
        ],
        axis=-1,
    )


def soft_probs(scaled, allowed):
    capped = SOFT_CAP * jnp.tanh(scaled / SOFT_CAP)
    capped = jnp.where(allowed, capped, MASKED)
    return jax.nn.softmax(capped, axis=-1)


def geglu_parts(gate_part, up_part):
    return jax.nn.gelu(gate_part, approximate=True) * up_part


def score_block(queries, keys_all):
    groups = keys_all.shape[0]
    seq_len = keys_all.shape[1]
    piece_len = queries.shape[0] // groups
    query_heads = queries.reshape(groups, piece_len, KV_HEADS, HEADS // KV_HEADS, HEAD_DIM)
    key_heads = keys_all.reshape(groups, seq_len, KV_HEADS, HEAD_DIM)
    raw_score = jnp.einsum(
        "spkgd,slkd->skgpl", query_heads, key_heads, preferred_element_type=jnp.float32
    )
    return raw_score * (1.0 / math.sqrt(HEAD_DIM))


def mix_values(weights_low, values_all):
    groups = values_all.shape[0]
    seq_len = values_all.shape[1]
    piece_len = weights_low.shape[3]
    value_heads = values_all.reshape(groups, seq_len, KV_HEADS, HEAD_DIM)
    mixed = jnp.einsum(
        "skgpl,slkd->spkgd", weights_low, value_heads, preferred_element_type=jnp.float32
    )
    return mixed.reshape(groups * piece_len, HEADS * HEAD_DIM).astype(jnp.bfloat16)


def add_slice(left, weight_piece):
    return jnp.dot(left, weight_piece, preferred_element_type=jnp.float32)


def times_rows(left, weight_piece):
    return lax.dot_general(
        left, weight_piece, (((1,), (1,)), ((), ())), preferred_element_type=jnp.float32
    )


def outer_rows(left, right):
    return lax.dot_general(
        left, right, (((0,), (0,)), ((), ())), preferred_element_type=jnp.float32
    )


MESH = pl.DeviceIdType.MESH
ANY = pl.BlockSpec(memory_space=pl.ANY)
DMA = pltpu.SemaphoreType.DMA


def remote(source, target, send_sem, recv_sem, device):
    return pltpu.make_async_remote_copy(
        src_ref=source,
        dst_ref=target,
        send_sem=send_sem,
        recv_sem=recv_sem,
        device_id=device,
        device_id_type=MESH,
    )


def plane_device(index):
    return {"chip": index // 2, "core": lax.rem(index, 2)}


def greet(n_plane, n_seq):
    me = lax.axis_index("chip") * 2 + lax.axis_index("core")
    barrier = pltpu.get_barrier_semaphore()
    for step in range(1, n_plane):
        pl.semaphore_signal(
            barrier,
            inc=1,
            device_id=plane_device(lax.rem(me + step, n_plane)),
            device_id_type=MESH,
        )
    count = n_plane - 1
    if n_seq > 1:
        s = lax.axis_index("seq")

        @pl.when(s > 0)
        def _():
            pl.semaphore_signal(barrier, inc=1, device_id={"seq": s - 1}, device_id_type=MESH)

        @pl.when(s < n_seq - 1)
        def _():
            pl.semaphore_signal(barrier, inc=1, device_id={"seq": s + 1}, device_id_type=MESH)

        count = count + jnp.where(s > 0, 1, 0) + jnp.where(s < n_seq - 1, 1, 0)
    pl.semaphore_wait(barrier, count)


def chip_at(q, flip):
    x, y = lax.rem(q, 2), q // 2
    x = 1 - x if flip in (1, 3) else x
    y = 1 - y if flip in (2, 3) else y
    return y * 2 + x


class Merge:
    def __init__(self, source, target, added, own_part, sems):
        self.source, self.target, self.added, self.own_part = source, target, added, own_part
        self.send_sems, self.recv_sems, self.load_sems, self.local_sems = sems
        self.q = lax.axis_index("chip")
        self.k = lax.axis_index("core")
        self.half = source.shape[1] // 2

    def rows(self, flip):
        return pl.ds(0 if flip == 1 else self.half, self.half)

    def direct(self, flip, core):
        chip = chip_at(self.q, flip)
        slot = 6 * (flip - 1) + core
        return remote(
            self.source.at[2 * chip + core, self.rows(flip)],
            self.target.at[1, self.k, self.rows(flip)],
            self.send_sems.at[slot],
            self.recv_sems.at[6 * (flip - 1) + self.k],
            {"chip": chip, "core": core},
        )

    def arrival(self, flip, core):
        return remote(
            self.source.at[0, self.rows(flip)],
            self.target.at[1, core, self.rows(flip)],
            self.send_sems.at[0],
            self.recv_sems.at[6 * (flip - 1) + core],
            {"chip": chip_at(self.q, flip)},
        )

    def across(self, flip, core):
        slot = 6 * (flip - 1) + 2 + core
        return remote(
            self.source.at[2 * chip_at(self.q, 3) + core, self.rows(flip)],
            self.added.at[flip - 1, core],
            self.send_sems.at[slot],
            self.recv_sems.at[slot],
            {"chip": chip_at(self.q, flip)},
        )

    def load(self, flip, core):
        return pltpu.make_async_copy(
            self.source.at[2 * chip_at(self.q, 3 - flip) + core, self.rows(flip)],
            self.own_part.at[flip - 1, core],
            self.load_sems.at[flip - 1, core],
        )

    def summed(self, flip, core):
        slot = 6 * (flip - 1) + 4 + core
        return remote(
            self.own_part.at[flip - 1, core],
            self.target.at[2, self.k, self.rows(flip)],
            self.send_sems.at[slot],
            self.recv_sems.at[6 * (flip - 1) + 4 + self.k],
            {"chip": chip_at(self.q, 3 - flip), "core": core},
        )

    def summed_arrival(self, flip, core):
        return remote(
            self.own_part.at[flip - 1, 0],
            self.target.at[2, core, self.rows(flip)],
            self.send_sems.at[0],
            self.recv_sems.at[6 * (flip - 1) + 4 + core],
            {"chip": chip_at(self.q, 3 - flip)},
        )

    def twin(self):
        return remote(
            self.source.at[2 * self.q + 1 - self.k],
            self.target.at[0, self.k],
            self.send_sems.at[12],
            self.recv_sems.at[12],
            {"core": 1 - self.k},
        )

    def twin_arrival(self):
        return remote(
            self.source.at[0],
            self.target.at[0, 1 - self.k],
            self.send_sems.at[12],
            self.recv_sems.at[12],
            {"core": 1 - self.k},
        )

    def own(self):
        return pltpu.make_async_copy(
            self.source.at[2 * self.q + self.k], self.target.at[0, self.k], self.local_sems.at[0]
        )

    def start(self):
        pairs = [(flip, core) for core in (0, 1) for flip in (1, 2)]
        for flip, core in pairs:
            self.across(flip, core).start()
        for flip, core in pairs:
            self.load(flip, core).start()
        for flip, core in pairs:
            self.direct(flip, core).start()
        self.twin().start()
        self.own().start()

    def pass_on(self):
        step = 16
        for core in (0, 1):
            for flip in (1, 2):
                self.load(flip, core).wait()
                self.across(flip, core).wait_recv()

                def body(i, carry, flip=flip, core=core):
                    rows = pl.ds(pl.multiple_of(i * step, step), step)
                    total = self.own_part[flip - 1, core, rows, :].astype(jnp.float32)
                    total = total + self.added[flip - 1, core, rows, :].astype(jnp.float32)
                    self.own_part[flip - 1, core, rows, :] = total.astype(self.own_part.dtype)
                    return carry

                lax.fori_loop(0, self.half // step, body, 0)
                self.summed(flip, core).start()

    def finish(self):
        for core in (0, 1):
            for flip in (1, 2):
                self.across(flip, core).wait_send()
                self.direct(flip, core).wait_send()
                self.arrival(flip, core).wait_recv()
                self.summed(flip, core).wait_send()
                self.summed_arrival(flip, core).wait_recv()
        self.twin().wait_send()
        self.twin_arrival().wait_recv()
        self.own().wait()


def merge_scratch(blocks):
    part = (2, 2, blocks.shape[1] // 2, blocks.shape[2])
    return [
        pltpu.VMEM(part, blocks.dtype),
        pltpu.VMEM(part, blocks.dtype),
        DMA((13,)),
        DMA((13,)),
        DMA((2, 2)),
        DMA((1,)),
    ]


def merged_shape(blocks):
    return jax.ShapeDtypeStruct((3, 2) + blocks.shape[1:], blocks.dtype)


class Spread:
    def __init__(self, source, target, send_sems, recv_sems, local_sem):
        self.source, self.target = source, target
        self.send_sems, self.recv_sems = send_sems, recv_sems
        self.local_sem = local_sem
        self.q = lax.axis_index("chip")
        self.k = lax.axis_index("core")
        self.half = source.shape[1] // 2

    def chip(self, flip):
        return chip_at(self.q, flip)

    def direct(self, flip, twin):
        core = 1 - self.k if twin else self.k
        slot = 2 * flip + twin
        return remote(
            self.source.at[core],
            self.target.at[2 * self.q + self.k],
            self.send_sems.at[slot],
            self.recv_sems.at[slot],
            {"chip": self.chip(flip), "core": core},
        )

    def passed(self, flip, twin):
        core = 1 - self.k if twin else self.k
        slot = 8 + 2 * (flip - 1) + twin
        rows = pl.ds(0 if flip == 1 else self.half, self.half)
        block = self.target.at[2 * self.chip(flip) + core, rows]
        return remote(
            block,
            block,
            self.send_sems.at[slot],
            self.recv_sems.at[slot],
            {"chip": self.chip(3 - flip)},
        )

    def own(self):
        return pltpu.make_async_copy(
            self.source.at[self.k],
            self.target.at[2 * self.q + self.k],
            self.local_sem.at[0],
        )

    def start(self):
        for twin in (0, 1):
            for flip in (1, 2):
                self.direct(flip, twin).start()
        self.direct(0, 1).start()
        self.own().start()

    def pass_on(self):
        for twin in (0, 1):
            for flip in (1, 2):
                self.direct(flip, twin).wait_recv()
                self.passed(flip, twin).start()

    def finish(self):
        for twin in (0, 1):
            for flip in (1, 2):
                self.passed(flip, twin).wait()
                self.direct(flip, twin).wait_send()
        self.direct(0, 1).wait()
        self.own().wait()


SPREAD_SLOTS = 12


def merge_kernel(n_plane, source, rows_x, rows_y, target, across, added, own_part, *sems):
    greet(n_plane, 1)
    merge = Merge(source, target, added, own_part, sems[:4])
    pass_send, pass_recv = sems[4:]
    merge.start()
    half = rows_x.shape[0] // 2
    passed = [
        remote(
            rows.at[pl.ds(i * half, half)],
            across.at[i],
            pass_send.at[i],
            pass_recv.at[i],
            {"chip": chip_at(merge.q, 2 - i)},
        )
        for i, rows in enumerate((rows_x, rows_y))
    ]
    for copy in passed:
        copy.start()
    merge.pass_on()
    merge.finish()
    for copy in passed:
        copy.wait()


def merge_plane(blocks, rows_x, rows_y, collective_id):
    half = (2, rows_x.shape[0] // 2, rows_x.shape[1])
    return pl.pallas_call(
        partial(merge_kernel, 2 * KV_HEADS),
        out_shape=[merged_shape(blocks), jax.ShapeDtypeStruct(half, rows_x.dtype)],
        in_specs=[ANY] * 3,
        out_specs=[ANY] * 2,
        scratch_shapes=merge_scratch(blocks) + [DMA((2,)), DMA((2,))],
        compiler_params=pltpu.CompilerParams(
            collective_id=collective_id, has_side_effects=True
        ),
    )(blocks, rows_x, rows_y)


def spread_kernel(
    n_plane,
    blocks,
    low_gate,
    low_up,
    tokens,
    target,
    grads,
    left,
    right,
    tile,
    send_sems,
    recv_sems,
    local_sem,
    load_sem,
    row_sem,
    tile_sem,
):
    greet(n_plane, 1)
    spread = Spread(blocks, target, send_sems, recv_sems, local_sem)
    spread.start()
    n_units, unit_rows, units = low_gate.shape
    width = right.shape[1]
    piece_len = tokens.shape[3]
    loads = []
    for i, source in enumerate((low_gate, low_up)):
        for u in range(n_units):
            place = left.at[i, pl.ds(u * unit_rows, unit_rows)]
            loads.append(pltpu.make_async_copy(source.at[u], place, load_sem.at[i, u]))
    for u in range(n_units):
        for half in range(2):
            place = right.at[pl.ds(u * unit_rows + half * piece_len, piece_len)]
            source = tokens.at[u // 2, u % 2, half]
            loads.append(pltpu.make_async_copy(source, place, row_sem.at[u, half]))
    for load in loads:
        load.start()
    for load in loads:
        load.wait()
    row_tile, col_tile = units // 3, width // 3

    def tile_store(i, r, c, slot):
        rows = pl.ds(pl.multiple_of(r * row_tile, 16), row_tile)
        cols = pl.ds(pl.multiple_of(i * width + c * col_tile, 128), col_tile)
        return pltpu.make_async_copy(tile.at[slot], grads.at[rows, cols], tile_sem.at[slot])

    def one_tile(j, carry):
        i, slot = lax.div(j, 9), lax.rem(j, 2)
        r, c = lax.div(lax.rem(j, 9), 3), lax.rem(j, 3)
        rows = pl.ds(pl.multiple_of(r * row_tile, 128), row_tile)
        cols = pl.ds(pl.multiple_of(c * col_tile, 128), col_tile)
        total = outer_rows(left[i, :, rows], right[:, cols])

        @pl.when(j >= 2)
        def _():
            tile_store(i, r, c, slot).wait()

        tile[slot] = total.astype(tile.dtype)
        tile_store(i, r, c, slot).start()
        return carry

    lax.fori_loop(0, PASS_TURN, one_tile, 0)
    spread.pass_on()
    lax.fori_loop(PASS_TURN, 18, one_tile, 0)
    for slot in range(2):
        tile_store(0, 0, 0, slot).wait()
    spread.finish()


PASS_TURN = 14


def spread_plane(blocks, low_gate, low_up, tokens):
    n_plane = 2 * KV_HEADS
    low = blocks.dtype
    n_units, unit_rows, units = low_gate.shape
    width = blocks.shape[2]
    return pl.pallas_call(
        partial(spread_kernel, n_plane),
        out_shape=[
            jax.ShapeDtypeStruct((n_plane,) + blocks.shape[1:], low),
            jax.ShapeDtypeStruct((units, 2 * width), low),
        ],
        in_specs=[ANY] * 4,
        out_specs=[ANY, ANY],
        scratch_shapes=[
            pltpu.VMEM((2, n_units * unit_rows, units), low),
            pltpu.VMEM((n_units * unit_rows, width), low),
            pltpu.VMEM((2, units // 3, width // 3), low),
            DMA((SPREAD_SLOTS,)),
            DMA((SPREAD_SLOTS,)),
            DMA((1,)),
            DMA((2, n_units)),
            DMA((n_units, 2)),
            DMA((2,)),
        ],
        compiler_params=pltpu.CompilerParams(
            collective_id=3, has_side_effects=True, vmem_limit_bytes=48 * 1024 * 1024
        ),
    )(blocks, low_gate, low_up, tokens)


def gather_kernel(
    n_seq,
    n_plane,
    hidden,
    blocks,
    hidden_all,
    blocks_all,
    hid_send,
    hid_recv,
    hid_local,
    chip_send,
    chip_recv,
    chip_local,
    left_send,
    right_send,
    line_recv,
    twin_send,
    twin_recv,
):
    n_chip = n_plane // 2
    s = lax.axis_index("seq")
    q = lax.axis_index("chip")
    k = lax.axis_index("core")
    greet(n_plane, n_seq)
    swaps = []
    for step in range(1, n_chip):
        to = lax.rem(q + step, n_chip)
        copy = remote(
            blocks.at[to],
            blocks_all.at[s, k, q],
            chip_send.at[step],
            chip_recv.at[step],
            {"chip": to},
        )
        copy.start()
        swaps.append(copy)
    own = pltpu.make_async_copy(blocks.at[q], blocks_all.at[s, k, q], chip_local.at[0])
    own.start()
    spread = Spread(hidden, hidden_all, hid_send, hid_recv, hid_local)
    for copy in swaps:
        copy.wait_recv()
    own.wait()
    spread.start()

    def to_left(d):
        return remote(
            blocks_all.at[d, k], blocks_all.at[d, k], left_send.at[d], line_recv.at[d], {"seq": s - 1}
        )

    def to_right(d):
        return remote(
            blocks_all.at[d, k], blocks_all.at[d, k], right_send.at[d], line_recv.at[d], {"seq": s + 1}
        )

    def to_twin(d):
        return remote(
            blocks_all.at[d, k], blocks_all.at[d, k], twin_send.at[d], twin_recv.at[d], {"core": 1 - k}
        )

    def from_twin(d):
        return remote(
            blocks_all.at[d, 1 - k],
            blocks_all.at[d, 1 - k],
            twin_send.at[d],
            twin_recv.at[d],
            {"core": 1 - k},
        )

    @pl.when(s > 0)
    def _():
        to_left(s).start()

    @pl.when(s < n_seq - 1)
    def _():
        to_right(s).start()

    to_twin(s).start()
    for hop in range(1, n_seq):
        if hop == 2:
            spread.pass_on()
        from_left = s - hop
        from_right = s + hop

        @pl.when(from_left >= 0)
        def _():
            to_left(from_left).wait_recv()

            @pl.when(s < n_seq - 1)
            def _():
                to_right(from_left).start()

            to_twin(from_left).start()

        @pl.when(from_right < n_seq)
        def _():
            to_right(from_right).wait_recv()

            @pl.when(s > 0)
            def _():
                to_left(from_right).start()

            to_twin(from_right).start()

    for d in range(n_seq):

        @pl.when((d >= s) & (s > 0))
        def _():
            to_left(d).wait_send()

        @pl.when((d <= s) & (s < n_seq - 1))
        def _():
            to_right(d).wait_send()

        to_twin(d).wait_send()
        from_twin(d).wait_recv()
    for copy in swaps:
        copy.wait_send()
    spread.finish()


def gather_first(n_seq, hidden, blocks):
    n_plane = 2 * KV_HEADS
    n_chip = KV_HEADS
    return pl.pallas_call(
        partial(gather_kernel, n_seq, n_plane),
        out_shape=[
            jax.ShapeDtypeStruct((n_plane,) + hidden.shape[1:], hidden.dtype),
            jax.ShapeDtypeStruct((n_seq, 2) + blocks.shape, blocks.dtype),
        ],
        in_specs=[ANY, ANY],
        out_specs=[ANY, ANY],
        scratch_shapes=[
            DMA((SPREAD_SLOTS,)),
            DMA((SPREAD_SLOTS,)),
            DMA((1,)),
            DMA((n_chip,)),
            DMA((n_chip,)),
            DMA((1,)),
            DMA((n_seq,)),
            DMA((n_seq,)),
            DMA((n_seq,)),
            DMA((n_seq,)),
            DMA((n_seq,)),
        ],
        compiler_params=pltpu.CompilerParams(collective_id=1, has_side_effects=True),
    )(hidden, blocks)


def last_kernel(
    n_seq,
    n_plane,
    parts,
    blocks,
    parts_all,
    sums,
    held,
    twin,
    line,
    part_added,
    part_own,
    part_send,
    part_recv,
    part_load,
    part_local,
    held_sem,
    twin_send,
    twin_recv,
    line_send,
    line_recv,
    chip_send,
    chip_recv,
    chip_local,
):
    n_chip = n_plane // 2
    s = lax.axis_index("seq")
    q = lax.axis_index("chip")
    k = lax.axis_index("core")
    greet(n_plane, n_seq)

    def load(d):
        return pltpu.make_async_copy(blocks.at[d, k], held.at[d], held_sem.at[d])

    def to_twin(d):
        return remote(
            blocks.at[d, 1 - k], twin.at[d], twin_send.at[d], twin_recv.at[d], {"core": 1 - k}
        )

    def to_left(d):
        return remote(held.at[d], line.at[d], line_send.at[d], line_recv.at[d], {"seq": s - 1})

    def to_right(d):
        return remote(
            held.at[d], line.at[d + 1], line_send.at[d], line_recv.at[d + 1], {"seq": s + 1}
        )

    def gather_terms(d, with_left, with_right):
        load(d).wait()
        to_twin(d).wait_recv()

        @pl.when(with_right)
        def _():
            to_left(d).wait_recv()

        @pl.when(with_left)
        def _():
            to_right(d).wait_recv()

        def body(i, carry):
            held[d, i] = (held[d, i].astype(jnp.float32) + twin[d, i].astype(jnp.float32)).astype(
                held.dtype
            )
            return carry

        def body_right(i, carry):
            total = held[d, i].astype(jnp.float32) + twin[d, i].astype(jnp.float32)
            held[d, i] = (total + line[d, i].astype(jnp.float32)).astype(held.dtype)
            return carry

        def body_left(i, carry):
            total = held[d, i].astype(jnp.float32) + twin[d, i].astype(jnp.float32)
            held[d, i] = (total + line[d + 1, i].astype(jnp.float32)).astype(held.dtype)
            return carry

        def body_both(i, carry):
            total = held[d, i].astype(jnp.float32) + twin[d, i].astype(jnp.float32)
            total = total + line[d, i].astype(jnp.float32)
            held[d, i] = (total + line[d + 1, i].astype(jnp.float32)).astype(held.dtype)
            return carry

        @pl.when(jnp.logical_not(with_left) & jnp.logical_not(with_right))
        def _():
            lax.fori_loop(0, n_chip, body, 0)

        @pl.when(jnp.logical_not(with_left) & with_right)
        def _():
            lax.fori_loop(0, n_chip, body_right, 0)

        @pl.when(with_left & jnp.logical_not(with_right))
        def _():
            lax.fori_loop(0, n_chip, body_left, 0)

        @pl.when(with_left & with_right)
        def _():
            lax.fori_loop(0, n_chip, body_both, 0)

    for d in range(n_seq):
        to_twin(d).start()
        load(d).start()
    part_sems = (part_send, part_recv, part_load, part_local)
    merge = Merge(parts, parts_all, part_added, part_own, part_sems)
    merge.start()
    never = s < 0
    for hop in range(1, n_seq):
        if hop == 2:
            merge.pass_on()
        left = hop - n_seq + s
        right = n_seq - hop + s

        @pl.when(left >= 0)
        def _():
            gather_terms(left, never, s < n_seq - 1)
            to_left(left).start()

        @pl.when(right <= n_seq - 1)
        def _():
            gather_terms(right, s > 0, never)
            to_right(right).start()

    gather_terms(s, s > 0, s < n_seq - 1)
    swaps = []
    for step in range(1, n_chip):
        to = lax.rem(q + step, n_chip)
        copy = remote(
            held.at[s, to], sums.at[q], chip_send.at[step], chip_recv.at[step], {"chip": to}
        )
        copy.start()
        swaps.append(copy)
    own = pltpu.make_async_copy(held.at[s, q], sums.at[q], chip_local.at[0])
    own.start()
    for d in range(n_seq):
        to_twin(d).wait_send()

        @pl.when(d < s)
        def _():
            to_left(d).wait_send()

        @pl.when(d > s)
        def _():
            to_right(d).wait_send()

    merge.finish()
    for copy in swaps:
        copy.wait()
    own.wait()


def sum_last(n_seq, parts, blocks):
    n_plane = 2 * KV_HEADS
    n_chip = KV_HEADS
    block = blocks.shape[2:]
    return pl.pallas_call(
        partial(last_kernel, n_seq, n_plane),
        out_shape=[
            merged_shape(parts),
            jax.ShapeDtypeStruct(block, blocks.dtype),
        ],
        in_specs=[ANY, ANY],
        out_specs=[ANY, ANY],
        scratch_shapes=[
            pltpu.VMEM((n_seq,) + block, blocks.dtype),
            pltpu.VMEM((n_seq,) + block, blocks.dtype),
            pltpu.VMEM((n_seq + 1,) + block, blocks.dtype),
            *merge_scratch(parts),
            DMA((n_seq,)),
            DMA((n_seq,)),
            DMA((n_seq,)),
            DMA((n_seq,)),
            DMA((n_seq + 1,)),
            DMA((n_chip,)),
            DMA((n_chip,)),
            DMA((1,)),
        ],
        compiler_params=pltpu.CompilerParams(
            collective_id=4, has_side_effects=True, vmem_limit_bytes=32 * 1024 * 1024
        ),
    )(parts, blocks)


QUERY_BLOCK = 256


def block_probs(query, keys, segment_col, segment_row, first):
    rows, width = query.shape[0], keys.shape[0]
    scaled = times_rows(query, keys) * (1.0 / math.sqrt(HEAD_DIM))
    bent = jnp.tanh(scaled / SOFT_CAP)
    row = first + lax.broadcasted_iota(jnp.int32, (rows, width), 0)
    col = lax.broadcasted_iota(jnp.int32, (rows, width), 1)
    allowed = ((segment_col == segment_row) & (col <= row)) | (col == row)
    capped = jnp.where(allowed, SOFT_CAP * bent, MASKED)
    raised = jnp.exp(capped - jnp.max(capped, axis=-1, keepdims=True))
    return raised / jnp.sum(raised, axis=-1, keepdims=True), bent


def attend_kernel(group_size, queries, keys, values, segment_col, segment_row, out):
    seq_len = keys.shape[0]
    for first in range(0, seq_len, QUERY_BLOCK):
        rows = slice(first, first + QUERY_BLOCK)
        width = first + QUERY_BLOCK
        for head in range(group_size):
            cols = slice(head * HEAD_DIM, (head + 1) * HEAD_DIM)
            probs, unused = block_probs(
                queries[rows, cols],
                keys[:width],
                segment_col[rows, :],
                segment_row[:, :width],
                first,
            )
            out[rows, cols] = add_slice(probs.astype(jnp.bfloat16), values[:width]).astype(
                out.dtype
            )


def attend(queries, keys, values, segment_col, segment_row):
    return pl.pallas_call(
        partial(attend_kernel, queries.shape[1] // HEAD_DIM),
        out_shape=jax.ShapeDtypeStruct(queries.shape, jnp.bfloat16),
        compiler_params=pltpu.CompilerParams(vmem_limit_bytes=40 * 1024 * 1024),
    )(queries, keys, values, segment_col, segment_row)


def turn_back(grads, cosine, sine_part):
    half = grads.shape[1] // 2
    first, second = grads[:, :half], grads[:, half:]
    return jnp.concatenate(
        [first * cosine + second * sine_part, second * cosine - first * sine_part], axis=1
    )


def attend_back_kernel(
    group_size,
    queries,
    keys,
    values,
    segment_col,
    segment_row,
    grads,
    cosine,
    sine_part,
    out,
    grad_keys,
    grad_values,
):
    seq_len = keys.shape[0]
    inverse_root = 1.0 / math.sqrt(HEAD_DIM)
    key_cols = slice(group_size * HEAD_DIM, (group_size + 1) * HEAD_DIM)
    value_cols = slice((group_size + 1) * HEAD_DIM, (group_size + 2) * HEAD_DIM)
    grad_keys[...] = jnp.zeros_like(grad_keys)
    grad_values[...] = jnp.zeros_like(grad_values)
    for first in range(0, seq_len, QUERY_BLOCK):
        rows = slice(first, first + QUERY_BLOCK)
        width = first + QUERY_BLOCK
        for head in range(group_size):
            cols = slice(head * HEAD_DIM, (head + 1) * HEAD_DIM)
            query = queries[rows, cols]
            probs, bent = block_probs(
                query, keys[:width], segment_col[rows, :], segment_row[:, :width], first
            )
            grad = grads[rows, cols]
            grad_probs = times_rows(grad, values[:width])
            mean = jnp.sum(probs * grad_probs, axis=-1, keepdims=True)
            grad_scaled = (probs * (grad_probs - mean) * (1.0 - bent * bent)).astype(jnp.bfloat16)
            grad_query = add_slice(grad_scaled, keys[:width]) * inverse_root
            out[rows, cols] = turn_back(grad_query, cosine[rows, :], sine_part[rows, :]).astype(
                out.dtype
            )
            grad_keys[:width, :] += outer_rows(grad_scaled, query) * inverse_root
            grad_values[:width, :] += outer_rows(probs.astype(jnp.bfloat16), grad)
    for first in range(0, seq_len, QUERY_BLOCK):
        rows = slice(first, first + QUERY_BLOCK)
        out[rows, key_cols] = turn_back(
            grad_keys[rows, :], cosine[rows, :], sine_part[rows, :]
        ).astype(out.dtype)
        out[rows, value_cols] = grad_values[rows, :].astype(out.dtype)


def attend_back(queries, keys, values, segment_col, segment_row, grads, cosine, sine_part):
    seq_len, own_width = queries.shape
    return pl.pallas_call(
        partial(attend_back_kernel, own_width // HEAD_DIM),
        out_shape=jax.ShapeDtypeStruct((seq_len, own_width + 2 * HEAD_DIM), jnp.bfloat16),
        scratch_shapes=[
            pltpu.VMEM((seq_len, HEAD_DIM), jnp.float32),
            pltpu.VMEM((seq_len, HEAD_DIM), jnp.float32),
        ],
        compiler_params=pltpu.CompilerParams(vmem_limit_bytes=40 * 1024 * 1024),
    )(queries, keys, values, segment_col, segment_row, grads, cosine, sine_part)


def weight_blocks_kernel(weight_rows, inputs, grads, grad_outs, outs, gains, blocks):
    n_first, n_core, n_chip, block_rows = blocks.shape[:4]
    columns = outs.shape[1]
    for c in range(blocks.shape[4] // columns):
        cols = slice(c * columns, (c + 1) * columns)
        if c * columns < grads.shape[1]:
            total = outer_rows(inputs[...], grads[:, cols])
        else:
            total = outer_rows(grad_outs[...], outs[...])
        for d in range(n_first):
            for q in range(n_chip):
                for core in range(n_core):
                    b = (d * n_chip + q) * n_core + core
                    part = total[b * weight_rows : (b + 1) * weight_rows]
                    part = jnp.concatenate([part, gains[b, :, cols]], axis=0)
                    blocks[d, core, q, :, cols] = part.astype(blocks.dtype)


def weight_blocks(n_seq, inputs, grads, grad_outs, outs, gains):
    seq_len, model_width = inputs.shape
    n_blocks, extra_rows, block_width = gains.shape
    weight_rows = model_width // n_blocks
    steps = 2
    part = model_width // steps
    block = (n_seq // steps, 2, KV_HEADS, weight_rows + extra_rows, block_width)
    whole = lambda i: (0, 0)
    return pl.pallas_call(
        partial(weight_blocks_kernel, weight_rows),
        grid=(steps,),
        out_shape=jax.ShapeDtypeStruct((n_seq,) + block[1:], jnp.bfloat16),
        in_specs=[
            pl.BlockSpec((seq_len, part), lambda i: (0, i)),
            pl.BlockSpec(grads.shape, whole),
            pl.BlockSpec((seq_len, part), lambda i: (0, i)),
            pl.BlockSpec(outs.shape, whole),
            pl.BlockSpec((n_blocks // steps, extra_rows, block_width), lambda i: (i, 0, 0)),
        ],
        out_specs=pl.BlockSpec(block, lambda i: (i, 0, 0, 0, 0)),
        compiler_params=pltpu.CompilerParams(vmem_limit_bytes=56 * 1024 * 1024),
    )(inputs, grads, grad_outs, outs, gains)


def chip_beside(c, flip):
    return c ^ flip


LATE = 3
PAIRS = 2
LATE_COLUMNS = 1


def chip_places(rows, late_rows):
    q = lax.axis_index("chip")
    x, y = lax.rem(q, 2), lax.div(q, 2)
    across = (2 * (1 - y) + 1 - x) * rows
    half = (rows - late_rows) // 2
    return (q * rows, (2 * y + 1 - x) * rows, (2 * (1 - y) + x) * rows, across, across + half)


def send_beside(part, flip):
    return lax.ppermute(part, "chip", [(c, chip_beside(c, flip)) for c in range(KV_HEADS)])


def unit_orders(n):
    units, sums = [], []
    for s in range(n):
        keyed = []
        for d in range(n):
            if d != s:
                near = abs(s - d)
                behind, past = (s, d) if d < s else (n - 1 - s, n - 1 - d)
                keyed += [(near, d, 0), (behind + past + 1, d, 1)]
        order = [(s, 0), (s, 1)] + [(d, h) for unused, d, h in sorted(keyed)]
        units.append([2 * d + h for d, h in order])
        if s in (0, n - 1):
            sums.append(units[-1][2:])
            continue
        keyed = []
        for d in range(n):
            if d != s:
                hops, place = (n - 2 - s, d) if d < s else (s - 1, n - 1 - d)
                keyed += [(n - 2 - place + hops, d, 0), (n - 1 + place + hops, d, 1)]
        sums.append([2 * d + h for unused, d, h in sorted(keyed)])
    return units, sums


def pick(table, s, i):
    width = len(table[0])
    place = s * width + i
    value = 0
    for k, entry in enumerate(entry for row in table for entry in row):
        value = jnp.where(place == k, entry, value)
    return value


SUBS = 1
SUM_TURNS = (0, 1, 4, 5, 8, 8)
GELU_SCALE = math.sqrt(2.0 / math.pi)


def gelu_pieces(gate):
    bend = jnp.tanh(GELU_SCALE * (gate + 0.044715 * gate * gate * gate))
    value = 0.5 * gate * (1.0 + bend)
    slope = 0.5 * (1.0 + bend) + 0.5 * gate * (1.0 - bend * bend) * GELU_SCALE * (
        1.0 + 3.0 * 0.044715 * gate * gate
    )
    return value, slope


def units_kernel(n_seq, backward, *refs):
    if backward:
        tokens, units = refs[:2]
        downs, late = refs[2:7], refs[7]
        kept_gate, kept_up, kept_hidden = refs[8:11]
        out, first_out, second_out, early_grads = refs[11:15]
        late_grads = refs[15 : 15 + LATE_COLUMNS]
        late_parts = refs[15 + LATE_COLUMNS : 15 + 2 * LATE_COLUMNS]
        stage_outs = (first_out, second_out)
        scratch = refs[15 + 2 * LATE_COLUMNS :]
    else:
        tokens, units = refs[:2]
        downs = refs[2:7]
        out, tokens_all, late, first_out, second_out, third_out = refs[7:13]
        stage_outs = (first_out, second_out, third_out)
        scratch = refs[13:]
    units_v, downs_v, held, own_sum, twin_sum, twin_out, line, stage = scratch[:8]
    scratch = scratch[8:]
    if backward:
        kept, kept_sem, tile, tile_sem, load_sem = scratch[:5]
        scratch = scratch[5:]
    else:
        own_hidden = scratch[0]
        scratch = scratch[1:]
    late_send, late_recv = scratch[:2]
    scratch = scratch[2:]
    (
        weight_sem,
        late_sem,
        own_sem,
        left_send,
        right_send,
        token_recv,
        twin_send,
        twin_recv,
        part_send,
        part_recv,
        line_send,
        line_recv,
        stage_sem,
        all_sem,
        out_sem,
    ) = scratch
    n = n_seq
    s = lax.axis_index("seq")
    k = lax.axis_index("core")
    twin = {"core": 1 - k}
    n_units, width = downs_v.shape
    piece_len = tokens.shape[1]
    at_end = (s == 0) | (s == n - 1)

    def token_left(d, h, source):
        return remote(
            source, held.at[d, h, 0], left_send.at[d, h], token_recv.at[d, h], {"seq": s - 1}
        )

    def token_right(d, h, source):
        return remote(
            source, held.at[d, h, 0], right_send.at[d, h], token_recv.at[d, h], {"seq": s + 1}
        )

    def token_twin(d, h, source):
        return remote(source, held.at[d, h, 1], twin_send.at[d, h], twin_recv.at[d, h], twin)

    def part_twin(d, h):
        return remote(
            twin_out.at[d, h], twin_sum.at[d, h], part_send.at[d, h], part_recv.at[d, h], twin
        )

    sub_len = piece_len // SUBS

    def part_line(d, h, sub):
        to_left = d < s
        slot = jnp.where(to_left, d, d + 1)
        rows = pl.ds(sub * sub_len, sub_len)
        return remote(
            twin_sum.at[d, h, rows],
            line.at[slot, h, rows],
            line_send.at[d, h, sub],
            line_recv.at[slot, h, sub],
            {"seq": jnp.where(to_left, s - 1, s + 1)},
        )

    def line_arrival(slot, h, sub):
        rows = pl.ds(sub * sub_len, sub_len)
        return remote(
            twin_sum.at[0, h, rows],
            line.at[slot, h, rows],
            line_send.at[0, h, sub],
            line_recv.at[slot, h, sub],
            {"seq": s},
        )

    def own_load(h):
        return pltpu.make_async_copy(tokens.at[h], held.at[s, h, 0], own_sem.at[h])

    def all_store(d, h):
        return pltpu.make_async_copy(held.at[d, h], tokens_all.at[d, h], all_sem.at[d, h])

    def stage_store(i, d, h, slot):
        return pltpu.make_async_copy(
            stage.at[i, slot], stage_outs[i].at[2 * d + h], stage_sem.at[i, slot]
        )

    def kept_load(i, d, h, slot):
        source = (kept_gate, kept_up)[i]
        return pltpu.make_async_copy(source.at[2 * d + h], kept.at[i, slot], kept_sem.at[i, slot])

    unit_table, sum_table = unit_orders(n)
    right_table = [
        [2 if d == 0 else unit_table[d].index(2 * (d - 1) + 1) + 1 for d in range(n)]
    ]
    left_table = [
        [2 if d == n - 1 else unit_table[d].index(2 * (d + 1) + 1) + 1 for d in range(n)]
    ]

    def source(t):
        unit = pick(unit_table, s, t)
        return lax.div(unit, 2), lax.rem(unit, 2)

    barrier = pltpu.get_barrier_semaphore()
    pl.semaphore_signal(barrier, inc=1, device_id=twin, device_id_type=MESH)

    @pl.when(s > 0)
    def _():
        pl.semaphore_signal(barrier, inc=1, device_id={"seq": s - 1}, device_id_type=MESH)

    @pl.when(s < n - 1)
    def _():
        pl.semaphore_signal(barrier, inc=1, device_id={"seq": s + 1}, device_id_type=MESH)

    greeted = 1 + jnp.where(s > 0, 1, 0) + jnp.where(s < n - 1, 1, 0)
    n_chip, late_rows = late.shape[:2]
    chip_rows = n_units // n_chip
    q = lax.axis_index("chip")
    for step in range(1, n_chip):
        pl.semaphore_signal(
            barrier,
            inc=1,
            device_id={"chip": lax.rem(q + step, n_chip)},
            device_id_type=MESH,
        )
    pl.semaphore_wait(barrier, greeted + n_chip - 1)

    def late_place(chip):
        first = chip * chip_rows + chip_rows - late_rows
        return downs_v.at[pl.ds(pl.multiple_of(first, 16), late_rows)]

    def late_copy(step):
        return remote(
            downs[0].at[pl.ds(chip_rows - late_rows, late_rows)],
            late_place(q),
            late_send.at[step],
            late_recv.at[step],
            {"chip": lax.rem(q + step, n_chip)},
        )

    def late_grad(i, step):
        chip = lax.rem(q + step, n_chip)
        return remote(
            late_grads[i].at[pl.ds(pl.multiple_of(chip * chip_rows, 16), chip_rows)],
            late_parts[i].at[q],
            late_send.at[n_chip * i + step],
            late_recv.at[n_chip * i + step],
            {"chip": chip},
        )

    def late_store(chip):
        return pltpu.make_async_copy(late_place(chip), late.at[chip], late_sem.at[chip])

    def late_load(chip):
        return pltpu.make_async_copy(late.at[chip], late_place(chip), late_sem.at[chip])

    def second_half(t):
        @pl.when((s < n - 1) & (t == pick(right_table, 0, s)))
        def _():
            d, h = jnp.maximum(s - 1, 0), jnp.where(s > 0, 1, 0)
            token_right(d, h, held.at[d, h, 0]).wait_send()
            token_right(s, 1, tokens.at[1]).start()

        @pl.when((s > 0) & (t == pick(left_table, 0, s)))
        def _():
            d, h = jnp.minimum(s + 1, n - 1), jnp.where(s < n - 1, 1, 0)
            token_left(d, h, held.at[d, h, 0]).wait_send()
            token_left(s, 1, tokens.at[1]).start()

    @pl.when(s < n - 1)
    def _():
        token_right(s, 0, tokens.at[0]).start()

    @pl.when(s > 0)
    def _():
        token_left(s, 0, tokens.at[0]).start()

    for h in range(2):
        token_twin(s, h, tokens.at[h]).start()
        own_load(h).start()
    load_units = pltpu.make_async_copy(units, units_v, weight_sem.at[0])
    load_downs = []
    for i, (first, part) in enumerate(zip(chip_places(chip_rows, late_rows), downs)):
        count = chip_rows - late_rows if i == 0 and backward else part.shape[0]
        load_downs.append(
            pltpu.make_async_copy(
                part.at[pl.ds(0, count)],
                downs_v.at[pl.ds(pl.multiple_of(first, 16), count)],
                weight_sem.at[1 + i],
            )
        )
    if backward:
        load_downs += [late_load(chip) for chip in range(n_chip)]
    else:
        for step in (2, 1, 3):
            late_copy(step).start()
    load_units.start()
    for load in load_downs:
        load.start()
    if backward:
        for i in range(2):
            kept_load(i, s, 0, 0).start()
    load_units.wait()
    for load in load_downs:
        load.wait()

    def add_rows(d, h, sub, into_own, use_line):
        step = 16

        def body(i, carry):
            rows = pl.ds(pl.multiple_of(sub * sub_len + i * step, step), step)
            total = own_sum[d, h, rows, :] + twin_sum[d, h, rows, :].astype(jnp.float32)
            for slot in use_line:
                total = total + line[slot, h, rows, :].astype(jnp.float32)
            if into_own:
                own_sum[d, h, rows, :] = total
            else:
                twin_sum[d, h, rows, :] = total.astype(twin_sum.dtype)
            return carry

        lax.fori_loop(0, sub_len // step, body, 0)

    def combine(d, h):
        to_left = d < s
        slot = jnp.where(to_left, d, d + 1)
        more = jnp.where(to_left, s < n - 1, s > 0)
        part_twin(d, h).wait_recv()

        @pl.when(more)
        def _():
            for sub in range(SUBS):
                line_arrival(slot, h, sub).wait_recv()
                add_rows(d, h, sub, False, (slot,))
                part_line(d, h, sub).start()

        @pl.when(jnp.logical_not(more))
        def _():
            for sub in range(SUBS):
                add_rows(d, h, sub, False, ())
                part_line(d, h, sub).start()

    columns = width // 3
    chunk = n_units // 3

    def hidden_forward(d, h, slot):
        rows = held[d, h].reshape(2 * piece_len, width)
        for c in range(3):
            cols = slice(c * chunk, (c + 1) * chunk)
            gate = times_rows(rows, units_v[cols, :width])
            up = times_rows(rows, units_v[cols, width:])
            value, unused = gelu_pieces(gate)
            stage[0, slot, :, cols] = gate.astype(stage.dtype)
            stage[1, slot, :, cols] = up.astype(stage.dtype)
            stage[2, slot, :, cols] = (value * up).astype(stage.dtype)

    def down_forward(d, h, hidden):
        for c in range(3):
            cols = slice(c * columns, (c + 1) * columns)
            part = add_slice(hidden[...], downs_v[:, cols])
            own_sum[d, h, :, cols] = part[:piece_len]
            twin_out[d, h, :, cols] = part[piece_len:].astype(twin_out.dtype)
        part_twin(d, h).start()

    def own_forward(h):
        down_forward(s, h, own_hidden.at[h])

    def compute_backward(d, h, slot):
        rows = held[d, h].reshape(2 * piece_len, width)
        for c in range(3):
            cols = slice(c * chunk, (c + 1) * chunk)
            grad = times_rows(rows, downs_v[cols, :])
            value, slope = gelu_pieces(kept[0, slot, :, cols].astype(jnp.float32))
            up = kept[1, slot, :, cols].astype(jnp.float32)
            stage[0, slot, :, cols] = (grad * up * slope).astype(stage.dtype)
            stage[1, slot, :, cols] = (grad * value).astype(stage.dtype)
        for c in range(3):
            cols = slice(c * columns, (c + 1) * columns)
            later = slice(width + c * columns, width + (c + 1) * columns)
            part = add_slice(stage[0, slot], units_v[:, cols])
            part = part + add_slice(stage[1, slot], units_v[:, later])
            own_sum[d, h, :, cols] = part[:piece_len]
            twin_out[d, h, :, cols] = part[piece_len:].astype(twin_out.dtype)

    row_tile, col_tile = n_units // 3, width // 3

    def down_gradient(between):
        unit_rows = 2 * piece_len
        group_rows = n * unit_rows

        def left_load(u):
            place = downs_v.at[
                pl.ds((u % n) * unit_rows, unit_rows), pl.ds((u // n) * n_units, n_units)
            ]
            return pltpu.make_async_copy(kept_hidden.at[u], place, load_sem.at[u])

        def left_rows(g, first):
            return downs_v[
                :group_rows, pl.ds(pl.multiple_of(g * n_units + first, 128), row_tile)
            ]

        def right_rows(g, first):
            cols = pl.ds(pl.multiple_of(first, 128), col_tile)
            part = held[g * n // 2 : (g + 1) * n // 2, :, :, :, cols]
            return part.reshape(group_rows, col_tile)

        def tile_store(r, c, slot):
            rows = pl.ds(pl.multiple_of(r * row_tile, 16), row_tile)
            if c < LATE_COLUMNS:
                place = late_grads[c].at[rows]
            else:
                place = early_grads.at[rows, pl.ds((c - LATE_COLUMNS) * col_tile, col_tile)]
            return pltpu.make_async_copy(tile.at[slot], place, tile_sem.at[slot])

        for u in range(2 * n):
            left_load(u).start()
        for u in range(2 * n):
            left_load(u).wait()

        def one_tile(c, r, carry):
            slot = lax.rem(r, 2)
            total = sum(
                outer_rows(left_rows(g, r * row_tile), right_rows(g, c * col_tile))
                for g in range(2)
            )

            @pl.when(r >= 2)
            def _():
                tile_store(r, c, slot).wait()

            tile[slot] = total.astype(tile.dtype)
            tile_store(r, c, slot).start()
            for step, turn in enumerate(SUM_TURNS):

                @pl.when(3 * c + r == turn)
                def _():
                    between(step)

            return carry

        for c in range(3):
            lax.fori_loop(0, 3, partial(one_tile, c), 0)
            for slot in range(2):
                tile_store(0, c, slot).wait()
            if c < LATE_COLUMNS:
                for step in (2, 1, 3):
                    late_grad(c, step).start()

    def arrive(t):
        d, h = source(t)
        piece = held.at[d, h, 0]
        token_left(d, h, piece).wait_recv()

        @pl.when((d < s) & (s < n - 1))
        def _():
            token_right(d, h, piece).start()

        @pl.when((d > s) & (s > 0))
        def _():
            token_left(d, h, piece).start()

        token_twin(d, h, piece).start()

    def unit(t, carry):
        d, h = source(t)
        slot = lax.rem(t, 2)

        @pl.when(at_end & (t >= 3))
        def _():
            combine(*source(t - 1))

        @pl.when(t < 2)
        def _():
            own_load(h).wait()

        inner = jnp.logical_not(at_end)
        pair = inner & (t >= 2) & (t < 2 + 2 * PAIRS)

        @pl.when((t >= 2) & (jnp.logical_not(pair) | (lax.rem(t, 2) == 0)))
        def _():
            arrive(t)

        @pl.when(pair & (lax.rem(t, 2) == 0))
        def _():
            arrive(t + 1)

        @pl.when(t >= 2)
        def _():
            for i in range(len(stage_outs)):
                stage_store(i, d, h, slot).wait()

        second_half(t)
        if backward:

            @pl.when(t < 2 * n - 1)
            def _():
                for i in range(2):
                    kept_load(i, *source(t + 1), 1 - slot).start()

            for i in range(2):
                kept_load(i, d, h, slot).wait()
        token_twin(d, h, held.at[d, h, 0]).wait_recv()
        if backward:
            compute_backward(d, h, slot)
            part_twin(d, h).start()
        else:
            hidden_forward(d, h, slot)

            @pl.when(t < 2)
            def _():
                own_hidden[slot] = stage[2, slot]

            @pl.when(t == 2)
            def _():
                for step in range(1, n_chip):
                    late_copy(step).wait_recv()

            @pl.when(t >= 2)
            def _():
                down_forward(d, h, stage.at[2, slot])

        if not backward:
            all_store(d, h).start()
        for i in range(len(stage_outs)):
            stage_store(i, d, h, slot).start()

        return carry

    lax.fori_loop(0, 2 * n, unit, 0)

    second_half(2 * n)

    @pl.when(at_end)
    def _():
        combine(*source(2 * n - 1))

    n_sums = 2 * (n - 1)

    def middle(i):
        @pl.when(jnp.logical_not(at_end) & (i < n_sums))
        def _():
            unit = pick(sum_table, s, i)
            combine(lax.div(unit, 2), lax.rem(unit, 2))

    if backward:
        down_gradient(middle)
    else:

        for chip in range(n_chip):
            late_store(chip).start()

        def one(i, carry):
            middle(i)

            @pl.when((i == 1) | (i == 2))
            def _():
                own_forward(i - 1)

            return carry

        lax.fori_loop(0, n_sums, one, 0)

    def finish(h, carry):
        part_twin(s, h).wait_recv()
        for sub in range(SUBS):

            @pl.when(s < n - 1)
            def _():
                line_arrival(s, h, sub).wait_recv()

            @pl.when(s > 0)
            def _():
                line_arrival(s + 1, h, sub).wait_recv()

            @pl.when(s == 0)
            def _():
                add_rows(s, h, sub, True, (s,))

            @pl.when(s == n - 1)
            def _():
                add_rows(s, h, sub, True, (s + 1,))

            @pl.when(jnp.logical_not(at_end))
            def _():
                add_rows(s, h, sub, True, (s, s + 1))

        pltpu.make_async_copy(own_sum.at[s, h], out.at[h], out_sem.at[h]).start()
        return carry

    lax.fori_loop(0, 2, finish, 0)

    def drain(t, carry):
        d = lax.div(t, 2)
        h = lax.rem(t, 2)
        piece = held.at[d, h, 0]

        right_seen = (d == jnp.maximum(s - 1, 0)) & (h == jnp.where(s > 0, 1, 0))
        left_seen = (d == jnp.minimum(s + 1, n - 1)) & (h == jnp.where(s < n - 1, 1, 0))

        @pl.when((d <= s) & (s < n - 1) & jnp.logical_not(right_seen))
        def _():
            token_right(d, h, piece).wait_send()

        @pl.when((d >= s) & (s > 0) & jnp.logical_not(left_seen))
        def _():
            token_left(d, h, piece).wait_send()

        token_twin(d, h, piece).wait_send()
        part_twin(d, h).wait_send()

        @pl.when(d != s)
        def _():
            for sub in range(SUBS):
                part_line(d, h, sub).wait_send()

        if not backward:
            all_store(d, h).wait()
        return carry

    lax.fori_loop(0, 2 * n, drain, 0)
    if backward:
        for i in range(LATE_COLUMNS):
            for step in range(1, n_chip):
                late_grad(i, step).wait()
    else:
        for step in range(1, n_chip):
            late_copy(step).wait_send()
        for chip in range(n_chip):
            late_store(chip).wait()
    for h in range(2):
        for i in range(len(stage_outs)):
            stage_store(i, 0, h, h).wait()
        pltpu.make_async_copy(own_sum.at[s, h], out.at[h], out_sem.at[h]).wait()


def run_units(n_seq, tokens, units, downs, kept=None):
    backward = kept is not None
    low = tokens.dtype
    n_units = units.shape[0]
    halves, piece_len, width = tokens.shape
    n_stage = 2 if backward else 3
    held = (n_seq, halves, 2, piece_len, width)
    unit_rows = (2 * n_seq, 2 * piece_len, n_units)
    sums = (n_seq, halves, piece_len, width)
    scratch = [
        pltpu.VMEM(units.shape, low),
        pltpu.VMEM((n_units, width), low),
        pltpu.VMEM(held, low),
        pltpu.VMEM(sums, jnp.float32),
        pltpu.VMEM(sums, low),
        pltpu.VMEM(sums, low),
        pltpu.VMEM((n_seq + 1,) + sums[1:], low),
        pltpu.VMEM((n_stage, 2) + unit_rows[1:], low),
    ]
    outs = [jax.ShapeDtypeStruct(tokens.shape, jnp.float32)]
    late_shape = (KV_HEADS, downs[0].shape[0] // LATE, width)
    if backward:
        scratch += [
            pltpu.VMEM((2, 2) + unit_rows[1:], low),
            DMA((2, 2)),
            pltpu.VMEM((2, n_units // 3, width // 3), low),
            DMA((2,)),
            DMA((2 * n_seq,)),
        ]
    else:
        scratch += [pltpu.VMEM((2,) + unit_rows[1:], low)]
        outs += [jax.ShapeDtypeStruct(held, low), jax.ShapeDtypeStruct(late_shape, low)]
    outs += [jax.ShapeDtypeStruct(unit_rows, low)] * n_stage
    if backward:
        column = width // 3
        outs += [jax.ShapeDtypeStruct((n_units, (3 - LATE_COLUMNS) * column), low)]
        outs += [jax.ShapeDtypeStruct((n_units, column), low)] * LATE_COLUMNS
        parts = (KV_HEADS, n_units // KV_HEADS, column)
        outs += [jax.ShapeDtypeStruct(parts, low)] * LATE_COLUMNS
    scratch += [DMA((KV_HEADS * LATE_COLUMNS,)), DMA((KV_HEADS * LATE_COLUMNS,))]
    pairs = DMA((n_seq, halves))
    scratch += [DMA((6,)), DMA((KV_HEADS,)), DMA((halves,))] + [pairs] * 7
    scratch += [DMA((n_seq, halves, SUBS)), DMA((n_seq + 1, halves, SUBS))]
    scratch += [DMA((n_stage, 2)), pairs, DMA((halves,))]
    operands = (tokens, units) + tuple(downs) + (tuple(kept) if backward else ())
    return pl.pallas_call(
        partial(units_kernel, n_seq, backward),
        out_shape=outs,
        in_specs=[ANY] * len(operands),
        out_specs=[ANY] * len(outs),
        scratch_shapes=scratch,
        compiler_params=pltpu.CompilerParams(
            collective_id=6 if backward else 5,
            has_side_effects=True,
            vmem_limit_bytes=63 * 1024 * 1024,
        ),
    )(*operands)


def per_device_general(
    hidden_in,
    norm_gains,
    qkv_weight,
    out_weight,
    gate_up_weight,
    down_weight,
    output_cotangent,
    segment_ids,
    padding,
    positions,
):
    everyone = ("seq", "chip", "core")
    plane = ("chip", "core")
    column = ("seq", "core")
    groups = hidden_in.shape[0]
    piece_len = hidden_in.shape[1]
    model_width = hidden_in.shape[2]
    row_count = groups * piece_len
    seq_len = segment_ids.shape[1]
    group_size = HEADS // KV_HEADS
    query_width = HEADS * HEAD_DIM
    key_width = KV_HEADS * HEAD_DIM
    proj_width = qkv_weight.shape[1]

    residual = hidden_in.reshape(row_count, model_width).astype(jnp.float32)
    factor = lax.rsqrt(jnp.mean(residual * residual, axis=-1, keepdims=True) + EPSILON)
    gain_cols = lax.all_gather(norm_gains, everyone, axis=0, tiled=True).astype(jnp.float32)
    qkv_full = lax.all_gather(qkv_weight, everyone, axis=0, tiled=True)
    attn_input = (residual * factor * gain_cols[:, 0]).astype(jnp.bfloat16)
    projected = add_slice(attn_input, qkv_full)
    cosine, sine_part = rotary_tables(positions.reshape(row_count), HEAD_DIM)
    queries = (
        rotate(projected[:, :query_width].reshape(row_count, HEADS, HEAD_DIM), cosine, sine_part)
        .astype(jnp.bfloat16)
        .reshape(row_count, query_width)
    )
    keys_here = (
        rotate(
            projected[:, query_width : query_width + key_width].reshape(
                row_count, KV_HEADS, HEAD_DIM
            ),
            cosine,
            sine_part,
        )
        .astype(jnp.bfloat16)
        .reshape(groups, piece_len, key_width)
    )
    values_here = (
        projected[:, query_width + key_width :]
        .astype(jnp.bfloat16)
        .reshape(groups, piece_len, key_width)
    )
    both_all = lax.all_gather(
        jnp.concatenate([keys_here, values_here], axis=2), plane, axis=1, tiled=True
    )
    keys_all = both_all[:, :, :key_width]
    values_all = both_all[:, :, key_width:]
    first_query = (lax.axis_index("chip") * 2 + lax.axis_index("core")) * piece_len
    query_rows = first_query + jnp.arange(piece_len, dtype=jnp.int32)
    key_rows = jnp.arange(seq_len, dtype=jnp.int32)
    segment_query = lax.dynamic_slice_in_dim(segment_ids, first_query, piece_len, 1)
    allowed = (segment_query[:, :, None] == segment_ids[:, None, :]) & (
        key_rows[None, None, :] <= query_rows[None, :, None]
    ) & (padding[:, None, :] == 1) | (key_rows[None, None, :] == query_rows[None, :, None])
    allowed = allowed[:, None, None]
    probs = soft_probs(score_block(queries, keys_all), allowed)
    attn_out = mix_values(probs.astype(jnp.bfloat16), values_all)
    out_full = lax.all_gather(out_weight, everyone, axis=0, tiled=True)
    attn_proj = times_rows(attn_out, out_full)
    after_attn = residual + rms_norm(attn_proj, gain_cols[:, 1])
    ffn_input = rms_norm(after_attn, gain_cols[:, 2]).astype(jnp.bfloat16)

    unit_weights = lax.all_gather(gate_up_weight, "chip", axis=0, tiled=True)
    down_units = lax.all_gather(down_weight, "chip", axis=0, tiled=True)
    ffn_all = lax.all_gather(ffn_input, column, axis=0, tiled=True)
    gate_part = times_rows(ffn_all, unit_weights[:, :model_width])
    up_part = times_rows(ffn_all, unit_weights[:, model_width:])
    hidden_part = geglu_parts(gate_part, up_part).astype(jnp.bfloat16)
    down_part = add_slice(hidden_part, down_units).astype(jnp.bfloat16)
    down_out = lax.psum_scatter(down_part, column, scatter_dimension=0, tiled=True).astype(
        jnp.float32
    )
    layer_out = after_attn + rms_norm(down_out, gain_cols[:, 3])
    layer_output = layer_out.astype(jnp.bfloat16).reshape(groups, piece_len, model_width)

    cotangent = output_cotangent.reshape(row_count, model_width).astype(jnp.float32)
    unused_last, pull_last = jax.vjp(rms_norm, down_out, gain_cols[:, 3])
    grad_down, grad_gain_last = pull_last(cotangent)
    grad_down_low = grad_down.astype(jnp.bfloat16)
    grad_down_all = lax.all_gather(grad_down_low, column, axis=0, tiled=True)
    grad_part = times_rows(grad_down_all, down_units)
    unused_units, pull_units = jax.vjp(geglu_parts, gate_part, up_part)
    grad_gate_part, grad_up_part = pull_units(grad_part)
    gate_low = grad_gate_part.astype(jnp.bfloat16)
    up_low = grad_up_part.astype(jnp.bfloat16)
    grad_ffn_part = add_slice(gate_low, unit_weights[:, :model_width]) + add_slice(
        up_low, unit_weights[:, model_width:]
    )
    grad_ffn_in = lax.psum_scatter(
        grad_ffn_part.astype(jnp.bfloat16), column, scatter_dimension=0, tiled=True
    ).astype(jnp.float32)
    gate_up_rows = jnp.concatenate(
        [
            outer_rows(gate_low, ffn_all).astype(jnp.bfloat16),
            outer_rows(up_low, ffn_all).astype(jnp.bfloat16),
        ],
        axis=1,
    )
    down_rows = outer_rows(hidden_part, grad_down_all).astype(jnp.bfloat16)
    gate_up_grad = lax.psum_scatter(
        gate_up_rows, "chip", scatter_dimension=0, tiled=True
    ).astype(jnp.float32)
    down_grad = lax.psum_scatter(down_rows, "chip", scatter_dimension=0, tiled=True).astype(
        jnp.float32
    )

    unused_mid, pull_mid = jax.vjp(rms_norm, after_attn, gain_cols[:, 2])
    grad_after_ffn, grad_gain_mid = pull_mid(grad_ffn_in)
    grad_after = cotangent + grad_after_ffn
    unused_post, pull_post = jax.vjp(rms_norm, attn_proj, gain_cols[:, 1])
    grad_proj, grad_gain_post = pull_post(grad_after)
    grad_proj_low = grad_proj.astype(jnp.bfloat16)
    grad_attn = add_slice(grad_proj_low, out_full).astype(jnp.bfloat16)
    scaled = score_block(queries, keys_all)
    probs, pull_probs = jax.vjp(partial(soft_probs, allowed=allowed), scaled)
    grad_heads = grad_attn.reshape(groups, piece_len, KV_HEADS, group_size, HEAD_DIM)
    query_heads = queries.reshape(groups, piece_len, KV_HEADS, group_size, HEAD_DIM)
    key_heads = keys_all.reshape(groups, seq_len, KV_HEADS, HEAD_DIM)
    value_heads = values_all.reshape(groups, seq_len, KV_HEADS, HEAD_DIM)
    grad_probs = jnp.einsum(
        "spkgd,slkd->skgpl", grad_heads, value_heads, preferred_element_type=jnp.float32
    )
    (grad_scaled,) = pull_probs(grad_probs)
    grad_scaled_low = grad_scaled.astype(jnp.bfloat16)
    inverse_root = 1.0 / math.sqrt(HEAD_DIM)
    grad_query_rot = (
        jnp.einsum(
            "skgpl,slkd->spkgd", grad_scaled_low, key_heads, preferred_element_type=jnp.float32
        )
        * inverse_root
    )
    grad_key_rot = (
        jnp.einsum(
            "skgpl,spkgd->slkd", grad_scaled_low, query_heads, preferred_element_type=jnp.float32
        )
        * inverse_root
    )
    grad_value_part = jnp.einsum(
        "skgpl,spkgd->slkd",
        probs.astype(jnp.bfloat16),
        grad_heads,
        preferred_element_type=jnp.float32,
    )
    both_grads = jnp.concatenate(
        [
            grad_key_rot.reshape(groups, seq_len, key_width),
            grad_value_part.reshape(groups, seq_len, key_width),
        ],
        axis=2,
    ).astype(jnp.bfloat16)
    both_summed = lax.psum_scatter(both_grads, plane, scatter_dimension=1, tiled=True)
    both_summed = both_summed.astype(jnp.float32).reshape(row_count, 2 * key_width)
    key_summed = both_summed[:, :key_width]
    value_summed = both_summed[:, key_width:]
    grad_queries = rotate_back(
        grad_query_rot.reshape(row_count, HEADS, HEAD_DIM), cosine, sine_part
    ).reshape(row_count, query_width)
    grad_keys = rotate_back(
        key_summed.reshape(row_count, KV_HEADS, HEAD_DIM), cosine, sine_part
    ).reshape(row_count, key_width)
    grad_projected = jnp.concatenate([grad_queries, grad_keys, value_summed], axis=1).astype(
        jnp.bfloat16
    )
    grad_attn_in = times_rows(grad_projected, qkv_full)
    unused_first, pull_first = jax.vjp(rms_norm, residual, gain_cols[:, 0])
    grad_res_first, grad_gain_first = pull_first(grad_attn_in)
    input_grad = (grad_after + grad_res_first).reshape(groups, piece_len, model_width)
    gain_terms = jnp.stack([grad_gain_first, grad_gain_post, grad_gain_mid, grad_gain_last], axis=1)
    qkv_part = outer_rows(attn_input, grad_projected).astype(jnp.bfloat16)
    out_part = outer_rows(grad_proj_low, attn_out).astype(jnp.bfloat16)
    qkv_grad = lax.psum_scatter(qkv_part, everyone, scatter_dimension=0, tiled=True).astype(
        jnp.float32
    )
    out_proj_grad = lax.psum_scatter(out_part, everyone, scatter_dimension=0, tiled=True).astype(
        jnp.float32
    )
    gain_grad = lax.psum_scatter(gain_terms, everyone, scatter_dimension=0, tiled=True)
    return (layer_output, input_grad, gain_grad, qkv_grad, out_proj_grad, gate_up_grad, down_grad)


def per_device_by_heads(
    n_seq,
    hidden_in,
    norm_gains,
    qkv_weight,
    out_weight,
    gate_up_weight,
    down_weight,
    output_cotangent,
    segment_ids,
    padding,
    positions,
):
    groups, piece_len, model_width = hidden_in.shape
    row_count = groups * piece_len
    seq_len = segment_ids.shape[1]
    n_chip = KV_HEADS
    n_plane = 2 * n_chip
    group_size = HEADS // KV_HEADS
    query_width = HEADS * HEAD_DIM
    key_width = KV_HEADS * HEAD_DIM
    own_width = group_size * HEAD_DIM
    part_width = own_width + 2 * HEAD_DIM
    block_width = part_width + own_width
    weight_rows = qkv_weight.shape[0]
    extra_rows = 16 - weight_rows % 16
    block_rows = weight_rows + extra_rows
    core = lax.axis_index("core")

    gain_rows = jnp.pad(
        norm_gains.T, ((0, extra_rows - norm_gains.shape[1]), (0, block_width - weight_rows))
    )
    blocks = jnp.stack(
        [
            jnp.concatenate(
                [
                    jnp.concatenate(
                        [
                            qkv_weight[:, c * own_width : (c + 1) * own_width],
                            qkv_weight[
                                :, query_width + c * HEAD_DIM : query_width + (c + 1) * HEAD_DIM
                            ],
                            qkv_weight[
                                :,
                                query_width + key_width + c * HEAD_DIM : query_width
                                + key_width
                                + (c + 1) * HEAD_DIM,
                            ],
                            out_weight[:, c * own_width : (c + 1) * own_width],
                        ],
                        axis=1,
                    ),
                    gain_rows,
                ],
                axis=0,
            )
            for c in range(n_chip)
        ]
    )
    hidden_all, blocks_all = gather_first(n_seq, hidden_in, blocks)
    unit_weights = lax.all_gather(gate_up_weight, "chip", axis=0, tiled=True)
    blocks_all, down_weight = lax.optimization_barrier((blocks_all, down_weight))
    early = down_weight.shape[0] - down_weight.shape[0] // LATE
    down_x, down_y = send_beside(down_weight[:early], 1), send_beside(down_weight[:early], 2)
    blocks_all = blocks_all.transpose(0, 2, 1, 3, 4)
    own_weights = blocks_all[:, :, :, :weight_rows].reshape(model_width, block_width)
    own_qkv = own_weights[:, :part_width]
    own_out = own_weights[:, part_width:]
    gain_cols = (
        blocks_all[:, :, :, weight_rows : weight_rows + norm_gains.shape[1], :weight_rows]
        .transpose(0, 1, 2, 4, 3)
        .reshape(model_width, norm_gains.shape[1])
        .astype(jnp.float32)
    )

    seq_rows = hidden_all.reshape(seq_len, model_width).astype(jnp.float32)
    seq_factor = lax.rsqrt(jnp.mean(seq_rows * seq_rows, axis=-1, keepdims=True) + EPSILON)
    attn_input = (seq_rows * seq_factor * gain_cols[:, 0]).astype(jnp.bfloat16)
    projected = add_slice(attn_input, own_qkv)
    segment = lax.dynamic_index_in_dim(segment_ids, core, 0, keepdims=False)
    valid = lax.dynamic_index_in_dim(padding, core, 0, keepdims=False)
    token = jnp.arange(seq_len, dtype=jnp.int32)
    document_start = jnp.min(
        jnp.where(segment[:, None] == segment[None, :], token[None, :], seq_len), axis=1
    )
    cosine, sine_part = rotary_tables(token - document_start, HEAD_DIM)
    queries = (
        rotate(projected[:, :own_width].reshape(seq_len, group_size, HEAD_DIM), cosine, sine_part)
        .astype(jnp.bfloat16)
        .reshape(seq_len, own_width)
    )
    keys = (
        rotate(
            projected[:, own_width : own_width + HEAD_DIM].reshape(seq_len, 1, HEAD_DIM),
            cosine,
            sine_part,
        )
        .astype(jnp.bfloat16)
        .reshape(seq_len, HEAD_DIM)
    )
    values = projected[:, own_width + HEAD_DIM :].astype(jnp.bfloat16)
    segment_col = segment[:, None]
    segment_row = jnp.where(valid == 1, segment, -1)[None, :]
    attn_out = attend(queries, keys, values, segment_col, segment_row)
    proj_parts = times_rows(attn_out, own_out).astype(jnp.bfloat16)
    proj_parts, down_across = merge_plane(
        proj_parts.reshape(n_plane, piece_len, model_width), down_x, down_y, 2
    )
    down_units = (down_weight, down_x, down_y, down_across[0], down_across[1])

    def sum_parts(parts):
        return jnp.sum(parts.astype(jnp.float32), axis=0).reshape(row_count, model_width)

    attn_proj = sum_parts(proj_parts)
    residual = hidden_in.reshape(row_count, model_width).astype(jnp.float32)
    after_attn = residual + rms_norm(attn_proj, gain_cols[:, 1])
    ffn_input = rms_norm(after_attn, gain_cols[:, 2]).astype(jnp.bfloat16)

    pieces = (groups, piece_len, model_width)
    down_out, ffn_all, down_late, gate_part, up_part, hidden_part = run_units(
        n_seq, ffn_input.reshape(pieces), unit_weights, down_units
    )
    down_out = down_out.reshape(row_count, model_width)
    layer_out = after_attn + rms_norm(down_out, gain_cols[:, 3])
    layer_output = layer_out.astype(jnp.bfloat16).reshape(pieces)

    cotangent = output_cotangent.reshape(row_count, model_width).astype(jnp.float32)
    unused_last, pull_last = jax.vjp(rms_norm, down_out, gain_cols[:, 3])
    grad_down, grad_gain_last = pull_last(cotangent)
    grad_ffn_in, gate_low, up_low, early_rows, *late = run_units(
        n_seq,
        grad_down.astype(jnp.bfloat16).reshape(pieces),
        unit_weights,
        down_units,
        (down_late, gate_part, up_part, hidden_part),
    )
    grad_ffn_in = grad_ffn_in.reshape(row_count, model_width)
    chip = lax.axis_index("chip")
    chips = jnp.arange(n_chip, dtype=jnp.int32)[:, None, None]
    down_columns = []
    for grads, parts in zip(late[:LATE_COLUMNS], late[LATE_COLUMNS:]):
        own = lax.dynamic_slice_in_dim(grads, chip * parts.shape[1], parts.shape[1], 0)
        parts = jnp.where(chips == chip, own[None], parts)
        down_columns.append(jnp.sum(parts.astype(jnp.float32), axis=0))
    if LATE_COLUMNS < 3:
        early_grad = lax.psum_scatter(early_rows, "chip", scatter_dimension=0, tiled=True)
        down_columns.append(early_grad.astype(jnp.float32))
    down_grad = jnp.concatenate(down_columns, axis=1)

    unused_mid, pull_mid = jax.vjp(rms_norm, after_attn, gain_cols[:, 2])
    grad_after_ffn, grad_gain_mid = pull_mid(grad_ffn_in)
    grad_after = cotangent + grad_after_ffn
    unused_post, pull_post = jax.vjp(rms_norm, attn_proj, gain_cols[:, 1])
    grad_proj, grad_gain_post = pull_post(grad_after)
    grad_proj_low = grad_proj.astype(jnp.bfloat16)

    grad_proj_all, gate_up_rows = spread_plane(
        grad_proj_low.reshape(groups, piece_len, model_width), gate_low, up_low, ffn_all
    )
    gate_up_grad = lax.psum_scatter(
        gate_up_rows, "chip", scatter_dimension=0, tiled=True
    ).astype(jnp.float32)
    grad_proj_all = grad_proj_all.reshape(seq_len, model_width)
    grad_attn = add_slice(grad_proj_all, own_out).astype(jnp.bfloat16)
    grad_projected = attend_back(
        queries,
        keys,
        values,
        segment_col,
        segment_row,
        grad_attn,
        cosine[:, 0],
        sine_part[:, 0],
    )
    grad_in_part = times_rows(grad_projected, own_qkv)
    grad_gain_first = jnp.sum(grad_in_part * seq_rows * seq_factor, axis=0)
    gain_terms = (
        jnp.stack([grad_gain_first, grad_gain_post, grad_gain_mid, grad_gain_last])
        .reshape(-1, n_seq * n_plane, weight_rows)
        .transpose(1, 0, 2)
    )
    gain_terms = jnp.pad(
        gain_terms,
        ((0, 0), (0, extra_rows - gain_terms.shape[1]), (0, block_width - weight_rows)),
    )
    grad_blocks = weight_blocks(
        n_seq, attn_input, grad_projected, grad_proj_all, attn_out, gain_terms
    )
    grad_in_parts, grad_sums = sum_last(
        n_seq,
        grad_in_part.astype(jnp.bfloat16).reshape(n_plane, piece_len, model_width),
        grad_blocks,
    )
    grad_attn_in = sum_parts(grad_in_parts)
    factor = lax.rsqrt(jnp.mean(residual * residual, axis=-1, keepdims=True) + EPSILON)
    unused_first, pull_first = jax.vjp(rms_norm, residual, gain_cols[:, 0])
    grad_res_first, unused_gain = pull_first(grad_attn_in)
    input_grad = (grad_after + grad_res_first).reshape(groups, piece_len, model_width)

    weight_sums = grad_sums[:, :weight_rows].astype(jnp.float32)
    qkv_grad = jnp.concatenate(
        [weight_sums[c, :, :own_width] for c in range(n_chip)]
        + [weight_sums[c, :, own_width : own_width + HEAD_DIM] for c in range(n_chip)]
        + [weight_sums[c, :, own_width + HEAD_DIM : part_width] for c in range(n_chip)],
        axis=1,
    )
    out_proj_grad = jnp.concatenate(
        [weight_sums[c, :, part_width:] for c in range(n_chip)], axis=1
    )
    gain_grad = jnp.sum(
        grad_sums[:, weight_rows : weight_rows + norm_gains.shape[1], :weight_rows].astype(
            jnp.float32
        ),
        axis=0,
    ).T
    return (layer_output, input_grad, gain_grad, qkv_grad, out_proj_grad, gate_up_grad, down_grad)


def solution(mesh):
    n_seq = mesh.shape["seq"]
    n_ctx = mesh.shape["ctx"]
    split_mesh = jax.sharding.Mesh(
        mesh.devices.reshape(n_seq, n_ctx // 2, 2), ("seq", "chip", "core")
    )
    plane = ("chip", "core")
    rows = P(("seq", "chip", "core"), None)
    tokens = P("seq", plane, None)
    placed = (
        tokens,
        rows,
        rows,
        rows,
        rows,
        rows,
        tokens,
        P("seq", None),
        P("seq", None),
        P("seq", plane),
    )

    def step(*arrays):
        groups = arrays[0].shape[0]
        if n_ctx // 2 == KV_HEADS and groups == 2 and n_seq == 4:
            return per_device_by_heads(n_seq, *arrays)
        return per_device_general(*arrays)

    return jax.shard_map(
        step,
        mesh=split_mesh,
        in_specs=placed,
        out_specs=(tokens, tokens, rows, rows, rows, rows, rows),
        check_vma=False,
    )
```

```python
from functools import partial
import math

import jax
import jax.numpy as jnp
from jax import lax
from jax.experimental import pallas as pl
from jax.experimental.pallas import tpu as pltpu
from jax.sharding import PartitionSpec as P

HEADS = 8
KV_HEADS = 4
HEAD_DIM = 256


EPSILON = 1e-06
SOFT_CAP = 50.0
MASKED = -1e30


def rms_norm(matrix, gain_col):
    factor = lax.rsqrt(jnp.mean(matrix * matrix, axis=-1, keepdims=True) + EPSILON)
    return matrix * factor * gain_col


def rotary_tables(positions, head_dim):
    half_dim = head_dim // 2
    frequency = jnp.exp(
        jnp.arange(half_dim, dtype=jnp.float32) * (-2.0 * math.log(10000.0) / head_dim)
    )
    phase_angle = positions.astype(jnp.float32)[:, None] * frequency[None, :]
    return (jnp.cos(phase_angle)[:, None, :], jnp.sin(phase_angle)[:, None, :])


def rotate(vectors, cosine, sine_part):
    half_dim = vectors.shape[-1] // 2
    first_half = vectors[..., :half_dim]
    second_half = vectors[..., half_dim:]
    return jnp.concatenate(
        [
            first_half * cosine - second_half * sine_part,
            second_half * cosine + first_half * sine_part,
        ],
        axis=-1,
    )


def rotate_back(grads, cosine, sine_part):
    half_dim = grads.shape[-1] // 2
    first_half = grads[..., :half_dim]
    second_half = grads[..., half_dim:]
    return jnp.concatenate(
        [
            first_half * cosine + second_half * sine_part,
            second_half * cosine - first_half * sine_part,
        ],
        axis=-1,
    )


def soft_probs(scaled, allowed):
    capped = SOFT_CAP * jnp.tanh(scaled / SOFT_CAP)
    capped = jnp.where(allowed, capped, MASKED)
    return jax.nn.softmax(capped, axis=-1)


def geglu_parts(gate_part, up_part):
    return jax.nn.gelu(gate_part, approximate=True) * up_part


def score_block(queries, keys_all):
    groups = keys_all.shape[0]
    seq_len = keys_all.shape[1]
    piece_len = queries.shape[0] // groups
    query_heads = queries.reshape(groups, piece_len, KV_HEADS, HEADS // KV_HEADS, HEAD_DIM)
    key_heads = keys_all.reshape(groups, seq_len, KV_HEADS, HEAD_DIM)
    raw_score = jnp.einsum(
        "spkgd,slkd->skgpl", query_heads, key_heads, preferred_element_type=jnp.float32
    )
    return raw_score * (1.0 / math.sqrt(HEAD_DIM))


def mix_values(weights_low, values_all):
    groups = values_all.shape[0]
    seq_len = values_all.shape[1]
    piece_len = weights_low.shape[3]
    value_heads = values_all.reshape(groups, seq_len, KV_HEADS, HEAD_DIM)
    mixed = jnp.einsum(
        "skgpl,slkd->spkgd", weights_low, value_heads, preferred_element_type=jnp.float32
    )
    return mixed.reshape(groups * piece_len, HEADS * HEAD_DIM).astype(jnp.bfloat16)


def add_slice(left, weight_piece):
    return jnp.dot(left, weight_piece, preferred_element_type=jnp.float32)


def times_rows(left, weight_piece):
    return lax.dot_general(
        left, weight_piece, (((1,), (1,)), ((), ())), preferred_element_type=jnp.float32
    )


def outer_rows(left, right):
    return lax.dot_general(
        left, right, (((0,), (0,)), ((), ())), preferred_element_type=jnp.float32
    )


MESH = pl.DeviceIdType.MESH
ANY = pl.BlockSpec(memory_space=pl.ANY)
DMA = pltpu.SemaphoreType.DMA


def remote(source, target, send_sem, recv_sem, device):
    return pltpu.make_async_remote_copy(
        src_ref=source,
        dst_ref=target,
        send_sem=send_sem,
        recv_sem=recv_sem,
        device_id=device,
        device_id_type=MESH,
    )


def line_neighbours(s, n_seq):
    return {"seq": jnp.maximum(s - 1, 0)}, {"seq": jnp.minimum(s + 1, n_seq - 1)}


def plane_device(index):
    return {"chip": index // 2, "core": lax.rem(index, 2)}


def greet(n_plane, n_seq):
    me = lax.axis_index("chip") * 2 + lax.axis_index("core")
    barrier = pltpu.get_barrier_semaphore()
    for step in range(1, n_plane):
        pl.semaphore_signal(
            barrier,
            inc=1,
            device_id=plane_device(lax.rem(me + step, n_plane)),
            device_id_type=MESH,
        )
    count = n_plane - 1
    if n_seq > 1:
        s = lax.axis_index("seq")

        @pl.when(s > 0)
        def _():
            pl.semaphore_signal(barrier, inc=1, device_id={"seq": s - 1}, device_id_type=MESH)

        @pl.when(s < n_seq - 1)
        def _():
            pl.semaphore_signal(barrier, inc=1, device_id={"seq": s + 1}, device_id_type=MESH)

        count = count + jnp.where(s > 0, 1, 0) + jnp.where(s < n_seq - 1, 1, 0)
    pl.semaphore_wait(barrier, count)


def chip_at(q, flip):
    x, y = lax.rem(q, 2), q // 2
    x = 1 - x if flip in (1, 3) else x
    y = 1 - y if flip in (2, 3) else y
    return y * 2 + x


class Merge:
    def __init__(self, source, target, added, own_part, sems):
        self.source, self.target, self.added, self.own_part = source, target, added, own_part
        self.send_sems, self.recv_sems, self.load_sems, self.local_sems = sems
        self.q = lax.axis_index("chip")
        self.k = lax.axis_index("core")
        self.half = source.shape[1] // 2

    def rows(self, flip):
        return pl.ds(0 if flip == 1 else self.half, self.half)

    def direct(self, flip, core):
        chip = chip_at(self.q, flip)
        slot = 6 * (flip - 1) + core
        return remote(
            self.source.at[2 * chip + core, self.rows(flip)],
            self.target.at[1, self.k, self.rows(flip)],
            self.send_sems.at[slot],
            self.recv_sems.at[6 * (flip - 1) + self.k],
            {"chip": chip, "core": core},
        )

    def arrival(self, flip, core):
        return remote(
            self.source.at[0, self.rows(flip)],
            self.target.at[1, core, self.rows(flip)],
            self.send_sems.at[0],
            self.recv_sems.at[6 * (flip - 1) + core],
            {"chip": chip_at(self.q, flip)},
        )

    def across(self, flip, core):
        slot = 6 * (flip - 1) + 2 + core
        return remote(
            self.source.at[2 * chip_at(self.q, 3) + core, self.rows(flip)],
            self.added.at[flip - 1, core],
            self.send_sems.at[slot],
            self.recv_sems.at[slot],
            {"chip": chip_at(self.q, flip)},
        )

    def load(self, flip, core):
        return pltpu.make_async_copy(
            self.source.at[2 * chip_at(self.q, 3 - flip) + core, self.rows(flip)],
            self.own_part.at[flip - 1, core],
            self.load_sems.at[flip - 1, core],
        )

    def summed(self, flip, core):
        slot = 6 * (flip - 1) + 4 + core
        return remote(
            self.own_part.at[flip - 1, core],
            self.target.at[2, self.k, self.rows(flip)],
            self.send_sems.at[slot],
            self.recv_sems.at[6 * (flip - 1) + 4 + self.k],
            {"chip": chip_at(self.q, 3 - flip), "core": core},
        )

    def summed_arrival(self, flip, core):
        return remote(
            self.own_part.at[flip - 1, 0],
            self.target.at[2, core, self.rows(flip)],
            self.send_sems.at[0],
            self.recv_sems.at[6 * (flip - 1) + 4 + core],
            {"chip": chip_at(self.q, 3 - flip)},
        )

    def twin(self):
        return remote(
            self.source.at[2 * self.q + 1 - self.k],
            self.target.at[0, self.k],
            self.send_sems.at[12],
            self.recv_sems.at[12],
            {"core": 1 - self.k},
        )

    def twin_arrival(self):
        return remote(
            self.source.at[0],
            self.target.at[0, 1 - self.k],
            self.send_sems.at[12],
            self.recv_sems.at[12],
            {"core": 1 - self.k},
        )

    def own(self):
        return pltpu.make_async_copy(
            self.source.at[2 * self.q + self.k], self.target.at[0, self.k], self.local_sems.at[0]
        )

    def start(self):
        pairs = [(flip, core) for core in (0, 1) for flip in (1, 2)]
        for flip, core in pairs:
            self.across(flip, core).start()
        for flip, core in pairs:
            self.load(flip, core).start()
        for flip, core in pairs:
            self.direct(flip, core).start()
        self.twin().start()
        self.own().start()

    def pass_on(self):
        step = 16
        for core in (0, 1):
            for flip in (1, 2):
                self.load(flip, core).wait()
                self.across(flip, core).wait_recv()

                def body(i, carry, flip=flip, core=core):
                    rows = pl.ds(pl.multiple_of(i * step, step), step)
                    total = self.own_part[flip - 1, core, rows, :].astype(jnp.float32)
                    total = total + self.added[flip - 1, core, rows, :].astype(jnp.float32)
                    self.own_part[flip - 1, core, rows, :] = total.astype(self.own_part.dtype)
                    return carry

                lax.fori_loop(0, self.half // step, body, 0)
                self.summed(flip, core).start()

    def finish(self):
        for core in (0, 1):
            for flip in (1, 2):
                self.across(flip, core).wait_send()
                self.direct(flip, core).wait_send()
                self.arrival(flip, core).wait_recv()
                self.summed(flip, core).wait_send()
                self.summed_arrival(flip, core).wait_recv()
        self.twin().wait_send()
        self.twin_arrival().wait_recv()
        self.own().wait()


def merge_scratch(blocks):
    part = (2, 2, blocks.shape[1] // 2, blocks.shape[2])
    return [
        pltpu.VMEM(part, blocks.dtype),
        pltpu.VMEM(part, blocks.dtype),
        DMA((13,)),
        DMA((13,)),
        DMA((2, 2)),
        DMA((1,)),
    ]


def merged_shape(blocks):
    return jax.ShapeDtypeStruct((3, 2) + blocks.shape[1:], blocks.dtype)


class Spread:
    def __init__(self, source, target, send_sems, recv_sems, local_sem):
        self.source, self.target = source, target
        self.send_sems, self.recv_sems = send_sems, recv_sems
        self.local_sem = local_sem
        self.q = lax.axis_index("chip")
        self.k = lax.axis_index("core")
        self.half = source.shape[1] // 2

    def chip(self, flip):
        return chip_at(self.q, flip)

    def direct(self, flip, twin):
        core = 1 - self.k if twin else self.k
        slot = 2 * flip + twin
        return remote(
            self.source.at[core],
            self.target.at[2 * self.q + self.k],
            self.send_sems.at[slot],
            self.recv_sems.at[slot],
            {"chip": self.chip(flip), "core": core},
        )

    def passed(self, flip, twin):
        core = 1 - self.k if twin else self.k
        slot = 8 + 2 * (flip - 1) + twin
        rows = pl.ds(0 if flip == 1 else self.half, self.half)
        block = self.target.at[2 * self.chip(flip) + core, rows]
        return remote(
            block,
            block,
            self.send_sems.at[slot],
            self.recv_sems.at[slot],
            {"chip": self.chip(3 - flip)},
        )

    def own(self):
        return pltpu.make_async_copy(
            self.source.at[self.k],
            self.target.at[2 * self.q + self.k],
            self.local_sem.at[0],
        )

    def start(self):
        for twin in (0, 1):
            for flip in (1, 2):
                self.direct(flip, twin).start()
        self.direct(0, 1).start()
        self.own().start()

    def pass_on(self):
        for twin in (0, 1):
            for flip in (1, 2):
                self.direct(flip, twin).wait_recv()
                self.passed(flip, twin).start()

    def finish(self):
        for twin in (0, 1):
            for flip in (1, 2):
                self.passed(flip, twin).wait()
                self.direct(flip, twin).wait_send()
        self.direct(0, 1).wait()
        self.own().wait()


SPREAD_SLOTS = 12


def merge_kernel(n_plane, source, rows_x, rows_y, target, across, added, own_part, *sems):
    greet(n_plane, 1)
    merge = Merge(source, target, added, own_part, sems[:4])
    pass_send, pass_recv = sems[4:]
    merge.start()
    half = rows_x.shape[0] // 2
    passed = [
        remote(
            rows.at[pl.ds(i * half, half)],
            across.at[i],
            pass_send.at[i],
            pass_recv.at[i],
            {"chip": chip_at(merge.q, 2 - i)},
        )
        for i, rows in enumerate((rows_x, rows_y))
    ]
    for copy in passed:
        copy.start()
    merge.pass_on()
    merge.finish()
    for copy in passed:
        copy.wait()


def merge_plane(blocks, rows_x, rows_y, collective_id):
    half = (2, rows_x.shape[0] // 2, rows_x.shape[1])
    return pl.pallas_call(
        partial(merge_kernel, 2 * KV_HEADS),
        out_shape=[merged_shape(blocks), jax.ShapeDtypeStruct(half, rows_x.dtype)],
        in_specs=[ANY] * 3,
        out_specs=[ANY] * 2,
        scratch_shapes=merge_scratch(blocks) + [DMA((2,)), DMA((2,))],
        compiler_params=pltpu.CompilerParams(
            collective_id=collective_id, has_side_effects=True
        ),
    )(blocks, rows_x, rows_y)


def spread_kernel(
    n_plane,
    blocks,
    low_gate,
    low_up,
    tokens,
    target,
    grads,
    left,
    right,
    tile,
    send_sems,
    recv_sems,
    local_sem,
    load_sem,
    row_sem,
    tile_sem,
):
    greet(n_plane, 1)
    spread = Spread(blocks, target, send_sems, recv_sems, local_sem)
    spread.start()
    n_units, unit_rows, units = low_gate.shape
    width = right.shape[1]
    piece_len = tokens.shape[3]
    loads = []
    for i, source in enumerate((low_gate, low_up)):
        for u in range(n_units):
            place = left.at[i, pl.ds(u * unit_rows, unit_rows)]
            loads.append(pltpu.make_async_copy(source.at[u], place, load_sem.at[i, u]))
    for u in range(n_units):
        for half in range(2):
            place = right.at[pl.ds(u * unit_rows + half * piece_len, piece_len)]
            source = tokens.at[u // 2, u % 2, half]
            loads.append(pltpu.make_async_copy(source, place, row_sem.at[u, half]))
    for load in loads:
        load.start()
    for load in loads:
        load.wait()
    row_tile, col_tile = units // 3, width // 3

    def tile_store(i, r, c, slot):
        rows = pl.ds(pl.multiple_of(r * row_tile, 16), row_tile)
        cols = pl.ds(pl.multiple_of(i * width + c * col_tile, 128), col_tile)
        return pltpu.make_async_copy(tile.at[slot], grads.at[rows, cols], tile_sem.at[slot])

    def one_tile(j, carry):
        i, slot = lax.div(j, 9), lax.rem(j, 2)
        r, c = lax.div(lax.rem(j, 9), 3), lax.rem(j, 3)
        rows = pl.ds(pl.multiple_of(r * row_tile, 128), row_tile)
        cols = pl.ds(pl.multiple_of(c * col_tile, 128), col_tile)
        total = outer_rows(left[i, :, rows], right[:, cols])

        @pl.when(j >= 2)
        def _():
            tile_store(i, r, c, slot).wait()

        tile[slot] = total.astype(tile.dtype)
        tile_store(i, r, c, slot).start()
        return carry

    lax.fori_loop(0, PASS_TURN, one_tile, 0)
    spread.pass_on()
    lax.fori_loop(PASS_TURN, 18, one_tile, 0)
    for slot in range(2):
        tile_store(0, 0, 0, slot).wait()
    spread.finish()


PASS_TURN = 14


def spread_plane(blocks, low_gate, low_up, tokens):
    n_plane = 2 * KV_HEADS
    low = blocks.dtype
    n_units, unit_rows, units = low_gate.shape
    width = blocks.shape[2]
    return pl.pallas_call(
        partial(spread_kernel, n_plane),
        out_shape=[
            jax.ShapeDtypeStruct((n_plane,) + blocks.shape[1:], low),
            jax.ShapeDtypeStruct((units, 2 * width), low),
        ],
        in_specs=[ANY] * 4,
        out_specs=[ANY, ANY],
        scratch_shapes=[
            pltpu.VMEM((2, n_units * unit_rows, units), low),
            pltpu.VMEM((n_units * unit_rows, width), low),
            pltpu.VMEM((2, units // 3, width // 3), low),
            DMA((SPREAD_SLOTS,)),
            DMA((SPREAD_SLOTS,)),
            DMA((1,)),
            DMA((2, n_units)),
            DMA((n_units, 2)),
            DMA((2,)),
        ],
        compiler_params=pltpu.CompilerParams(
            collective_id=3, has_side_effects=True, vmem_limit_bytes=48 * 1024 * 1024
        ),
    )(blocks, low_gate, low_up, tokens)


def gather_kernel(
    n_seq,
    n_plane,
    hidden,
    blocks,
    hidden_all,
    blocks_all,
    hid_send,
    hid_recv,
    hid_local,
    chip_send,
    chip_recv,
    chip_local,
    left_send,
    right_send,
    line_recv,
    twin_send,
    twin_recv,
):
    n_chip = n_plane // 2
    s = lax.axis_index("seq")
    q = lax.axis_index("chip")
    k = lax.axis_index("core")
    before, after = line_neighbours(s, n_seq)
    greet(n_plane, n_seq)
    swaps = []
    for step in range(1, n_chip):
        to = lax.rem(q + step, n_chip)
        copy = remote(
            blocks.at[to],
            blocks_all.at[s, k, q],
            chip_send.at[step],
            chip_recv.at[step],
            {"chip": to},
        )
        copy.start()
        swaps.append(copy)
    own = pltpu.make_async_copy(blocks.at[q], blocks_all.at[s, k, q], chip_local.at[0])
    own.start()
    spread = Spread(hidden, hidden_all, hid_send, hid_recv, hid_local)
    for copy in swaps:
        copy.wait_recv()
    own.wait()
    spread.start()

    def to_left(d):
        return remote(
            blocks_all.at[d, k], blocks_all.at[d, k], left_send.at[d], line_recv.at[d], before
        )

    def to_right(d):
        return remote(
            blocks_all.at[d, k], blocks_all.at[d, k], right_send.at[d], line_recv.at[d], after
        )

    def to_twin(d):
        return remote(
            blocks_all.at[d, k], blocks_all.at[d, k], twin_send.at[d], twin_recv.at[d], {"core": 1 - k}
        )

    def from_twin(d):
        return remote(
            blocks_all.at[d, 1 - k],
            blocks_all.at[d, 1 - k],
            twin_send.at[d],
            twin_recv.at[d],
            {"core": 1 - k},
        )

    @pl.when(s > 0)
    def _():
        to_left(s).start()

    @pl.when(s < n_seq - 1)
    def _():
        to_right(s).start()

    to_twin(s).start()
    for hop in range(1, n_seq):
        if hop == 2:
            spread.pass_on()
        from_left = s - hop
        from_right = s + hop

        @pl.when(from_left >= 0)
        def _():
            to_left(from_left).wait_recv()

            @pl.when(s < n_seq - 1)
            def _():
                to_right(from_left).start()

            to_twin(from_left).start()

        @pl.when(from_right < n_seq)
        def _():
            to_right(from_right).wait_recv()

            @pl.when(s > 0)
            def _():
                to_left(from_right).start()

            to_twin(from_right).start()

    for d in range(n_seq):

        @pl.when((d >= s) & (s > 0))
        def _():
            to_left(d).wait_send()

        @pl.when((d <= s) & (s < n_seq - 1))
        def _():
            to_right(d).wait_send()

        to_twin(d).wait_send()
        from_twin(d).wait_recv()
    for copy in swaps:
        copy.wait_send()
    spread.finish()


def gather_first(n_seq, hidden, blocks):
    n_plane = 2 * KV_HEADS
    n_chip = KV_HEADS
    return pl.pallas_call(
        partial(gather_kernel, n_seq, n_plane),
        out_shape=[
            jax.ShapeDtypeStruct((n_plane,) + hidden.shape[1:], hidden.dtype),
            jax.ShapeDtypeStruct((n_seq, 2) + blocks.shape, blocks.dtype),
        ],
        in_specs=[ANY, ANY],
        out_specs=[ANY, ANY],
        scratch_shapes=[
            DMA((SPREAD_SLOTS,)),
            DMA((SPREAD_SLOTS,)),
            DMA((1,)),
            DMA((n_chip,)),
            DMA((n_chip,)),
            DMA((1,)),
            DMA((n_seq,)),
            DMA((n_seq,)),
            DMA((n_seq,)),
            DMA((n_seq,)),
            DMA((n_seq,)),
        ],
        compiler_params=pltpu.CompilerParams(collective_id=1, has_side_effects=True),
    )(hidden, blocks)


def last_kernel(
    n_seq,
    n_plane,
    parts,
    blocks,
    parts_all,
    sums,
    held,
    twin,
    line,
    part_added,
    part_own,
    part_send,
    part_recv,
    part_load,
    part_local,
    held_sem,
    twin_send,
    twin_recv,
    line_send,
    line_recv,
    chip_send,
    chip_recv,
    chip_local,
):
    n_chip = n_plane // 2
    s = lax.axis_index("seq")
    q = lax.axis_index("chip")
    k = lax.axis_index("core")
    before, after = line_neighbours(s, n_seq)
    greet(n_plane, n_seq)

    def load(d):
        return pltpu.make_async_copy(blocks.at[d, k], held.at[d], held_sem.at[d])

    def to_twin(d):
        return remote(
            blocks.at[d, 1 - k], twin.at[d], twin_send.at[d], twin_recv.at[d], {"core": 1 - k}
        )

    def to_left(d):
        return remote(held.at[d], line.at[d], line_send.at[d], line_recv.at[d], before)

    def to_right(d):
        return remote(
            held.at[d], line.at[d + 1], line_send.at[d], line_recv.at[d + 1], after
        )

    def gather_terms(d, with_left, with_right):
        load(d).wait()
        to_twin(d).wait_recv()

        @pl.when(with_right)
        def _():
            to_left(d).wait_recv()

        @pl.when(with_left)
        def _():
            to_right(d).wait_recv()

        def body(i, carry):
            held[d, i] = (held[d, i].astype(jnp.float32) + twin[d, i].astype(jnp.float32)).astype(
                held.dtype
            )
            return carry

        def body_right(i, carry):
            total = held[d, i].astype(jnp.float32) + twin[d, i].astype(jnp.float32)
            held[d, i] = (total + line[d, i].astype(jnp.float32)).astype(held.dtype)
            return carry

        def body_left(i, carry):
            total = held[d, i].astype(jnp.float32) + twin[d, i].astype(jnp.float32)
            held[d, i] = (total + line[d + 1, i].astype(jnp.float32)).astype(held.dtype)
            return carry

        def body_both(i, carry):
            total = held[d, i].astype(jnp.float32) + twin[d, i].astype(jnp.float32)
            total = total + line[d, i].astype(jnp.float32)
            held[d, i] = (total + line[d + 1, i].astype(jnp.float32)).astype(held.dtype)
            return carry

        @pl.when(jnp.logical_not(with_left) & jnp.logical_not(with_right))
        def _():
            lax.fori_loop(0, n_chip, body, 0)

        @pl.when(jnp.logical_not(with_left) & with_right)
        def _():
            lax.fori_loop(0, n_chip, body_right, 0)

        @pl.when(with_left & jnp.logical_not(with_right))
        def _():
            lax.fori_loop(0, n_chip, body_left, 0)

        @pl.when(with_left & with_right)
        def _():
            lax.fori_loop(0, n_chip, body_both, 0)

    for d in range(n_seq):
        to_twin(d).start()
        load(d).start()
    part_sems = (part_send, part_recv, part_load, part_local)
    merge = Merge(parts, parts_all, part_added, part_own, part_sems)
    merge.start()
    never = s < 0
    for hop in range(1, n_seq):
        if hop == 2:
            merge.pass_on()
        left = hop - n_seq + s
        right = n_seq - hop + s

        @pl.when(left >= 0)
        def _():
            gather_terms(left, never, s < n_seq - 1)
            to_left(left).start()

        @pl.when(right <= n_seq - 1)
        def _():
            gather_terms(right, s > 0, never)
            to_right(right).start()

    gather_terms(s, s > 0, s < n_seq - 1)
    swaps = []
    for step in range(1, n_chip):
        to = lax.rem(q + step, n_chip)
        copy = remote(
            held.at[s, to], sums.at[q], chip_send.at[step], chip_recv.at[step], {"chip": to}
        )
        copy.start()
        swaps.append(copy)
    own = pltpu.make_async_copy(held.at[s, q], sums.at[q], chip_local.at[0])
    own.start()
    for d in range(n_seq):
        to_twin(d).wait_send()

        @pl.when(d < s)
        def _():
            to_left(d).wait_send()

        @pl.when(d > s)
        def _():
            to_right(d).wait_send()

    merge.finish()
    for copy in swaps:
        copy.wait()
    own.wait()


def sum_last(n_seq, parts, blocks):
    n_plane = 2 * KV_HEADS
    n_chip = KV_HEADS
    block = blocks.shape[2:]
    return pl.pallas_call(
        partial(last_kernel, n_seq, n_plane),
        out_shape=[
            merged_shape(parts),
            jax.ShapeDtypeStruct(block, blocks.dtype),
        ],
        in_specs=[ANY, ANY],
        out_specs=[ANY, ANY],
        scratch_shapes=[
            pltpu.VMEM((n_seq,) + block, blocks.dtype),
            pltpu.VMEM((n_seq,) + block, blocks.dtype),
            pltpu.VMEM((n_seq + 1,) + block, blocks.dtype),
            *merge_scratch(parts),
            DMA((n_seq,)),
            DMA((n_seq,)),
            DMA((n_seq,)),
            DMA((n_seq,)),
            DMA((n_seq + 1,)),
            DMA((n_chip,)),
            DMA((n_chip,)),
            DMA((1,)),
        ],
        compiler_params=pltpu.CompilerParams(
            collective_id=4, has_side_effects=True, vmem_limit_bytes=32 * 1024 * 1024
        ),
    )(parts, blocks)


QUERY_BLOCK = 256


def block_probs(query, keys, segment_col, segment_row, first):
    rows, width = query.shape[0], keys.shape[0]
    scaled = times_rows(query, keys) * (1.0 / math.sqrt(HEAD_DIM))
    bent = jnp.tanh(scaled / SOFT_CAP)
    row = first + lax.broadcasted_iota(jnp.int32, (rows, width), 0)
    col = lax.broadcasted_iota(jnp.int32, (rows, width), 1)
    allowed = ((segment_col == segment_row) & (col <= row)) | (col == row)
    capped = jnp.where(allowed, SOFT_CAP * bent, MASKED)
    raised = jnp.exp(capped - jnp.max(capped, axis=-1, keepdims=True))
    return raised / jnp.sum(raised, axis=-1, keepdims=True), bent


def attend_kernel(group_size, queries, keys, values, segment_col, segment_row, out):
    seq_len = keys.shape[0]
    for first in range(0, seq_len, QUERY_BLOCK):
        rows = slice(first, first + QUERY_BLOCK)
        width = first + QUERY_BLOCK
        for head in range(group_size):
            cols = slice(head * HEAD_DIM, (head + 1) * HEAD_DIM)
            probs, unused = block_probs(
                queries[rows, cols],
                keys[:width],
                segment_col[rows, :],
                segment_row[:, :width],
                first,
            )
            out[rows, cols] = add_slice(probs.astype(jnp.bfloat16), values[:width]).astype(
                out.dtype
            )


def attend(queries, keys, values, segment_col, segment_row):
    return pl.pallas_call(
        partial(attend_kernel, queries.shape[1] // HEAD_DIM),
        out_shape=jax.ShapeDtypeStruct(queries.shape, jnp.bfloat16),
        compiler_params=pltpu.CompilerParams(vmem_limit_bytes=40 * 1024 * 1024),
    )(queries, keys, values, segment_col, segment_row)


def turn_back(grads, cosine, sine_part):
    half = grads.shape[1] // 2
    first, second = grads[:, :half], grads[:, half:]
    return jnp.concatenate(
        [first * cosine + second * sine_part, second * cosine - first * sine_part], axis=1
    )


def attend_back_kernel(
    group_size,
    queries,
    keys,
    values,
    segment_col,
    segment_row,
    grads,
    cosine,
    sine_part,
    out,
    grad_keys,
    grad_values,
):
    seq_len = keys.shape[0]
    inverse_root = 1.0 / math.sqrt(HEAD_DIM)
    key_cols = slice(group_size * HEAD_DIM, (group_size + 1) * HEAD_DIM)
    value_cols = slice((group_size + 1) * HEAD_DIM, (group_size + 2) * HEAD_DIM)
    grad_keys[...] = jnp.zeros_like(grad_keys)
    grad_values[...] = jnp.zeros_like(grad_values)
    for first in range(0, seq_len, QUERY_BLOCK):
        rows = slice(first, first + QUERY_BLOCK)
        width = first + QUERY_BLOCK
        for head in range(group_size):
            cols = slice(head * HEAD_DIM, (head + 1) * HEAD_DIM)
            query = queries[rows, cols]
            probs, bent = block_probs(
                query, keys[:width], segment_col[rows, :], segment_row[:, :width], first
            )
            grad = grads[rows, cols]
            grad_probs = times_rows(grad, values[:width])
            mean = jnp.sum(probs * grad_probs, axis=-1, keepdims=True)
            grad_scaled = (probs * (grad_probs - mean) * (1.0 - bent * bent)).astype(jnp.bfloat16)
            grad_query = add_slice(grad_scaled, keys[:width]) * inverse_root
            out[rows, cols] = turn_back(grad_query, cosine[rows, :], sine_part[rows, :]).astype(
                out.dtype
            )
            grad_keys[:width, :] += outer_rows(grad_scaled, query) * inverse_root
            grad_values[:width, :] += outer_rows(probs.astype(jnp.bfloat16), grad)
    for first in range(0, seq_len, QUERY_BLOCK):
        rows = slice(first, first + QUERY_BLOCK)
        out[rows, key_cols] = turn_back(
            grad_keys[rows, :], cosine[rows, :], sine_part[rows, :]
        ).astype(out.dtype)
        out[rows, value_cols] = grad_values[rows, :].astype(out.dtype)


def attend_back(queries, keys, values, segment_col, segment_row, grads, cosine, sine_part):
    seq_len, own_width = queries.shape
    return pl.pallas_call(
        partial(attend_back_kernel, own_width // HEAD_DIM),
        out_shape=jax.ShapeDtypeStruct((seq_len, own_width + 2 * HEAD_DIM), jnp.bfloat16),
        scratch_shapes=[
            pltpu.VMEM((seq_len, HEAD_DIM), jnp.float32),
            pltpu.VMEM((seq_len, HEAD_DIM), jnp.float32),
        ],
        compiler_params=pltpu.CompilerParams(vmem_limit_bytes=40 * 1024 * 1024),
    )(queries, keys, values, segment_col, segment_row, grads, cosine, sine_part)


def weight_blocks_kernel(weight_rows, inputs, grads, grad_outs, outs, gains, blocks):
    n_first, n_core, n_chip, block_rows = blocks.shape[:4]
    columns = outs.shape[1]
    for c in range(blocks.shape[4] // columns):
        cols = slice(c * columns, (c + 1) * columns)
        if c * columns < grads.shape[1]:
            total = outer_rows(inputs[...], grads[:, cols])
        else:
            total = outer_rows(grad_outs[...], outs[...])
        for d in range(n_first):
            for q in range(n_chip):
                for core in range(n_core):
                    b = (d * n_chip + q) * n_core + core
                    part = total[b * weight_rows : (b + 1) * weight_rows]
                    part = jnp.concatenate([part, gains[b, :, cols]], axis=0)
                    blocks[d, core, q, :, cols] = part.astype(blocks.dtype)


def weight_blocks(n_seq, inputs, grads, grad_outs, outs, gains):
    seq_len, model_width = inputs.shape
    n_blocks, extra_rows, block_width = gains.shape
    weight_rows = model_width // n_blocks
    steps = 2
    part = model_width // steps
    block = (n_seq // steps, 2, KV_HEADS, weight_rows + extra_rows, block_width)
    whole = lambda i: (0, 0)
    return pl.pallas_call(
        partial(weight_blocks_kernel, weight_rows),
        grid=(steps,),
        out_shape=jax.ShapeDtypeStruct((n_seq,) + block[1:], jnp.bfloat16),
        in_specs=[
            pl.BlockSpec((seq_len, part), lambda i: (0, i)),
            pl.BlockSpec(grads.shape, whole),
            pl.BlockSpec((seq_len, part), lambda i: (0, i)),
            pl.BlockSpec(outs.shape, whole),
            pl.BlockSpec((n_blocks // steps, extra_rows, block_width), lambda i: (i, 0, 0)),
        ],
        out_specs=pl.BlockSpec(block, lambda i: (i, 0, 0, 0, 0)),
        compiler_params=pltpu.CompilerParams(vmem_limit_bytes=56 * 1024 * 1024),
    )(inputs, grads, grad_outs, outs, gains)


def chip_beside(c, flip):
    return c ^ flip


LATE = 3
PAIRS = 2
LATE_COLUMNS = 1


def chip_places(rows, late_rows):
    q = lax.axis_index("chip")
    x, y = lax.rem(q, 2), lax.div(q, 2)
    across = (2 * (1 - y) + 1 - x) * rows
    half = (rows - late_rows) // 2
    return (q * rows, (2 * y + 1 - x) * rows, (2 * (1 - y) + x) * rows, across, across + half)


def send_beside(part, flip):
    return lax.ppermute(part, "chip", [(c, chip_beside(c, flip)) for c in range(KV_HEADS)])


def unit_orders(n):
    units, sums = [], []
    for s in range(n):
        keyed = []
        for d in range(n):
            if d != s:
                near = abs(s - d)
                behind, past = (s, d) if d < s else (n - 1 - s, n - 1 - d)
                keyed += [(near, d, 0), (behind + past + 1, d, 1)]
        order = [(s, 0), (s, 1)] + [(d, h) for unused, d, h in sorted(keyed)]
        units.append([2 * d + h for d, h in order])
        if s in (0, n - 1):
            sums.append(units[-1][2:])
            continue
        keyed = []
        for d in range(n):
            if d != s:
                hops, place = (n - 2 - s, d) if d < s else (s - 1, n - 1 - d)
                keyed += [(n - 2 - place + hops, d, 0), (n - 1 + place + hops, d, 1)]
        sums.append([2 * d + h for unused, d, h in sorted(keyed)])
    return units, sums


def pick(table, s, i):
    width = len(table[0])
    place = s * width + i
    value = 0
    for k, entry in enumerate(entry for row in table for entry in row):
        value = jnp.where(place == k, entry, value)
    return value


SUBS = 1
SUM_TURNS = (0, 1, 4, 5, 8, 8)
GELU_SCALE = math.sqrt(2.0 / math.pi)


def gelu_pieces(gate):
    bend = jnp.tanh(GELU_SCALE * (gate + 0.044715 * gate * gate * gate))
    value = 0.5 * gate * (1.0 + bend)
    slope = 0.5 * (1.0 + bend) + 0.5 * gate * (1.0 - bend * bend) * GELU_SCALE * (
        1.0 + 3.0 * 0.044715 * gate * gate
    )
    return value, slope


def units_kernel(n_seq, backward, *refs):
    if backward:
        tokens, units = refs[:2]
        downs, late = refs[2:7], refs[7]
        kept_gate, kept_up, kept_hidden = refs[8:11]
        out, first_out, second_out, early_grads = refs[11:15]
        late_grads = refs[15 : 15 + LATE_COLUMNS]
        late_parts = refs[15 + LATE_COLUMNS : 15 + 2 * LATE_COLUMNS]
        stage_outs = (first_out, second_out)
        scratch = refs[15 + 2 * LATE_COLUMNS :]
    else:
        tokens, units = refs[:2]
        downs = refs[2:7]
        out, tokens_all, late, first_out, second_out, third_out = refs[7:13]
        stage_outs = (first_out, second_out, third_out)
        scratch = refs[13:]
    units_v, downs_v, held, own_sum, twin_sum, twin_out, line, stage = scratch[:8]
    scratch = scratch[8:]
    if backward:
        kept, kept_sem, tile, tile_sem, load_sem = scratch[:5]
        scratch = scratch[5:]
    else:
        own_hidden = scratch[0]
        scratch = scratch[1:]
    late_send, late_recv = scratch[:2]
    scratch = scratch[2:]
    (
        weight_sem,
        late_sem,
        own_sem,
        left_send,
        right_send,
        token_recv,
        twin_send,
        twin_recv,
        part_send,
        part_recv,
        line_send,
        line_recv,
        stage_sem,
        all_sem,
        out_sem,
    ) = scratch
    n = n_seq
    s = lax.axis_index("seq")
    k = lax.axis_index("core")
    before, after = line_neighbours(s, n)
    twin = {"core": 1 - k}
    n_units, width = downs_v.shape
    piece_len = tokens.shape[1]
    at_end = (s == 0) | (s == n - 1)

    def token_left(d, h, source):
        return remote(
            source, held.at[d, h, 0], left_send.at[d, h], token_recv.at[d, h], before
        )

    def token_right(d, h, source):
        return remote(
            source, held.at[d, h, 0], right_send.at[d, h], token_recv.at[d, h], after
        )

    def token_twin(d, h, source):
        return remote(source, held.at[d, h, 1], twin_send.at[d, h], twin_recv.at[d, h], twin)

    def part_twin(d, h):
        return remote(
            twin_out.at[d, h], twin_sum.at[d, h], part_send.at[d, h], part_recv.at[d, h], twin
        )

    sub_len = piece_len // SUBS

    def part_line(d, h, sub):
        to_left = d < s
        slot = jnp.where(to_left, d, d + 1)
        rows = pl.ds(sub * sub_len, sub_len)
        return remote(
            twin_sum.at[d, h, rows],
            line.at[slot, h, rows],
            line_send.at[d, h, sub],
            line_recv.at[slot, h, sub],
            {"seq": jnp.where(to_left, s - 1, s + 1)},
        )

    def line_arrival(slot, h, sub):
        rows = pl.ds(sub * sub_len, sub_len)
        return remote(
            twin_sum.at[0, h, rows],
            line.at[slot, h, rows],
            line_send.at[0, h, sub],
            line_recv.at[slot, h, sub],
            {"seq": s},
        )

    def own_load(h):
        return pltpu.make_async_copy(tokens.at[h], held.at[s, h, 0], own_sem.at[h])

    def all_store(d, h):
        return pltpu.make_async_copy(held.at[d, h], tokens_all.at[d, h], all_sem.at[d, h])

    def stage_store(i, d, h, slot):
        return pltpu.make_async_copy(
            stage.at[i, slot], stage_outs[i].at[2 * d + h], stage_sem.at[i, slot]
        )

    def kept_load(i, d, h, slot):
        source = (kept_gate, kept_up)[i]
        return pltpu.make_async_copy(source.at[2 * d + h], kept.at[i, slot], kept_sem.at[i, slot])

    unit_table, sum_table = unit_orders(n)
    right_table = [
        [2 if d == 0 else unit_table[d].index(2 * (d - 1) + 1) + 1 for d in range(n)]
    ]
    left_table = [
        [2 if d == n - 1 else unit_table[d].index(2 * (d + 1) + 1) + 1 for d in range(n)]
    ]

    def source(t):
        unit = pick(unit_table, s, t)
        return lax.div(unit, 2), lax.rem(unit, 2)

    barrier = pltpu.get_barrier_semaphore()
    pl.semaphore_signal(barrier, inc=1, device_id=twin, device_id_type=MESH)

    @pl.when(s > 0)
    def _():
        pl.semaphore_signal(barrier, inc=1, device_id={"seq": s - 1}, device_id_type=MESH)

    @pl.when(s < n - 1)
    def _():
        pl.semaphore_signal(barrier, inc=1, device_id={"seq": s + 1}, device_id_type=MESH)

    greeted = 1 + jnp.where(s > 0, 1, 0) + jnp.where(s < n - 1, 1, 0)
    n_chip, late_rows = late.shape[:2]
    chip_rows = n_units // n_chip
    q = lax.axis_index("chip")
    for step in range(1, n_chip):
        pl.semaphore_signal(
            barrier,
            inc=1,
            device_id={"chip": lax.rem(q + step, n_chip)},
            device_id_type=MESH,
        )
    pl.semaphore_wait(barrier, greeted + n_chip - 1)

    def late_place(chip):
        first = chip * chip_rows + chip_rows - late_rows
        return downs_v.at[pl.ds(pl.multiple_of(first, 16), late_rows)]

    def late_copy(step):
        return remote(
            downs[0].at[pl.ds(chip_rows - late_rows, late_rows)],
            late_place(q),
            late_send.at[step],
            late_recv.at[step],
            {"chip": lax.rem(q + step, n_chip)},
        )

    def late_grad(i, step):
        chip = lax.rem(q + step, n_chip)
        return remote(
            late_grads[i].at[pl.ds(pl.multiple_of(chip * chip_rows, 16), chip_rows)],
            late_parts[i].at[q],
            late_send.at[n_chip * i + step],
            late_recv.at[n_chip * i + step],
            {"chip": chip},
        )

    def late_store(chip):
        return pltpu.make_async_copy(late_place(chip), late.at[chip], late_sem.at[chip])

    def late_load(chip):
        return pltpu.make_async_copy(late.at[chip], late_place(chip), late_sem.at[chip])

    def second_half(t):
        @pl.when((s < n - 1) & (t == pick(right_table, 0, s)))
        def _():
            d, h = jnp.maximum(s - 1, 0), jnp.where(s > 0, 1, 0)
            token_right(d, h, held.at[d, h, 0]).wait_send()
            token_right(s, 1, tokens.at[1]).start()

        @pl.when((s > 0) & (t == pick(left_table, 0, s)))
        def _():
            d, h = jnp.minimum(s + 1, n - 1), jnp.where(s < n - 1, 1, 0)
            token_left(d, h, held.at[d, h, 0]).wait_send()
            token_left(s, 1, tokens.at[1]).start()

    @pl.when(s < n - 1)
    def _():
        token_right(s, 0, tokens.at[0]).start()

    @pl.when(s > 0)
    def _():
        token_left(s, 0, tokens.at[0]).start()

    for h in range(2):
        token_twin(s, h, tokens.at[h]).start()
        own_load(h).start()
    load_units = pltpu.make_async_copy(units, units_v, weight_sem.at[0])
    load_downs = []
    for i, (first, part) in enumerate(zip(chip_places(chip_rows, late_rows), downs)):
        count = chip_rows - late_rows if i == 0 and backward else part.shape[0]
        load_downs.append(
            pltpu.make_async_copy(
                part.at[pl.ds(0, count)],
                downs_v.at[pl.ds(pl.multiple_of(first, 16), count)],
                weight_sem.at[1 + i],
            )
        )
    if backward:
        load_downs += [late_load(chip) for chip in range(n_chip)]
    else:
        for step in (2, 1, 3):
            late_copy(step).start()
    load_units.start()
    for load in load_downs:
        load.start()
    if backward:
        for i in range(2):
            kept_load(i, s, 0, 0).start()
    load_units.wait()
    for load in load_downs:
        load.wait()

    def add_rows(d, h, sub, into_own, use_line):
        step = 16

        def body(i, carry):
            rows = pl.ds(pl.multiple_of(sub * sub_len + i * step, step), step)
            total = own_sum[d, h, rows, :] + twin_sum[d, h, rows, :].astype(jnp.float32)
            for slot in use_line:
                total = total + line[slot, h, rows, :].astype(jnp.float32)
            if into_own:
                own_sum[d, h, rows, :] = total
            else:
                twin_sum[d, h, rows, :] = total.astype(twin_sum.dtype)
            return carry

        lax.fori_loop(0, sub_len // step, body, 0)

    def combine(d, h):
        to_left = d < s
        slot = jnp.where(to_left, d, d + 1)
        more = jnp.where(to_left, s < n - 1, s > 0)
        part_twin(d, h).wait_recv()

        @pl.when(more)
        def _():
            for sub in range(SUBS):
                line_arrival(slot, h, sub).wait_recv()
                add_rows(d, h, sub, False, (slot,))
                part_line(d, h, sub).start()

        @pl.when(jnp.logical_not(more))
        def _():
            for sub in range(SUBS):
                add_rows(d, h, sub, False, ())
                part_line(d, h, sub).start()

    columns = width // 3
    chunk = n_units // 3

    def hidden_forward(d, h, slot):
        rows = held[d, h].reshape(2 * piece_len, width)
        for c in range(3):
            cols = slice(c * chunk, (c + 1) * chunk)
            gate = times_rows(rows, units_v[cols, :width])
            up = times_rows(rows, units_v[cols, width:])
            value, unused = gelu_pieces(gate)
            stage[0, slot, :, cols] = gate.astype(stage.dtype)
            stage[1, slot, :, cols] = up.astype(stage.dtype)
            stage[2, slot, :, cols] = (value * up).astype(stage.dtype)

    def down_forward(d, h, hidden):
        for c in range(3):
            cols = slice(c * columns, (c + 1) * columns)
            part = add_slice(hidden[...], downs_v[:, cols])
            own_sum[d, h, :, cols] = part[:piece_len]
            twin_out[d, h, :, cols] = part[piece_len:].astype(twin_out.dtype)
        part_twin(d, h).start()

    def own_forward(h):
        down_forward(s, h, own_hidden.at[h])

    def compute_backward(d, h, slot):
        rows = held[d, h].reshape(2 * piece_len, width)
        for c in range(3):
            cols = slice(c * chunk, (c + 1) * chunk)
            grad = times_rows(rows, downs_v[cols, :])
            value, slope = gelu_pieces(kept[0, slot, :, cols].astype(jnp.float32))
            up = kept[1, slot, :, cols].astype(jnp.float32)
            stage[0, slot, :, cols] = (grad * up * slope).astype(stage.dtype)
            stage[1, slot, :, cols] = (grad * value).astype(stage.dtype)
        for c in range(3):
            cols = slice(c * columns, (c + 1) * columns)
            later = slice(width + c * columns, width + (c + 1) * columns)
            part = add_slice(stage[0, slot], units_v[:, cols])
            part = part + add_slice(stage[1, slot], units_v[:, later])
            own_sum[d, h, :, cols] = part[:piece_len]
            twin_out[d, h, :, cols] = part[piece_len:].astype(twin_out.dtype)

    row_tile, col_tile = n_units // 3, width // 3

    def down_gradient(between):
        unit_rows = 2 * piece_len
        group_rows = n * unit_rows

        def left_load(u):
            place = downs_v.at[
                pl.ds((u % n) * unit_rows, unit_rows), pl.ds((u // n) * n_units, n_units)
            ]
            return pltpu.make_async_copy(kept_hidden.at[u], place, load_sem.at[u])

        def left_rows(g, first):
            return downs_v[
                :group_rows, pl.ds(pl.multiple_of(g * n_units + first, 128), row_tile)
            ]

        def right_rows(g, first):
            cols = pl.ds(pl.multiple_of(first, 128), col_tile)
            part = held[g * n // 2 : (g + 1) * n // 2, :, :, :, cols]
            return part.reshape(group_rows, col_tile)

        def tile_store(r, c, slot):
            rows = pl.ds(pl.multiple_of(r * row_tile, 16), row_tile)
            if c < LATE_COLUMNS:
                place = late_grads[c].at[rows]
            else:
                place = early_grads.at[rows, pl.ds((c - LATE_COLUMNS) * col_tile, col_tile)]
            return pltpu.make_async_copy(tile.at[slot], place, tile_sem.at[slot])

        for u in range(2 * n):
            left_load(u).start()
        for u in range(2 * n):
            left_load(u).wait()

        def one_tile(c, r, carry):
            slot = lax.rem(r, 2)
            total = sum(
                outer_rows(left_rows(g, r * row_tile), right_rows(g, c * col_tile))
                for g in range(2)
            )

            @pl.when(r >= 2)
            def _():
                tile_store(r, c, slot).wait()

            tile[slot] = total.astype(tile.dtype)
            tile_store(r, c, slot).start()
            for step, turn in enumerate(SUM_TURNS):

                @pl.when(3 * c + r == turn)
                def _():
                    between(step)

            return carry

        for c in range(3):
            lax.fori_loop(0, 3, partial(one_tile, c), 0)
            for slot in range(2):
                tile_store(0, c, slot).wait()
            if c < LATE_COLUMNS:
                for step in (2, 1, 3):
                    late_grad(c, step).start()

    def arrive(t):
        d, h = source(t)
        piece = held.at[d, h, 0]
        token_left(d, h, piece).wait_recv()

        @pl.when((d < s) & (s < n - 1))
        def _():
            token_right(d, h, piece).start()

        @pl.when((d > s) & (s > 0))
        def _():
            token_left(d, h, piece).start()

        token_twin(d, h, piece).start()

    def unit(t, carry):
        d, h = source(t)
        slot = lax.rem(t, 2)

        @pl.when(at_end & (t >= 3))
        def _():
            combine(*source(t - 1))

        @pl.when(t < 2)
        def _():
            own_load(h).wait()

        inner = jnp.logical_not(at_end)
        pair = inner & (t >= 2) & (t < 2 + 2 * PAIRS)

        @pl.when((t >= 2) & (jnp.logical_not(pair) | (lax.rem(t, 2) == 0)))
        def _():
            arrive(t)

        @pl.when(pair & (lax.rem(t, 2) == 0))
        def _():
            arrive(t + 1)

        @pl.when(t >= 2)
        def _():
            for i in range(len(stage_outs)):
                stage_store(i, d, h, slot).wait()

        second_half(t)
        if backward:

            @pl.when(t < 2 * n - 1)
            def _():
                for i in range(2):
                    kept_load(i, *source(t + 1), 1 - slot).start()

            for i in range(2):
                kept_load(i, d, h, slot).wait()
        token_twin(d, h, held.at[d, h, 0]).wait_recv()
        if backward:
            compute_backward(d, h, slot)
            part_twin(d, h).start()
        else:
            hidden_forward(d, h, slot)

            @pl.when(t < 2)
            def _():
                own_hidden[slot] = stage[2, slot]

            @pl.when(t == 2)
            def _():
                for step in range(1, n_chip):
                    late_copy(step).wait_recv()

            @pl.when(t >= 2)
            def _():
                down_forward(d, h, stage.at[2, slot])

        if not backward:
            all_store(d, h).start()
        for i in range(len(stage_outs)):
            stage_store(i, d, h, slot).start()

        return carry

    lax.fori_loop(0, 2 * n, unit, 0)

    second_half(2 * n)

    @pl.when(at_end)
    def _():
        combine(*source(2 * n - 1))

    n_sums = 2 * (n - 1)

    def middle(i):
        @pl.when(jnp.logical_not(at_end) & (i < n_sums))
        def _():
            unit = pick(sum_table, s, i)
            combine(lax.div(unit, 2), lax.rem(unit, 2))

    if backward:
        down_gradient(middle)
    else:

        for chip in range(n_chip):
            late_store(chip).start()

        def one(i, carry):
            middle(i)

            @pl.when((i == 1) | (i == 2))
            def _():
                own_forward(i - 1)

            return carry

        lax.fori_loop(0, n_sums, one, 0)

    def finish(h, carry):
        part_twin(s, h).wait_recv()
        for sub in range(SUBS):

            @pl.when(s < n - 1)
            def _():
                line_arrival(s, h, sub).wait_recv()

            @pl.when(s > 0)
            def _():
                line_arrival(s + 1, h, sub).wait_recv()

            @pl.when(s == 0)
            def _():
                add_rows(s, h, sub, True, (s,))

            @pl.when(s == n - 1)
            def _():
                add_rows(s, h, sub, True, (s + 1,))

            @pl.when(jnp.logical_not(at_end))
            def _():
                add_rows(s, h, sub, True, (s, s + 1))

        pltpu.make_async_copy(own_sum.at[s, h], out.at[h], out_sem.at[h]).start()
        return carry

    lax.fori_loop(0, 2, finish, 0)

    def drain(t, carry):
        d = lax.div(t, 2)
        h = lax.rem(t, 2)
        piece = held.at[d, h, 0]

        right_seen = (d == jnp.maximum(s - 1, 0)) & (h == jnp.where(s > 0, 1, 0))
        left_seen = (d == jnp.minimum(s + 1, n - 1)) & (h == jnp.where(s < n - 1, 1, 0))

        @pl.when((d <= s) & (s < n - 1) & jnp.logical_not(right_seen))
        def _():
            token_right(d, h, piece).wait_send()

        @pl.when((d >= s) & (s > 0) & jnp.logical_not(left_seen))
        def _():
            token_left(d, h, piece).wait_send()

        token_twin(d, h, piece).wait_send()
        part_twin(d, h).wait_send()

        @pl.when(d != s)
        def _():
            for sub in range(SUBS):
                part_line(d, h, sub).wait_send()

        if not backward:
            all_store(d, h).wait()
        return carry

    lax.fori_loop(0, 2 * n, drain, 0)
    if backward:
        for i in range(LATE_COLUMNS):
            for step in range(1, n_chip):
                late_grad(i, step).wait()
    else:
        for step in range(1, n_chip):
            late_copy(step).wait_send()
        for chip in range(n_chip):
            late_store(chip).wait()
    for h in range(2):
        for i in range(len(stage_outs)):
            stage_store(i, 0, h, h).wait()
        pltpu.make_async_copy(own_sum.at[s, h], out.at[h], out_sem.at[h]).wait()


def run_units(n_seq, tokens, units, downs, kept=None):
    backward = kept is not None
    low = tokens.dtype
    n_units = units.shape[0]
    halves, piece_len, width = tokens.shape
    n_stage = 2 if backward else 3
    held = (n_seq, halves, 2, piece_len, width)
    unit_rows = (2 * n_seq, 2 * piece_len, n_units)
    sums = (n_seq, halves, piece_len, width)
    scratch = [
        pltpu.VMEM(units.shape, low),
        pltpu.VMEM((n_units, width), low),
        pltpu.VMEM(held, low),
        pltpu.VMEM(sums, jnp.float32),
        pltpu.VMEM(sums, low),
        pltpu.VMEM(sums, low),
        pltpu.VMEM((n_seq + 1,) + sums[1:], low),
        pltpu.VMEM((n_stage, 2) + unit_rows[1:], low),
    ]
    outs = [jax.ShapeDtypeStruct(tokens.shape, jnp.float32)]
    late_shape = (KV_HEADS, downs[0].shape[0] // LATE, width)
    if backward:
        scratch += [
            pltpu.VMEM((2, 2) + unit_rows[1:], low),
            DMA((2, 2)),
            pltpu.VMEM((2, n_units // 3, width // 3), low),
            DMA((2,)),
            DMA((2 * n_seq,)),
        ]
    else:
        scratch += [pltpu.VMEM((2,) + unit_rows[1:], low)]
        outs += [jax.ShapeDtypeStruct(held, low), jax.ShapeDtypeStruct(late_shape, low)]
    outs += [jax.ShapeDtypeStruct(unit_rows, low)] * n_stage
    if backward:
        column = width // 3
        outs += [jax.ShapeDtypeStruct((n_units, (3 - LATE_COLUMNS) * column), low)]
        outs += [jax.ShapeDtypeStruct((n_units, column), low)] * LATE_COLUMNS
        parts = (KV_HEADS, n_units // KV_HEADS, column)
        outs += [jax.ShapeDtypeStruct(parts, low)] * LATE_COLUMNS
    scratch += [DMA((KV_HEADS * LATE_COLUMNS,)), DMA((KV_HEADS * LATE_COLUMNS,))]
    pairs = DMA((n_seq, halves))
    scratch += [DMA((6,)), DMA((KV_HEADS,)), DMA((halves,))] + [pairs] * 7
    scratch += [DMA((n_seq, halves, SUBS)), DMA((n_seq + 1, halves, SUBS))]
    scratch += [DMA((n_stage, 2)), pairs, DMA((halves,))]
    operands = (tokens, units) + tuple(downs) + (tuple(kept) if backward else ())
    return pl.pallas_call(
        partial(units_kernel, n_seq, backward),
        out_shape=outs,
        in_specs=[ANY] * len(operands),
        out_specs=[ANY] * len(outs),
        scratch_shapes=scratch,
        compiler_params=pltpu.CompilerParams(
            collective_id=6 if backward else 5,
            has_side_effects=True,
            vmem_limit_bytes=63 * 1024 * 1024,
        ),
    )(*operands)


def per_device_general(
    hidden_in,
    norm_gains,
    qkv_weight,
    out_weight,
    gate_up_weight,
    down_weight,
    output_cotangent,
    segment_ids,
    padding,
    positions,
):
    everyone = ("seq", "chip", "core")
    plane = ("chip", "core")
    column = ("seq", "core")
    groups = hidden_in.shape[0]
    piece_len = hidden_in.shape[1]
    model_width = hidden_in.shape[2]
    row_count = groups * piece_len
    seq_len = segment_ids.shape[1]
    group_size = HEADS // KV_HEADS
    query_width = HEADS * HEAD_DIM
    key_width = KV_HEADS * HEAD_DIM
    proj_width = qkv_weight.shape[1]

    residual = hidden_in.reshape(row_count, model_width).astype(jnp.float32)
    factor = lax.rsqrt(jnp.mean(residual * residual, axis=-1, keepdims=True) + EPSILON)
    gain_cols = lax.all_gather(norm_gains, everyone, axis=0, tiled=True).astype(jnp.float32)
    qkv_full = lax.all_gather(qkv_weight, everyone, axis=0, tiled=True)
    attn_input = (residual * factor * gain_cols[:, 0]).astype(jnp.bfloat16)
    projected = add_slice(attn_input, qkv_full)
    cosine, sine_part = rotary_tables(positions.reshape(row_count), HEAD_DIM)
    queries = (
        rotate(projected[:, :query_width].reshape(row_count, HEADS, HEAD_DIM), cosine, sine_part)
        .astype(jnp.bfloat16)
        .reshape(row_count, query_width)
    )
    keys_here = (
        rotate(
            projected[:, query_width : query_width + key_width].reshape(
                row_count, KV_HEADS, HEAD_DIM
            ),
            cosine,
            sine_part,
        )
        .astype(jnp.bfloat16)
        .reshape(groups, piece_len, key_width)
    )
    values_here = (
        projected[:, query_width + key_width :]
        .astype(jnp.bfloat16)
        .reshape(groups, piece_len, key_width)
    )
    both_all = lax.all_gather(
        jnp.concatenate([keys_here, values_here], axis=2), plane, axis=1, tiled=True
    )
    keys_all = both_all[:, :, :key_width]
    values_all = both_all[:, :, key_width:]
    first_query = (lax.axis_index("chip") * 2 + lax.axis_index("core")) * piece_len
    query_rows = first_query + jnp.arange(piece_len, dtype=jnp.int32)
    key_rows = jnp.arange(seq_len, dtype=jnp.int32)
    segment_query = lax.dynamic_slice_in_dim(segment_ids, first_query, piece_len, 1)
    allowed = (segment_query[:, :, None] == segment_ids[:, None, :]) & (
        key_rows[None, None, :] <= query_rows[None, :, None]
    ) & (padding[:, None, :] == 1) | (key_rows[None, None, :] == query_rows[None, :, None])
    allowed = allowed[:, None, None]
    probs = soft_probs(score_block(queries, keys_all), allowed)
    attn_out = mix_values(probs.astype(jnp.bfloat16), values_all)
    out_full = lax.all_gather(out_weight, everyone, axis=0, tiled=True)
    attn_proj = times_rows(attn_out, out_full)
    after_attn = residual + rms_norm(attn_proj, gain_cols[:, 1])
    ffn_input = rms_norm(after_attn, gain_cols[:, 2]).astype(jnp.bfloat16)

    unit_weights = lax.all_gather(gate_up_weight, "chip", axis=0, tiled=True)
    down_units = lax.all_gather(down_weight, "chip", axis=0, tiled=True)
    ffn_all = lax.all_gather(ffn_input, column, axis=0, tiled=True)
    gate_part = times_rows(ffn_all, unit_weights[:, :model_width])
    up_part = times_rows(ffn_all, unit_weights[:, model_width:])
    hidden_part = geglu_parts(gate_part, up_part).astype(jnp.bfloat16)
    down_part = add_slice(hidden_part, down_units).astype(jnp.bfloat16)
    down_out = lax.psum_scatter(down_part, column, scatter_dimension=0, tiled=True).astype(
        jnp.float32
    )
    layer_out = after_attn + rms_norm(down_out, gain_cols[:, 3])
    layer_output = layer_out.astype(jnp.bfloat16).reshape(groups, piece_len, model_width)

    cotangent = output_cotangent.reshape(row_count, model_width).astype(jnp.float32)
    unused_last, pull_last = jax.vjp(rms_norm, down_out, gain_cols[:, 3])
    grad_down, grad_gain_last = pull_last(cotangent)
    grad_down_low = grad_down.astype(jnp.bfloat16)
    grad_down_all = lax.all_gather(grad_down_low, column, axis=0, tiled=True)
    grad_part = times_rows(grad_down_all, down_units)
    unused_units, pull_units = jax.vjp(geglu_parts, gate_part, up_part)
    grad_gate_part, grad_up_part = pull_units(grad_part)
    gate_low = grad_gate_part.astype(jnp.bfloat16)
    up_low = grad_up_part.astype(jnp.bfloat16)
    grad_ffn_part = add_slice(gate_low, unit_weights[:, :model_width]) + add_slice(
        up_low, unit_weights[:, model_width:]
    )
    grad_ffn_in = lax.psum_scatter(
        grad_ffn_part.astype(jnp.bfloat16), column, scatter_dimension=0, tiled=True
    ).astype(jnp.float32)
    gate_up_rows = jnp.concatenate(
        [
            outer_rows(gate_low, ffn_all).astype(jnp.bfloat16),
            outer_rows(up_low, ffn_all).astype(jnp.bfloat16),
        ],
        axis=1,
    )
    down_rows = outer_rows(hidden_part, grad_down_all).astype(jnp.bfloat16)
    gate_up_grad = lax.psum_scatter(
        gate_up_rows, "chip", scatter_dimension=0, tiled=True
    ).astype(jnp.float32)
    down_grad = lax.psum_scatter(down_rows, "chip", scatter_dimension=0, tiled=True).astype(
        jnp.float32
    )

    unused_mid, pull_mid = jax.vjp(rms_norm, after_attn, gain_cols[:, 2])
    grad_after_ffn, grad_gain_mid = pull_mid(grad_ffn_in)
    grad_after = cotangent + grad_after_ffn
    unused_post, pull_post = jax.vjp(rms_norm, attn_proj, gain_cols[:, 1])
    grad_proj, grad_gain_post = pull_post(grad_after)
    grad_proj_low = grad_proj.astype(jnp.bfloat16)
    grad_attn = add_slice(grad_proj_low, out_full).astype(jnp.bfloat16)
    scaled = score_block(queries, keys_all)
    probs, pull_probs = jax.vjp(partial(soft_probs, allowed=allowed), scaled)
    grad_heads = grad_attn.reshape(groups, piece_len, KV_HEADS, group_size, HEAD_DIM)
    query_heads = queries.reshape(groups, piece_len, KV_HEADS, group_size, HEAD_DIM)
    key_heads = keys_all.reshape(groups, seq_len, KV_HEADS, HEAD_DIM)
    value_heads = values_all.reshape(groups, seq_len, KV_HEADS, HEAD_DIM)
    grad_probs = jnp.einsum(
        "spkgd,slkd->skgpl", grad_heads, value_heads, preferred_element_type=jnp.float32
    )
    (grad_scaled,) = pull_probs(grad_probs)
    grad_scaled_low = grad_scaled.astype(jnp.bfloat16)
    inverse_root = 1.0 / math.sqrt(HEAD_DIM)
    grad_query_rot = (
        jnp.einsum(
            "skgpl,slkd->spkgd", grad_scaled_low, key_heads, preferred_element_type=jnp.float32
        )
        * inverse_root
    )
    grad_key_rot = (
        jnp.einsum(
            "skgpl,spkgd->slkd", grad_scaled_low, query_heads, preferred_element_type=jnp.float32
        )
        * inverse_root
    )
    grad_value_part = jnp.einsum(
        "skgpl,spkgd->slkd",
        probs.astype(jnp.bfloat16),
        grad_heads,
        preferred_element_type=jnp.float32,
    )
    both_grads = jnp.concatenate(
        [
            grad_key_rot.reshape(groups, seq_len, key_width),
            grad_value_part.reshape(groups, seq_len, key_width),
        ],
        axis=2,
    ).astype(jnp.bfloat16)
    both_summed = lax.psum_scatter(both_grads, plane, scatter_dimension=1, tiled=True)
    both_summed = both_summed.astype(jnp.float32).reshape(row_count, 2 * key_width)
    key_summed = both_summed[:, :key_width]
    value_summed = both_summed[:, key_width:]
    grad_queries = rotate_back(
        grad_query_rot.reshape(row_count, HEADS, HEAD_DIM), cosine, sine_part
    ).reshape(row_count, query_width)
    grad_keys = rotate_back(
        key_summed.reshape(row_count, KV_HEADS, HEAD_DIM), cosine, sine_part
    ).reshape(row_count, key_width)
    grad_projected = jnp.concatenate([grad_queries, grad_keys, value_summed], axis=1).astype(
        jnp.bfloat16
    )
    grad_attn_in = times_rows(grad_projected, qkv_full)
    unused_first, pull_first = jax.vjp(rms_norm, residual, gain_cols[:, 0])
    grad_res_first, grad_gain_first = pull_first(grad_attn_in)
    input_grad = (grad_after + grad_res_first).reshape(groups, piece_len, model_width)
    gain_terms = jnp.stack([grad_gain_first, grad_gain_post, grad_gain_mid, grad_gain_last], axis=1)
    qkv_part = outer_rows(attn_input, grad_projected).astype(jnp.bfloat16)
    out_part = outer_rows(grad_proj_low, attn_out).astype(jnp.bfloat16)
    qkv_grad = lax.psum_scatter(qkv_part, everyone, scatter_dimension=0, tiled=True).astype(
        jnp.float32
    )
    out_proj_grad = lax.psum_scatter(out_part, everyone, scatter_dimension=0, tiled=True).astype(
        jnp.float32
    )
    gain_grad = lax.psum_scatter(gain_terms, everyone, scatter_dimension=0, tiled=True)
    return (layer_output, input_grad, gain_grad, qkv_grad, out_proj_grad, gate_up_grad, down_grad)


def per_device_by_heads(
    n_seq,
    hidden_in,
    norm_gains,
    qkv_weight,
    out_weight,
    gate_up_weight,
    down_weight,
    output_cotangent,
    segment_ids,
    padding,
    positions,
):
    groups, piece_len, model_width = hidden_in.shape
    row_count = groups * piece_len
    seq_len = segment_ids.shape[1]
    n_chip = KV_HEADS
    n_plane = 2 * n_chip
    group_size = HEADS // KV_HEADS
    query_width = HEADS * HEAD_DIM
    key_width = KV_HEADS * HEAD_DIM
    own_width = group_size * HEAD_DIM
    part_width = own_width + 2 * HEAD_DIM
    block_width = part_width + own_width
    weight_rows = qkv_weight.shape[0]
    extra_rows = 16 - weight_rows % 16
    block_rows = weight_rows + extra_rows
    core = lax.axis_index("core")

    gain_rows = jnp.pad(
        norm_gains.T, ((0, extra_rows - norm_gains.shape[1]), (0, block_width - weight_rows))
    )
    blocks = jnp.stack(
        [
            jnp.concatenate(
                [
                    jnp.concatenate(
                        [
                            qkv_weight[:, c * own_width : (c + 1) * own_width],
                            qkv_weight[
                                :, query_width + c * HEAD_DIM : query_width + (c + 1) * HEAD_DIM
                            ],
                            qkv_weight[
                                :,
                                query_width + key_width + c * HEAD_DIM : query_width
                                + key_width
                                + (c + 1) * HEAD_DIM,
                            ],
                            out_weight[:, c * own_width : (c + 1) * own_width],
                        ],
                        axis=1,
                    ),
                    gain_rows,
                ],
                axis=0,
            )
            for c in range(n_chip)
        ]
    )
    hidden_all, blocks_all = gather_first(n_seq, hidden_in, blocks)
    unit_weights = lax.all_gather(gate_up_weight, "chip", axis=0, tiled=True)
    blocks_all, down_weight = lax.optimization_barrier((blocks_all, down_weight))
    early = down_weight.shape[0] - down_weight.shape[0] // LATE
    down_x, down_y = send_beside(down_weight[:early], 1), send_beside(down_weight[:early], 2)
    blocks_all = blocks_all.transpose(0, 2, 1, 3, 4)
    own_weights = blocks_all[:, :, :, :weight_rows].reshape(model_width, block_width)
    own_qkv = own_weights[:, :part_width]
    own_out = own_weights[:, part_width:]
    gain_cols = (
        blocks_all[:, :, :, weight_rows : weight_rows + norm_gains.shape[1], :weight_rows]
        .transpose(0, 1, 2, 4, 3)
        .reshape(model_width, norm_gains.shape[1])
        .astype(jnp.float32)
    )

    seq_rows = hidden_all.reshape(seq_len, model_width).astype(jnp.float32)
    seq_factor = lax.rsqrt(jnp.mean(seq_rows * seq_rows, axis=-1, keepdims=True) + EPSILON)
    attn_input = (seq_rows * seq_factor * gain_cols[:, 0]).astype(jnp.bfloat16)
    projected = add_slice(attn_input, own_qkv)
    segment = lax.dynamic_index_in_dim(segment_ids, core, 0, keepdims=False)
    valid = lax.dynamic_index_in_dim(padding, core, 0, keepdims=False)
    token = jnp.arange(seq_len, dtype=jnp.int32)
    document_start = jnp.min(
        jnp.where(segment[:, None] == segment[None, :], token[None, :], seq_len), axis=1
    )
    cosine, sine_part = rotary_tables(token - document_start, HEAD_DIM)
    queries = (
        rotate(projected[:, :own_width].reshape(seq_len, group_size, HEAD_DIM), cosine, sine_part)
        .astype(jnp.bfloat16)
        .reshape(seq_len, own_width)
    )
    keys = (
        rotate(
            projected[:, own_width : own_width + HEAD_DIM].reshape(seq_len, 1, HEAD_DIM),
            cosine,
            sine_part,
        )
        .astype(jnp.bfloat16)
        .reshape(seq_len, HEAD_DIM)
    )
    values = projected[:, own_width + HEAD_DIM :].astype(jnp.bfloat16)
    segment_col = segment[:, None]
    segment_row = jnp.where(valid == 1, segment, -1)[None, :]
    attn_out = attend(queries, keys, values, segment_col, segment_row)
    proj_parts = times_rows(attn_out, own_out).astype(jnp.bfloat16)
    proj_parts, down_across = merge_plane(
        proj_parts.reshape(n_plane, piece_len, model_width), down_x, down_y, 2
    )
    down_units = (down_weight, down_x, down_y, down_across[0], down_across[1])

    def sum_parts(parts):
        return jnp.sum(parts.astype(jnp.float32), axis=0).reshape(row_count, model_width)

    attn_proj = sum_parts(proj_parts)
    residual = hidden_in.reshape(row_count, model_width).astype(jnp.float32)
    after_attn = residual + rms_norm(attn_proj, gain_cols[:, 1])
    ffn_input = rms_norm(after_attn, gain_cols[:, 2]).astype(jnp.bfloat16)

    pieces = (groups, piece_len, model_width)
    down_out, ffn_all, down_late, gate_part, up_part, hidden_part = run_units(
        n_seq, ffn_input.reshape(pieces), unit_weights, down_units
    )
    down_out = down_out.reshape(row_count, model_width)
    layer_out = after_attn + rms_norm(down_out, gain_cols[:, 3])
    layer_output = layer_out.astype(jnp.bfloat16).reshape(pieces)

    cotangent = output_cotangent.reshape(row_count, model_width).astype(jnp.float32)
    unused_last, pull_last = jax.vjp(rms_norm, down_out, gain_cols[:, 3])
    grad_down, grad_gain_last = pull_last(cotangent)
    grad_ffn_in, gate_low, up_low, early_rows, *late = run_units(
        n_seq,
        grad_down.astype(jnp.bfloat16).reshape(pieces),
        unit_weights,
        down_units,
        (down_late, gate_part, up_part, hidden_part),
    )
    grad_ffn_in = grad_ffn_in.reshape(row_count, model_width)
    chip = lax.axis_index("chip")
    chips = jnp.arange(n_chip, dtype=jnp.int32)[:, None, None]
    down_columns = []
    for grads, parts in zip(late[:LATE_COLUMNS], late[LATE_COLUMNS:]):
        own = lax.dynamic_slice_in_dim(grads, chip * parts.shape[1], parts.shape[1], 0)
        parts = jnp.where(chips == chip, own[None], parts)
        down_columns.append(jnp.sum(parts.astype(jnp.float32), axis=0))
    if LATE_COLUMNS < 3:
        early_grad = lax.psum_scatter(early_rows, "chip", scatter_dimension=0, tiled=True)
        down_columns.append(early_grad.astype(jnp.float32))
    down_grad = jnp.concatenate(down_columns, axis=1)

    unused_mid, pull_mid = jax.vjp(rms_norm, after_attn, gain_cols[:, 2])
    grad_after_ffn, grad_gain_mid = pull_mid(grad_ffn_in)
    grad_after = cotangent + grad_after_ffn
    unused_post, pull_post = jax.vjp(rms_norm, attn_proj, gain_cols[:, 1])
    grad_proj, grad_gain_post = pull_post(grad_after)
    grad_proj_low = grad_proj.astype(jnp.bfloat16)

    grad_proj_all, gate_up_rows = spread_plane(
        grad_proj_low.reshape(groups, piece_len, model_width), gate_low, up_low, ffn_all
    )
    gate_up_grad = lax.psum_scatter(
        gate_up_rows, "chip", scatter_dimension=0, tiled=True
    ).astype(jnp.float32)
    grad_proj_all = grad_proj_all.reshape(seq_len, model_width)
    grad_attn = add_slice(grad_proj_all, own_out).astype(jnp.bfloat16)
    grad_projected = attend_back(
        queries,
        keys,
        values,
        segment_col,
        segment_row,
        grad_attn,
        cosine[:, 0],
        sine_part[:, 0],
    )
    grad_in_part = times_rows(grad_projected, own_qkv)
    grad_gain_first = jnp.sum(grad_in_part * seq_rows * seq_factor, axis=0)
    gain_terms = (
        jnp.stack([grad_gain_first, grad_gain_post, grad_gain_mid, grad_gain_last])
        .reshape(-1, n_seq * n_plane, weight_rows)
        .transpose(1, 0, 2)
    )
    gain_terms = jnp.pad(
        gain_terms,
        ((0, 0), (0, extra_rows - gain_terms.shape[1]), (0, block_width - weight_rows)),
    )
    grad_blocks = weight_blocks(
        n_seq, attn_input, grad_projected, grad_proj_all, attn_out, gain_terms
    )
    grad_in_parts, grad_sums = sum_last(
        n_seq,
        grad_in_part.astype(jnp.bfloat16).reshape(n_plane, piece_len, model_width),
        grad_blocks,
    )
    grad_attn_in = sum_parts(grad_in_parts)
    factor = lax.rsqrt(jnp.mean(residual * residual, axis=-1, keepdims=True) + EPSILON)
    unused_first, pull_first = jax.vjp(rms_norm, residual, gain_cols[:, 0])
    grad_res_first, unused_gain = pull_first(grad_attn_in)
    input_grad = (grad_after + grad_res_first).reshape(groups, piece_len, model_width)

    weight_sums = grad_sums[:, :weight_rows].astype(jnp.float32)
    qkv_grad = jnp.concatenate(
        [weight_sums[c, :, :own_width] for c in range(n_chip)]
        + [weight_sums[c, :, own_width : own_width + HEAD_DIM] for c in range(n_chip)]
        + [weight_sums[c, :, own_width + HEAD_DIM : part_width] for c in range(n_chip)],
        axis=1,
    )
    out_proj_grad = jnp.concatenate(
        [weight_sums[c, :, part_width:] for c in range(n_chip)], axis=1
    )
    gain_grad = jnp.sum(
        grad_sums[:, weight_rows : weight_rows + norm_gains.shape[1], :weight_rows].astype(
            jnp.float32
        ),
        axis=0,
    ).T
    return (layer_output, input_grad, gain_grad, qkv_grad, out_proj_grad, gate_up_grad, down_grad)


def solution(mesh):
    n_seq = mesh.shape["seq"]
    n_ctx = mesh.shape["ctx"]
    split_mesh = jax.sharding.Mesh(
        mesh.devices.reshape(n_seq, n_ctx // 2, 2), ("seq", "chip", "core")
    )
    plane = ("chip", "core")
    rows = P(("seq", "chip", "core"), None)
    tokens = P("seq", plane, None)
    placed = (
        tokens,
        rows,
        rows,
        rows,
        rows,
        rows,
        tokens,
        P("seq", None),
        P("seq", None),
        P("seq", plane),
    )

    def step(*arrays):
        groups = arrays[0].shape[0]
        if n_ctx // 2 == KV_HEADS and groups == 2 and n_seq == 4:
            return per_device_by_heads(n_seq, *arrays)
        return per_device_general(*arrays)

    return jax.shard_map(
        step,
        mesh=split_mesh,
        in_specs=placed,
        out_specs=(tokens, tokens, rows, rows, rows, rows, rows),
        check_vma=False,
    )
```
